32 devices in a mesh: groups: 2 (over x), pts: 8 (over z, y), probe: 2 (over core).
Axes of the slice: x: 2, y: 2, z: 4, core: 2. Of those that a mesh axis runs over, the one named last changes fastest.
Arguments:
- systems: float32 [32, 12288], P('probe', ('groups', 'pts')), parts along dimension 1, may hold values from -16 to 16, as said below
- features: float32 [8, 12288], P(None, ('groups', 'pts')), parts along dimension 1, may hold values from -4 to 4
- task_ids: int32 [12288], P(('groups', 'pts')), parts along dimension 0, may hold values from 0 to 15
- pattern: int32 [48, 7], P(('groups', 'pts')), parts along dimension 0, may hold values from 0 to 1, as said below
- aggregate: int32 [12288], P(('groups', 'pts')), parts along dimension 0, may hold values from 0 to 23
- coarse_inverse: float32 [48, 24], P(('groups', 'pts')), parts along dimension 0, as said below
- task_cov: float32 [32, 16], P('groups'), parts along dimension 0, as said below
- lengthscales: float32 [16], P('groups'), parts along dimension 0, may hold values from 1.5 to 4
- noise: float32 [32], P('groups'), parts along dimension 0, may hold values from 0.3 to 1
Outputs:
- solution: float32 [32, 12288], P('probe', ('groups', 'pts')), parts along dimension 1
- grad_lengths: float32 [16], P('groups'), parts along dimension 0
- grad_tasks: float32 [32, 16], P('groups'), parts along dimension 0
The draws below stay inside these ranges and needn't reach their ends.
There are 2 independent parts, one for each index of `groups`. The reference program is written for one: setup_inputs(seed, part) draws one part's arguments, and reference() takes and returns one part's arrays. A program takes and returns all parts, laid end to end along the dimension named above; each array names one. Nothing has to cross between parts.
Inputs may be any that keep to these rules, and one draw needn't show every extreme that they name: pattern[I, 3] = 1 for every block I; pattern[I, 3 + o] = pattern[I + o, 3 - o]; entries whose block I + o lies outside 0 to 23 are 0. `coarse_inverse`: symmetric and positive definite. `task_cov`: symmetric and positive definite. `systems`: row 0 holds the targets, the other rows probe vectors.
All inputs are finite; a program needn't handle non-finite values.
Results may differ from the reference program's by a relative error of at most 0.0003.
Values sent between devices are 32-bit elements; how exact they have to be, the bound alone decides.
No kernel may reach another device: no remote copies, remote signals or barrier semaphores. Data moves between devices by JAX's collectives and lax.ppermute only.
A program may use at most 128 MiB of HBM per device.

```python
import math
import jax
import jax.numpy as jnp
from jax import lax

BS = 256
REACH = 3
FEAT = 8
TASKS = 16
ITERS = 3
BLK_DEV = 3
NB = 24
NPTS = 6144
COARSE = 24
RHS = 32


def positive_matrix(key, order, low, high, coupling):
    entry_key, diag_key, scale_key, common_key = jax.random.split(key, 4)
    raw = jax.random.uniform(entry_key, (order, order), jnp.float32, -1.0, 1.0)
    symmetric = (raw + raw.T) * 0.5
    identity = jnp.eye(order, dtype=jnp.float32)
    lead = 1.0 + 0.4 * jax.random.uniform(diag_key, (order,), jnp.float32)
    core = identity * lead[:, None] + (1.0 - identity) * symmetric * (0.9 / order)
    common = jax.random.uniform(common_key, (order,), jnp.float32, 0.8, 1.2)
    mixed = (1.0 - coupling) * core + coupling * common[:, None] * common[None, :]
    scales = jnp.exp(jax.random.uniform(scale_key, (order,), jnp.float32, jnp.log(low), jnp.log(high)))
    root = jnp.sqrt(scales)
    return mixed * root[:, None] * root[None, :]


def draw_systems(key, part):
    key = jax.random.fold_in(key, 5)
    position = jnp.arange(NPTS, dtype=jnp.float32) / NPTS
    values = jnp.clip(jax.random.normal(key, (RHS, NPTS), jnp.float32), -4.0, 4.0)
    rise = jnp.exp(jnp.log(3.0) * position)
    return values * rise[None, :]


def draw_pattern(key, part):
    key = jax.random.fold_in(key, 11)
    rate_key, bit_key = jax.random.split(key)
    rates = jax.random.randint(rate_key, (NB // BLK_DEV,), 0, 5)
    block_rate = jnp.repeat(rates, BLK_DEV)
    bits = jax.random.randint(bit_key, (NB, REACH), 0, 4)
    index = jnp.arange(NB, dtype=jnp.int32)
    offsets = jnp.arange(1, REACH + 1, dtype=jnp.int32)
    inside = index[:, None] + offsets[None, :] < NB
    forward = ((bits < block_rate[:, None]) & inside).astype(jnp.int32)
    padded = jnp.pad(forward, ((REACH, 0), (0, 0)))
    backward = padded[index[:, None] + REACH - offsets[None, :], offsets[None, :] - 1]
    ones = jnp.ones((NB, 1), jnp.int32)
    return jnp.concatenate([backward[:, ::-1], ones, forward], axis=1)


def draw_coarse_inverse(key, part):
    key = jax.random.fold_in(key, 7)
    return positive_matrix(key, COARSE, 0.01, 0.05, 0.0)


def draw_task_cov(key, part):
    key = jax.random.fold_in(key, 9)
    return positive_matrix(key, TASKS, 0.5, 2.0, 0.7)


def plant(result, stream_key, smallest, top_value):
    index_at = [jax.random.randint(jax.random.fold_in(stream_key, axis), (), 0, length) for axis, length in enumerate(result.shape)]
    longest = result.shape.index(max(result.shape))
    beside = index_at[:longest] + [(index_at[longest] + 1) % result.shape[longest]] + index_at[longest + 1:]
    return result.at[tuple(index_at)].set(smallest).at[tuple(beside)].set(top_value)


def shard_levels(rng, dims, cuts, low, top_value):
    def one(dim, shards_of):
        draws = jax.random.uniform(jax.random.fold_in(jax.random.fold_in(rng, 6), dim), (shards_of,), jnp.float32, low / len(cuts), top_value / len(cuts))
        return jnp.repeat(jnp.exp(draws), dims[dim] // shards_of).reshape((-1,) + (1,) * (len(dims) - dim - 1))

    factor_of = one(*cuts[0])
    for cut in cuts[1:]:
        factor_of = factor_of * one(*cut)
    return factor_of


def bell_draw(key, dims, width, bound, cuts=(), kind=jnp.bfloat16):
    entries = width * jax.random.normal(key, dims, jnp.float32)
    if cuts:
        entries = entries * shard_levels(key, dims, cuts, -0.22, 0.18)
    return jnp.clip(entries, -bound, bound).astype(kind)


def setup_inputs(seed: int = 0, part: int = 0) -> dict:
    splits = jax.random.split(jax.random.key(seed), 10)
    own_keys = jax.random.split(jax.random.fold_in(splits[9], part), 10)
    systems = draw_systems(jax.random.fold_in(jax.random.fold_in(splits[9], part), 71), part)
    features = bell_draw(own_keys[1], (FEAT, NPTS), 1.0, 4.0, ((1, 8),), jnp.float32)
    task_ids = plant(jax.random.randint(own_keys[2], (NPTS,), 0, TASKS), jax.random.fold_in(own_keys[2], 1), 0, TASKS - 1).astype(jnp.int32)
    pattern = draw_pattern(jax.random.fold_in(jax.random.fold_in(splits[9], part), 71), part)
    aggregate = plant(jax.random.randint(own_keys[4], (NPTS,), 0, COARSE), jax.random.fold_in(own_keys[4], 1), 0, COARSE - 1).astype(jnp.int32)
    coarse_inverse = draw_coarse_inverse(jax.random.fold_in(jax.random.fold_in(splits[9], part), 71), part)
    task_cov = draw_task_cov(jax.random.fold_in(jax.random.fold_in(splits[9], part), 71), part)
    lengthscales = jnp.clip(jnp.exp(jax.random.uniform(own_keys[7], (FEAT,), jnp.float32, math.log(1.5), math.log(4.0))), 1.5, 4.0)
    noise = jnp.clip(jnp.exp(jax.random.uniform(own_keys[8], (TASKS,), jnp.float32, math.log(0.3), math.log(1.0))), 0.3, 1.0)
    return {"systems": systems, "features": features, "task_ids": task_ids, "pattern": pattern, "aggregate": aggregate, "coarse_inverse": coarse_inverse, "task_cov": task_cov, "lengthscales": lengthscales, "noise": noise}


highest = lax.Precision.HIGHEST

def row_terms(index, scaled, task_table, scaled_pad, table_pad, weights, task_cov):
    start = (index * BS).astype(jnp.int32)
    span = (2 * REACH + 1) * BS
    left_scaled = lax.dynamic_slice_in_dim(scaled, start, BS, axis=1)
    left_table = lax.dynamic_slice_in_dim(task_table, start, BS, axis=1)
    near_scaled = lax.dynamic_slice_in_dim(scaled_pad, start, span, axis=1)
    near_table = lax.dynamic_slice_in_dim(table_pad, start, span, axis=1)
    cross = jnp.dot(left_scaled.T, near_scaled, precision=highest)
    distance = jnp.sum(left_scaled * left_scaled, axis=0)[:, None] + jnp.sum(near_scaled * near_scaled, axis=0)[None, :] - 2.0 * cross
    pair = jnp.dot(jnp.dot(left_table.T, task_cov, precision=highest), near_table, precision=highest)
    spread = jnp.repeat(weights[index], BS)
    similar = spread[None, :] * jnp.exp(-0.5 * distance)
    return (similar * pair, similar, left_scaled, left_table, near_scaled, near_table)

def reference(systems, features, task_ids, pattern, aggregate, coarse_inverse, task_cov, lengthscales, noise):
    slots = 2 * REACH + 1
    margin = REACH * BS
    scaled = features / lengthscales[:, None]
    task_table = (task_ids[None, :] == jnp.arange(TASKS, dtype=jnp.int32)[:, None]).astype(jnp.float32)
    scaled_pad = jnp.pad(scaled, ((0, 0), (margin, margin)))
    table_pad = jnp.pad(task_table, ((0, 0), (margin, margin)))
    column = jnp.arange(slots, dtype=jnp.int32)[None, :]
    weights = jnp.where(column == REACH, jnp.sum(pattern, axis=1)[:, None], pattern).astype(jnp.float32)
    noise_points = noise[task_ids]
    indices = jnp.arange(NB, dtype=jnp.int32)
    identity = jnp.eye(BS, dtype=jnp.float32)

    def terms(index):
        return row_terms(index, scaled, task_table, scaled_pad, table_pad, weights, task_cov)

    def operate(vectors):
        padded = jnp.pad(vectors, ((0, 0), (margin, margin)))

        def one_row(index):
            kernel = terms(index)[0]
            near = lax.dynamic_slice_in_dim(padded, (index * BS).astype(jnp.int32), slots * BS, axis=1)
            return jnp.dot(near, kernel.T, precision=highest)
        rows = lax.map(one_row, indices)
        return jnp.transpose(rows, (1, 0, 2)).reshape(vectors.shape) + noise_points[None, :] * vectors

    def invert(index):
        kernel = terms(index)[0]
        local_noise = lax.dynamic_slice_in_dim(noise_points, (index * BS).astype(jnp.int32), BS)
        block = kernel[:, REACH * BS:(REACH + 1) * BS] + jnp.diag(local_noise)
        factor = jnp.linalg.cholesky(block)
        return jax.scipy.linalg.cho_solve((factor, True), identity)
    jacobi = lax.map(invert, indices)

    def precondition(residual):
        local = jnp.einsum('bij,rbj->rbi', jacobi, residual.reshape(RHS, NB, BS), precision=highest).reshape(RHS, NPTS)
        totals = jax.ops.segment_sum(residual.T, aggregate, COARSE).T
        coarse = jnp.dot(totals, coarse_inverse.T, precision=highest)
        return local + coarse[:, aggregate]
    solution = jnp.zeros_like(systems)
    residual = systems
    pre = precondition(residual)
    direction = pre
    gamma = jnp.sum(residual * pre, axis=1)
    for step in range(ITERS):
        image = operate(direction)
        alpha = gamma / jnp.sum(direction * image, axis=1)
        solution = solution + alpha[:, None] * direction
        residual = residual - alpha[:, None] * image
        if step + 1 < ITERS:
            pre = precondition(residual)
            gamma_new = jnp.sum(residual * pre, axis=1)
            direction = pre + (gamma_new / gamma)[:, None] * direction
            gamma = gamma_new
    rows = jnp.arange(RHS, dtype=jnp.int32)
    coef = jnp.where(rows == 0, 0.5, -0.5 / (RHS - 1)) / NPTS
    right = jnp.where((rows == 0)[:, None], solution, systems)
    weighted = solution * coef[:, None]
    right_pad = jnp.pad(right, ((0, 0), (margin, margin)))

    def gradient_row(index):
        kernel, similar, left_scaled, left_table, near_scaled, near_table = terms(index)
        start = (index * BS).astype(jnp.int32)
        left = lax.dynamic_slice_in_dim(weighted, start, BS, axis=1)
        near = lax.dynamic_slice_in_dim(right_pad, start, slots * BS, axis=1)
        outer = jnp.dot(left.T, near, precision=highest)
        energy = outer * kernel
        held = outer * similar
        projected = jnp.dot(energy, near_scaled.T, precision=highest)
        lengths = jnp.dot(left_scaled * left_scaled, jnp.sum(energy, axis=1), precision=highest)
        lengths = lengths + jnp.dot(near_scaled * near_scaled, jnp.sum(energy, axis=0), precision=highest)
        lengths = lengths - 2.0 * jnp.sum(left_scaled * projected.T, axis=1)
        tasks = jnp.dot(jnp.dot(left_table, held, precision=highest), near_table.T, precision=highest)
        return (lengths, tasks)
    lengths, tasks = lax.map(gradient_row, indices)
    return (solution, jnp.sum(lengths, axis=0), jnp.sum(tasks, axis=0))
```

```python
import functools

import jax
import jax.numpy as jnp
from jax import lax
from jax.experimental import pallas as pl
from jax.experimental.pallas import tpu as pltpu
from jax.sharding import PartitionSpec as P

BS = 256
REACH = 3
FEAT = 8
TASKS = 16
ITERS = 3
SLOTS = 2 * REACH + 1
BAND = SLOTS * BS
BASE = 32
GROUP = 4
LANES = 128

highest = lax.Precision.HIGHEST
f32 = jnp.float32
bf16 = jnp.bfloat16
NN = (((1,), (0,)), ((), ()))
NT = (((1,), (1,)), ((), ()))
TN = (((0,), (0,)), ((), ()))


def dot(a, b, dims=NN, precision=None):
    return lax.dot_general(a, b, dims, precision=precision, preferred_element_type=f32)


def iota(shape, dim):
    return lax.broadcasted_iota(jnp.int32, shape, dim)


def split(x, parts):
    out = []
    for _ in range(parts - 1):
        head = x.astype(bf16).astype(f32)
        out.append(head)
        x = x - head
    out.append(x.astype(bf16).astype(f32))
    return out


def column(ref, size):
    rows = iota((size, 1), 0)
    out = jnp.zeros((size, 1), f32)
    for i in range(size):
        out = jnp.where(rows == i, ref[i], out)
    return out


def one_hot(ids, size):
    return (iota((size, ids.shape[1]), 0).astype(f32) == ids).astype(f32)


def noise_row(noise_ref, ids):
    out = jnp.zeros(ids.shape, f32)
    for t in range(TASKS):
        out = jnp.where(ids == float(t), noise_ref[t], out)
    return out


def weight(pat_ref, block, offset):
    if offset != REACH:
        return pat_ref[block, offset].astype(f32)
    total = pat_ref[block, 0]
    for o in range(1, SLOTS):
        total = total + pat_ref[block, o]
    return total.astype(f32)


def near_stack(scaled, table):
    s0, s1, s2 = split(scaled, 3)
    n0, n1, n2 = split(-0.5 * jnp.sum(scaled * scaled, axis=0, keepdims=True), 3)
    rows = iota(scaled.shape, 0)
    norms = jnp.where(rows == 0, n0, jnp.where(rows == 1, n1, jnp.where(rows == 2, n2, 0.0)))
    pad = jnp.zeros((LANES - 7 * FEAT - 3 * TASKS, scaled.shape[1]), f32)
    return jnp.concatenate(
        [s0, s0, s1, s1, s0, s2, norms, table, table, table, pad], axis=0
    ).astype(bf16)


def own_stack(scaled, table, cov):
    s0, s1, s2 = split(scaled, 3)
    rows = iota(scaled.shape, 0)
    ones = jnp.where(rows < 3, 1.0, 0.0)
    count = scaled.shape[1]
    c0, c1, c2 = split(cov, 3)
    picked = dot(
        jnp.concatenate([c0, c1, c2], axis=0).astype(bf16), table.astype(bf16)
    )
    tail = LANES - 7 * FEAT - 3 * TASKS
    left = jnp.concatenate(
        [s0, s1, s0, s1, s2, s0, ones, jnp.zeros((3 * TASKS + tail, count), f32)], axis=0
    ).astype(bf16)
    right = jnp.concatenate(
        [jnp.zeros((7 * FEAT, count), f32), picked, jnp.zeros((tail, count), f32)], axis=0
    ).astype(bf16)
    return left, right, -0.5 * jnp.sum(scaled * scaled, axis=0, keepdims=True)


def small_inverse(p):
    n = len(p)
    if n == 1:
        return [[1.0 / p[0][0]]]
    if n == 2:
        a, b, d = p[0][0], p[0][1], p[1][1]
        r = 1.0 / (a * d - b * b)
        off = -b * r
        return [[d * r, off], [off, a * r]]
    h = n // 2
    ainv = small_inverse([row[:h] for row in p[:h]])
    b = [row[h:] for row in p[:h]]
    t = [[sum(ainv[i][k] * b[k][j] for k in range(h)) for j in range(h)] for i in range(h)]
    s = [[None] * h for _ in range(h)]
    for i in range(h):
        for j in range(i, h):
            s[i][j] = s[j][i] = p[h + i][h + j] - sum(b[k][i] * t[k][j] for k in range(h))
    sinv = small_inverse(s)
    u = [[sum(t[i][k] * sinv[k][j] for k in range(h)) for j in range(h)] for i in range(h)]
    out = [[None] * n for _ in range(n)]
    for i in range(h):
        for j in range(h):
            out[h + i][h + j] = sinv[i][j]
            out[i][h + j] = out[h + j][i] = -u[i][j]
    for i in range(h):
        for j in range(i, h):
            out[i][j] = out[j][i] = ainv[i][j] + sum(u[i][k] * t[j][k] for k in range(h))
    return out


def sweep_base(cells):
    lane = iota((BASE, LANES), 1)
    start = lane - lane % BASE
    inner = iota((1, LANES), 1) % BASE
    sub = iota((BASE, 1), 0)
    for g in range(BASE // GROUP):
        first = g * GROUP
        cols = [
            jnp.take_along_axis(cells, start + (first + t), axis=1, mode="promise_in_bounds")
            for t in range(GROUP)
        ]
        rows = [cells[first + t : first + t + 1, :] for t in range(GROUP)]
        pivots = [[cols[u][first + t : first + t + 1, :] for u in range(GROUP)] for t in range(GROUP)]
        inv = small_inverse(pivots)
        rows = [jnp.where(inner == first + t, -1.0, rows[t]) for t in range(GROUP)]
        group = (inner >= first) & (inner < first + GROUP)
        for t in range(GROUP):
            rows[t] = jnp.where(group & (inner != first + t), 0.0, rows[t])
        new = [sum(inv[t][u] * rows[u] for u in range(GROUP)) for t in range(GROUP)]
        cells = jnp.where(group, 0.0, cells)
        for t in range(GROUP):
            cells = cells - cols[t] * new[t]
        for t in range(GROUP):
            cells = jnp.where(sub == first + t, new[t], cells)
    return cells


def invert_kernel(pat_ref, len_ref, noise_ref, pack_ref, cov_ref, jac_ref, pre_ref, work):
    blocks = work.shape[0]
    scaled = pack_ref[0:FEAT, :] / column(len_ref, FEAT)
    ids = pack_ref[FEAT : FEAT + 1, :]
    table = one_hot(ids, TASKS)
    noise = noise_row(noise_ref, ids)
    cov = cov_ref[...]
    near = near_stack(scaled, table)
    left, right, norm = own_stack(scaled, table, cov)
    eye = iota((BS, BS), 0) == iota((BS, BS), 1)
    for m in range(blocks):
        at = slice(m * BS, (m + 1) * BS)
        exponent = dot(near[:, at], left[:, at], TN) + norm[:, at]
        pair = dot(near[:, at], right[:, at], TN)
        block = weight(pat_ref, m, REACH) * jnp.exp(exponent) * pair
        work[m] = block + jnp.where(eye, noise[:, at], 0.0)
    seg = iota((BASE, LANES), 1) // BASE
    wide = iota((BASE, BS), 1)
    deep = iota((BASE, BS), 0)
    for k in range(BS // BASE):
        first = k * BASE
        tile, inside = first // LANES, first % LANES
        strips = [work[m, first : first + BASE, :] for m in range(blocks)]
        cells = jnp.where(iota((BASE, LANES), 1) % BASE == iota((BASE, LANES), 0), 1.0, 0.0)
        for m in range(blocks):
            piece = strips[m][:, tile * LANES : (tile + 1) * LANES]
            shift = (BASE * m - inside) % LANES
            if shift:
                piece = pltpu.roll(piece, shift, axis=1)
            cells = jnp.where(seg == m, piece, cells)
        inv = -sweep_base(cells)
        held = (wide >= first) & (wide < first + BASE)
        minus = jnp.where(wide - first == deep, -1.0, 0.0)
        stack = jnp.concatenate(
            [jnp.where(held, minus, s) for s in strips]
            + [jnp.zeros((LANES - blocks * BASE, BS), f32)],
            axis=0,
        )
        spread = jnp.concatenate([jnp.where(seg == m, inv, 0.0) for m in range(blocks)], axis=0)
        new = dot(spread, stack, precision=highest)
        gone = (iota((1, BS), 1) >= first) & (iota((1, BS), 1) < first + BASE)
        for m in range(blocks):
            row = new[m * BASE : (m + 1) * BASE, :]
            r0, r1, r2 = split(strips[m], 3)
            p0, p1, p2 = split(row, 3)
            a = jnp.concatenate([r0, r0, r1, r1, r0, r2], axis=0).astype(bf16)
            b = jnp.concatenate([p0, p1, p0, p1, p2, p0], axis=0).astype(bf16)
            work[m] = jnp.where(gone, 0.0, work[m]) - dot(a, b, TN)
            work[m, first : first + BASE, :] = row
    base = FEAT + 8
    for m in range(blocks):
        at = slice(m * BS, (m + 1) * BS)
        inv = -work[m]
        jac_ref[m] = inv
        pre_ref[:, at] = dot(pack_ref[base:, at], inv, precision=highest)


def build_kernel(
    pat_ref, len_ref, own_ref, left_ref, right_ref, cov_ref, hi_ref, lo_ref, sim_ref
):
    blocks = hi_ref.shape[0]
    lens = column(len_ref, FEAT)
    pack = jnp.concatenate(
        [left_ref[0 : FEAT + 8, :], own_ref[0 : FEAT + 8, :], right_ref[0 : FEAT + 8, :]], axis=1
    )
    scaled = pack[0:FEAT] / lens
    table = one_hot(pack[FEAT : FEAT + 1], TASKS)
    near = near_stack(scaled, table)
    width = blocks * BS
    own = slice(width, 2 * width)
    left, right, norm = own_stack(scaled[:, own], table[:, own], cov_ref[...])
    edge = width - REACH * BS
    for m in range(blocks):
        at = slice(m * BS, (m + 1) * BS)
        for o in range(SLOTS):
            j = edge + (m + o) * BS
            part = near[:, j : j + BS]
            exponent = dot(part, left[:, at], TN) + norm[:, at]
            pair = dot(part, right[:, at], TN)
            similar = weight(pat_ref, m, o) * jnp.exp(exponent)
            kernel = similar * pair
            head = kernel.astype(bf16)
            rows = slice(o * BS, (o + 1) * BS)
            sim_ref[m, rows, :] = similar
            hi_ref[m, rows, :] = head
            lo_ref[m, rows, :] = (kernel - head.astype(f32)).astype(bf16)


def operate(vectors, noise, own, hi_ref, lo_ref):
    rows = vectors.shape[0]
    head, tail = (part.astype(bf16) for part in split(vectors, 2))
    both = jnp.concatenate([head, tail], axis=0)
    out = []
    for m in range(hi_ref.shape[0]):
        at = slice(m * BS, m * BS + BAND)
        first = dot(both[:, at], hi_ref[m])
        out.append(first[:rows] + first[rows:] + dot(head[:, at], lo_ref[m]))
    return jnp.concatenate(out, axis=1) + noise * own


def smooth(image, jac_ref):
    return jnp.concatenate(
        [
            dot(image[:, m * BS : (m + 1) * BS], jac_ref[m], precision=highest)
            for m in range(jac_ref.shape[0])
        ],
        axis=1,
    )


def first_kernel(
    noise_ref, own_ref, left_ref, right_ref, pre_ref, prel_ref, prer_ref, hi_ref, lo_ref, jac_ref,
    image_ref, next_ref,
):
    count, width = pre_ref.shape
    coarse = image_ref.shape[0] - count
    pre = jnp.concatenate([prel_ref[...], pre_ref[...], prer_ref[...]], axis=1)
    row = slice(FEAT + 1, FEAT + 2)
    which = jnp.concatenate([left_ref[row, :], own_ref[row, :], right_ref[row, :]], axis=1)
    ext = jnp.concatenate([pre, one_hot(which, coarse)], axis=0)
    edge = width - REACH * BS
    noise = noise_row(noise_ref, own_ref[FEAT : FEAT + 1, :])
    image = operate(
        ext[:, edge : 3 * width - edge], noise, ext[:, width : 2 * width], hi_ref, lo_ref
    )
    image_ref[...] = image
    next_ref[...] = smooth(image, jac_ref)


def second_kernel(
    noise_ref, own_ref, vec_ref, vecl_ref, vecr_ref, hi_ref, lo_ref, jac_ref, image_ref, next_ref
):
    width = vec_ref.shape[1]
    edge = width - REACH * BS
    ext = jnp.concatenate([vecl_ref[:, edge:], vec_ref[...], vecr_ref[:, : width - edge]], axis=1)
    noise = noise_row(noise_ref, own_ref[FEAT : FEAT + 1, :])
    image = operate(ext, noise, vec_ref[...], hi_ref, lo_ref)
    image_ref[...] = image
    next_ref[...] = smooth(image, jac_ref)


def moment_kernel(
    noise_ref, own_ref, vec_ref, vecl_ref, vecr_ref, hi_ref, lo_ref, pre_ref, d1_ref, v0_ref,
    v1_ref, coarse_ref, out_ref,
):
    count, width = pre_ref.shape
    rows = vec_ref.shape[0]
    coarse = rows - count
    lanes = out_ref.shape[1]
    pitch = pitch_of(coarse)
    edge = width - REACH * BS
    ext = jnp.concatenate([vecl_ref[:, edge:], vec_ref[...], vecr_ref[:, : width - edge]], axis=1)
    noise = noise_row(noise_ref, own_ref[FEAT : FEAT + 1, :])
    d2 = vec_ref[...]
    v2 = operate(ext, noise, d2, hi_ref, lo_ref)
    base = FEAT + 8
    systems = own_ref[base:, :]
    pre = pre_ref[...]
    z = one_hot(own_ref[FEAT + 1 : FEAT + 2, :], coarse)
    d1, v0, v1 = d1_ref[...], v0_ref[...], v1_ref[...]
    gap = jnp.zeros((pitch - coarse, width), f32)

    def stacked(parts):
        cells = []
        for k in range(lanes // pitch):
            if k in parts:
                cells.append(jnp.concatenate([parts[k], gap], axis=0))
            else:
                cells.append(jnp.zeros((pitch, width), f32))
        return jnp.concatenate(cells, axis=0)

    high = lax.Precision.HIGH
    residual = jnp.concatenate([systems, jnp.zeros((coarse, width), f32)], axis=0)
    total = dot(v0, stacked({0: z, 1: d1[count:]}), NT, high)
    total = total + dot(v1, stacked({2: d1[count:], 3: d2[count:]}), NT, high)
    total = total + dot(v2, stacked({4: d2[count:]}), NT, high)
    total = total + dot(residual, stacked({5: z}), NT, high)
    own = [
        pre * v0[:count],
        d1[:count] * v0[:count],
        d1[:count] * v1[:count],
        d2[:count] * v1[:count],
        d2[:count] * v2[:count],
        systems * pre,
    ]
    lane = iota((count, lanes), 1)
    top = total[:count]
    for k, value in enumerate(own):
        top = jnp.where(lane == k * pitch + coarse, jnp.sum(value, axis=1, keepdims=True), top)
    out_ref[...] = jnp.concatenate([top, total[count:]], axis=0) + coarse_ref[...]


def pitch_of(coarse):
    return BASE if coarse < BASE else -(-(coarse + 1) // LANES) * LANES


def lanes_of(coarse):
    return -(-7 * pitch_of(coarse) // LANES) * LANES


def final_kernel(
    scalar_ref, len_ref, gram_ref, own_ref, left_ref, right_ref, pre_ref, prel_ref, prer_ref,
    d1_ref, d1l_ref, d1r_ref, d2_ref, d2l_ref, d2r_ref, hi_ref, lo_ref, sim_ref, coef_ref, cov_ref,
    sol_ref, grad_ref,
):
    count, width = pre_ref.shape
    rows = d1_ref.shape[0]
    coarse = rows - count
    pitch = pitch_of(coarse)
    wide = -(-3 * pitch // LANES) * LANES
    blocks = width // BS
    edge = width - REACH * BS
    gram = gram_ref[...]
    lane = iota((1, wide), 1)
    slot, inside = lane // pitch, lane % pitch
    live = lane < 3 * pitch
    is_vec = live & (inside < coarse)
    is_one = live & (inside == coarse)

    def shifted(j):
        return jnp.where(live, gram[:, j * pitch : j * pitch + wide], 0.0)

    moved = [shifted(j) for j in range(3)]
    own = [m[:count] for m in moved]
    gap = jnp.zeros((pitch - coarse, wide), f32)
    hankel = jnp.concatenate(
        [
            jnp.concatenate([jnp.where(is_vec, m[count:], 0.0), gap], axis=0)
            for m in moved
        ]
        + ([jnp.zeros((wide - 3 * pitch, wide), f32)] if wide > 3 * pitch else []),
        axis=0,
    )
    block0 = lane < pitch
    inverse = gram[:coarse, 6 * pitch : 7 * pitch]
    if pitch < wide:
        inverse = jnp.concatenate([inverse, jnp.zeros((coarse, wide - pitch), f32)], axis=1)
    inverse = jnp.where(lane < coarse, inverse, 0.0)
    inverse = jnp.concatenate([inverse, jnp.zeros((wide - coarse, wide), f32)], axis=0)
    start = gram[:count, 5 * pitch : 6 * pitch]
    if pitch < wide:
        start = jnp.concatenate([start, jnp.zeros((count, wide - pitch), f32)], axis=1)
    against = jnp.where(
        block0, start, jnp.where(live, pltpu.roll(jnp.where(live, own[0], 0.0), pitch, axis=1), 0.0)
    )

    def total(x):
        return jnp.sum(x, axis=1, keepdims=True)

    def scalars(u, i):
        return total(jnp.where(lane == i * pitch + coarse, u, 0.0))

    def metric(u):
        out = dot(jnp.where(is_vec, u, 0.0), hankel, precision=highest)
        for j in range(3):
            out = out + scalars(u, j) * own[j]
        out = jnp.where(is_vec, out, 0.0)
        for i in range(3):
            out = jnp.where(lane == i * pitch + coarse, total(u * own[i]), out)
        return out

    def corrected(w):
        return dot(jnp.where(lane < coarse, w, 0.0), inverse, precision=highest)

    pre = corrected(against) + jnp.where(lane == coarse, 1.0, 0.0)
    direction = pre
    gamma = total(pre * against)
    answer = jnp.zeros_like(pre)
    image_sum = jnp.zeros_like(pre)
    for step in range(ITERS):
        image = metric(direction)
        alpha = gamma / total(direction * image)
        answer = answer + alpha * direction
        if step + 1 < ITERS:
            image_sum = image_sum + alpha * image
            moved_on = jnp.where(live & (slot > 0), pltpu.roll(direction, pitch, axis=1), 0.0)
            pre = pre - alpha * (moved_on + corrected(image))
            gamma_new = total(pre * (against - image_sum))
            direction = pre + (gamma_new / gamma) * direction
            gamma = gamma_new

    row = slice(FEAT + 1, FEAT + 2)
    which = jnp.concatenate(
        [left_ref[row, edge:], own_ref[row, :], right_ref[row, : width - edge]], axis=1
    )
    z = one_hot(which, coarse)
    q0 = jnp.concatenate([prel_ref[:, edge:], pre_ref[...], prer_ref[:, : width - edge]], axis=1)
    d1 = jnp.concatenate([d1l_ref[:, edge:], d1_ref[...], d1r_ref[:, : width - edge]], axis=1)
    d2 = jnp.concatenate([d2l_ref[:, edge:], d2_ref[...], d2r_ref[:, : width - edge]], axis=1)
    span = q0.shape[1]
    pad = jnp.zeros((pitch - coarse, span), f32)
    basis = [z, pad, d1[count:], pad, d2[count:], pad]
    if wide > 3 * pitch:
        basis.append(jnp.zeros((wide - 3 * pitch, span), f32))
    x = dot(jnp.where(is_vec, answer, 0.0), jnp.concatenate(basis, axis=0), precision=highest)
    x = x + scalars(answer, 0) * q0 + scalars(answer, 1) * d1[:count]
    x = x + scalars(answer, 2) * d2[:count]
    mine = slice(REACH * BS, REACH * BS + width)
    sol_ref[...] = x[:, mine]

    base = FEAT + 8
    systems = jnp.concatenate(
        [left_ref[base:, edge:], own_ref[base:, :], right_ref[base:, : width - edge]], axis=1
    )
    target = (iota((count, 1), 0) == 0) & (scalar_ref[0] == 0)
    right = jnp.where(target, x, systems)
    weighted = x[:, mine] * coef_ref[...][:, 0:1]
    r0, r1 = split(right, 2)
    w0, w1 = split(weighted, 2)
    near = jnp.concatenate([r0, r1, r0], axis=0).astype(bf16)
    mate = jnp.concatenate([w0, w0, w1], axis=0).astype(bf16)
    pack = jnp.concatenate(
        [left_ref[0:16, edge:], own_ref[0:16, :], right_ref[0:16, : width - edge]], axis=1
    )
    scaled = pack[0:FEAT] / column(len_ref, FEAT)
    table = one_hot(pack[FEAT : FEAT + 1], TASKS)
    ones = jnp.ones((8, span), f32)
    terms = jnp.concatenate([scaled, ones, scaled * scaled], axis=0)
    t0, t1 = split(terms, 2)
    pad8 = jnp.zeros((8, span), f32)
    both = jnp.concatenate([t0, pad8, t1, pad8], axis=0).astype(bf16)
    heads = jnp.concatenate([t0, pad8], axis=0).astype(bf16)
    tables = table.astype(bf16)
    high = 32
    length_total = jnp.zeros((FEAT, 1), f32)
    task_total = jnp.zeros((TASKS, TASKS), f32)
    for m in range(blocks):
        at = slice(m * BS, (m + 1) * BS)
        sums = jnp.zeros((high, BS), f32)
        held_sums = jnp.zeros((TASKS, BS), f32)
        for o in range(SLOTS):
            j = slice((m + o) * BS, (m + o + 1) * BS)
            rows_at = slice(o * BS, (o + 1) * BS)
            outer = dot(near[:, j], mate[:, at], TN)
            kernel = hi_ref[m, rows_at, :].astype(f32) + lo_ref[m, rows_at, :].astype(f32)
            energy = outer * kernel
            held = outer * sim_ref[m, rows_at, :]
            e0, e1 = (part.astype(bf16) for part in split(energy, 2))
            h0, h1 = (part.astype(bf16) for part in split(held, 2))
            first = dot(both[:, j], e0)
            sums = sums + first[:high] + first[high:] + dot(heads[:, j], e1)
            held_sums = held_sums + dot(tables[:, j], h0) + dot(tables[:, j], h1)
        mid = slice((REACH + m) * BS, (REACH + m + 1) * BS)
        left = scaled[:, mid]
        value = left * left * sums[FEAT : FEAT + 1] + sums[2 * FEAT : 3 * FEAT]
        value = value - 2.0 * left * sums[:FEAT]
        length_total = length_total + jnp.sum(value, axis=1, keepdims=True)
        task_total = task_total + dot(table[:, mid], held_sums, NT, highest)
    lane = iota((TASKS, LANES), 1)
    lengths = jnp.concatenate([length_total, jnp.zeros((TASKS - FEAT, 1), f32)], axis=0)
    wide_tasks = jnp.concatenate([task_total, jnp.zeros((TASKS, LANES - TASKS), f32)], axis=1)
    grad_ref[...] = jnp.where(lane == TASKS, lengths, wide_tasks)


def call(body, outs, args, smem, name, scratch=(), flops=0):
    vm = pl.BlockSpec(memory_space=pltpu.VMEM)
    sm = pl.BlockSpec(memory_space=pltpu.SMEM)
    return pl.pallas_call(
        body,
        out_shape=outs,
        in_specs=[sm] * smem + [vm] * (len(args) - smem),
        out_specs=[vm] * len(outs),
        scratch_shapes=scratch,
        compiler_params=pltpu.CompilerParams(vmem_limit_bytes=48 * 1024 * 1024),
        cost_estimate=pl.CostEstimate(flops=flops, bytes_accessed=1 << 20, transcendentals=0),
        name=name,
    )(*args)


def both_sides(cells):
    count = lax.axis_size("pts")
    up = [(i, i + 1) for i in range(count - 1)]
    down = [(i + 1, i) for i in range(count - 1)]
    return lax.ppermute(cells, "pts", up), lax.ppermute(cells, "pts", down)


def shards(
    systems, features, task_ids, pattern, aggregate, coarse_inverse, task_cov, lengthscales, noise
):
    count, width = systems.shape
    blocks = width // BS
    coarse = coarse_inverse.shape[1]
    rows = count + coarse
    pitch, lanes = pitch_of(coarse), lanes_of(coarse)

    def shape(*dims, kind=f32):
        return jax.ShapeDtypeStruct(dims, kind)

    pack = jnp.concatenate(
        [
            features,
            task_ids.astype(f32)[None],
            aggregate.astype(f32)[None],
            jnp.zeros((6, width), f32),
            systems,
        ],
        axis=0,
    )
    pack_l, pack_r = both_sides(pack)
    jac, pre = call(
        invert_kernel,
        [shape(blocks, BS, BS), shape(count, width)],
        [pattern, lengthscales, noise, pack, task_cov],
        3,
        "invert",
        [pltpu.VMEM((blocks, BS, BS), f32)],
        flops=10**10,
    )
    pre_l, pre_r = both_sides(pre)
    hi, lo, sim = call(
        build_kernel,
        [
            shape(blocks, BAND, BS, kind=bf16),
            shape(blocks, BAND, BS, kind=bf16),
            shape(blocks, BAND, BS),
        ],
        [pattern, lengthscales, pack, pack_l, pack_r, task_cov],
        2,
        "build",
        flops=3 * 10**9,
    )
    v0, d1 = call(
        first_kernel,
        [shape(rows, width), shape(rows, width)],
        [noise, pack, pack_l, pack_r, pre, pre_l, pre_r, hi, lo, jac],
        1,
        "first",
        flops=10**9,
    )
    d1_l, d1_r = both_sides(d1)
    v1, d2 = call(
        second_kernel,
        [shape(rows, width), shape(rows, width)],
        [noise, pack, d1, d1_l, d1_r, hi, lo, jac],
        1,
        "second",
        flops=10**9,
    )
    d2_l, d2_r = both_sides(d2)
    own_rows = coarse_inverse.shape[0]
    placed = lax.dynamic_update_slice(
        jnp.zeros((rows, lanes), f32),
        coarse_inverse,
        (lax.axis_index("pts") * own_rows, 6 * pitch),
    )
    (partial_gram,) = call(
        moment_kernel,
        [shape(rows, lanes)],
        [noise, pack, d2, d2_l, d2_r, hi, lo, pre, d1, v0, v1, placed],
        1,
        "moments",
        flops=10**9,
    )
    gram = lax.psum(partial_gram, "pts")
    probe = lax.axis_index("probe")
    line = probe * count + jnp.arange(count, dtype=jnp.int32)
    total_points = lax.axis_size("pts") * width
    total_sides = lax.axis_size("probe") * count
    coef = jnp.where(line == 0, 0.5, -0.5 / (total_sides - 1)) / total_points
    coef = jnp.broadcast_to(coef[:, None], (count, LANES)).astype(f32)
    answer, grads = call(
        final_kernel,
        [shape(count, width), shape(TASKS, LANES)],
        [
            probe.astype(jnp.int32)[None], lengthscales, gram, pack, pack_l, pack_r, pre, pre_l,
            pre_r, d1, d1_l, d1_r, d2, d2_l, d2_r, hi, lo, sim, coef, task_cov,
        ],
        2,
        "final",
        flops=10**9,
    )
    grads = lax.psum(grads, ("pts", "probe"))
    return answer, grads[:FEAT, TASKS], grads[:, :TASKS]


def solution(mesh):
    return jax.shard_map(
        shards,
        mesh=mesh,
        in_specs=(
            P("probe", ("groups", "pts")),
            P(None, ("groups", "pts")),
            P(("groups", "pts")),
            P(("groups", "pts"), None),
            P(("groups", "pts")),
            P(("groups", "pts"), None),
            P("groups", None),
            P("groups"),
            P("groups"),
        ),
        out_specs=(P("probe", ("groups", "pts")), P("groups"), P("groups", None)),
        check_vma=False,
    )
```

```python
import functools

import jax
import jax.numpy as jnp
from jax import lax
from jax.experimental import pallas as pl
from jax.experimental.pallas import tpu as pltpu
from jax.sharding import PartitionSpec as P

BS = 256
REACH = 3
FEAT = 8
TASKS = 16
ITERS = 3
SLOTS = 2 * REACH + 1
BAND = SLOTS * BS
BASE = 32
GROUP = 4
LANES = 128
SYS = 2 * FEAT

highest = lax.Precision.HIGHEST
f32 = jnp.float32
bf16 = jnp.bfloat16
NN = (((1,), (0,)), ((), ()))
NT = (((1,), (1,)), ((), ()))
TN = (((0,), (0,)), ((), ()))


def dot(a, b, dims=NN, precision=None):
    return lax.dot_general(a, b, dims, precision=precision, preferred_element_type=f32)


def iota(shape, dim):
    return lax.broadcasted_iota(jnp.int32, shape, dim)


def split(x, parts):
    out = []
    for _ in range(parts - 1):
        head = x.astype(bf16).astype(f32)
        out.append(head)
        x = x - head
    out.append(x.astype(bf16).astype(f32))
    return out


def column(ref, size):
    rows = iota((size, 1), 0)
    out = jnp.zeros((size, 1), f32)
    for i in range(size):
        out = jnp.where(rows == i, ref[i], out)
    return out


def one_hot(ids, size):
    return (iota((size, ids.shape[1]), 0).astype(f32) == ids).astype(f32)


def noise_row(noise_ref, ids):
    out = jnp.zeros(ids.shape, f32)
    for t in range(TASKS):
        out = jnp.where(ids == float(t), noise_ref[t], out)
    return out


def weight(pat_ref, block, offset):
    if offset != REACH:
        return pat_ref[block, offset].astype(f32)
    total = pat_ref[block, 0]
    for o in range(1, SLOTS):
        total = total + pat_ref[block, o]
    return total.astype(f32)


def near_stack(scaled, table):
    s0, s1, s2 = split(scaled, 3)
    n0, n1, n2 = split(-0.5 * jnp.sum(scaled * scaled, axis=0, keepdims=True), 3)
    rows = iota(scaled.shape, 0)
    norms = jnp.where(rows == 0, n0, jnp.where(rows == 1, n1, jnp.where(rows == 2, n2, 0.0)))
    pad = jnp.zeros((LANES - 7 * FEAT - 3 * TASKS, scaled.shape[1]), f32)
    return jnp.concatenate(
        [s0, s0, s1, s1, s0, s2, norms, table, table, table, pad], axis=0
    ).astype(bf16)


def own_stack(scaled, picked):
    s0, s1, s2 = split(scaled, 3)
    rows = iota(scaled.shape, 0)
    ones = jnp.where(rows < 3, 1.0, 0.0)
    count = scaled.shape[1]
    tail = LANES - 7 * FEAT - 3 * TASKS
    left = jnp.concatenate(
        [s0, s1, s0, s1, s2, s0, ones, jnp.zeros((3 * TASKS + tail, count), f32)], axis=0
    ).astype(bf16)
    right = jnp.concatenate(
        [jnp.zeros((7 * FEAT, count), f32)] + split(picked, 3) + [jnp.zeros((tail, count), f32)],
        axis=0,
    ).astype(bf16)
    return left, right, -0.5 * jnp.sum(scaled * scaled, axis=0, keepdims=True)


def small_inverse(p):
    n = len(p)
    if n == 1:
        return [[1.0 / p[0][0]]]
    if n == 2:
        a, b, d = p[0][0], p[0][1], p[1][1]
        r = 1.0 / (a * d - b * b)
        off = -b * r
        return [[d * r, off], [off, a * r]]
    h = n // 2
    ainv = small_inverse([row[:h] for row in p[:h]])
    b = [row[h:] for row in p[:h]]
    t = [[sum(ainv[i][k] * b[k][j] for k in range(h)) for j in range(h)] for i in range(h)]
    s = [[None] * h for _ in range(h)]
    for i in range(h):
        for j in range(i, h):
            s[i][j] = s[j][i] = p[h + i][h + j] - sum(b[k][i] * t[k][j] for k in range(h))
    sinv = small_inverse(s)
    u = [[sum(t[i][k] * sinv[k][j] for k in range(h)) for j in range(h)] for i in range(h)]
    out = [[None] * n for _ in range(n)]
    for i in range(h):
        for j in range(h):
            out[h + i][h + j] = sinv[i][j]
            out[i][h + j] = out[h + j][i] = -u[i][j]
    for i in range(h):
        for j in range(i, h):
            out[i][j] = out[j][i] = ainv[i][j] + sum(u[i][k] * t[j][k] for k in range(h))
    return out


def sweep_base(cells):
    lane = iota((BASE, LANES), 1)
    start = lane - lane % BASE
    inner = iota((1, LANES), 1) % BASE
    sub = iota((BASE, 1), 0)
    for g in range(BASE // GROUP):
        first = g * GROUP
        cols = [
            jnp.take_along_axis(cells, start + (first + t), axis=1, mode="promise_in_bounds")
            for t in range(GROUP)
        ]
        rows = [cells[first + t : first + t + 1, :] for t in range(GROUP)]
        pivots = [[cols[u][first + t : first + t + 1, :] for u in range(GROUP)] for t in range(GROUP)]
        inv = small_inverse(pivots)
        rows = [jnp.where(inner == first + t, -1.0, rows[t]) for t in range(GROUP)]
        group = (inner >= first) & (inner < first + GROUP)
        for t in range(GROUP):
            rows[t] = jnp.where(group & (inner != first + t), 0.0, rows[t])
        new = [sum(inv[t][u] * rows[u] for u in range(GROUP)) for t in range(GROUP)]
        cells = jnp.where(group, 0.0, cells)
        for t in range(GROUP):
            cells = cells - cols[t] * new[t]
        for t in range(GROUP):
            cells = jnp.where(sub == first + t, new[t], cells)
    return cells


def invert_kernel(
    feat_hbm, ids_hbm, agg_hbm, sys_hbm, cov_hbm, coarse_hbm, pat_hbm, len_hbm, noise_hbm,
    jac_ref, pack_ref, extra_ref,
    work, feat_ref, ids_ref, agg_ref, sys_ref, cov_ref, coarse_ref, pat_ref, len_ref, noise_ref, sems,
):
    blocks = work.shape[0]
    width = blocks * BS
    pairs = [
        (feat_hbm, feat_ref), (ids_hbm, ids_ref), (agg_hbm, agg_ref), (cov_hbm, cov_ref),
        (pat_hbm, pat_ref), (len_hbm, len_ref), (noise_hbm, noise_ref), (coarse_hbm, coarse_ref),
        (sys_hbm, sys_ref),
    ]
    copies = [pltpu.make_async_copy(a, b, sems.at[i]) for i, (a, b) in enumerate(pairs)]
    for copy in copies:
        copy.start()
    for copy in copies:
        copy.wait()
    scaled = feat_ref[...] / column(len_ref, FEAT)
    ids = ids_ref[...].astype(f32)
    table = one_hot(ids, TASKS)
    noise = noise_row(noise_ref, ids)
    c0, c1, c2 = split(cov_ref[...], 3)
    tab = table.astype(bf16)
    picked = (dot(c2.astype(bf16), tab) + dot(c1.astype(bf16), tab)) + dot(c0.astype(bf16), tab)
    rows = iota((FEAT, width), 0)
    weights = jnp.zeros((1, width), f32)
    places = iota((1, width), 1)
    for m in range(blocks):
        for o in range(SLOTS):
            weights = jnp.where(places == m * SLOTS + o, weight(pat_ref, m, o), weights)
    pack_ref[0:FEAT, :] = scaled
    pack_ref[FEAT : 2 * FEAT, :] = jnp.where(
        rows == 0, ids, jnp.where(rows == 1, agg_ref[...].astype(f32), 0.0)
    )
    count = sys_ref.shape[0]
    pack_ref[SYS : SYS + count, :] = sys_ref[...]
    extra_ref[0:TASKS, :] = picked
    tail = jnp.where(rows == 0, noise, jnp.where(rows == 1, weights, 0.0))
    held = coarse_ref.shape[0]
    inverse = jnp.concatenate(
        [coarse_ref[...], jnp.zeros((held, width - coarse_ref.shape[1]), f32)], axis=1
    )
    for r in range(held):
        tail = jnp.where(rows == 2 + r, inverse[r : r + 1], tail)
    extra_ref[TASKS : TASKS + FEAT, :] = tail
    near = near_stack(scaled, table)
    left, right, norm = own_stack(scaled, picked)
    eye = iota((BS, BS), 0) == iota((BS, BS), 1)
    for m in range(blocks):
        at = slice(m * BS, (m + 1) * BS)
        exponent = dot(near[:, at], left[:, at], TN) + norm[:, at]
        pair = dot(near[:, at], right[:, at], TN)
        block = weight(pat_ref, m, REACH) * jnp.exp(exponent) * pair
        work[m] = block + jnp.where(eye, noise[:, at], 0.0)
    seg = iota((BASE, LANES), 1) // BASE
    wide = iota((BASE, BS), 1)
    deep = iota((BASE, BS), 0)
    for k in range(BS // BASE):
        first = k * BASE
        tile, inside = first // LANES, first % LANES
        strips = [work[m, first : first + BASE, :] for m in range(blocks)]
        cells = jnp.where(iota((BASE, LANES), 1) % BASE == iota((BASE, LANES), 0), 1.0, 0.0)
        for m in range(blocks):
            piece = strips[m][:, tile * LANES : (tile + 1) * LANES]
            shift = (BASE * m - inside) % LANES
            if shift:
                piece = pltpu.roll(piece, shift, axis=1)
            cells = jnp.where(seg == m, piece, cells)
        inv = -sweep_base(cells)
        held = (wide >= first) & (wide < first + BASE)
        minus = jnp.where(wide - first == deep, -1.0, 0.0)
        stack = jnp.concatenate(
            [jnp.where(held, minus, s) for s in strips]
            + [jnp.zeros((LANES - blocks * BASE, BS), f32)],
            axis=0,
        )
        spread = jnp.concatenate([jnp.where(seg == m, inv, 0.0) for m in range(blocks)], axis=0)
        new = dot(spread, stack, precision=highest)
        gone = (iota((1, BS), 1) >= first) & (iota((1, BS), 1) < first + BASE)
        for m in range(blocks):
            row = new[m * BASE : (m + 1) * BASE, :]
            r0, r1, r2 = split(strips[m], 3)
            p0, p1, p2 = split(row, 3)
            a = jnp.concatenate([r0, r0, r1, r1, r0, r2], axis=0).astype(bf16)
            b = jnp.concatenate([p0, p1, p0, p1, p2, p0], axis=0).astype(bf16)
            work[m] = jnp.where(gone, 0.0, work[m]) - dot(a, b, TN)
            work[m, first : first + BASE, :] = row
    for m in range(blocks):
        at = slice(m * BS, (m + 1) * BS)
        inv = -work[m]
        jac_ref[m] = inv
        pack_ref[SYS + count :, at] = dot(sys_ref[:, at], inv, precision=highest)


def build_kernel(own_ref, left_ref, right_ref, extra_ref, hi_ref, lo_ref, sim_ref):
    blocks = hi_ref.shape[0]
    pack = jnp.concatenate([left_ref[0:SYS, :], own_ref[0:SYS, :], right_ref[0:SYS, :]], axis=1)
    scaled = pack[0:FEAT]
    table = one_hot(pack[FEAT : FEAT + 1], TASKS)
    near = near_stack(scaled, table)
    width = blocks * BS
    left, right, norm = own_stack(own_ref[0:FEAT, :], extra_ref[0:TASKS, :])
    weights = extra_ref[TASKS + 1 : TASKS + 2, :]
    edge = width - REACH * BS
    for m in range(blocks):
        at = slice(m * BS, (m + 1) * BS)
        for o in range(SLOTS):
            j = edge + (m + o) * BS
            part = near[:, j : j + BS]
            exponent = dot(part, left[:, at], TN) + norm[:, at]
            pair = dot(part, right[:, at], TN)
            place = m * SLOTS + o
            similar = weights[:, place : place + 1] * jnp.exp(exponent)
            kernel = similar * pair
            head = kernel.astype(bf16)
            rows = slice(o * BS, (o + 1) * BS)
            sim_ref[m, rows, :] = similar
            hi_ref[m, rows, :] = head
            lo_ref[m, rows, :] = (kernel - head.astype(f32)).astype(bf16)


def operate(vectors, noise, own, hi_ref, lo_ref):
    rows = vectors.shape[0]
    head, tail = (part.astype(bf16) for part in split(vectors, 2))
    both = jnp.concatenate([head, tail], axis=0)
    out = []
    for m in range(hi_ref.shape[0]):
        at = slice(m * BS, m * BS + BAND)
        first = dot(both[:, at], hi_ref[m])
        out.append(first[:rows] + first[rows:] + dot(head[:, at], lo_ref[m]))
    return jnp.concatenate(out, axis=1) + noise * own


def smooth(image, jac_ref):
    return jnp.concatenate(
        [
            dot(image[:, m * BS : (m + 1) * BS], jac_ref[m], precision=highest)
            for m in range(jac_ref.shape[0])
        ],
        axis=1,
    )


def first_kernel(own_ref, left_ref, right_ref, extra_ref, hi_ref, lo_ref, jac_ref, image_ref, next_ref):
    width = own_ref.shape[1]
    count = (own_ref.shape[0] - SYS) // 2
    coarse = image_ref.shape[0] - count
    edge = width - REACH * BS
    pack = jnp.concatenate(
        [left_ref[:, edge:], own_ref[...], right_ref[:, : width - edge]], axis=1
    )
    ext = jnp.concatenate(
        [pack[SYS + count :], one_hot(pack[FEAT + 1 : FEAT + 2], coarse)], axis=0
    )
    noise = extra_ref[TASKS : TASKS + 1, :]
    image = operate(ext, noise, ext[:, REACH * BS : REACH * BS + width], hi_ref, lo_ref)
    image_ref[...] = image
    next_ref[...] = smooth(image, jac_ref)


def second_kernel(
    extra_ref, vec_ref, vecl_ref, vecr_ref, hi_ref, lo_ref, jac_ref, image_ref, next_ref
):
    width = vec_ref.shape[1]
    edge = width - REACH * BS
    ext = jnp.concatenate([vecl_ref[:, edge:], vec_ref[...], vecr_ref[:, : width - edge]], axis=1)
    noise = extra_ref[TASKS : TASKS + 1, :]
    image = operate(ext, noise, vec_ref[...], hi_ref, lo_ref)
    image_ref[...] = image
    next_ref[...] = smooth(image, jac_ref)


def moment_kernel(
    place_ref, own_ref, extra_ref, vec_ref, vecl_ref, vecr_ref, hi_ref, lo_ref, d1_ref, v0_ref,
    v1_ref, out_ref, *, held,
):
    width = own_ref.shape[1]
    count = (own_ref.shape[0] - SYS) // 2
    rows = vec_ref.shape[0]
    coarse = rows - count
    copies, _, lanes = out_ref.shape
    pitch = pitch_of(coarse)
    edge = width - REACH * BS
    ext = jnp.concatenate([vecl_ref[:, edge:], vec_ref[...], vecr_ref[:, : width - edge]], axis=1)
    noise = extra_ref[TASKS : TASKS + 1, :]
    d2 = vec_ref[...]
    v2 = operate(ext, noise, d2, hi_ref, lo_ref)
    systems = own_ref[SYS : SYS + count, :]
    pre = own_ref[SYS + count :, :]
    z = one_hot(own_ref[FEAT + 1 : FEAT + 2, :], coarse)
    d1, v0, v1 = d1_ref[...], v0_ref[...], v1_ref[...]
    gap = jnp.zeros((pitch - coarse, width), f32)

    def stacked(parts):
        cells = []
        for k in range(lanes // pitch):
            if k in parts:
                cells.append(jnp.concatenate([parts[k], gap], axis=0))
            else:
                cells.append(jnp.zeros((pitch, width), f32))
        return jnp.concatenate(cells, axis=0)

    high = lax.Precision.HIGH
    residual = jnp.concatenate([systems, jnp.zeros((coarse, width), f32)], axis=0)
    total = dot(v0, stacked({0: z, 1: d1[count:]}), NT, high)
    total = total + dot(v1, stacked({2: d1[count:], 3: d2[count:]}), NT, high)
    total = total + dot(v2, stacked({4: d2[count:]}), NT, high)
    total = total + dot(residual, stacked({5: z}), NT, high)
    own = [
        pre * v0[:count],
        d1[:count] * v0[:count],
        d1[:count] * v1[:count],
        d2[:count] * v1[:count],
        d2[:count] * v2[:count],
        systems * pre,
    ]
    lane = iota((count, lanes), 1)
    top = total[:count]
    for k, value in enumerate(own):
        top = jnp.where(lane == k * pitch + coarse, jnp.sum(value, axis=1, keepdims=True), top)
    value = jnp.concatenate([top, total[count:]], axis=0)
    row = iota((rows, 1), 0)
    start = place_ref[0] * held
    front = jnp.zeros((1, 6 * pitch), f32)
    back = jnp.zeros((1, lanes - 6 * pitch - coarse), f32)
    for r in range(held):
        line = extra_ref[TASKS + 2 + r : TASKS + 3 + r, 0:coarse]
        line = jnp.concatenate([front, line, back], axis=1)
        value = value + jnp.where(row == start + r, line, 0.0)
    for c in range(copies):
        out_ref[c] = value


def pitch_of(coarse):
    return BASE if coarse < BASE else -(-(coarse + 1) // LANES) * LANES


def lanes_of(coarse):
    return -(-7 * pitch_of(coarse) // LANES) * LANES


def final_kernel(
    probe_ref, gram_ref, own_ref, left_ref, right_ref, d1_ref, d1l_ref, d1r_ref, d2_ref, d2l_ref,
    d2r_ref, hi_ref, lo_ref, sim_ref, sol_ref, grad_ref, *, sides, points,
):
    width = own_ref.shape[1]
    count = (own_ref.shape[0] - SYS) // 2
    rows = d1_ref.shape[0]
    coarse = rows - count
    pitch = pitch_of(coarse)
    wide = -(-3 * pitch // LANES) * LANES
    blocks = width // BS
    edge = width - REACH * BS
    gram = gram_ref[0]
    for c in range(1, gram_ref.shape[0]):
        gram = gram + gram_ref[c]
    lane = iota((1, wide), 1)
    slot, inside = lane // pitch, lane % pitch
    live = lane < 3 * pitch
    is_vec = live & (inside < coarse)
    is_one = live & (inside == coarse)

    def shifted(j):
        return jnp.where(live, gram[:, j * pitch : j * pitch + wide], 0.0)

    moved = [shifted(j) for j in range(3)]
    own = [m[:count] for m in moved]
    gap = jnp.zeros((pitch - coarse, wide), f32)
    hankel = jnp.concatenate(
        [
            jnp.concatenate([jnp.where(is_vec, m[count:], 0.0), gap], axis=0)
            for m in moved
        ]
        + ([jnp.zeros((wide - 3 * pitch, wide), f32)] if wide > 3 * pitch else []),
        axis=0,
    )
    block0 = lane < pitch
    inverse = gram[:coarse, 6 * pitch : 7 * pitch]
    if pitch < wide:
        inverse = jnp.concatenate([inverse, jnp.zeros((coarse, wide - pitch), f32)], axis=1)
    inverse = jnp.where(lane < coarse, inverse, 0.0)
    inverse = jnp.concatenate([inverse, jnp.zeros((wide - coarse, wide), f32)], axis=0)
    start = gram[:count, 5 * pitch : 6 * pitch]
    if pitch < wide:
        start = jnp.concatenate([start, jnp.zeros((count, wide - pitch), f32)], axis=1)
    against = jnp.where(
        block0, start, jnp.where(live, pltpu.roll(jnp.where(live, own[0], 0.0), pitch, axis=1), 0.0)
    )

    def total(x):
        return jnp.sum(x, axis=1, keepdims=True)

    def scalars(u, i):
        return total(jnp.where(lane == i * pitch + coarse, u, 0.0))

    def metric(u):
        out = dot(jnp.where(is_vec, u, 0.0), hankel, precision=highest)
        for j in range(3):
            out = out + scalars(u, j) * own[j]
        out = jnp.where(is_vec, out, 0.0)
        for i in range(3):
            out = jnp.where(lane == i * pitch + coarse, total(u * own[i]), out)
        return out

    def corrected(w):
        return dot(jnp.where(lane < coarse, w, 0.0), inverse, precision=highest)

    pre = corrected(against) + jnp.where(lane == coarse, 1.0, 0.0)
    direction = pre
    gamma = total(pre * against)
    answer = jnp.zeros_like(pre)
    image_sum = jnp.zeros_like(pre)
    for step in range(ITERS):
        image = metric(direction)
        alpha = gamma / total(direction * image)
        answer = answer + alpha * direction
        if step + 1 < ITERS:
            image_sum = image_sum + alpha * image
            moved_on = jnp.where(live & (slot > 0), pltpu.roll(direction, pitch, axis=1), 0.0)
            pre = pre - alpha * (moved_on + corrected(image))
            gamma_new = total(pre * (against - image_sum))
            direction = pre + (gamma_new / gamma) * direction
            gamma = gamma_new

    pack = jnp.concatenate(
        [left_ref[:, edge:], own_ref[...], right_ref[:, : width - edge]], axis=1
    )
    z = one_hot(pack[FEAT + 1 : FEAT + 2], coarse)
    q0 = pack[SYS + count :]
    d1 = jnp.concatenate([d1l_ref[:, edge:], d1_ref[...], d1r_ref[:, : width - edge]], axis=1)
    d2 = jnp.concatenate([d2l_ref[:, edge:], d2_ref[...], d2r_ref[:, : width - edge]], axis=1)
    span = q0.shape[1]
    pad = jnp.zeros((pitch - coarse, span), f32)
    basis = [z, pad, d1[count:], pad, d2[count:], pad]
    if wide > 3 * pitch:
        basis.append(jnp.zeros((wide - 3 * pitch, span), f32))
    x = dot(jnp.where(is_vec, answer, 0.0), jnp.concatenate(basis, axis=0), precision=highest)
    x = x + scalars(answer, 0) * q0 + scalars(answer, 1) * d1[:count]
    x = x + scalars(answer, 2) * d2[:count]
    mine = slice(REACH * BS, REACH * BS + width)
    sol_ref[...] = x[:, mine]

    systems = pack[SYS : SYS + count]
    line = iota((count, 1), 0) + probe_ref[0] * count
    right = jnp.where(line == 0, x, systems)
    coef = jnp.where(line == 0, 0.5 / points, -0.5 / (sides - 1) / points)
    weighted = x[:, mine] * coef
    r0, r1 = split(right, 2)
    w0, w1 = split(weighted, 2)
    near = jnp.concatenate([r0, r1, r0], axis=0).astype(bf16)
    mate = jnp.concatenate([w0, w0, w1], axis=0).astype(bf16)
    scaled = pack[0:FEAT]
    table = one_hot(pack[FEAT : FEAT + 1], TASKS)
    ones = jnp.ones((8, span), f32)
    terms = jnp.concatenate([scaled, ones, scaled * scaled], axis=0)
    t0, t1 = split(terms, 2)
    pad8 = jnp.zeros((8, span), f32)
    both = jnp.concatenate([t0, pad8, t1, pad8], axis=0).astype(bf16)
    heads = jnp.concatenate([t0, pad8], axis=0).astype(bf16)
    tables = table.astype(bf16)
    high = 32
    length_total = jnp.zeros((FEAT, 1), f32)
    task_total = jnp.zeros((TASKS, TASKS), f32)
    for m in range(blocks):
        at = slice(m * BS, (m + 1) * BS)
        sums = jnp.zeros((high, BS), f32)
        held_sums = jnp.zeros((TASKS, BS), f32)
        for o in range(SLOTS):
            j = slice((m + o) * BS, (m + o + 1) * BS)
            rows_at = slice(o * BS, (o + 1) * BS)
            outer = dot(near[:, j], mate[:, at], TN)
            kernel = hi_ref[m, rows_at, :].astype(f32) + lo_ref[m, rows_at, :].astype(f32)
            energy = outer * kernel
            held = outer * sim_ref[m, rows_at, :]
            e0, e1 = (part.astype(bf16) for part in split(energy, 2))
            h0, h1 = (part.astype(bf16) for part in split(held, 2))
            first = dot(both[:, j], e0)
            sums = sums + first[:high] + first[high:] + dot(heads[:, j], e1)
            held_sums = held_sums + dot(tables[:, j], h0) + dot(tables[:, j], h1)
        mid = slice((REACH + m) * BS, (REACH + m + 1) * BS)
        left = scaled[:, mid]
        value = left * left * sums[FEAT : FEAT + 1] + sums[2 * FEAT : 3 * FEAT]
        value = value - 2.0 * left * sums[:FEAT]
        length_total = length_total + jnp.sum(value, axis=1, keepdims=True)
        task_total = task_total + dot(table[:, mid], held_sums, NT, highest)
    lane = iota((TASKS, LANES), 1)
    lengths = jnp.concatenate([length_total, jnp.zeros((TASKS - FEAT, 1), f32)], axis=0)
    wide_tasks = jnp.concatenate([task_total, jnp.zeros((TASKS, LANES - TASKS), f32)], axis=1)
    value = jnp.where(lane == TASKS, lengths, wide_tasks)
    for c in range(grad_ref.shape[0]):
        grad_ref[c] = value


MIB = 1024 * 1024


def call(body, outs, args, name, smem=0, hbm=0, scratch=(), flops=0, limit=16):
    vm = pl.BlockSpec(memory_space=pltpu.VMEM)
    sm = pl.BlockSpec(memory_space=pltpu.SMEM)
    far = pl.BlockSpec(memory_space=pltpu.HBM)
    return pl.pallas_call(
        body,
        out_shape=outs,
        in_specs=[sm] * smem + [far] * hbm + [vm] * (len(args) - smem - hbm),
        out_specs=[vm] * len(outs),
        scratch_shapes=scratch,
        compiler_params=pltpu.CompilerParams(vmem_limit_bytes=limit * MIB),
        cost_estimate=pl.CostEstimate(flops=flops, bytes_accessed=1 << 20, transcendentals=0),
        name=name,
    )(*args)


def both_sides(cells):
    count = lax.axis_size("pts")
    up = [(i, i + 1) for i in range(count - 1)]
    down = [(i + 1, i) for i in range(count - 1)]
    return lax.ppermute(cells, "pts", up), lax.ppermute(cells, "pts", down)


def shards(
    systems, features, task_ids, pattern, aggregate, coarse_inverse, task_cov, lengthscales, noise
):
    count, width = systems.shape
    blocks = width // BS
    coarse = coarse_inverse.shape[1]
    rows = count + coarse
    lanes = lanes_of(coarse)
    ranks = lax.axis_size("pts")
    sides = lax.axis_size("probe")

    def shape(*dims, kind=f32):
        return jax.ShapeDtypeStruct(dims, kind)

    ids, which = task_ids[None], aggregate[None]
    jac, pack, extra = call(
        invert_kernel,
        [shape(blocks, BS, BS), shape(SYS + 2 * count, width), shape(TASKS + FEAT, width)],
        [features, ids, which, systems, task_cov, coarse_inverse, pattern, lengthscales, noise],
        "invert",
        hbm=9,
        scratch=[
            pltpu.VMEM((blocks, BS, BS), f32),
            pltpu.VMEM(features.shape, f32),
            pltpu.VMEM(ids.shape, jnp.int32),
            pltpu.VMEM(which.shape, jnp.int32),
            pltpu.VMEM(systems.shape, f32),
            pltpu.VMEM(task_cov.shape, f32),
            pltpu.VMEM(coarse_inverse.shape, f32),
            pltpu.SMEM(pattern.shape, jnp.int32),
            pltpu.SMEM(lengthscales.shape, f32),
            pltpu.SMEM(noise.shape, f32),
            pltpu.SemaphoreType.DMA((9,)),
        ],
        flops=10**10,
    )
    pack_l, pack_r = both_sides(pack)
    hi, lo, sim = call(
        build_kernel,
        [
            shape(blocks, BAND, BS, kind=bf16),
            shape(blocks, BAND, BS, kind=bf16),
            shape(blocks, BAND, BS),
        ],
        [pack, pack_l, pack_r, extra],
        "build",
        flops=3 * 10**9,
        limit=24,
    )
    v0, d1 = call(
        first_kernel,
        [shape(rows, width), shape(rows, width)],
        [pack, pack_l, pack_r, extra, hi, lo, jac],
        "first",
        flops=10**9,
    )
    d1_l, d1_r = both_sides(d1)
    v1, d2 = call(
        second_kernel,
        [shape(rows, width), shape(rows, width)],
        [extra, d1, d1_l, d1_r, hi, lo, jac],
        "second",
        flops=10**9,
    )
    d2_l, d2_r = both_sides(d2)
    place = lax.axis_index("pts").astype(jnp.int32)[None]
    probe = lax.axis_index("probe").astype(jnp.int32)[None]
    (gram,) = call(
        functools.partial(moment_kernel, held=coarse_inverse.shape[0]),
        [shape(ranks, rows, lanes)],
        [place, pack, extra, d2, d2_l, d2_r, hi, lo, d1, v0, v1],
        "moments",
        smem=1,
        flops=10**9,
    )
    gram = lax.all_to_all(gram, "pts", 0, 0, tiled=True)
    answer, grads = call(
        functools.partial(final_kernel, sides=sides * count, points=ranks * width),
        [shape(count, width), shape(ranks * sides, TASKS, LANES)],
        [probe, gram, pack, pack_l, pack_r, d1, d1_l, d1_r, d2, d2_l, d2_r, hi, lo, sim],
        "final",
        smem=1,
        flops=10**9,
        limit=24,
    )
    grads = lax.all_to_all(grads, ("pts", "probe"), 0, 0, tiled=True)
    grads = jnp.sum(grads, axis=0)
    return answer, grads[:FEAT, TASKS], grads[:, :TASKS]


def solution(mesh):
    return jax.shard_map(
        shards,
        mesh=mesh,
        in_specs=(
            P("probe", ("groups", "pts")),
            P(None, ("groups", "pts")),
            P(("groups", "pts")),
            P(("groups", "pts"), None),
            P(("groups", "pts")),
            P(("groups", "pts"), None),
            P("groups", None),
            P("groups"),
            P("groups"),
        ),
        out_specs=(P("probe", ("groups", "pts")), P("groups"), P("groups", None)),
        check_vma=False,
    )
```

```python
import functools

import jax
import jax.numpy as jnp
from jax import lax
from jax.experimental import pallas as pl
from jax.experimental.pallas import tpu as pltpu
from jax.sharding import PartitionSpec as P

BS = 256
REACH = 3
FEAT = 8
TASKS = 16
ITERS = 3
SLOTS = 2 * REACH + 1
BAND = SLOTS * BS
BASE = 32
GROUP = 4
LANES = 128
SYS = 2 * FEAT

highest = lax.Precision.HIGHEST
f32 = jnp.float32
bf16 = jnp.bfloat16
NN = (((1,), (0,)), ((), ()))
NT = (((1,), (1,)), ((), ()))
TN = (((0,), (0,)), ((), ()))


def dot(a, b, dims=NN, precision=None):
    return lax.dot_general(a, b, dims, precision=precision, preferred_element_type=f32)


def iota(shape, dim):
    return lax.broadcasted_iota(jnp.int32, shape, dim)


def split(x, parts):
    out = []
    for _ in range(parts - 1):
        head = x.astype(bf16).astype(f32)
        out.append(head)
        x = x - head
    out.append(x.astype(bf16).astype(f32))
    return out


def column(ref, size):
    rows = iota((size, 1), 0)
    out = jnp.zeros((size, 1), f32)
    for i in range(size):
        out = jnp.where(rows == i, ref[i], out)
    return out


def one_hot(ids, size):
    return (iota((size, ids.shape[1]), 0).astype(f32) == ids).astype(f32)


def noise_row(noise_ref, ids):
    out = jnp.zeros(ids.shape, f32)
    for t in range(TASKS):
        out = jnp.where(ids == float(t), noise_ref[t], out)
    return out


def weight(pat_ref, block, offset):
    if offset != REACH:
        return pat_ref[block, offset].astype(f32)
    total = pat_ref[block, 0]
    for o in range(1, SLOTS):
        total = total + pat_ref[block, o]
    return total.astype(f32)


def near_stack(scaled, table):
    s0, s1, s2 = split(scaled, 3)
    n0, n1, n2 = split(-0.5 * jnp.sum(scaled * scaled, axis=0, keepdims=True), 3)
    rows = iota(scaled.shape, 0)
    norms = jnp.where(rows == 0, n0, jnp.where(rows == 1, n1, jnp.where(rows == 2, n2, 0.0)))
    pad = jnp.zeros((LANES - 7 * FEAT - 3 * TASKS, scaled.shape[1]), f32)
    return jnp.concatenate(
        [s0, s0, s1, s1, s0, s2, norms, table, table, table, pad], axis=0
    ).astype(bf16)


def own_stack(scaled, picked):
    s0, s1, s2 = split(scaled, 3)
    rows = iota(scaled.shape, 0)
    ones = jnp.where(rows < 3, 1.0, 0.0)
    count = scaled.shape[1]
    tail = LANES - 7 * FEAT - 3 * TASKS
    left = jnp.concatenate(
        [s0, s1, s0, s1, s2, s0, ones, jnp.zeros((3 * TASKS + tail, count), f32)], axis=0
    ).astype(bf16)
    right = jnp.concatenate(
        [jnp.zeros((7 * FEAT, count), f32)] + split(picked, 3) + [jnp.zeros((tail, count), f32)],
        axis=0,
    ).astype(bf16)
    return left, right, -0.5 * jnp.sum(scaled * scaled, axis=0, keepdims=True)


def small_inverse(p):
    n = len(p)
    if n == 1:
        return [[1.0 / p[0][0]]]
    if n == 2:
        a, b, d = p[0][0], p[0][1], p[1][1]
        r = 1.0 / (a * d - b * b)
        off = -b * r
        return [[d * r, off], [off, a * r]]
    h = n // 2
    ainv = small_inverse([row[:h] for row in p[:h]])
    b = [row[h:] for row in p[:h]]
    t = [[sum(ainv[i][k] * b[k][j] for k in range(h)) for j in range(h)] for i in range(h)]
    s = [[None] * h for _ in range(h)]
    for i in range(h):
        for j in range(i, h):
            s[i][j] = s[j][i] = p[h + i][h + j] - sum(b[k][i] * t[k][j] for k in range(h))
    sinv = small_inverse(s)
    u = [[sum(t[i][k] * sinv[k][j] for k in range(h)) for j in range(h)] for i in range(h)]
    out = [[None] * n for _ in range(n)]
    for i in range(h):
        for j in range(h):
            out[h + i][h + j] = sinv[i][j]
            out[i][h + j] = out[h + j][i] = -u[i][j]
    for i in range(h):
        for j in range(i, h):
            out[i][j] = out[j][i] = ainv[i][j] + sum(u[i][k] * t[j][k] for k in range(h))
    return out


def sweep_base(cells):
    lane = iota((BASE, LANES), 1)
    start = lane - lane % BASE
    inner = iota((1, LANES), 1) % BASE
    sub = iota((BASE, 1), 0)
    for g in range(BASE // GROUP):
        first = g * GROUP
        cols = [
            jnp.take_along_axis(cells, start + (first + t), axis=1, mode="promise_in_bounds")
            for t in range(GROUP)
        ]
        rows = [cells[first + t : first + t + 1, :] for t in range(GROUP)]
        pivots = [[cols[u][first + t : first + t + 1, :] for u in range(GROUP)] for t in range(GROUP)]
        inv = small_inverse(pivots)
        rows = [jnp.where(inner == first + t, -1.0, rows[t]) for t in range(GROUP)]
        group = (inner >= first) & (inner < first + GROUP)
        for t in range(GROUP):
            rows[t] = jnp.where(group & (inner != first + t), 0.0, rows[t])
        new = [sum(inv[t][u] * rows[u] for u in range(GROUP)) for t in range(GROUP)]
        cells = jnp.where(group, 0.0, cells)
        for t in range(GROUP):
            cells = cells - cols[t] * new[t]
        for t in range(GROUP):
            cells = jnp.where(sub == first + t, new[t], cells)
    return cells


def fetch(pairs, sems):
    copies = [pltpu.make_async_copy(a, b, sems.at[i]) for i, (a, b) in enumerate(pairs)]
    for copy in copies:
        copy.start()
    return copies


def invert_kernel(
    feat_hbm, ids_hbm, agg_hbm, sys_hbm, cov_hbm, coarse_hbm, pat_hbm, len_hbm, noise_hbm,
    jac_ref, pack_ref, extra_ref,
    work, feat_ref, ids_ref, agg_ref, sys_ref, cov_ref, coarse_ref, pat_ref, len_ref, noise_ref, sems,
):
    blocks = work.shape[0]
    width = blocks * BS
    pairs = [
        (feat_hbm, feat_ref), (ids_hbm, ids_ref), (agg_hbm, agg_ref), (cov_hbm, cov_ref),
        (pat_hbm, pat_ref), (len_hbm, len_ref), (noise_hbm, noise_ref), (coarse_hbm, coarse_ref),
        (sys_hbm, sys_ref),
    ]
    for copy in fetch(pairs, sems):
        copy.wait()
    scaled = feat_ref[...] / column(len_ref, FEAT)
    ids = ids_ref[...].astype(f32).reshape(1, width)
    which = agg_ref[...].astype(f32).reshape(1, width)
    table = one_hot(ids, TASKS)
    noise = noise_row(noise_ref, ids)
    c0, c1, c2 = split(cov_ref[...], 3)
    tab = table.astype(bf16)
    picked = (dot(c2.astype(bf16), tab) + dot(c1.astype(bf16), tab)) + dot(c0.astype(bf16), tab)
    rows = iota((FEAT, width), 0)
    weights = jnp.zeros((1, width), f32)
    places = iota((1, width), 1)
    for m in range(blocks):
        for o in range(SLOTS):
            weights = jnp.where(places == m * SLOTS + o, weight(pat_ref, m, o), weights)
    pack_ref[0:FEAT, :] = scaled
    pack_ref[FEAT : 2 * FEAT, :] = jnp.where(
        rows == 0, ids, jnp.where(rows == 1, which, 0.0)
    )
    count = sys_ref.shape[0]
    pack_ref[SYS : SYS + count, :] = sys_ref[...]
    extra_ref[0:TASKS, :] = picked
    tail = jnp.where(rows == 0, noise, jnp.where(rows == 1, weights, 0.0))
    held = coarse_ref.shape[0]
    inverse = jnp.concatenate(
        [coarse_ref[...], jnp.zeros((held, width - coarse_ref.shape[1]), f32)], axis=1
    )
    for r in range(held):
        tail = jnp.where(rows == 2 + r, inverse[r : r + 1], tail)
    extra_ref[TASKS : TASKS + FEAT, :] = tail
    near = near_stack(scaled, table)
    left, right, norm = own_stack(scaled, picked)
    eye = iota((BS, BS), 0) == iota((BS, BS), 1)
    for m in range(blocks):
        at = slice(m * BS, (m + 1) * BS)
        exponent = dot(near[:, at], left[:, at], TN) + norm[:, at]
        pair = dot(near[:, at], right[:, at], TN)
        block = weight(pat_ref, m, REACH) * jnp.exp(exponent) * pair
        work[m] = block + jnp.where(eye, noise[:, at], 0.0)
    seg = iota((BASE, LANES), 1) // BASE
    wide = iota((BASE, BS), 1)
    deep = iota((BASE, BS), 0)
    for k in range(BS // BASE):
        first = k * BASE
        tile, inside = first // LANES, first % LANES
        strips = [work[m, first : first + BASE, :] for m in range(blocks)]
        cells = jnp.where(iota((BASE, LANES), 1) % BASE == iota((BASE, LANES), 0), 1.0, 0.0)
        for m in range(blocks):
            piece = strips[m][:, tile * LANES : (tile + 1) * LANES]
            shift = (BASE * m - inside) % LANES
            if shift:
                piece = pltpu.roll(piece, shift, axis=1)
            cells = jnp.where(seg == m, piece, cells)
        inv = -sweep_base(cells)
        held = (wide >= first) & (wide < first + BASE)
        minus = jnp.where(wide - first == deep, -1.0, 0.0)
        stack = jnp.concatenate(
            [jnp.where(held, minus, s) for s in strips]
            + [jnp.zeros((LANES - blocks * BASE, BS), f32)],
            axis=0,
        )
        spread = jnp.concatenate([jnp.where(seg == m, inv, 0.0) for m in range(blocks)], axis=0)
        new = dot(spread, stack, precision=highest)
        gone = (iota((1, BS), 1) >= first) & (iota((1, BS), 1) < first + BASE)
        for m in range(blocks):
            row = new[m * BASE : (m + 1) * BASE, :]
            r0, r1, r2 = split(strips[m], 3)
            p0, p1, p2 = split(row, 3)
            a = jnp.concatenate([r0, r0, r1, r1, r0, r2], axis=0).astype(bf16)
            b = jnp.concatenate([p0, p1, p0, p1, p2, p0], axis=0).astype(bf16)
            work[m] = jnp.where(gone, 0.0, work[m]) - dot(a, b, TN)
            work[m, first : first + BASE, :] = row
    for m in range(blocks):
        at = slice(m * BS, (m + 1) * BS)
        inv = -work[m]
        jac_ref[m] = inv
        pack_ref[SYS + count :, at] = dot(sys_ref[:, at], inv, precision=highest)


def build_kernel(
    own_ref, left_ref, right_ref, extra_ref, hi_ref, lo_ref, sim_hbm, sim_ref, sems
):
    blocks = hi_ref.shape[0]
    pack = jnp.concatenate([left_ref[0:SYS, :], own_ref[0:SYS, :], right_ref[0:SYS, :]], axis=1)
    scaled = pack[0:FEAT]
    table = one_hot(pack[FEAT : FEAT + 1], TASKS)
    near = near_stack(scaled, table)
    width = blocks * BS
    left, right, norm = own_stack(own_ref[0:FEAT, :], extra_ref[0:TASKS, :])
    weights = extra_ref[TASKS + 1 : TASKS + 2, :]
    edge = width - REACH * BS
    for m in range(blocks):
        at = slice(m * BS, (m + 1) * BS)
        for o in range(SLOTS):
            j = edge + (m + o) * BS
            part = near[:, j : j + BS]
            exponent = dot(part, left[:, at], TN) + norm[:, at]
            pair = dot(part, right[:, at], TN)
            place = m * SLOTS + o
            similar = weights[:, place : place + 1] * jnp.exp(exponent)
            kernel = similar * pair
            head = kernel.astype(bf16)
            rows = slice(o * BS, (o + 1) * BS)
            sim_ref[m, rows, :] = similar
            hi_ref[m, rows, :] = head
            lo_ref[m, rows, :] = (kernel - head.astype(f32)).astype(bf16)
        pltpu.make_async_copy(sim_ref.at[m], sim_hbm.at[m], sems.at[m]).start()
    for m in range(blocks):
        pltpu.make_async_copy(sim_ref.at[m], sim_hbm.at[m], sems.at[m]).wait()


def operate(vectors, noise, own, hi_ref, lo_ref):
    rows = vectors.shape[0]
    head, tail = (part.astype(bf16) for part in split(vectors, 2))
    both = jnp.concatenate([head, tail], axis=0)
    out = []
    for m in range(hi_ref.shape[0]):
        at = slice(m * BS, m * BS + BAND)
        first = dot(both[:, at], hi_ref[m])
        out.append(first[:rows] + first[rows:] + dot(head[:, at], lo_ref[m]))
    return jnp.concatenate(out, axis=1) + noise * own


def smooth(image, jac_ref):
    return jnp.concatenate(
        [
            dot(image[:, m * BS : (m + 1) * BS], jac_ref[m], precision=highest)
            for m in range(jac_ref.shape[0])
        ],
        axis=1,
    )


def first_kernel(own_ref, left_ref, right_ref, extra_ref, hi_ref, lo_ref, jac_ref, image_ref, next_ref):
    width = own_ref.shape[1]
    count = (own_ref.shape[0] - SYS) // 2
    coarse = image_ref.shape[0] - count
    edge = width - REACH * BS
    pack = jnp.concatenate(
        [left_ref[:, edge:], own_ref[...], right_ref[:, : width - edge]], axis=1
    )
    ext = jnp.concatenate(
        [pack[SYS + count :], one_hot(pack[FEAT + 1 : FEAT + 2], coarse)], axis=0
    )
    noise = extra_ref[TASKS : TASKS + 1, :]
    image = operate(ext, noise, ext[:, REACH * BS : REACH * BS + width], hi_ref, lo_ref)
    image_ref[...] = image
    next_ref[...] = smooth(image, jac_ref)


def second_kernel(
    extra_ref, vec_ref, vecl_ref, vecr_ref, hi_ref, lo_ref, jac_ref, image_ref, next_ref
):
    width = vec_ref.shape[1]
    edge = width - REACH * BS
    ext = jnp.concatenate([vecl_ref[:, edge:], vec_ref[...], vecr_ref[:, : width - edge]], axis=1)
    noise = extra_ref[TASKS : TASKS + 1, :]
    image = operate(ext, noise, vec_ref[...], hi_ref, lo_ref)
    image_ref[...] = image
    next_ref[...] = smooth(image, jac_ref)


def pitch_of(coarse):
    return coarse + 1


def shape_of(count, coarse):
    lanes = -(-5 * pitch_of(coarse) // LANES) * LANES
    return count + coarse, max(count, coarse), lanes, -(-pitch_of(coarse) // BASE) * BASE


def moment(vectors, images, pairs):
    count = pairs.shape[0]
    table = dot(images, vectors, NT, lax.Precision.HIGH)
    own = jnp.sum(pairs, axis=1, keepdims=True)
    if images.shape[0] > count:
        own = jnp.concatenate([own, jnp.zeros((images.shape[0] - count, 1), f32)], axis=0)
    return jnp.concatenate([table, own], axis=1)


def spread_out(parts, lanes):
    rows, pitch = next(iter(parts.values())).shape
    cells = [parts.get(k, jnp.zeros((rows, pitch), f32)) for k in range(5)]
    if lanes > 5 * pitch:
        cells.append(jnp.zeros((rows, lanes - 5 * pitch), f32))
    return jnp.concatenate(cells, axis=1)


def early_moments_kernel(own_ref, d1_ref, v0_ref, out_ref):
    count = (own_ref.shape[0] - SYS) // 2
    coarse = d1_ref.shape[0] - count
    rows, below, lanes, _ = shape_of(count, coarse)
    systems = own_ref[SYS : SYS + count, :]
    pre = own_ref[SYS + count :, :]
    z = one_hot(own_ref[FEAT + 1 : FEAT + 2, :], coarse)
    d1, v0 = d1_ref[...], v0_ref[...]
    parts = {
        0: moment(z, v0, pre * v0[:count]),
        1: moment(d1[count:], v0, d1[:count] * v0[:count]),
    }
    out_ref[0:rows, :] = spread_out(parts, lanes)
    start = spread_out({0: moment(z, systems, systems * pre)}, lanes)
    if below > count:
        start = jnp.concatenate([start, jnp.zeros((below - count, lanes), f32)], axis=0)
    out_ref[rows:, :] = start


def late_moments_kernel(before_ref, d1_ref, d2_ref, v1_ref, out_ref, *, count):
    rows = d1_ref.shape[0]
    d1, d2, v1 = d1_ref[...], d2_ref[...], v1_ref[...]
    parts = {
        2: moment(d1[count:], v1, d1[:count] * v1[:count]),
        3: moment(d2[count:], v1, d2[:count] * v1[:count]),
    }
    out_ref[0:rows, :] = before_ref[0:rows, :] + spread_out(parts, out_ref.shape[1])
    out_ref[rows:, :] = before_ref[rows:, :]


def third_kernel(
    place_ref, extra_ref, before_ref, vec_ref, vecl_ref, vecr_ref, hi_ref, lo_ref, out_ref,
    *, count, held,
):
    width = vec_ref.shape[1]
    coarse = vec_ref.shape[0] - count
    rows, below, lanes, stand = shape_of(count, coarse)
    edge = width - REACH * BS
    ext = jnp.concatenate([vecl_ref[:, edge:], vec_ref[...], vecr_ref[:, : width - edge]], axis=1)
    d2 = vec_ref[...]
    v2 = operate(ext, extra_ref[TASKS : TASKS + 1, :], d2, hi_ref, lo_ref)
    last = spread_out({4: moment(d2[count:], v2, d2[:count] * v2[:count])}, lanes)
    top = before_ref[0:rows, :] + last
    row = iota((below, 1), 0)
    start = place_ref[0] * held
    bottom = before_ref[rows:, :]
    front = jnp.zeros((1, stand), f32)
    back = jnp.zeros((1, lanes - stand - coarse), f32)
    for r in range(held):
        line = extra_ref[TASKS + 2 + r : TASKS + 3 + r, 0:coarse]
        line = jnp.concatenate([front, line, back], axis=1)
        bottom = bottom + jnp.where(row == start + r, line, 0.0)
    for c in range(out_ref.shape[0]):
        out_ref[c, 0:rows, :] = top
        out_ref[c, rows:, :] = bottom


def final_kernel(
    probe_ref, gram_ref, *refs, sides, points,
):
    far, (sol_ref, grad_ref), near_refs, sems = refs[:12], refs[12:14], refs[14:26], refs[26]
    copies = fetch(list(zip(far, near_refs)), sems)
    (
        own_ref, left_ref, right_ref, d1_ref, d1l_ref, d1r_ref, d2_ref, d2l_ref, d2r_ref,
        hi_ref, lo_ref, sim_ref,
    ) = near_refs
    width = own_ref.shape[1]
    count = (own_ref.shape[0] - SYS) // 2
    rows = d1_ref.shape[0]
    coarse = rows - count
    pitch = pitch_of(coarse)
    wide = -(-3 * pitch // LANES) * LANES
    blocks = width // BS
    edge = width - REACH * BS
    gram = gram_ref[0]
    for c in range(1, gram_ref.shape[0]):
        gram = gram + gram_ref[c]
    _, _, lanes, stand = shape_of(count, coarse)
    bottom = gram[rows:, :]
    gram = jnp.concatenate([gram[:rows], jnp.zeros((rows, wide), f32)], axis=1)
    lane = iota((1, wide), 1)
    slot, inside = lane // pitch, lane % pitch
    live = lane < 3 * pitch
    is_vec = live & (inside < coarse)
    is_one = live & (inside == coarse)

    def shifted(j):
        return jnp.where(live, gram[:, j * pitch : j * pitch + wide], 0.0)

    moved = [shifted(j) for j in range(3)]
    own = [m[:count] for m in moved]
    gap = jnp.zeros((pitch - coarse, wide), f32)
    hankel = jnp.concatenate(
        [
            jnp.concatenate([jnp.where(is_vec, m[count:], 0.0), gap], axis=0)
            for m in moved
        ]
        + ([jnp.zeros((wide - 3 * pitch, wide), f32)] if wide > 3 * pitch else []),
        axis=0,
    )
    block0 = lane < pitch
    inverse = bottom[:coarse, stand : stand + coarse]
    inverse = jnp.concatenate([inverse, jnp.zeros((coarse, wide - coarse), f32)], axis=1)
    inverse = jnp.concatenate([inverse, jnp.zeros((wide - coarse, wide), f32)], axis=0)
    start = bottom[:count, :pitch]
    start = jnp.concatenate([start, jnp.zeros((count, wide - pitch), f32)], axis=1)
    against = jnp.where(
        block0, start, jnp.where(live, pltpu.roll(jnp.where(live, own[0], 0.0), pitch, axis=1), 0.0)
    )

    def total(x):
        return jnp.sum(x, axis=1, keepdims=True)

    def scalars(u, i):
        return total(jnp.where(lane == i * pitch + coarse, u, 0.0))

    def metric(u):
        out = dot(jnp.where(is_vec, u, 0.0), hankel, precision=highest)
        for j in range(3):
            out = out + scalars(u, j) * own[j]
        out = jnp.where(is_vec, out, 0.0)
        for i in range(3):
            out = jnp.where(lane == i * pitch + coarse, total(u * own[i]), out)
        return out

    def corrected(w):
        return dot(jnp.where(lane < coarse, w, 0.0), inverse, precision=highest)

    pre = corrected(against) + jnp.where(lane == coarse, 1.0, 0.0)
    direction = pre
    gamma = total(pre * against)
    answer = jnp.zeros_like(pre)
    image_sum = jnp.zeros_like(pre)
    for step in range(ITERS):
        image = metric(direction)
        alpha = gamma / total(direction * image)
        answer = answer + alpha * direction
        if step + 1 < ITERS:
            image_sum = image_sum + alpha * image
            moved_on = jnp.where(live & (slot > 0), pltpu.roll(direction, pitch, axis=1), 0.0)
            pre = pre - alpha * (moved_on + corrected(image))
            gamma_new = total(pre * (against - image_sum))
            direction = pre + (gamma_new / gamma) * direction
            gamma = gamma_new

    for copy in copies[:9]:
        copy.wait()
    pack = jnp.concatenate(
        [left_ref[:, edge:], own_ref[...], right_ref[:, : width - edge]], axis=1
    )
    z = one_hot(pack[FEAT + 1 : FEAT + 2], coarse)
    q0 = pack[SYS + count :]
    d1 = jnp.concatenate([d1l_ref[:, edge:], d1_ref[...], d1r_ref[:, : width - edge]], axis=1)
    d2 = jnp.concatenate([d2l_ref[:, edge:], d2_ref[...], d2r_ref[:, : width - edge]], axis=1)
    span = q0.shape[1]
    step = -(-coarse // FEAT) * FEAT
    deep = -(-3 * step // LANES) * LANES
    parts, basis = [], []
    for i, rest in enumerate((z, d1[count:], d2[count:])):
        parts.append(answer[:, i * pitch : i * pitch + coarse])
        basis.append(rest)
        if step > coarse:
            parts.append(jnp.zeros((count, step - coarse), f32))
            basis.append(jnp.zeros((step - coarse, span), f32))
    if deep > 3 * step:
        parts.append(jnp.zeros((count, deep - 3 * step), f32))
        basis.append(jnp.zeros((deep - 3 * step, span), f32))
    x = dot(
        jnp.concatenate(parts, axis=1), jnp.concatenate(basis, axis=0), precision=highest
    )
    x = x + scalars(answer, 0) * q0 + scalars(answer, 1) * d1[:count]
    x = x + scalars(answer, 2) * d2[:count]
    mine = slice(REACH * BS, REACH * BS + width)
    sol_ref[...] = x[:, mine]

    systems = pack[SYS : SYS + count]
    line = iota((count, 1), 0) + probe_ref[0] * count
    right = jnp.where(line == 0, x, systems)
    coef = jnp.where(line == 0, 0.5 / points, -0.5 / (sides - 1) / points)
    weighted = x[:, mine] * coef
    r0, r1 = split(right, 2)
    w0, w1 = split(weighted, 2)
    near = jnp.concatenate([r0, r1, r0], axis=0).astype(bf16)
    mate = jnp.concatenate([w0, w0, w1], axis=0).astype(bf16)
    scaled = pack[0:FEAT]
    table = one_hot(pack[FEAT : FEAT + 1], TASKS)
    ones = jnp.ones((8, span), f32)
    terms = jnp.concatenate([scaled, ones, scaled * scaled], axis=0)
    t0, t1 = split(terms, 2)
    pad8 = jnp.zeros((8, span), f32)
    both = jnp.concatenate([t0, pad8, t1, pad8], axis=0).astype(bf16)
    heads = jnp.concatenate([t0, pad8], axis=0).astype(bf16)
    tables = table.astype(bf16)
    high = 32
    for copy in copies[9:]:
        copy.wait()
    length_total = jnp.zeros((FEAT, 1), f32)
    task_total = jnp.zeros((TASKS, TASKS), f32)
    for m in range(blocks):
        at = slice(m * BS, (m + 1) * BS)
        sums = jnp.zeros((high, BS), f32)
        held_sums = jnp.zeros((TASKS, BS), f32)
        for o in range(SLOTS):
            j = slice((m + o) * BS, (m + o + 1) * BS)
            rows_at = slice(o * BS, (o + 1) * BS)
            outer = dot(near[:, j], mate[:, at], TN)
            kernel = hi_ref[m, rows_at, :].astype(f32) + lo_ref[m, rows_at, :].astype(f32)
            energy = outer * kernel
            held = outer * sim_ref[m, rows_at, :]
            e0, e1 = (part.astype(bf16) for part in split(energy, 2))
            h0, h1 = (part.astype(bf16) for part in split(held, 2))
            first = dot(both[:, j], e0)
            sums = sums + first[:high] + first[high:] + dot(heads[:, j], e1)
            held_sums = held_sums + dot(tables[:, j], h0) + dot(tables[:, j], h1)
        mid = slice((REACH + m) * BS, (REACH + m + 1) * BS)
        left = scaled[:, mid]
        value = left * left * sums[FEAT : FEAT + 1] + sums[2 * FEAT : 3 * FEAT]
        value = value - 2.0 * left * sums[:FEAT]
        length_total = length_total + jnp.sum(value, axis=1, keepdims=True)
        task_total = task_total + dot(table[:, mid], held_sums, NT, highest)
    lane = iota((TASKS, LANES), 1)
    lengths = jnp.concatenate([length_total, jnp.zeros((TASKS - FEAT, 1), f32)], axis=0)
    wide_tasks = jnp.concatenate([task_total, jnp.zeros((TASKS, LANES - TASKS), f32)], axis=1)
    value = jnp.where(lane == TASKS, lengths, wide_tasks)
    for c in range(grad_ref.shape[0]):
        grad_ref[c] = value


MIB = 1024 * 1024


def call(body, outs, args, name, smem=0, hbm=0, far_outs=0, scratch=(), flops=0, limit=16):
    if hbm:
        args = args[:-hbm] + [pltpu.with_memory_space_constraint(a, pltpu.HBM) for a in args[-hbm:]]
    if far_outs:
        outs = outs[:-far_outs] + [pltpu.HBM(o.shape, o.dtype) for o in outs[-far_outs:]]
    vm = pl.BlockSpec(memory_space=pltpu.VMEM)
    sm = pl.BlockSpec(memory_space=pltpu.SMEM)
    far = pl.BlockSpec(memory_space=pltpu.HBM)
    return pl.pallas_call(
        body,
        out_shape=outs,
        in_specs=[sm] * smem + [vm] * (len(args) - smem - hbm) + [far] * hbm,
        out_specs=[vm] * (len(outs) - far_outs) + [far] * far_outs,
        scratch_shapes=scratch,
        compiler_params=pltpu.CompilerParams(vmem_limit_bytes=limit * MIB),
        cost_estimate=pl.CostEstimate(flops=flops, bytes_accessed=1 << 20, transcendentals=0),
        name=name,
    )(*args)


def both_sides(cells):
    count = lax.axis_size("pts")
    up = [(i, i + 1) for i in range(count - 1)]
    down = [(i + 1, i) for i in range(count - 1)]
    return lax.ppermute(cells, "pts", up), lax.ppermute(cells, "pts", down)


def shards(
    systems, features, task_ids, pattern, aggregate, coarse_inverse, task_cov, lengthscales, noise
):
    count, width = systems.shape
    blocks = width // BS
    coarse = coarse_inverse.shape[1]
    rows = count + coarse
    top, below, lanes, _ = shape_of(count, coarse)
    ranks = lax.axis_size("pts")
    sides = lax.axis_size("probe")

    def shape(*dims, kind=f32):
        return jax.ShapeDtypeStruct(dims, kind)

    jac, pack, extra = call(
        invert_kernel,
        [shape(blocks, BS, BS), shape(SYS + 2 * count, width), shape(TASKS + FEAT, width)],
        [features, task_ids, aggregate, systems, task_cov, coarse_inverse, pattern, lengthscales, noise],
        "invert",
        hbm=9,
        scratch=[
            pltpu.VMEM((blocks, BS, BS), f32),
            pltpu.VMEM(features.shape, f32),
            pltpu.VMEM(task_ids.shape, jnp.int32),
            pltpu.VMEM(aggregate.shape, jnp.int32),
            pltpu.VMEM(systems.shape, f32),
            pltpu.VMEM(task_cov.shape, f32),
            pltpu.VMEM(coarse_inverse.shape, f32),
            pltpu.SMEM(pattern.shape, jnp.int32),
            pltpu.SMEM(lengthscales.shape, f32),
            pltpu.SMEM(noise.shape, f32),
            pltpu.SemaphoreType.DMA((9,)),
        ],
        flops=10**10,
    )
    pack_l, pack_r = both_sides(pack)
    hi, lo, sim = call(
        build_kernel,
        [
            shape(blocks, BAND, BS, kind=bf16),
            shape(blocks, BAND, BS, kind=bf16),
            shape(blocks, BAND, BS),
        ],
        [pack, pack_l, pack_r, extra],
        "build",
        far_outs=1,
        scratch=[pltpu.VMEM((blocks, BAND, BS), f32), pltpu.SemaphoreType.DMA((blocks,))],
        flops=3 * 10**9,
        limit=24,
    )
    v0, d1 = call(
        first_kernel,
        [shape(rows, width), shape(rows, width)],
        [pack, pack_l, pack_r, extra, hi, lo, jac],
        "first",
        flops=10**9,
    )
    d1_l, d1_r = both_sides(d1)
    (early,) = call(
        early_moments_kernel, [shape(top + below, lanes)], [pack, d1, v0], "early", flops=10**9
    )
    v1, d2 = call(
        second_kernel,
        [shape(rows, width), shape(rows, width)],
        [extra, d1, d1_l, d1_r, hi, lo, jac],
        "second",
        flops=10**9,
    )
    d2_l, d2_r = both_sides(d2)
    (late,) = call(
        functools.partial(late_moments_kernel, count=count),
        [shape(top + below, lanes)],
        [early, d1, d2, v1],
        "late",
        flops=10**9,
    )
    place = lax.axis_index("pts").astype(jnp.int32)[None]
    probe = lax.axis_index("probe").astype(jnp.int32)[None]
    (gram,) = call(
        functools.partial(third_kernel, count=count, held=coarse_inverse.shape[0]),
        [shape(ranks, top + below, lanes)],
        [place, extra, late, d2, d2_l, d2_r, hi, lo],
        "third",
        smem=1,
        flops=10**9,
    )
    gram = lax.all_to_all(gram, "pts", 0, 0, tiled=True)
    stored = [pack, pack_l, pack_r, d1, d1_l, d1_r, d2, d2_l, d2_r, hi, lo, sim]
    answer, grads = call(
        functools.partial(final_kernel, sides=sides * count, points=ranks * width),
        [shape(count, width), shape(ranks * sides, TASKS, LANES)],
        [probe, gram] + stored,
        "final",
        smem=1,
        hbm=len(stored),
        scratch=[pltpu.VMEM(a.shape, a.dtype) for a in stored]
        + [pltpu.SemaphoreType.DMA((len(stored),))],
        flops=10**9,
        limit=32,
    )
    grads = lax.all_to_all(grads, ("pts", "probe"), 0, 0, tiled=True)
    grads = jnp.sum(grads, axis=0)
    return answer, grads[:FEAT, TASKS], grads[:, :TASKS]


def solution(mesh):
    return jax.shard_map(
        shards,
        mesh=mesh,
        in_specs=(
            P("probe", ("groups", "pts")),
            P(None, ("groups", "pts")),
            P(("groups", "pts")),
            P(("groups", "pts"), None),
            P(("groups", "pts")),
            P(("groups", "pts"), None),
            P("groups", None),
            P("groups"),
            P("groups"),
        ),
        out_specs=(P("probe", ("groups", "pts")), P("groups"), P("groups", None)),
        check_vma=False,
    )
```

```python
import functools

import jax
import jax.numpy as jnp
from jax import lax
from jax.experimental import pallas as pl
from jax.experimental.pallas import tpu as pltpu
from jax.sharding import PartitionSpec as P

BS = 256
REACH = 3
FEAT = 8
TASKS = 16
ITERS = 3
SLOTS = 2 * REACH + 1
BAND = SLOTS * BS
BASE = 32
GROUP = 4
LANES = 128
SYS = 2 * FEAT

highest = lax.Precision.HIGHEST
f32 = jnp.float32
bf16 = jnp.bfloat16
NN = (((1,), (0,)), ((), ()))
NT = (((1,), (1,)), ((), ()))
TN = (((0,), (0,)), ((), ()))


def dot(a, b, dims=NN, precision=None):
    return lax.dot_general(a, b, dims, precision=precision, preferred_element_type=f32)


def iota(shape, dim):
    return lax.broadcasted_iota(jnp.int32, shape, dim)


def split(x, parts):
    out = []
    for _ in range(parts - 1):
        head = x.astype(bf16).astype(f32)
        out.append(head)
        x = x - head
    out.append(x.astype(bf16).astype(f32))
    return out


def column(ref, size):
    rows = iota((size, 1), 0)
    out = jnp.zeros((size, 1), f32)
    for i in range(size):
        out = jnp.where(rows == i, ref[i], out)
    return out


def one_hot(ids, size):
    return (iota((size, ids.shape[1]), 0).astype(f32) == ids).astype(f32)


def noise_row(noise_ref, ids):
    out = jnp.zeros(ids.shape, f32)
    for t in range(TASKS):
        out = jnp.where(ids == float(t), noise_ref[t], out)
    return out


def weight(pat_ref, block, offset):
    if offset != REACH:
        return pat_ref[block, offset].astype(f32)
    total = pat_ref[block, 0]
    for o in range(1, SLOTS):
        total = total + pat_ref[block, o]
    return total.astype(f32)


def near_stack(scaled, table):
    s0, s1, s2 = split(scaled, 3)
    n0, n1, n2 = split(-0.5 * jnp.sum(scaled * scaled, axis=0, keepdims=True), 3)
    rows = iota(scaled.shape, 0)
    norms = jnp.where(rows == 0, n0, jnp.where(rows == 1, n1, jnp.where(rows == 2, n2, 0.0)))
    pad = jnp.zeros((LANES - 7 * FEAT - 3 * TASKS, scaled.shape[1]), f32)
    stack = jnp.concatenate([s0, s0, s1, s1, s0, s2, norms, table, table, table, pad], axis=0)
    return stack.T.astype(bf16)


def own_stack(scaled, picked):
    s0, s1, s2 = split(scaled, 3)
    rows = iota(scaled.shape, 0)
    ones = jnp.where(rows < 3, 1.0, 0.0)
    count = scaled.shape[1]
    tail = LANES - 7 * FEAT - 3 * TASKS
    left = jnp.concatenate(
        [s0, s1, s0, s1, s2, s0, ones, jnp.zeros((3 * TASKS + tail, count), f32)], axis=0
    ).astype(bf16)
    right = jnp.concatenate(
        [jnp.zeros((7 * FEAT, count), f32)] + split(picked, 3) + [jnp.zeros((tail, count), f32)],
        axis=0,
    ).astype(bf16)
    sides = [
        jnp.concatenate([left[:, i : i + BS], right[:, i : i + BS]], axis=1)
        for i in range(0, count, BS)
    ]
    return sides, -0.5 * jnp.sum(scaled * scaled, axis=0, keepdims=True)


def small_inverse(p):
    n = len(p)
    if n == 1:
        return [[1.0 / p[0][0]]]
    if n == 2:
        a, b, d = p[0][0], p[0][1], p[1][1]
        r = 1.0 / (a * d - b * b)
        off = -b * r
        return [[d * r, off], [off, a * r]]
    h = n // 2
    ainv = small_inverse([row[:h] for row in p[:h]])
    b = [row[h:] for row in p[:h]]
    t = [[sum(ainv[i][k] * b[k][j] for k in range(h)) for j in range(h)] for i in range(h)]
    s = [[None] * h for _ in range(h)]
    for i in range(h):
        for j in range(i, h):
            s[i][j] = s[j][i] = p[h + i][h + j] - sum(b[k][i] * t[k][j] for k in range(h))
    sinv = small_inverse(s)
    u = [[sum(t[i][k] * sinv[k][j] for k in range(h)) for j in range(h)] for i in range(h)]
    out = [[None] * n for _ in range(n)]
    for i in range(h):
        for j in range(h):
            out[h + i][h + j] = sinv[i][j]
            out[i][h + j] = out[h + j][i] = -u[i][j]
    for i in range(h):
        for j in range(i, h):
            out[i][j] = out[j][i] = ainv[i][j] + sum(u[i][k] * t[j][k] for k in range(h))
    return out


def sweep_base(cells):
    lane = iota((BASE, LANES), 1)
    start = lane - lane % BASE
    inner = iota((1, LANES), 1) % BASE
    sub = iota((BASE, 1), 0)
    for g in range(BASE // GROUP):
        first = g * GROUP
        cols = [
            jnp.take_along_axis(cells, start + (first + t), axis=1, mode="promise_in_bounds")
            for t in range(GROUP)
        ]
        rows = [cells[first + t : first + t + 1, :] for t in range(GROUP)]
        pivots = [[cols[u][first + t : first + t + 1, :] for u in range(GROUP)] for t in range(GROUP)]
        inv = small_inverse(pivots)
        rows = [jnp.where(inner == first + t, -1.0, rows[t]) for t in range(GROUP)]
        group = (inner >= first) & (inner < first + GROUP)
        for t in range(GROUP):
            rows[t] = jnp.where(group & (inner != first + t), 0.0, rows[t])
        new = [sum(inv[t][u] * rows[u] for u in range(GROUP)) for t in range(GROUP)]
        cells = jnp.where(group, 0.0, cells)
        for t in range(GROUP):
            cells = cells - cols[t] * new[t]
        for t in range(GROUP):
            cells = jnp.where(sub == first + t, new[t], cells)
    return cells


def fetch(pairs, sems):
    copies = [pltpu.make_async_copy(a, b, sems.at[i]) for i, (a, b) in enumerate(pairs)]
    for copy in copies:
        copy.start()
    return copies


def invert_kernel(
    feat_hbm, ids_hbm, agg_hbm, sys_hbm, cov_hbm, coarse_hbm, pat_hbm, len_hbm, noise_hbm,
    jac_ref, pack_ref, extra_ref,
    work, feat_ref, ids_ref, agg_ref, sys_ref, cov_ref, coarse_ref, pat_ref, len_ref, noise_ref, sems,
):
    blocks = work.shape[0]
    width = blocks * BS
    pairs = [
        (feat_hbm, feat_ref), (ids_hbm, ids_ref), (agg_hbm, agg_ref), (cov_hbm, cov_ref),
        (pat_hbm, pat_ref), (len_hbm, len_ref), (noise_hbm, noise_ref), (coarse_hbm, coarse_ref),
        (sys_hbm, sys_ref),
    ]
    for copy in fetch(pairs, sems):
        copy.wait()
    scaled = feat_ref[...] / column(len_ref, FEAT)
    ids = ids_ref[...].astype(f32).reshape(1, width)
    which = agg_ref[...].astype(f32).reshape(1, width)
    table = one_hot(ids, TASKS)
    noise = noise_row(noise_ref, ids)
    c0, c1, c2 = split(cov_ref[...], 3)
    tab = table.astype(bf16)
    picked = (dot(c2.astype(bf16), tab) + dot(c1.astype(bf16), tab)) + dot(c0.astype(bf16), tab)
    rows = iota((FEAT, width), 0)
    weights = jnp.zeros((1, width), f32)
    places = iota((1, width), 1)
    for m in range(blocks):
        for o in range(SLOTS):
            weights = jnp.where(places == m * SLOTS + o, weight(pat_ref, m, o), weights)
    pack_ref[0:FEAT, :] = scaled
    pack_ref[FEAT : 2 * FEAT, :] = jnp.where(
        rows == 0, ids, jnp.where(rows == 1, which, 0.0)
    )
    count = sys_ref.shape[0]
    pack_ref[SYS : SYS + count, :] = sys_ref[...]
    extra_ref[0:TASKS, :] = picked
    tail = jnp.where(rows == 0, noise, jnp.where(rows == 1, weights, 0.0))
    held = coarse_ref.shape[0]
    inverse = jnp.concatenate(
        [coarse_ref[...], jnp.zeros((held, width - coarse_ref.shape[1]), f32)], axis=1
    )
    for r in range(held):
        tail = jnp.where(rows == 2 + r, inverse[r : r + 1], tail)
    extra_ref[TASKS : TASKS + FEAT, :] = tail
    near = near_stack(scaled, table)
    mates, norm = own_stack(scaled, picked)
    eye = iota((BS, BS), 0) == iota((BS, BS), 1)
    for m in range(blocks):
        at = slice(m * BS, (m + 1) * BS)
        both = dot(near[at], mates[m])
        block = weight(pat_ref, m, REACH) * jnp.exp(both[:, :BS] + norm[:, at]) * both[:, BS:]
        work[m] = block + jnp.where(eye, noise[:, at], 0.0)
    seg = iota((BASE, LANES), 1) // BASE
    wide = iota((BASE, BS), 1)
    deep = iota((BASE, BS), 0)
    for k in range(BS // BASE):
        first = k * BASE
        tile, inside = first // LANES, first % LANES
        strips = [work[m, first : first + BASE, :] for m in range(blocks)]
        cells = jnp.where(iota((BASE, LANES), 1) % BASE == iota((BASE, LANES), 0), 1.0, 0.0)
        for m in range(blocks):
            piece = strips[m][:, tile * LANES : (tile + 1) * LANES]
            shift = (BASE * m - inside) % LANES
            if shift:
                piece = pltpu.roll(piece, shift, axis=1)
            cells = jnp.where(seg == m, piece, cells)
        inv = -sweep_base(cells)
        held = (wide >= first) & (wide < first + BASE)
        minus = jnp.where(wide - first == deep, -1.0, 0.0)
        stack = jnp.concatenate(
            [jnp.where(held, minus, s) for s in strips]
            + [jnp.zeros((LANES - blocks * BASE, BS), f32)],
            axis=0,
        )
        spread = jnp.concatenate([jnp.where(seg == m, inv, 0.0) for m in range(blocks)], axis=0)
        new = dot(spread, stack, precision=highest)
        gone = (iota((1, BS), 1) >= first) & (iota((1, BS), 1) < first + BASE)
        for m in range(blocks):
            row = new[m * BASE : (m + 1) * BASE, :]
            r0, r1, r2 = split(strips[m], 3)
            p0, p1, p2 = split(row, 3)
            a = jnp.concatenate([r0, r0, r1, r1, r0, r2], axis=0).astype(bf16)
            b = jnp.concatenate([p0, p1, p0, p1, p2, p0], axis=0).astype(bf16)
            work[m] = jnp.where(gone, 0.0, work[m]) - dot(a, b, TN)
            work[m, first : first + BASE, :] = row
    for m in range(blocks):
        at = slice(m * BS, (m + 1) * BS)
        inv = -work[m]
        for i, part in enumerate(split(inv, 3)):
            jac_ref[i, m] = part.astype(bf16)
        pack_ref[SYS + count :, at] = dot(sys_ref[:, at], inv, precision=highest)


def own_places(m):
    return [(j, j, REACH + j - m) for j in range(REACH)]


def halo_places(m):
    lefts = [(j - m, j, j - m) for j in range(m, REACH)]
    return lefts + [(REACH - m + j, REACH + j, 2 * REACH - m + j) for j in range(m + 1)]


def build_kernel(*refs, places, sides):
    cells, (own_ref, extra_ref) = refs[:sides], refs[sides : sides + 2]
    hi_ref, lo_ref, sim_hbm, sim_ref, sems = refs[sides + 2 :]
    blocks = hi_ref.shape[0]
    near = []
    for ref in cells:
        near.append(near_stack(ref[0:FEAT, :], one_hot(ref[FEAT : FEAT + 1, :], TASKS)))
    mates, norm = own_stack(own_ref[0:FEAT, :], extra_ref[0:TASKS, :])
    weights = extra_ref[TASKS + 1 : TASKS + 2, :]
    for m in range(blocks):
        for row, j, o in places(m):
            part = near[j // REACH][(j % REACH) * BS : (j % REACH + 1) * BS]
            both = dot(part, mates[m])
            place = m * SLOTS + o
            exponent = both[:, :BS] + norm[:, m * BS : (m + 1) * BS]
            similar = weights[:, place : place + 1] * jnp.exp(exponent)
            kernel = similar * both[:, BS:]
            head = kernel.astype(bf16)
            rows = slice(row * BS, (row + 1) * BS)
            sim_ref[m, rows, :] = similar
            hi_ref[m, rows, :] = head
            lo_ref[m, rows, :] = (kernel - head.astype(f32)).astype(bf16)
        pltpu.make_async_copy(sim_ref.at[m], sim_hbm.at[m], sems.at[m]).start()
    for m in range(blocks):
        pltpu.make_async_copy(sim_ref.at[m], sim_hbm.at[m], sems.at[m]).wait()


def operate(own, left, right, noise, own_hi, own_lo, halo_hi, halo_lo):
    rows = own.shape[0]
    width = own.shape[1]

    def pieces(vectors):
        head, tail = split(vectors, 2)
        return jnp.concatenate([head, tail], axis=0).astype(bf16)

    mine, lefts, rights = pieces(own), pieces(left), pieces(right)
    out = []
    for m in range(REACH):
        beyond = jnp.concatenate([lefts[:, m * BS :], rights[:, : (m + 1) * BS]], axis=1)
        first = dot(mine, own_hi[m]) + dot(beyond, halo_hi[m])
        second = dot(mine[:rows], own_lo[m]) + dot(beyond[:rows], halo_lo[m])
        out.append(first[:rows] + first[rows:] + second)
    return jnp.concatenate(out, axis=1) + noise * own


def smooth(image, jac_ref):
    rows = image.shape[0]
    out = []
    for m in range(jac_ref.shape[1]):
        pieces = jnp.concatenate(split(image[:, m * BS : (m + 1) * BS], 3), axis=0).astype(bf16)
        a = dot(pieces, jac_ref[0, m])
        b = dot(pieces[: 2 * rows], jac_ref[1, m])
        c = dot(pieces[:rows], jac_ref[2, m])
        out.append(a[:rows] + (a[rows : 2 * rows] + b[:rows] + (a[2 * rows :] + b[rows:] + c)))
    return jnp.concatenate(out, axis=1)


def first_kernel(own_ref, left_ref, right_ref, extra_ref, *refs):
    kernel, (jac_ref, image_ref, next_ref) = refs[:4], refs[4:]
    count = (own_ref.shape[0] - SYS) // 2
    coarse = image_ref.shape[0] - count

    def basis(ref):
        z = one_hot(ref[FEAT + 1 : FEAT + 2, :], coarse)
        return jnp.concatenate([ref[SYS + count :, :], z], axis=0)

    noise = extra_ref[TASKS : TASKS + 1, :]
    image = operate(basis(own_ref), basis(left_ref), basis(right_ref), noise, *kernel)
    image_ref[...] = image
    next_ref[...] = smooth(image, jac_ref)


def second_kernel(extra_ref, vec_ref, left_ref, right_ref, early_ref, *refs):
    kernel, (jac_ref, image_ref, next_ref) = refs[:4], refs[4:]
    noise = extra_ref[TASKS : TASKS + 1, :]
    image = operate(vec_ref[...], left_ref[...], right_ref[...], noise, *kernel)
    image_ref[...] = image
    next_ref[...] = smooth(image, jac_ref)


def pitch_of(coarse):
    return coarse + 1


def lanes_of(coarse):
    return -(-5 * pitch_of(coarse) // LANES) * LANES


def moment(vectors, images, pairs):
    count = pairs.shape[0]
    table = dot(images, vectors, NT, lax.Precision.HIGH)
    own = jnp.sum(pairs, axis=1, keepdims=True)
    if images.shape[0] > count:
        own = jnp.concatenate([own, jnp.zeros((images.shape[0] - count, 1), f32)], axis=0)
    return jnp.concatenate([table, own], axis=1)


def spread_out(parts, lanes):
    rows, pitch = next(iter(parts.values())).shape
    cells = [parts.get(k, jnp.zeros((rows, pitch), f32)) for k in range(5)]
    if lanes > 5 * pitch:
        cells.append(jnp.zeros((rows, lanes - 5 * pitch), f32))
    return jnp.concatenate(cells, axis=1)


def folded(low, high):
    order = low.shape[0]
    row, col = iota((order, order), 0), iota((order, order), 1)
    diagonal = jnp.sum(jnp.where(row == col, high, 0.0), axis=1, keepdims=True)
    return jnp.concatenate([jnp.where(row >= col, low, high), diagonal], axis=1)


def unfolded(cells):
    order = cells.shape[0]
    row, col = iota((order, order), 0), iota((order, order), 1)
    square = cells[:, :order]
    turned = dot(square, jnp.where(row == col, 1.0, 0.0), TN, highest)
    low = jnp.where(row >= col, square, turned)
    high = jnp.where(row < col, square, jnp.where(row > col, turned, cells[:, order:]))
    return low, high


def early_moments_kernel(own_ref, d1_ref, v0_ref, out_ref):
    count = (own_ref.shape[0] - SYS) // 2
    coarse = d1_ref.shape[0] - count
    lanes = out_ref.shape[1]
    pitch = pitch_of(coarse)
    systems = own_ref[SYS : SYS + count, :]
    pre = own_ref[SYS + count :, :]
    z = one_hot(own_ref[FEAT + 1 : FEAT + 2, :], coarse)
    d1, v0 = d1_ref[...], v0_ref[...]
    m0 = moment(z, v0, pre * v0[:count])
    m1 = moment(d1[count:], v0, d1[:count] * v0[:count])
    out_ref[0:count, :] = spread_out({0: m0[:count], 1: m1[:count]}, lanes)
    start = moment(z, systems, systems * pre)
    if coarse > count:
        start = jnp.concatenate([start, jnp.zeros((coarse - count, pitch), f32)], axis=0)
    fold = folded(m0[count:, :coarse], m1[count:, :coarse])
    out_ref[count:, :] = spread_out({0: fold, 3: start}, lanes)


def late_moments_kernel(before_ref, d1_ref, d2_ref, v1_ref, out_ref, *, count):
    lanes = out_ref.shape[1]
    d1, d2, v1 = d1_ref[...], d2_ref[...], v1_ref[...]
    coarse = d1.shape[0] - count
    m2 = moment(d1[count:], v1, d1[:count] * v1[:count])
    m3 = moment(d2[count:], v1, d2[:count] * v1[:count])
    out_ref[0:count, :] = before_ref[0:count, :] + spread_out({2: m2[:count], 3: m3[:count]}, lanes)
    fold = folded(m2[count:, :coarse], m3[count:, :coarse])
    out_ref[count:, :] = before_ref[count:, :] + spread_out({1: fold}, lanes)


def third_kernel(
    place_ref, extra_ref, before_ref, vec_ref, left_ref, right_ref, *refs, count, held
):
    kernel, out_ref = refs[:4], refs[4]
    coarse = vec_ref.shape[0] - count
    lanes = out_ref.shape[2]
    pitch = pitch_of(coarse)
    d2 = vec_ref[...]
    noise = extra_ref[TASKS : TASKS + 1, :]
    v2 = operate(d2, left_ref[...], right_ref[...], noise, *kernel)
    m4 = moment(d2[count:], v2, d2[:count] * v2[:count])
    row = iota((coarse, 1), 0)
    start = place_ref[0] * held
    inverse = jnp.zeros((coarse, pitch), f32)
    for r in range(held):
        line = extra_ref[TASKS + 2 + r : TASKS + 3 + r, 0:pitch]
        inverse = jnp.where(row == start + r, line, inverse)
    top = before_ref[0:count, :] + spread_out({4: m4[:count]}, lanes)
    bottom = before_ref[count:, :] + spread_out({2: m4[count:], 4: inverse}, lanes)
    for c in range(out_ref.shape[0]):
        out_ref[c, 0:count, :] = top
        out_ref[c, count:, :] = bottom


def final_kernel(
    probe_ref, gram_ref, *refs, sides, points,
):
    far, (sol_ref, grad_ref), near_refs, sems = refs[:15], refs[15:17], refs[17:32], refs[32]
    copies = fetch(list(zip(far, near_refs)), sems)
    (
        own_ref, left_ref, right_ref, d1_ref, d1l_ref, d1r_ref, d2_ref, d2l_ref, d2r_ref,
        *kernel_refs,
    ) = near_refs
    width = own_ref.shape[1]
    count = (own_ref.shape[0] - SYS) // 2
    rows = d1_ref.shape[0]
    coarse = rows - count
    pitch = pitch_of(coarse)
    wide = -(-3 * pitch // LANES) * LANES
    blocks = width // BS
    edge = width - REACH * BS
    gram = gram_ref[0]
    for c in range(1, gram_ref.shape[0]):
        gram = gram + gram_ref[c]
    bottom = gram[count:]
    gram = jnp.concatenate([gram[:count], jnp.zeros((count, wide), f32)], axis=1)
    squares = list(unfolded(bottom[:, :pitch])) + list(unfolded(bottom[:, pitch : 2 * pitch]))
    squares.append(bottom[:, 2 * pitch : 2 * pitch + coarse])
    lane = iota((1, wide), 1)
    slot, inside = lane // pitch, lane % pitch
    live = lane < 3 * pitch
    is_vec = live & (inside < coarse)
    is_one = live & (inside == coarse)

    def shifted(j):
        return jnp.where(live, gram[:, j * pitch : j * pitch + wide], 0.0)

    own = [shifted(j) for j in range(3)]
    gap = jnp.zeros((coarse, 1), f32)
    rest = jnp.zeros((coarse, wide - 3 * pitch), f32)
    hankel = []
    for i in range(3):
        line = [squares[i], gap, squares[i + 1], gap, squares[i + 2], gap]
        hankel.append(jnp.concatenate(line + ([rest] if wide > 3 * pitch else []), axis=1))
        hankel.append(jnp.zeros((1, wide), f32))
    if wide > 3 * pitch:
        hankel.append(jnp.zeros((wide - 3 * pitch, wide), f32))
    hankel = jnp.concatenate(hankel, axis=0)
    block0 = lane < pitch
    inverse = bottom[:, 4 * pitch : 4 * pitch + coarse]
    inverse = jnp.concatenate([inverse, jnp.zeros((coarse, wide - coarse), f32)], axis=1)
    inverse = jnp.concatenate([inverse, jnp.zeros((wide - coarse, wide), f32)], axis=0)
    start = bottom[:count, 3 * pitch : 4 * pitch]
    start = jnp.concatenate([start, jnp.zeros((count, wide - pitch), f32)], axis=1)
    against = jnp.where(
        block0, start, jnp.where(live, pltpu.roll(jnp.where(live, own[0], 0.0), pitch, axis=1), 0.0)
    )

    def total(x):
        return jnp.sum(x, axis=1, keepdims=True)

    def scalars(u, i):
        return total(jnp.where(lane == i * pitch + coarse, u, 0.0))

    def metric(u):
        out = dot(jnp.where(is_vec, u, 0.0), hankel, precision=highest)
        for j in range(3):
            out = out + scalars(u, j) * own[j]
        out = jnp.where(is_vec, out, 0.0)
        for i in range(3):
            out = jnp.where(lane == i * pitch + coarse, total(u * own[i]), out)
        return out

    def corrected(w):
        return dot(jnp.where(lane < coarse, w, 0.0), inverse, precision=highest)

    pre = corrected(against) + jnp.where(lane == coarse, 1.0, 0.0)
    direction = pre
    gamma = total(pre * against)
    answer = jnp.zeros_like(pre)
    image_sum = jnp.zeros_like(pre)
    for step in range(ITERS):
        image = metric(direction)
        alpha = gamma / total(direction * image)
        answer = answer + alpha * direction
        if step + 1 < ITERS:
            image_sum = image_sum + alpha * image
            moved_on = jnp.where(live & (slot > 0), pltpu.roll(direction, pitch, axis=1), 0.0)
            pre = pre - alpha * (moved_on + corrected(image))
            gamma_new = total(pre * (against - image_sum))
            direction = pre + (gamma_new / gamma) * direction
            gamma = gamma_new

    for copy in copies[:9]:
        copy.wait()
    pack = jnp.concatenate(
        [left_ref[:, edge:], own_ref[...], right_ref[:, : width - edge]], axis=1
    )
    z = one_hot(pack[FEAT + 1 : FEAT + 2], coarse)
    q0 = pack[SYS + count :]
    d1 = jnp.concatenate([d1l_ref[:, edge:], d1_ref[...], d1r_ref[:, : width - edge]], axis=1)
    d2 = jnp.concatenate([d2l_ref[:, edge:], d2_ref[...], d2r_ref[:, : width - edge]], axis=1)
    span = q0.shape[1]
    step = -(-coarse // FEAT) * FEAT
    deep = -(-3 * step // LANES) * LANES
    parts, basis = [], []
    for i, rest in enumerate((z, d1[count:], d2[count:])):
        parts.append(answer[:, i * pitch : i * pitch + coarse])
        basis.append(rest)
        if step > coarse:
            parts.append(jnp.zeros((count, step - coarse), f32))
            basis.append(jnp.zeros((step - coarse, span), f32))
    if deep > 3 * step:
        parts.append(jnp.zeros((count, deep - 3 * step), f32))
        basis.append(jnp.zeros((deep - 3 * step, span), f32))
    x = dot(
        jnp.concatenate(parts, axis=1), jnp.concatenate(basis, axis=0), precision=highest
    )
    x = x + scalars(answer, 0) * q0 + scalars(answer, 1) * d1[:count]
    x = x + scalars(answer, 2) * d2[:count]
    mine = slice(REACH * BS, REACH * BS + width)
    sol_ref[...] = x[:, mine]

    systems = pack[SYS : SYS + count]
    line = iota((count, 1), 0) + probe_ref[0] * count
    right = jnp.where(line == 0, x, systems)
    coef = jnp.where(line == 0, 0.5 / points, -0.5 / (sides - 1) / points)
    weighted = x[:, mine] * coef
    r0, r1 = split(right, 2)
    w0, w1 = split(weighted, 2)
    near = jnp.concatenate([r0, r1, r0], axis=0).astype(bf16)
    mate = jnp.concatenate([w0, w0, w1], axis=0).astype(bf16)
    scaled = pack[0:FEAT]
    table = one_hot(pack[FEAT : FEAT + 1], TASKS)
    ones = jnp.ones((8, span), f32)
    terms = jnp.concatenate([scaled, ones, scaled * scaled], axis=0)
    t0, t1 = split(terms, 2)
    pad8 = jnp.zeros((8, span), f32)
    both = jnp.concatenate([t0, pad8, t1, pad8], axis=0).astype(bf16)
    heads = jnp.concatenate([t0, pad8], axis=0).astype(bf16)
    tables = table.astype(bf16)
    high = 32
    for copy in copies[9:]:
        copy.wait()
    length_total = jnp.zeros((FEAT, 1), f32)
    task_total = jnp.zeros((TASKS, TASKS), f32)
    for m in range(blocks):
        at = slice(m * BS, (m + 1) * BS)
        sums = jnp.zeros((high, BS), f32)
        held_sums = jnp.zeros((TASKS, BS), f32)
        places = [(0, row, j + REACH) for row, j, _ in own_places(m)]
        places += [(1, row, j if j < REACH else j + REACH) for row, j, _ in halo_places(m)]
        for side, row, block in places:
            hi_ref, lo_ref, sim_ref = kernel_refs[3 * side : 3 * side + 3]
            j = slice(block * BS, (block + 1) * BS)
            rows_at = slice(row * BS, (row + 1) * BS)
            outer = dot(near[:, j], mate[:, at], TN)
            kernel = hi_ref[m, rows_at, :].astype(f32) + lo_ref[m, rows_at, :].astype(f32)
            energy = outer * kernel
            held = outer * sim_ref[m, rows_at, :]
            e0, e1 = (part.astype(bf16) for part in split(energy, 2))
            h0, h1 = (part.astype(bf16) for part in split(held, 2))
            first = dot(both[:, j], e0)
            sums = sums + first[:high] + first[high:] + dot(heads[:, j], e1)
            held_sums = held_sums + dot(tables[:, j], h0) + dot(tables[:, j], h1)
        mid = slice((REACH + m) * BS, (REACH + m + 1) * BS)
        left = scaled[:, mid]
        value = left * left * sums[FEAT : FEAT + 1] + sums[2 * FEAT : 3 * FEAT]
        value = value - 2.0 * left * sums[:FEAT]
        length_total = length_total + jnp.sum(value, axis=1, keepdims=True)
        task_total = task_total + dot(table[:, mid], held_sums, NT, highest)
    lane = iota((TASKS, LANES), 1)
    lengths = jnp.concatenate([length_total, jnp.zeros((TASKS - FEAT, 1), f32)], axis=0)
    wide_tasks = jnp.concatenate([task_total, jnp.zeros((TASKS, LANES - TASKS), f32)], axis=1)
    value = jnp.where(lane == TASKS, lengths, wide_tasks)
    for c in range(grad_ref.shape[0]):
        grad_ref[c] = value


MIB = 1024 * 1024


def call(body, outs, args, name, smem=0, hbm=0, far_outs=0, scratch=(), flops=0, limit=16):
    if hbm:
        args = args[:-hbm] + [pltpu.with_memory_space_constraint(a, pltpu.HBM) for a in args[-hbm:]]
    if far_outs:
        outs = outs[:-far_outs] + [pltpu.HBM(o.shape, o.dtype) for o in outs[-far_outs:]]
    vm = pl.BlockSpec(memory_space=pltpu.VMEM)
    sm = pl.BlockSpec(memory_space=pltpu.SMEM)
    far = pl.BlockSpec(memory_space=pltpu.HBM)
    return pl.pallas_call(
        body,
        out_shape=outs,
        in_specs=[sm] * smem + [vm] * (len(args) - smem - hbm) + [far] * hbm,
        out_specs=[vm] * (len(outs) - far_outs) + [far] * far_outs,
        scratch_shapes=scratch,
        compiler_params=pltpu.CompilerParams(vmem_limit_bytes=limit * MIB),
        cost_estimate=pl.CostEstimate(flops=flops, bytes_accessed=1 << 20, transcendentals=0),
        name=name,
    )(*args)


def both_sides(cells):
    count = lax.axis_size("pts")
    up = [(i, i + 1) for i in range(count - 1)]
    down = [(i + 1, i) for i in range(count - 1)]
    return lax.ppermute(cells, "pts", up), lax.ppermute(cells, "pts", down)


def shards(
    systems, features, task_ids, pattern, aggregate, coarse_inverse, task_cov, lengthscales, noise
):
    count, width = systems.shape
    blocks = width // BS
    coarse = coarse_inverse.shape[1]
    rows = count + coarse
    lanes = lanes_of(coarse)
    assert blocks == REACH
    ranks = lax.axis_size("pts")
    sides = lax.axis_size("probe")

    def shape(*dims, kind=f32):
        return jax.ShapeDtypeStruct(dims, kind)

    jac, pack, extra = call(
        invert_kernel,
        [shape(3, blocks, BS, BS, kind=bf16), shape(SYS + 2 * count, width), shape(TASKS + FEAT, width)],
        [features, task_ids, aggregate, systems, task_cov, coarse_inverse, pattern, lengthscales, noise],
        "invert",
        hbm=9,
        scratch=[
            pltpu.VMEM((blocks, BS, BS), f32),
            pltpu.VMEM(features.shape, f32),
            pltpu.VMEM(task_ids.shape, jnp.int32),
            pltpu.VMEM(aggregate.shape, jnp.int32),
            pltpu.VMEM(systems.shape, f32),
            pltpu.VMEM(task_cov.shape, f32),
            pltpu.VMEM(coarse_inverse.shape, f32),
            pltpu.SMEM(pattern.shape, jnp.int32),
            pltpu.SMEM(lengthscales.shape, f32),
            pltpu.SMEM(noise.shape, f32),
            pltpu.SemaphoreType.DMA((9,)),
        ],
        flops=10**10,
    )
    pack_l, pack_r = both_sides(pack)

    def build(places, deep, cells, name):
        return call(
            functools.partial(build_kernel, places=places, sides=len(cells)),
            [
                shape(blocks, deep, BS, kind=bf16),
                shape(blocks, deep, BS, kind=bf16),
                shape(blocks, deep, BS),
            ],
            cells + [pack, extra],
            name,
            far_outs=1,
            scratch=[pltpu.VMEM((blocks, deep, BS), f32), pltpu.SemaphoreType.DMA((blocks,))],
            flops=10**9,
        )

    own_hi, own_lo, own_sim = build(own_places, width, [pack], "build_own")
    halo_hi, halo_lo, halo_sim = build(
        halo_places, BAND - width, [pack_l, pack_r], "build_halo"
    )
    kernel = [own_hi, own_lo, halo_hi, halo_lo]
    v0, d1 = call(
        first_kernel,
        [shape(rows, width), shape(rows, width)],
        [pack, pack_l, pack_r, extra] + kernel + [jac],
        "first",
        flops=10**9,
    )
    d1_l, d1_r = both_sides(d1)
    (early,) = call(
        early_moments_kernel, [shape(rows, lanes)], [pack, d1, v0], "early", flops=10**9
    )
    v1, d2 = call(
        second_kernel,
        [shape(rows, width), shape(rows, width)],
        [extra, d1, d1_l, d1_r, early] + kernel + [jac],
        "second",
        flops=10**9,
    )
    d2_l, d2_r = both_sides(d2)
    (late,) = call(
        functools.partial(late_moments_kernel, count=count),
        [shape(rows, lanes)],
        [early, d1, d2, v1],
        "late",
        flops=10**9,
    )
    place = lax.axis_index("pts").astype(jnp.int32)[None]
    probe = lax.axis_index("probe").astype(jnp.int32)[None]
    (gram,) = call(
        functools.partial(third_kernel, count=count, held=coarse_inverse.shape[0]),
        [shape(ranks, rows, lanes)],
        [place, extra, late, d2, d2_l, d2_r] + kernel,
        "third",
        smem=1,
        flops=10**9,
    )
    gram = lax.all_to_all(gram, "pts", 0, 0, tiled=True)
    stored = [pack, pack_l, pack_r, d1, d1_l, d1_r, d2, d2_l, d2_r]
    stored += [own_hi, own_lo, own_sim, halo_hi, halo_lo, halo_sim]
    answer, grads = call(
        functools.partial(final_kernel, sides=sides * count, points=ranks * width),
        [shape(count, width), shape(ranks * sides, TASKS, LANES)],
        [probe, gram] + stored,
        "final",
        smem=1,
        hbm=len(stored),
        scratch=[pltpu.VMEM(a.shape, a.dtype) for a in stored]
        + [pltpu.SemaphoreType.DMA((len(stored),))],
        flops=10**9,
        limit=32,
    )
    grads = lax.all_to_all(grads, ("pts", "probe"), 0, 0, tiled=True)
    grads = jnp.sum(grads, axis=0)
    return answer, grads[:FEAT, TASKS], grads[:, :TASKS]


def solution(mesh):
    return jax.shard_map(
        shards,
        mesh=mesh,
        in_specs=(
            P("probe", ("groups", "pts")),
            P(None, ("groups", "pts")),
            P(("groups", "pts")),
            P(("groups", "pts"), None),
            P(("groups", "pts")),
            P(("groups", "pts"), None),
            P("groups", None),
            P("groups"),
            P("groups"),
        ),
        out_specs=(P("probe", ("groups", "pts")), P("groups"), P("groups", None)),
        check_vma=False,
    )
```

```python
import functools

import jax
import jax.numpy as jnp
from jax import lax
from jax.experimental import pallas as pl
from jax.experimental.pallas import tpu as pltpu
from jax.sharding import PartitionSpec as P

BS = 256
REACH = 3
FEAT = 8
TASKS = 16
ITERS = 3
SLOTS = 2 * REACH + 1
BAND = SLOTS * BS
BASE = 32
GROUP = 4
LANES = 128
SYS = 2 * FEAT

highest = lax.Precision.HIGHEST
f32 = jnp.float32
bf16 = jnp.bfloat16
NN = (((1,), (0,)), ((), ()))
NT = (((1,), (1,)), ((), ()))
TN = (((0,), (0,)), ((), ()))


def dot(a, b, dims=NN, precision=None):
    return lax.dot_general(a, b, dims, precision=precision, preferred_element_type=f32)


def iota(shape, dim):
    return lax.broadcasted_iota(jnp.int32, shape, dim)


def split(x, parts):
    out = []
    for _ in range(parts - 1):
        head = x.astype(bf16).astype(f32)
        out.append(head)
        x = x - head
    out.append(x.astype(bf16).astype(f32))
    return out


def column(ref, size):
    rows = iota((size, 1), 0)
    out = jnp.zeros((size, 1), f32)
    for i in range(size):
        out = jnp.where(rows == i, ref[i], out)
    return out


def one_hot(ids, size):
    return (iota((size, ids.shape[1]), 0).astype(f32) == ids).astype(f32)


def noise_row(noise_ref, ids):
    out = jnp.zeros(ids.shape, f32)
    for t in range(TASKS):
        out = jnp.where(ids == float(t), noise_ref[t], out)
    return out


def weight(pat_ref, block, offset):
    if offset != REACH:
        return pat_ref[block, offset].astype(f32)
    total = pat_ref[block, 0]
    for o in range(1, SLOTS):
        total = total + pat_ref[block, o]
    return total.astype(f32)


def near_stack(scaled, table):
    s0, s1, s2 = split(scaled, 3)
    n0, n1, n2 = split(-0.5 * jnp.sum(scaled * scaled, axis=0, keepdims=True), 3)
    rows = iota(scaled.shape, 0)
    norms = jnp.where(rows == 0, n0, jnp.where(rows == 1, n1, jnp.where(rows == 2, n2, 0.0)))
    pad = jnp.zeros((LANES - 7 * FEAT - 3 * TASKS, scaled.shape[1]), f32)
    stack = jnp.concatenate([s0, s0, s1, s1, s0, s2, norms, table, table, table, pad], axis=0)
    return stack.T.astype(bf16)


def own_stack(scaled, picked):
    s0, s1, s2 = split(scaled, 3)
    rows = iota(scaled.shape, 0)
    ones = jnp.where(rows < 3, 1.0, 0.0)
    count = scaled.shape[1]
    tail = LANES - 7 * FEAT - 3 * TASKS
    left = jnp.concatenate(
        [s0, s1, s0, s1, s2, s0, ones, jnp.zeros((3 * TASKS + tail, count), f32)], axis=0
    ).astype(bf16)
    right = jnp.concatenate(
        [jnp.zeros((7 * FEAT, count), f32)] + split(picked, 3) + [jnp.zeros((tail, count), f32)],
        axis=0,
    ).astype(bf16)
    sides = [
        jnp.concatenate([left[:, i : i + BS], right[:, i : i + BS]], axis=1)
        for i in range(0, count, BS)
    ]
    return sides, -0.5 * jnp.sum(scaled * scaled, axis=0, keepdims=True)


def small_inverse(p):
    n = len(p)
    if n == 1:
        return [[1.0 / p[0][0]]]
    if n == 2:
        a, b, d = p[0][0], p[0][1], p[1][1]
        r = 1.0 / (a * d - b * b)
        off = -b * r
        return [[d * r, off], [off, a * r]]
    h = n // 2
    ainv = small_inverse([row[:h] for row in p[:h]])
    b = [row[h:] for row in p[:h]]
    t = [[sum(ainv[i][k] * b[k][j] for k in range(h)) for j in range(h)] for i in range(h)]
    s = [[None] * h for _ in range(h)]
    for i in range(h):
        for j in range(i, h):
            s[i][j] = s[j][i] = p[h + i][h + j] - sum(b[k][i] * t[k][j] for k in range(h))
    sinv = small_inverse(s)
    u = [[sum(t[i][k] * sinv[k][j] for k in range(h)) for j in range(h)] for i in range(h)]
    out = [[None] * n for _ in range(n)]
    for i in range(h):
        for j in range(h):
            out[h + i][h + j] = sinv[i][j]
            out[i][h + j] = out[h + j][i] = -u[i][j]
    for i in range(h):
        for j in range(i, h):
            out[i][j] = out[j][i] = ainv[i][j] + sum(u[i][k] * t[j][k] for k in range(h))
    return out


def sweep_base(cells):
    lane = iota((BASE, LANES), 1)
    start = lane - lane % BASE
    inner = iota((1, LANES), 1) % BASE
    sub = iota((BASE, 1), 0)
    for g in range(BASE // GROUP):
        first = g * GROUP
        cols = [
            jnp.take_along_axis(cells, start + (first + t), axis=1, mode="promise_in_bounds")
            for t in range(GROUP)
        ]
        rows = [cells[first + t : first + t + 1, :] for t in range(GROUP)]
        pivots = [[cols[u][first + t : first + t + 1, :] for u in range(GROUP)] for t in range(GROUP)]
        inv = small_inverse(pivots)
        rows = [jnp.where(inner == first + t, -1.0, rows[t]) for t in range(GROUP)]
        group = (inner >= first) & (inner < first + GROUP)
        for t in range(GROUP):
            rows[t] = jnp.where(group & (inner != first + t), 0.0, rows[t])
        new = [sum(inv[t][u] * rows[u] for u in range(GROUP)) for t in range(GROUP)]
        cells = jnp.where(group, 0.0, cells)
        for t in range(GROUP):
            cells = cells - cols[t] * new[t]
        for t in range(GROUP):
            cells = jnp.where(sub == first + t, new[t], cells)
    return cells


def fetch(pairs, sems):
    copies = [pltpu.make_async_copy(a, b, sems.at[i]) for i, (a, b) in enumerate(pairs)]
    for copy in copies:
        copy.start()
    return copies


def invert_kernel(
    feat_hbm, ids_hbm, agg_hbm, sys_hbm, cov_hbm, coarse_hbm, pat_hbm, len_hbm, noise_hbm,
    jac_ref, pack_ref, extra_ref,
    work, feat_ref, ids_ref, agg_ref, sys_ref, cov_ref, coarse_ref, pat_ref, len_ref, noise_ref, sems,
):
    blocks = work.shape[0]
    width = blocks * BS
    pairs = [
        (feat_hbm, feat_ref), (ids_hbm, ids_ref), (agg_hbm, agg_ref), (cov_hbm, cov_ref),
        (pat_hbm, pat_ref), (len_hbm, len_ref), (noise_hbm, noise_ref), (coarse_hbm, coarse_ref),
        (sys_hbm, sys_ref),
    ]
    for copy in fetch(pairs, sems):
        copy.wait()
    scaled = feat_ref[...] / column(len_ref, FEAT)
    ids = ids_ref[...].astype(f32).reshape(1, width)
    which = agg_ref[...].astype(f32).reshape(1, width)
    table = one_hot(ids, TASKS)
    noise = noise_row(noise_ref, ids)
    c0, c1, c2 = split(cov_ref[...], 3)
    tab = table.astype(bf16)
    picked = (dot(c2.astype(bf16), tab) + dot(c1.astype(bf16), tab)) + dot(c0.astype(bf16), tab)
    rows = iota((FEAT, width), 0)
    weights = jnp.zeros((1, width), f32)
    places = iota((1, width), 1)
    for m in range(blocks):
        for o in range(SLOTS):
            weights = jnp.where(places == m * SLOTS + o, weight(pat_ref, m, o), weights)
    pack_ref[0:FEAT, :] = scaled
    pack_ref[FEAT : 2 * FEAT, :] = jnp.where(
        rows == 0, ids, jnp.where(rows == 1, which, 0.0)
    )
    extra_ref[0:TASKS, :] = picked
    tail = jnp.where(rows == 0, noise, jnp.where(rows == 1, weights, 0.0))
    held = coarse_ref.shape[0]
    inverse = jnp.concatenate(
        [coarse_ref[...], jnp.zeros((held, width - coarse_ref.shape[1]), f32)], axis=1
    )
    for r in range(held):
        tail = jnp.where(rows == 2 + r, inverse[r : r + 1], tail)
    extra_ref[TASKS : TASKS + FEAT, :] = tail
    near = near_stack(scaled, table)
    mates, norm = own_stack(scaled, picked)
    eye = iota((BS, BS), 0) == iota((BS, BS), 1)
    for m in range(blocks):
        at = slice(m * BS, (m + 1) * BS)
        both = dot(near[at], mates[m])
        block = weight(pat_ref, m, REACH) * jnp.exp(both[:, :BS] + norm[:, at]) * both[:, BS:]
        work[m] = block + jnp.where(eye, noise[:, at], 0.0)
    seg = iota((BASE, LANES), 1) // BASE
    wide = iota((BASE, BS), 1)
    deep = iota((BASE, BS), 0)
    for k in range(BS // BASE):
        first = k * BASE
        tile, inside = first // LANES, first % LANES
        strips = [work[m, first : first + BASE, :] for m in range(blocks)]
        cells = jnp.where(iota((BASE, LANES), 1) % BASE == iota((BASE, LANES), 0), 1.0, 0.0)
        for m in range(blocks):
            piece = strips[m][:, tile * LANES : (tile + 1) * LANES]
            shift = (BASE * m - inside) % LANES
            if shift:
                piece = pltpu.roll(piece, shift, axis=1)
            cells = jnp.where(seg == m, piece, cells)
        inv = -sweep_base(cells)
        held = (wide >= first) & (wide < first + BASE)
        minus = jnp.where(wide - first == deep, -1.0, 0.0)
        stack = jnp.concatenate(
            [jnp.where(held, minus, s) for s in strips]
            + [jnp.zeros((LANES - blocks * BASE, BS), f32)],
            axis=0,
        )
        spread = jnp.concatenate([jnp.where(seg == m, inv, 0.0) for m in range(blocks)], axis=0)
        new = dot(spread, stack, precision=highest)
        gone = (iota((1, BS), 1) >= first) & (iota((1, BS), 1) < first + BASE)
        for m in range(blocks):
            row = new[m * BASE : (m + 1) * BASE, :]
            r0, r1, r2 = split(strips[m], 3)
            p0, p1, p2 = split(row, 3)
            a = jnp.concatenate([r0, r0, r1, r1, r0, r2], axis=0).astype(bf16)
            b = jnp.concatenate([p0, p1, p0, p1, p2, p0], axis=0).astype(bf16)
            work[m] = jnp.where(gone, 0.0, work[m]) - dot(a, b, TN)
            work[m, first : first + BASE, :] = row
    for m in range(blocks):
        at = slice(m * BS, (m + 1) * BS)
        inv = -work[m]
        for i, part in enumerate(split(inv, 3)):
            jac_ref[i, m] = part.astype(bf16)
        pack_ref[SYS:, at] = dot(sys_ref[:, at], inv, precision=highest)


def own_places(m):
    return [(j, j, REACH + j - m) for j in range(REACH)]


def halo_places(m):
    lefts = [(j - m, j, j - m) for j in range(m, REACH)]
    return lefts + [(REACH - m + j, REACH + j, 2 * REACH - m + j) for j in range(m + 1)]


def build_kernel(*refs, places, sides):
    cells, (own_ref, extra_ref) = refs[:sides], refs[sides : sides + 2]
    hi_ref, lo_ref, sim_ref = refs[sides + 2 :]
    blocks = hi_ref.shape[0]
    near = []
    for ref in cells:
        near.append(near_stack(ref[0:FEAT, :], one_hot(ref[FEAT : FEAT + 1, :], TASKS)))
    mates, norm = own_stack(own_ref[0:FEAT, :], extra_ref[0:TASKS, :])
    weights = extra_ref[TASKS + 1 : TASKS + 2, :]
    for m in range(blocks):
        for row, j, o in places(m):
            part = near[j // REACH][(j % REACH) * BS : (j % REACH + 1) * BS]
            both = dot(part, mates[m])
            place = m * SLOTS + o
            exponent = both[:, :BS] + norm[:, m * BS : (m + 1) * BS]
            similar = weights[:, place : place + 1] * jnp.exp(exponent)
            kernel = similar * both[:, BS:]
            head = kernel.astype(bf16)
            rows = slice(row * BS, (row + 1) * BS)
            sim_ref[m, rows, :] = similar
            hi_ref[m, rows, :] = head
            lo_ref[m, rows, :] = (kernel - head.astype(f32)).astype(bf16)


def operate(own, left, right, noise, own_hi, own_lo, halo_hi, halo_lo):
    rows = own.shape[0]
    width = own.shape[1]

    def pieces(vectors):
        head, tail = split(vectors, 2)
        return jnp.concatenate([head, tail], axis=0).astype(bf16)

    mine, lefts, rights = pieces(own), pieces(left), pieces(right)
    out = []
    for m in range(REACH):
        beyond = jnp.concatenate([lefts[:, m * BS :], rights[:, : (m + 1) * BS]], axis=1)
        first = dot(mine, own_hi[m]) + dot(beyond, halo_hi[m])
        second = dot(mine[:rows], own_lo[m]) + dot(beyond[:rows], halo_lo[m])
        out.append(first[:rows] + first[rows:] + second)
    return jnp.concatenate(out, axis=1) + noise * own


def smooth(image, jac_ref):
    rows = image.shape[0]
    out = []
    for m in range(jac_ref.shape[1]):
        pieces = jnp.concatenate(split(image[:, m * BS : (m + 1) * BS], 3), axis=0).astype(bf16)
        a = dot(pieces, jac_ref[0, m])
        b = dot(pieces[: 2 * rows], jac_ref[1, m])
        c = dot(pieces[:rows], jac_ref[2, m])
        out.append(a[:rows] + (a[rows : 2 * rows] + b[:rows] + (a[2 * rows :] + b[rows:] + c)))
    return jnp.concatenate(out, axis=1)


def first_kernel(own_ref, left_ref, right_ref, extra_ref, *refs):
    kernel, (jac_ref, image_ref, next_ref) = refs[:4], refs[4:]
    count = own_ref.shape[0] - SYS
    coarse = image_ref.shape[0] - count

    def basis(ref):
        z = one_hot(ref[FEAT + 1 : FEAT + 2, :], coarse)
        return jnp.concatenate([ref[SYS:, :], z], axis=0)

    noise = extra_ref[TASKS : TASKS + 1, :]
    image = operate(basis(own_ref), basis(left_ref), basis(right_ref), noise, *kernel)
    image_ref[...] = image
    next_ref[...] = smooth(image, jac_ref)


def second_kernel(extra_ref, vec_ref, left_ref, right_ref, early_ref, *refs):
    kernel, (jac_ref, image_ref, next_ref) = refs[:4], refs[4:]
    noise = extra_ref[TASKS : TASKS + 1, :]
    image = operate(vec_ref[...], left_ref[...], right_ref[...], noise, *kernel)
    image_ref[...] = image
    next_ref[...] = smooth(image, jac_ref)


def pitch_of(coarse):
    return coarse + 1


def lanes_of(coarse):
    return -(-5 * pitch_of(coarse) // LANES) * LANES


def moment(vectors, images, pairs):
    count = pairs.shape[0]
    table = dot(images, vectors, NT, lax.Precision.HIGH)
    own = jnp.sum(pairs, axis=1, keepdims=True)
    if images.shape[0] > count:
        own = jnp.concatenate([own, jnp.zeros((images.shape[0] - count, 1), f32)], axis=0)
    return jnp.concatenate([table, own], axis=1)


def spread_out(parts, lanes):
    rows, pitch = next(iter(parts.values())).shape
    cells = [parts.get(k, jnp.zeros((rows, pitch), f32)) for k in range(5)]
    if lanes > 5 * pitch:
        cells.append(jnp.zeros((rows, lanes - 5 * pitch), f32))
    return jnp.concatenate(cells, axis=1)


def folded(low, high):
    order = low.shape[0]
    row, col = iota((order, order), 0), iota((order, order), 1)
    diagonal = jnp.sum(jnp.where(row == col, high, 0.0), axis=1, keepdims=True)
    return jnp.concatenate([jnp.where(row >= col, low, high), diagonal], axis=1)


def unfolded(cells):
    order = cells.shape[0]
    row, col = iota((order, order), 0), iota((order, order), 1)
    square = cells[:, :order]
    turned = dot(square, jnp.where(row == col, 1.0, 0.0), TN, highest)
    low = jnp.where(row >= col, square, turned)
    high = jnp.where(row < col, square, jnp.where(row > col, turned, cells[:, order:]))
    return low, high


def early_moments_kernel(own_ref, sys_ref, d1_ref, v0_ref, *refs):
    sources, (out_ref, *stashes), sems = refs[:6], refs[6:13], refs[13]
    copies = fetch(list(zip(sources, stashes)), sems)
    count = own_ref.shape[0] - SYS
    coarse = d1_ref.shape[0] - count
    lanes = out_ref.shape[1]
    pitch = pitch_of(coarse)
    systems = sys_ref[...]
    pre = own_ref[SYS:, :]
    z = one_hot(own_ref[FEAT + 1 : FEAT + 2, :], coarse)
    d1, v0 = d1_ref[...], v0_ref[...]
    m0 = moment(z, v0, pre * v0[:count])
    m1 = moment(d1[count:], v0, d1[:count] * v0[:count])
    out_ref[0:count, :] = spread_out({0: m0[:count], 1: m1[:count]}, lanes)
    start = moment(z, systems, systems * pre)
    if coarse > count:
        start = jnp.concatenate([start, jnp.zeros((coarse - count, pitch), f32)], axis=0)
    fold = folded(m0[count:, :coarse], m1[count:, :coarse])
    out_ref[count:, :] = spread_out({0: fold, 3: start}, lanes)
    for copy in copies:
        copy.wait()


def late_moments_kernel(before_ref, d1_ref, d2_ref, v1_ref, out_ref, *, count):
    lanes = out_ref.shape[1]
    d1, d2, v1 = d1_ref[...], d2_ref[...], v1_ref[...]
    coarse = d1.shape[0] - count
    m2 = moment(d1[count:], v1, d1[:count] * v1[:count])
    m3 = moment(d2[count:], v1, d2[:count] * v1[:count])
    out_ref[0:count, :] = before_ref[0:count, :] + spread_out({2: m2[:count], 3: m3[:count]}, lanes)
    fold = folded(m2[count:, :coarse], m3[count:, :coarse])
    out_ref[count:, :] = before_ref[count:, :] + spread_out({1: fold}, lanes)


def third_kernel(
    place_ref, extra_ref, before_ref, vec_ref, left_ref, right_ref, *refs, count, held
):
    kernel, out_ref = refs[:4], refs[4]
    coarse = vec_ref.shape[0] - count
    lanes = out_ref.shape[2]
    pitch = pitch_of(coarse)
    d2 = vec_ref[...]
    noise = extra_ref[TASKS : TASKS + 1, :]
    v2 = operate(d2, left_ref[...], right_ref[...], noise, *kernel)
    m4 = moment(d2[count:], v2, d2[:count] * v2[:count])
    row = iota((coarse, 1), 0)
    start = place_ref[0] * held
    inverse = jnp.zeros((coarse, pitch), f32)
    for r in range(held):
        line = extra_ref[TASKS + 2 + r : TASKS + 3 + r, 0:pitch]
        inverse = jnp.where(row == start + r, line, inverse)
    top = before_ref[0:count, :] + spread_out({4: m4[:count]}, lanes)
    bottom = before_ref[count:, :] + spread_out({2: m4[count:], 4: inverse}, lanes)
    for c in range(out_ref.shape[0]):
        out_ref[c, 0:count, :] = top
        out_ref[c, count:, :] = bottom


def final_kernel(
    probe_ref, gram_ref, *refs, sides, points,
):
    far, (sol_ref, grad_ref), near_refs, sems = refs[:16], refs[16:18], refs[18:34], refs[34]
    copies = fetch(list(zip(far, near_refs)), sems)
    (
        sys_ref, own_ref, left_ref, right_ref, d1_ref, d1l_ref, d1r_ref, d2_ref, d2l_ref, d2r_ref,
        *kernel_refs,
    ) = near_refs
    width = own_ref.shape[1]
    count = own_ref.shape[0] - SYS
    rows = d1_ref.shape[0]
    coarse = rows - count
    pitch = pitch_of(coarse)
    wide = -(-3 * pitch // LANES) * LANES
    blocks = width // BS
    edge = width - REACH * BS
    gram = gram_ref[0]
    for c in range(1, gram_ref.shape[0]):
        gram = gram + gram_ref[c]
    bottom = gram[count:]
    gram = jnp.concatenate([gram[:count], jnp.zeros((count, wide), f32)], axis=1)
    squares = list(unfolded(bottom[:, :pitch])) + list(unfolded(bottom[:, pitch : 2 * pitch]))
    squares.append(bottom[:, 2 * pitch : 2 * pitch + coarse])
    lane = iota((1, wide), 1)
    slot, inside = lane // pitch, lane % pitch
    live = lane < 3 * pitch
    is_vec = live & (inside < coarse)
    is_one = live & (inside == coarse)

    def shifted(j):
        return jnp.where(live, gram[:, j * pitch : j * pitch + wide], 0.0)

    own = [shifted(j) for j in range(3)]
    gap = jnp.zeros((coarse, 1), f32)
    rest = jnp.zeros((coarse, wide - 3 * pitch), f32)
    hankel = []
    for i in range(3):
        line = [squares[i], gap, squares[i + 1], gap, squares[i + 2], gap]
        hankel.append(jnp.concatenate(line + ([rest] if wide > 3 * pitch else []), axis=1))
        hankel.append(jnp.zeros((1, wide), f32))
    if wide > 3 * pitch:
        hankel.append(jnp.zeros((wide - 3 * pitch, wide), f32))
    hankel = jnp.concatenate(hankel, axis=0)
    block0 = lane < pitch
    inverse = bottom[:, 4 * pitch : 4 * pitch + coarse]
    inverse = jnp.concatenate([inverse, jnp.zeros((coarse, wide - coarse), f32)], axis=1)
    inverse = jnp.concatenate([inverse, jnp.zeros((wide - coarse, wide), f32)], axis=0)
    start = bottom[:count, 3 * pitch : 4 * pitch]
    start = jnp.concatenate([start, jnp.zeros((count, wide - pitch), f32)], axis=1)
    against = jnp.where(
        block0, start, jnp.where(live, pltpu.roll(jnp.where(live, own[0], 0.0), pitch, axis=1), 0.0)
    )

    def total(x):
        return jnp.sum(x, axis=1, keepdims=True)

    def scalars(u, i):
        return total(jnp.where(lane == i * pitch + coarse, u, 0.0))

    def metric(u):
        out = dot(jnp.where(is_vec, u, 0.0), hankel, precision=highest)
        for j in range(3):
            out = out + scalars(u, j) * own[j]
        out = jnp.where(is_vec, out, 0.0)
        for i in range(3):
            out = jnp.where(lane == i * pitch + coarse, total(u * own[i]), out)
        return out

    def corrected(w):
        return dot(jnp.where(lane < coarse, w, 0.0), inverse, precision=highest)

    pre = corrected(against) + jnp.where(lane == coarse, 1.0, 0.0)
    direction = pre
    gamma = total(pre * against)
    answer = jnp.zeros_like(pre)
    image_sum = jnp.zeros_like(pre)
    for step in range(ITERS):
        image = metric(direction)
        alpha = gamma / total(direction * image)
        answer = answer + alpha * direction
        if step + 1 < ITERS:
            image_sum = image_sum + alpha * image
            moved_on = jnp.where(live & (slot > 0), pltpu.roll(direction, pitch, axis=1), 0.0)
            pre = pre - alpha * (moved_on + corrected(image))
            gamma_new = total(pre * (against - image_sum))
            direction = pre + (gamma_new / gamma) * direction
            gamma = gamma_new

    for copy in copies[:10]:
        copy.wait()
    pack = jnp.concatenate(
        [left_ref[:, edge:], own_ref[...], right_ref[:, : width - edge]], axis=1
    )
    z = one_hot(pack[FEAT + 1 : FEAT + 2], coarse)
    q0 = pack[SYS:]
    d1 = jnp.concatenate([d1l_ref[:, edge:], d1_ref[...], d1r_ref[:, : width - edge]], axis=1)
    d2 = jnp.concatenate([d2l_ref[:, edge:], d2_ref[...], d2r_ref[:, : width - edge]], axis=1)
    span = q0.shape[1]
    step = -(-coarse // FEAT) * FEAT
    deep = -(-3 * step // LANES) * LANES
    parts, basis = [], []
    for i, rest in enumerate((z, d1[count:], d2[count:])):
        parts.append(answer[:, i * pitch : i * pitch + coarse])
        basis.append(rest)
        if step > coarse:
            parts.append(jnp.zeros((count, step - coarse), f32))
            basis.append(jnp.zeros((step - coarse, span), f32))
    if deep > 3 * step:
        parts.append(jnp.zeros((count, deep - 3 * step), f32))
        basis.append(jnp.zeros((deep - 3 * step, span), f32))
    x = dot(
        jnp.concatenate(parts, axis=1), jnp.concatenate(basis, axis=0), precision=highest
    )
    x = x + scalars(answer, 0) * q0 + scalars(answer, 1) * d1[:count]
    x = x + scalars(answer, 2) * d2[:count]
    mine = slice(REACH * BS, REACH * BS + width)
    sol_ref[...] = x[:, mine]

    line = iota((count, 1), 0) + probe_ref[0] * count
    right = jnp.where(line == 0, x[:, mine], sys_ref[...])
    coef = jnp.where(line == 0, 0.5 / points, -0.5 / (sides - 1) / points)
    r0, r1 = split(right, 2)
    w0, w1 = split(x * coef, 2)
    rest = LANES - 3 * count
    near = jnp.concatenate([w0, w1, w0, jnp.zeros((rest, span), f32)], axis=0).T.astype(bf16)
    mate = jnp.concatenate([r0, r0, r1, jnp.zeros((rest, width), f32)], axis=0).astype(bf16)
    scaled = pack[0:FEAT]
    table = one_hot(pack[FEAT : FEAT + 1], TASKS)
    ones = jnp.ones((8, span), f32)
    terms = jnp.concatenate([scaled, ones, scaled * scaled], axis=0)
    t0, t1 = split(terms, 2)
    pad8 = jnp.zeros((8, span), f32)
    both = jnp.concatenate([t0, pad8, t1, pad8], axis=0).astype(bf16)
    heads = jnp.concatenate([t0, pad8], axis=0).astype(bf16)
    tables = table.astype(bf16)
    high = 32
    for copy in copies[10:]:
        copy.wait()
    length_total = jnp.zeros((FEAT, 1), f32)
    task_total = jnp.zeros((TASKS, TASKS), f32)
    for m in range(blocks):
        at = slice(m * BS, (m + 1) * BS)
        sums = jnp.zeros((high, BS), f32)
        held_sums = jnp.zeros((TASKS, BS), f32)
        places = [(0, row, j + REACH) for row, j, _ in own_places(m)]
        places += [(1, row, j if j < REACH else j + REACH) for row, j, _ in halo_places(m)]
        for side, row, block in places:
            hi_ref, lo_ref, sim_ref = kernel_refs[3 * side : 3 * side + 3]
            j = slice(block * BS, (block + 1) * BS)
            rows_at = slice(row * BS, (row + 1) * BS)
            outer = dot(near[j], mate[:, at])
            kernel = hi_ref[m, rows_at, :].astype(f32) + lo_ref[m, rows_at, :].astype(f32)
            energy = outer * kernel
            held = outer * sim_ref[m, rows_at, :]
            e0, e1 = (part.astype(bf16) for part in split(energy, 2))
            h0, h1 = (part.astype(bf16) for part in split(held, 2))
            first = dot(both[:, j], e0)
            sums = sums + first[:high] + first[high:] + dot(heads[:, j], e1)
            held_sums = held_sums + dot(tables[:, j], h0) + dot(tables[:, j], h1)
        mid = slice((REACH + m) * BS, (REACH + m + 1) * BS)
        left = scaled[:, mid]
        value = left * left * sums[FEAT : FEAT + 1] + sums[2 * FEAT : 3 * FEAT]
        value = value - 2.0 * left * sums[:FEAT]
        length_total = length_total + jnp.sum(value, axis=1, keepdims=True)
        task_total = task_total + dot(held_sums, table[:, mid], NT, highest)
    half = TASKS // 2
    value = jnp.concatenate(
        [
            task_total[:half],
            task_total[half:],
            length_total,
            jnp.zeros((half, LANES - 2 * TASKS - 1), f32),
        ],
        axis=1,
    )
    for c in range(grad_ref.shape[0]):
        grad_ref[c] = value


def tail_kernel(parts_ref, length_ref, task_ref):
    total = parts_ref[0]
    for c in range(1, parts_ref.shape[0]):
        total = total + parts_ref[c]
    half = TASKS // 2
    task_ref[0:half, :] = total[:, :TASKS]
    task_ref[half:, :] = total[:, TASKS : 2 * TASKS]
    length_ref[...] = total[:, 2 * TASKS : 2 * TASKS + 1]


MIB = 1024 * 1024


def call(body, outs, args, name, smem=0, hbm=0, far_outs=0, scratch=(), flops=0, limit=16):
    if hbm:
        args = args[:-hbm] + [pltpu.with_memory_space_constraint(a, pltpu.HBM) for a in args[-hbm:]]
    if far_outs:
        outs = outs[:-far_outs] + [pltpu.HBM(o.shape, o.dtype) for o in outs[-far_outs:]]
    vm = pl.BlockSpec(memory_space=pltpu.VMEM)
    sm = pl.BlockSpec(memory_space=pltpu.SMEM)
    far = pl.BlockSpec(memory_space=pltpu.HBM)
    return pl.pallas_call(
        body,
        out_shape=outs,
        in_specs=[sm] * smem + [vm] * (len(args) - smem - hbm) + [far] * hbm,
        out_specs=[vm] * (len(outs) - far_outs) + [far] * far_outs,
        scratch_shapes=scratch,
        compiler_params=pltpu.CompilerParams(vmem_limit_bytes=limit * MIB),
        cost_estimate=pl.CostEstimate(flops=flops, bytes_accessed=1 << 20, transcendentals=0),
        name=name,
    )(*args)


def both_sides(cells):
    count = lax.axis_size("pts")
    up = [(i, i + 1) for i in range(count - 1)]
    down = [(i + 1, i) for i in range(count - 1)]
    return lax.ppermute(cells, "pts", up), lax.ppermute(cells, "pts", down)


def shards(
    systems, features, task_ids, pattern, aggregate, coarse_inverse, task_cov, lengthscales, noise
):
    count, width = systems.shape
    blocks = width // BS
    coarse = coarse_inverse.shape[1]
    rows = count + coarse
    lanes = lanes_of(coarse)
    assert blocks == REACH
    ranks = lax.axis_size("pts")
    sides = lax.axis_size("probe")

    def shape(*dims, kind=f32):
        return jax.ShapeDtypeStruct(dims, kind)

    jac, pack, extra = call(
        invert_kernel,
        [shape(3, blocks, BS, BS, kind=bf16), shape(SYS + count, width), shape(TASKS + FEAT, width)],
        [features, task_ids, aggregate, systems, task_cov, coarse_inverse, pattern, lengthscales, noise],
        "invert",
        hbm=9,
        scratch=[
            pltpu.VMEM((blocks, BS, BS), f32),
            pltpu.VMEM(features.shape, f32),
            pltpu.VMEM(task_ids.shape, jnp.int32),
            pltpu.VMEM(aggregate.shape, jnp.int32),
            pltpu.VMEM(systems.shape, f32),
            pltpu.VMEM(task_cov.shape, f32),
            pltpu.VMEM(coarse_inverse.shape, f32),
            pltpu.SMEM(pattern.shape, jnp.int32),
            pltpu.SMEM(lengthscales.shape, f32),
            pltpu.SMEM(noise.shape, f32),
            pltpu.SemaphoreType.DMA((9,)),
        ],
        flops=10**10,
    )
    pack_l, pack_r = both_sides(pack)

    def build(places, deep, cells, name):
        return call(
            functools.partial(build_kernel, places=places, sides=len(cells)),
            [
                shape(blocks, deep, BS, kind=bf16),
                shape(blocks, deep, BS, kind=bf16),
                shape(blocks, deep, BS),
            ],
            cells + [pack, extra],
            name,
            flops=10**9,
        )

    own_hi, own_lo, own_sim = build(own_places, width, [pack], "build_own")
    halo_hi, halo_lo, halo_sim = build(
        halo_places, BAND - width, [pack_l, pack_r], "build_halo"
    )
    kernel = [own_hi, own_lo, halo_hi, halo_lo]
    v0, d1 = call(
        first_kernel,
        [shape(rows, width), shape(rows, width)],
        [pack, pack_l, pack_r, extra] + kernel + [jac],
        "first",
        flops=10**9,
    )
    d1_l, d1_r = both_sides(d1)
    cells = [own_hi, own_lo, own_sim, halo_hi, halo_lo, halo_sim]
    early, *stashed = call(
        early_moments_kernel,
        [shape(rows, lanes)] + [shape(*a.shape, kind=a.dtype) for a in cells],
        [pack, systems, d1, v0] + cells,
        "early",
        far_outs=len(cells),
        scratch=[pltpu.SemaphoreType.DMA((len(cells),))],
        flops=10**9,
    )
    v1, d2 = call(
        second_kernel,
        [shape(rows, width), shape(rows, width)],
        [extra, d1, d1_l, d1_r, early] + kernel + [jac],
        "second",
        flops=10**9,
    )
    d2_l, d2_r = both_sides(d2)
    (late,) = call(
        functools.partial(late_moments_kernel, count=count),
        [shape(rows, lanes)],
        [early, d1, d2, v1],
        "late",
        flops=10**9,
    )
    place = lax.axis_index("pts").astype(jnp.int32)[None]
    probe = lax.axis_index("probe").astype(jnp.int32)[None]
    (gram,) = call(
        functools.partial(third_kernel, count=count, held=coarse_inverse.shape[0]),
        [shape(ranks, rows, lanes)],
        [place, extra, late, d2, d2_l, d2_r] + kernel,
        "third",
        smem=1,
        flops=10**9,
    )
    gram = lax.all_to_all(gram, "pts", 0, 0, tiled=True)
    stored = [systems, pack, pack_l, pack_r, d1, d1_l, d1_r, d2, d2_l, d2_r] + stashed
    answer, grads = call(
        functools.partial(final_kernel, sides=sides * count, points=ranks * width),
        [shape(count, width), shape(ranks * sides, FEAT, LANES)],
        [probe, gram] + stored,
        "final",
        smem=1,
        hbm=len(stored),
        scratch=[pltpu.VMEM(a.shape, a.dtype) for a in stored]
        + [pltpu.SemaphoreType.DMA((len(stored),))],
        flops=10**9,
        limit=32,
    )
    grads = lax.all_to_all(grads, ("pts", "probe"), 0, 0, tiled=True)
    lengths, tasks = call(
        tail_kernel, [shape(FEAT, 1), shape(TASKS, TASKS)], [grads], "tail", flops=10**5
    )
    return answer, lengths[:, 0], tasks


def solution(mesh):
    return jax.shard_map(
        shards,
        mesh=mesh,
        in_specs=(
            P("probe", ("groups", "pts")),
            P(None, ("groups", "pts")),
            P(("groups", "pts")),
            P(("groups", "pts"), None),
            P(("groups", "pts")),
            P(("groups", "pts"), None),
            P("groups", None),
            P("groups"),
            P("groups"),
        ),
        out_specs=(P("probe", ("groups", "pts")), P("groups"), P("groups", None)),
        check_vma=False,
    )
```

```python
import functools

import jax
import jax.numpy as jnp
from jax import lax
from jax.experimental import pallas as pl
from jax.experimental.pallas import tpu as pltpu
from jax.sharding import PartitionSpec as P

BS = 256
REACH = 3
FEAT = 8
TASKS = 16
ITERS = 3
SLOTS = 2 * REACH + 1
BAND = SLOTS * BS
BASE = 32
GROUP = 4
LANES = 128
SYS = 2 * FEAT

highest = lax.Precision.HIGHEST
f32 = jnp.float32
bf16 = jnp.bfloat16
NN = (((1,), (0,)), ((), ()))
NT = (((1,), (1,)), ((), ()))
TN = (((0,), (0,)), ((), ()))


def dot(a, b, dims=NN, precision=None):
    return lax.dot_general(a, b, dims, precision=precision, preferred_element_type=f32)


def iota(shape, dim):
    return lax.broadcasted_iota(jnp.int32, shape, dim)


def split(x, parts):
    out = []
    for _ in range(parts - 1):
        head = x.astype(bf16).astype(f32)
        out.append(head)
        x = x - head
    out.append(x.astype(bf16).astype(f32))
    return out


def column(ref, size):
    rows = iota((size, 1), 0)
    out = jnp.zeros((size, 1), f32)
    for i in range(size):
        out = jnp.where(rows == i, ref[i], out)
    return out


def one_hot(ids, size):
    return (iota((size, ids.shape[1]), 0).astype(f32) == ids).astype(f32)


def noise_row(noise_ref, ids):
    out = jnp.zeros(ids.shape, f32)
    for t in range(TASKS):
        out = jnp.where(ids == float(t), noise_ref[t], out)
    return out


def weight(pat_ref, block, offset):
    if offset != REACH:
        return pat_ref[block, offset].astype(f32)
    total = pat_ref[block, 0]
    for o in range(1, SLOTS):
        total = total + pat_ref[block, o]
    return total.astype(f32)


def near_stack(scaled, table):
    s0, s1, s2 = split(scaled, 3)
    n0, n1, n2 = split(-0.5 * jnp.sum(scaled * scaled, axis=0, keepdims=True), 3)
    rows = iota(scaled.shape, 0)
    norms = jnp.where(rows == 0, n0, jnp.where(rows == 1, n1, jnp.where(rows == 2, n2, 0.0)))
    pad = jnp.zeros((LANES - 7 * FEAT - 3 * TASKS, scaled.shape[1]), f32)
    stack = jnp.concatenate([s0, s0, s1, s1, s0, s2, norms, table, table, table, pad], axis=0)
    return stack.T.astype(bf16)


def own_stack(scaled, picked):
    s0, s1, s2 = split(scaled, 3)
    rows = iota(scaled.shape, 0)
    ones = jnp.where(rows < 3, 1.0, 0.0)
    count = scaled.shape[1]
    tail = LANES - 7 * FEAT - 3 * TASKS
    left = jnp.concatenate(
        [s0, s1, s0, s1, s2, s0, ones, jnp.zeros((3 * TASKS + tail, count), f32)], axis=0
    ).astype(bf16)
    right = jnp.concatenate(
        [jnp.zeros((7 * FEAT, count), f32)] + split(picked, 3) + [jnp.zeros((tail, count), f32)],
        axis=0,
    ).astype(bf16)
    sides = [
        jnp.concatenate([left[:, i : i + BS], right[:, i : i + BS]], axis=1)
        for i in range(0, count, BS)
    ]
    return sides, -0.5 * jnp.sum(scaled * scaled, axis=0, keepdims=True)


def small_inverse(p):
    n = len(p)
    if n == 1:
        return [[1.0 / p[0][0]]]
    if n == 2:
        a, b, d = p[0][0], p[0][1], p[1][1]
        r = 1.0 / (a * d - b * b)
        off = -b * r
        return [[d * r, off], [off, a * r]]
    h = n // 2
    ainv = small_inverse([row[:h] for row in p[:h]])
    b = [row[h:] for row in p[:h]]
    t = [[sum(ainv[i][k] * b[k][j] for k in range(h)) for j in range(h)] for i in range(h)]
    s = [[None] * h for _ in range(h)]
    for i in range(h):
        for j in range(i, h):
            s[i][j] = s[j][i] = p[h + i][h + j] - sum(b[k][i] * t[k][j] for k in range(h))
    sinv = small_inverse(s)
    u = [[sum(t[i][k] * sinv[k][j] for k in range(h)) for j in range(h)] for i in range(h)]
    out = [[None] * n for _ in range(n)]
    for i in range(h):
        for j in range(h):
            out[h + i][h + j] = sinv[i][j]
            out[i][h + j] = out[h + j][i] = -u[i][j]
    for i in range(h):
        for j in range(i, h):
            out[i][j] = out[j][i] = ainv[i][j] + sum(u[i][k] * t[j][k] for k in range(h))
    return out


def with_rows(cells, first, rows):
    top = first - first % 8
    part = cells[top : top + 8]
    sub = iota((8, 1), 0)
    for t, row in enumerate(rows):
        part = jnp.where(sub == first - top + t, row, part)
    pieces = [cells[:top], part, cells[top + 8 :]]
    return jnp.concatenate([p for p in pieces if p.shape[0]], axis=0)


def sweep_base(cells):
    lane = iota((BASE, LANES), 1)
    start = lane - lane % BASE
    inner = iota((1, LANES), 1) % BASE

    def columns(first):
        return [
            jnp.take_along_axis(cells, start + (first + t), axis=1, mode="promise_in_bounds")
            for t in range(GROUP)
        ]

    cols = columns(0)
    for first in range(0, BASE, GROUP):
        ahead = columns(first + GROUP) if first + GROUP < BASE else []
        pivots = [[cols[u][first + t : first + t + 1, :] for u in range(GROUP)] for t in range(GROUP)]
        inv = small_inverse(pivots)
        coming = []
        for col in ahead:
            head = [col[first + t : first + t + 1, :] for t in range(GROUP)]
            factor = [sum(inv[t][u] * head[u] for u in range(GROUP)) for t in range(GROUP)]
            for t in range(GROUP):
                col = col - cols[t] * factor[t]
            coming.append(with_rows(col, first, factor))
        rows = [cells[first + t : first + t + 1, :] for t in range(GROUP)]
        group = (inner >= first) & (inner < first + GROUP)
        for t in range(GROUP):
            rows[t] = jnp.where(inner == first + t, -1.0, jnp.where(group, 0.0, rows[t]))
        new = [sum(inv[t][u] * rows[u] for u in range(GROUP)) for t in range(GROUP)]
        cells = jnp.where(group, 0.0, cells)
        for t in range(GROUP):
            cells = cells - cols[t] * new[t]
        cells = with_rows(cells, first, new)
        cols = coming
    return cells


def fetch(pairs, sems):
    copies = [pltpu.make_async_copy(a, b, sems.at[i]) for i, (a, b) in enumerate(pairs)]
    for copy in copies:
        copy.start()
    return copies


def invert_kernel(
    feat_hbm, ids_hbm, agg_hbm, sys_hbm, cov_hbm, coarse_hbm, pat_hbm, len_hbm, noise_hbm,
    jac_ref, pack_ref, extra_ref,
    work, feat_ref, ids_ref, agg_ref, sys_ref, cov_ref, coarse_ref, pat_ref, len_ref, noise_ref, sems,
):
    blocks = work.shape[0]
    width = blocks * BS
    pairs = [
        (feat_hbm, feat_ref), (ids_hbm, ids_ref), (agg_hbm, agg_ref), (cov_hbm, cov_ref),
        (pat_hbm, pat_ref), (len_hbm, len_ref), (noise_hbm, noise_ref), (coarse_hbm, coarse_ref),
        (sys_hbm, sys_ref),
    ]
    for copy in fetch(pairs, sems):
        copy.wait()
    scaled = feat_ref[...] / column(len_ref, FEAT)
    ids = ids_ref[...].astype(f32).reshape(1, width)
    which = agg_ref[...].astype(f32).reshape(1, width)
    table = one_hot(ids, TASKS)
    noise = noise_row(noise_ref, ids)
    c0, c1, c2 = split(cov_ref[...], 3)
    tab = table.astype(bf16)
    picked = (dot(c2.astype(bf16), tab) + dot(c1.astype(bf16), tab)) + dot(c0.astype(bf16), tab)
    rows = iota((FEAT, width), 0)
    weights = jnp.zeros((1, width), f32)
    places = iota((1, width), 1)
    for m in range(blocks):
        for o in range(SLOTS):
            weights = jnp.where(places == m * SLOTS + o, weight(pat_ref, m, o), weights)
    pack_ref[0:FEAT, :] = scaled
    pack_ref[FEAT : 2 * FEAT, :] = jnp.where(
        rows == 0, ids, jnp.where(rows == 1, which, 0.0)
    )
    extra_ref[0:TASKS, :] = picked
    tail = jnp.where(rows == 0, noise, jnp.where(rows == 1, weights, 0.0))
    held = coarse_ref.shape[0]
    inverse = jnp.concatenate(
        [coarse_ref[...], jnp.zeros((held, width - coarse_ref.shape[1]), f32)], axis=1
    )
    for r in range(held):
        tail = jnp.where(rows == 2 + r, inverse[r : r + 1], tail)
    extra_ref[TASKS : TASKS + FEAT, :] = tail
    near = near_stack(scaled, table)
    mates, norm = own_stack(scaled, picked)
    eye = iota((BS, BS), 0) == iota((BS, BS), 1)
    for m in range(blocks):
        at = slice(m * BS, (m + 1) * BS)
        both = dot(near[at], mates[m])
        block = weight(pat_ref, m, REACH) * jnp.exp(both[:, :BS] + norm[:, at]) * both[:, BS:]
        work[m] = block + jnp.where(eye, noise[:, at], 0.0)
    seg = iota((BASE, LANES), 1) // BASE
    wide = iota((BASE, BS), 1)
    deep = iota((BASE, BS), 0)
    strips = [work[m, 0:BASE, :] for m in range(blocks)]
    for k in range(BS // BASE):
        first = k * BASE
        tile, inside = first // LANES, first % LANES
        cells = jnp.where(iota((BASE, LANES), 1) % BASE == iota((BASE, LANES), 0), 1.0, 0.0)
        for m in range(blocks):
            piece = strips[m][:, tile * LANES : (tile + 1) * LANES]
            shift = (BASE * m - inside) % LANES
            if shift:
                piece = pltpu.roll(piece, shift, axis=1)
            cells = jnp.where(seg == m, piece, cells)
        inv = -sweep_base(cells)
        held = (wide >= first) & (wide < first + BASE)
        minus = jnp.where(wide - first == deep, -1.0, 0.0)
        stack = jnp.concatenate(
            [jnp.where(held, minus, s) for s in strips]
            + [jnp.zeros((LANES - blocks * BASE, BS), f32)],
            axis=0,
        )
        spread = jnp.concatenate([jnp.where(seg == m, inv, 0.0) for m in range(blocks)], axis=0)
        new = dot(spread, stack, precision=highest)
        gone = (iota((1, BS), 1) >= first) & (iota((1, BS), 1) < first + BASE)
        coming = []
        for m in range(blocks):
            row = new[m * BASE : (m + 1) * BASE, :]
            r0, r1, r2 = split(strips[m], 3)
            p0, p1, p2 = split(row, 3)
            a = jnp.concatenate([r0, r0, r1, r1, r0, r2], axis=0).astype(bf16)
            b = jnp.concatenate([p0, p1, p0, p1, p2, p0], axis=0).astype(bf16)
            value = jnp.where(gone, 0.0, work[m]) - dot(a, b, TN)
            coming.append(value[first + BASE : first + 2 * BASE])
            work[m] = value
            work[m, first : first + BASE, :] = row
        strips = coming
    for m in range(blocks):
        inv = -work[m]
        for i, part in enumerate(split(inv, 3)):
            jac_ref[i, m] = part.astype(bf16)
    pack_ref[SYS:, :] = smooth(sys_ref[...], jac_ref)


def own_places(m):
    return [(j, j, REACH + j - m) for j in range(REACH)]


def halo_places(m):
    lefts = [(j - m, j, j - m) for j in range(m, REACH)]
    return lefts + [(REACH - m + j, REACH + j, 2 * REACH - m + j) for j in range(m + 1)]


def build_kernel(*refs, places, sides):
    cells, (own_ref, extra_ref) = refs[:sides], refs[sides : sides + 2]
    hi_ref, lo_ref, sim_ref = refs[sides + 2 :]
    blocks = hi_ref.shape[0]
    near = []
    for ref in cells:
        near.append(near_stack(ref[0:FEAT, :], one_hot(ref[FEAT : FEAT + 1, :], TASKS)))
    mates, norm = own_stack(own_ref[0:FEAT, :], extra_ref[0:TASKS, :])
    weights = extra_ref[TASKS + 1 : TASKS + 2, :]
    for m in range(blocks):
        for row, j, o in places(m):
            part = near[j // REACH][(j % REACH) * BS : (j % REACH + 1) * BS]
            both = dot(part, mates[m])
            place = m * SLOTS + o
            exponent = both[:, :BS] + norm[:, m * BS : (m + 1) * BS]
            similar = weights[:, place : place + 1] * jnp.exp(exponent)
            kernel = similar * both[:, BS:]
            head = kernel.astype(bf16)
            rows = slice(row * BS, (row + 1) * BS)
            sim_ref[m, rows, :] = similar
            hi_ref[m, rows, :] = head
            lo_ref[m, rows, :] = (kernel - head.astype(f32)).astype(bf16)


def operate(own, left, right, noise, own_hi, own_lo, halo_hi, halo_lo):
    rows = own.shape[0]
    width = own.shape[1]

    def pieces(vectors):
        head, tail = split(vectors, 2)
        return jnp.concatenate([head, tail], axis=0).astype(bf16)

    mine, lefts, rights = pieces(own), pieces(left), pieces(right)
    out = []
    for m in range(REACH):
        beyond = jnp.concatenate([lefts[:, m * BS :], rights[:, : (m + 1) * BS]], axis=1)
        first = dot(mine, own_hi[m]) + dot(beyond, halo_hi[m])
        second = dot(mine[:rows], own_lo[m]) + dot(beyond[:rows], halo_lo[m])
        out.append(first[:rows] + first[rows:] + second)
    return jnp.concatenate(out, axis=1) + noise * own


def smooth(image, jac_ref):
    rows = image.shape[0]
    out = []
    for m in range(jac_ref.shape[1]):
        pieces = jnp.concatenate(split(image[:, m * BS : (m + 1) * BS], 3), axis=0).astype(bf16)
        a = dot(pieces, jac_ref[0, m])
        b = dot(pieces[: 2 * rows], jac_ref[1, m])
        c = dot(pieces[:rows], jac_ref[2, m])
        out.append(a[:rows] + (a[rows : 2 * rows] + b[:rows] + (a[2 * rows :] + b[rows:] + c)))
    return jnp.concatenate(out, axis=1)


def first_kernel(own_ref, left_ref, right_ref, extra_ref, *refs):
    kernel, (jac_ref, image_ref, next_ref) = refs[:4], refs[4:]
    count = own_ref.shape[0] - SYS
    coarse = image_ref.shape[0] - count

    def basis(ref):
        z = one_hot(ref[FEAT + 1 : FEAT + 2, :], coarse)
        return jnp.concatenate([ref[SYS:, :], z], axis=0)

    noise = extra_ref[TASKS : TASKS + 1, :]
    image = operate(basis(own_ref), basis(left_ref), basis(right_ref), noise, *kernel)
    image_ref[...] = image
    next_ref[...] = smooth(image, jac_ref)


def second_kernel(extra_ref, vec_ref, left_ref, right_ref, early_ref, *refs):
    kernel, (jac_ref, image_ref, next_ref) = refs[:4], refs[4:]
    noise = extra_ref[TASKS : TASKS + 1, :]
    image = operate(vec_ref[...], left_ref[...], right_ref[...], noise, *kernel)
    image_ref[...] = image
    next_ref[...] = smooth(image, jac_ref)


def pitch_of(coarse):
    return coarse + 1


def lanes_of(coarse):
    return -(-5 * pitch_of(coarse) // LANES) * LANES


def moment(vectors, images, pairs):
    count = pairs.shape[0]
    table = dot(images, vectors, NT, lax.Precision.HIGH)
    own = jnp.sum(pairs, axis=1, keepdims=True)
    if images.shape[0] > count:
        own = jnp.concatenate([own, jnp.zeros((images.shape[0] - count, 1), f32)], axis=0)
    return jnp.concatenate([table, own], axis=1)


def spread_out(parts, lanes):
    rows, pitch = next(iter(parts.values())).shape
    cells = [parts.get(k, jnp.zeros((rows, pitch), f32)) for k in range(5)]
    if lanes > 5 * pitch:
        cells.append(jnp.zeros((rows, lanes - 5 * pitch), f32))
    return jnp.concatenate(cells, axis=1)


def folded(low, high):
    order = low.shape[0]
    row, col = iota((order, order), 0), iota((order, order), 1)
    diagonal = jnp.sum(jnp.where(row == col, high, 0.0), axis=1, keepdims=True)
    return jnp.concatenate([jnp.where(row >= col, low, high), diagonal], axis=1)


def unfolded(cells):
    order = cells.shape[0]
    row, col = iota((order, order), 0), iota((order, order), 1)
    square = cells[:, :order]
    turned = dot(square, jnp.where(row == col, 1.0, 0.0), TN, highest)
    low = jnp.where(row >= col, square, turned)
    high = jnp.where(row < col, square, jnp.where(row > col, turned, cells[:, order:]))
    return low, high


def early_moments_kernel(own_ref, sys_ref, d1_ref, v0_ref, *refs):
    sources, (out_ref, *stashes), sems = refs[:6], refs[6:13], refs[13]
    copies = fetch(list(zip(sources, stashes)), sems)
    count = own_ref.shape[0] - SYS
    coarse = d1_ref.shape[0] - count
    lanes = out_ref.shape[1]
    pitch = pitch_of(coarse)
    systems = sys_ref[...]
    pre = own_ref[SYS:, :]
    z = one_hot(own_ref[FEAT + 1 : FEAT + 2, :], coarse)
    d1, v0 = d1_ref[...], v0_ref[...]
    m0 = moment(z, v0, pre * v0[:count])
    m1 = moment(d1[count:], v0, d1[:count] * v0[:count])
    out_ref[0:count, :] = spread_out({0: m0[:count], 1: m1[:count]}, lanes)
    start = moment(z, systems, systems * pre)
    if coarse > count:
        start = jnp.concatenate([start, jnp.zeros((coarse - count, pitch), f32)], axis=0)
    fold = folded(m0[count:, :coarse], m1[count:, :coarse])
    out_ref[count:, :] = spread_out({0: fold, 3: start}, lanes)
    for copy in copies:
        copy.wait()


def late_moments_kernel(before_ref, d1_ref, d2_ref, v1_ref, out_ref, *, count):
    lanes = out_ref.shape[1]
    d1, d2, v1 = d1_ref[...], d2_ref[...], v1_ref[...]
    coarse = d1.shape[0] - count
    m2 = moment(d1[count:], v1, d1[:count] * v1[:count])
    m3 = moment(d2[count:], v1, d2[:count] * v1[:count])
    out_ref[0:count, :] = before_ref[0:count, :] + spread_out({2: m2[:count], 3: m3[:count]}, lanes)
    fold = folded(m2[count:, :coarse], m3[count:, :coarse])
    out_ref[count:, :] = before_ref[count:, :] + spread_out({1: fold}, lanes)


def third_kernel(
    place_ref, extra_ref, before_ref, vec_ref, left_ref, right_ref, *refs, count, held
):
    kernel, others, (out_ref, *stashes), sems = refs[:4], refs[4:10], refs[10:20], refs[20]
    copies = fetch(list(zip([*others, vec_ref, left_ref, right_ref], stashes)), sems)
    coarse = vec_ref.shape[0] - count
    lanes = out_ref.shape[2]
    pitch = pitch_of(coarse)
    d2 = vec_ref[...]
    noise = extra_ref[TASKS : TASKS + 1, :]
    v2 = operate(d2, left_ref[...], right_ref[...], noise, *kernel)
    m4 = moment(d2[count:], v2, d2[:count] * v2[:count])
    row = iota((coarse, 1), 0)
    start = place_ref[0] * held
    inverse = jnp.zeros((coarse, pitch), f32)
    for r in range(held):
        line = extra_ref[TASKS + 2 + r : TASKS + 3 + r, 0:pitch]
        inverse = jnp.where(row == start + r, line, inverse)
    top = before_ref[0:count, :] + spread_out({4: m4[:count]}, lanes)
    bottom = before_ref[count:, :] + spread_out({2: m4[count:], 4: inverse}, lanes)
    for c in range(out_ref.shape[0]):
        out_ref[c, 0:count, :] = top
        out_ref[c, count:, :] = bottom
    for copy in copies:
        copy.wait()


def final_kernel(
    probe_ref, gram_ref, *refs, sides, points,
):
    far, (sol_ref, grad_ref), near_refs, sems = refs[:16], refs[16:18], refs[18:34], refs[34]
    copies = fetch(list(zip(far, near_refs)), sems)
    (
        sys_ref, own_ref, left_ref, right_ref, d1_ref, d1l_ref, d1r_ref, d2_ref, d2l_ref, d2r_ref,
        *kernel_refs,
    ) = near_refs
    width = own_ref.shape[1]
    count = own_ref.shape[0] - SYS
    rows = d1_ref.shape[0]
    coarse = rows - count
    pitch = pitch_of(coarse)
    wide = -(-3 * pitch // LANES) * LANES
    blocks = width // BS
    edge = width - REACH * BS
    gram = gram_ref[0]
    for c in range(1, gram_ref.shape[0]):
        gram = gram + gram_ref[c]
    bottom = gram[count:]
    gram = jnp.concatenate([gram[:count], jnp.zeros((count, wide), f32)], axis=1)
    squares = list(unfolded(bottom[:, :pitch])) + list(unfolded(bottom[:, pitch : 2 * pitch]))
    squares.append(bottom[:, 2 * pitch : 2 * pitch + coarse])
    lane = iota((1, wide), 1)
    slot, inside = lane // pitch, lane % pitch
    live = lane < 3 * pitch
    is_vec = live & (inside < coarse)
    is_one = live & (inside == coarse)

    def shifted(j):
        return jnp.where(live, gram[:, j * pitch : j * pitch + wide], 0.0)

    own = [shifted(j) for j in range(3)]
    gap = jnp.zeros((coarse, 1), f32)
    rest = jnp.zeros((coarse, wide - 3 * pitch), f32)
    hankel = []
    for i in range(3):
        line = [squares[i], gap, squares[i + 1], gap, squares[i + 2], gap]
        hankel.append(jnp.concatenate(line + ([rest] if wide > 3 * pitch else []), axis=1))
        hankel.append(jnp.zeros((1, wide), f32))
    if wide > 3 * pitch:
        hankel.append(jnp.zeros((wide - 3 * pitch, wide), f32))
    hankel = jnp.concatenate(hankel, axis=0)
    block0 = lane < pitch
    inverse = bottom[:, 4 * pitch : 4 * pitch + coarse]
    inverse = jnp.concatenate([inverse, jnp.zeros((coarse, wide - coarse), f32)], axis=1)
    inverse = jnp.concatenate([inverse, jnp.zeros((wide - coarse, wide), f32)], axis=0)
    start = bottom[:count, 3 * pitch : 4 * pitch]
    start = jnp.concatenate([start, jnp.zeros((count, wide - pitch), f32)], axis=1)
    against = jnp.where(
        block0, start, jnp.where(live, pltpu.roll(jnp.where(live, own[0], 0.0), pitch, axis=1), 0.0)
    )

    def total(x):
        return jnp.sum(x, axis=1, keepdims=True)

    def scalars(u, i):
        return total(jnp.where(lane == i * pitch + coarse, u, 0.0))

    def metric(u):
        out = dot(jnp.where(is_vec, u, 0.0), hankel, precision=highest)
        for j in range(3):
            out = out + scalars(u, j) * own[j]
        out = jnp.where(is_vec, out, 0.0)
        for i in range(3):
            out = jnp.where(lane == i * pitch + coarse, total(u * own[i]), out)
        return out

    def corrected(w):
        return dot(jnp.where(lane < coarse, w, 0.0), inverse, precision=highest)

    pre = corrected(against) + jnp.where(lane == coarse, 1.0, 0.0)
    direction = pre
    gamma = total(pre * against)
    answer = jnp.zeros_like(pre)
    image_sum = jnp.zeros_like(pre)
    for step in range(ITERS):
        image = metric(direction)
        alpha = gamma / total(direction * image)
        answer = answer + alpha * direction
        if step + 1 < ITERS:
            image_sum = image_sum + alpha * image
            moved_on = jnp.where(live & (slot > 0), pltpu.roll(direction, pitch, axis=1), 0.0)
            pre = pre - alpha * (moved_on + corrected(image))
            gamma_new = total(pre * (against - image_sum))
            direction = pre + (gamma_new / gamma) * direction
            gamma = gamma_new

    for copy in copies[:10]:
        copy.wait()
    pack = jnp.concatenate(
        [left_ref[:, edge:], own_ref[...], right_ref[:, : width - edge]], axis=1
    )
    z = one_hot(pack[FEAT + 1 : FEAT + 2], coarse)
    q0 = pack[SYS:]
    d1 = jnp.concatenate([d1l_ref[:, edge:], d1_ref[...], d1r_ref[:, : width - edge]], axis=1)
    d2 = jnp.concatenate([d2l_ref[:, edge:], d2_ref[...], d2r_ref[:, : width - edge]], axis=1)
    span = q0.shape[1]
    step = -(-coarse // FEAT) * FEAT
    deep = -(-3 * step // LANES) * LANES
    parts, basis = [], []
    for i, rest in enumerate((z, d1[count:], d2[count:])):
        parts.append(answer[:, i * pitch : i * pitch + coarse])
        basis.append(rest)
        if step > coarse:
            parts.append(jnp.zeros((count, step - coarse), f32))
            basis.append(jnp.zeros((step - coarse, span), f32))
    if deep > 3 * step:
        parts.append(jnp.zeros((count, deep - 3 * step), f32))
        basis.append(jnp.zeros((deep - 3 * step, span), f32))
    x = dot(
        jnp.concatenate(parts, axis=1), jnp.concatenate(basis, axis=0), precision=highest
    )
    x = x + scalars(answer, 0) * q0 + scalars(answer, 1) * d1[:count]
    x = x + scalars(answer, 2) * d2[:count]
    mine = slice(REACH * BS, REACH * BS + width)
    sol_ref[...] = x[:, mine]

    line = iota((count, 1), 0) + probe_ref[0] * count
    right = jnp.where(line == 0, x[:, mine], sys_ref[...])
    coef = jnp.where(line == 0, 0.5 / points, -0.5 / (sides - 1) / points)
    r0, r1 = split(right, 2)
    w0, w1 = split(x * coef, 2)
    rest = LANES - 3 * count
    near = jnp.concatenate([w0, w1, w0, jnp.zeros((rest, span), f32)], axis=0).T.astype(bf16)
    mate = jnp.concatenate([r0, r0, r1, jnp.zeros((rest, width), f32)], axis=0).astype(bf16)
    scaled = pack[0:FEAT]
    table = one_hot(pack[FEAT : FEAT + 1], TASKS)
    ones = jnp.ones((8, span), f32)
    terms = jnp.concatenate([scaled, ones, scaled * scaled], axis=0)
    t0, t1 = split(terms, 2)
    pad8 = jnp.zeros((8, span), f32)
    both = jnp.concatenate([t0, pad8, t1, pad8], axis=0).astype(bf16)
    heads = jnp.concatenate([t0, pad8], axis=0).astype(bf16)
    tables = table.astype(bf16)
    high = 32
    for copy in copies[10:]:
        copy.wait()
    length_total = jnp.zeros((FEAT, 1), f32)
    task_total = jnp.zeros((TASKS, TASKS), f32)
    for m in range(blocks):
        at = slice(m * BS, (m + 1) * BS)
        sums = jnp.zeros((high, BS), f32)
        held_sums = jnp.zeros((TASKS, BS), f32)
        places = [(0, row, j + REACH) for row, j, _ in own_places(m)]
        places += [(1, row, j if j < REACH else j + REACH) for row, j, _ in halo_places(m)]
        for side, row, block in places:
            hi_ref, lo_ref, sim_ref = kernel_refs[3 * side : 3 * side + 3]
            j = slice(block * BS, (block + 1) * BS)
            rows_at = slice(row * BS, (row + 1) * BS)
            outer = dot(near[j], mate[:, at])
            kernel = hi_ref[m, rows_at, :].astype(f32) + lo_ref[m, rows_at, :].astype(f32)
            energy = outer * kernel
            held = outer * sim_ref[m, rows_at, :]
            e0, e1 = (part.astype(bf16) for part in split(energy, 2))
            h0, h1 = (part.astype(bf16) for part in split(held, 2))
            first = dot(both[:, j], e0)
            sums = sums + first[:high] + first[high:] + dot(heads[:, j], e1)
            held_sums = held_sums + dot(tables[:, j], h0) + dot(tables[:, j], h1)
        mid = slice((REACH + m) * BS, (REACH + m + 1) * BS)
        left = scaled[:, mid]
        value = left * left * sums[FEAT : FEAT + 1] + sums[2 * FEAT : 3 * FEAT]
        value = value - 2.0 * left * sums[:FEAT]
        length_total = length_total + jnp.sum(value, axis=1, keepdims=True)
        task_total = task_total + dot(held_sums, table[:, mid], NT, highest)
    half = TASKS // 2
    value = jnp.concatenate(
        [
            task_total[:half],
            task_total[half:],
            jnp.where(iota((half, FEAT), 0) == iota((half, FEAT), 1), length_total, 0.0),
            jnp.zeros((half, LANES - 2 * TASKS - FEAT), f32),
        ],
        axis=1,
    )
    for c in range(grad_ref.shape[0]):
        grad_ref[c] = value


def tail_kernel(parts_ref, length_ref, task_ref):
    total = parts_ref[0]
    for c in range(1, parts_ref.shape[0]):
        total = total + parts_ref[c]
    half = TASKS // 2
    task_ref[0:half, :] = total[:, :TASKS]
    task_ref[half:, :] = total[:, TASKS : 2 * TASKS]
    length_ref[...] = jnp.sum(total[:, 2 * TASKS : 2 * TASKS + FEAT], axis=0)


MIB = 1024 * 1024


def call(body, outs, args, name, smem=0, hbm=0, far_outs=0, scratch=(), flops=0, limit=16):
    if hbm:
        args = args[:-hbm] + [pltpu.with_memory_space_constraint(a, pltpu.HBM) for a in args[-hbm:]]
    if far_outs:
        outs = outs[:-far_outs] + [pltpu.HBM(o.shape, o.dtype) for o in outs[-far_outs:]]
    vm = pl.BlockSpec(memory_space=pltpu.VMEM)
    sm = pl.BlockSpec(memory_space=pltpu.SMEM)
    far = pl.BlockSpec(memory_space=pltpu.HBM)
    return pl.pallas_call(
        body,
        out_shape=outs,
        in_specs=[sm] * smem + [vm] * (len(args) - smem - hbm) + [far] * hbm,
        out_specs=[vm] * (len(outs) - far_outs) + [far] * far_outs,
        scratch_shapes=scratch,
        compiler_params=pltpu.CompilerParams(vmem_limit_bytes=limit * MIB),
        cost_estimate=pl.CostEstimate(flops=flops, bytes_accessed=1 << 20, transcendentals=0),
        name=name,
    )(*args)


def both_sides(cells):
    count = lax.axis_size("pts")
    up = [(i, i + 1) for i in range(count - 1)]
    down = [(i + 1, i) for i in range(count - 1)]
    return lax.ppermute(cells, "pts", up), lax.ppermute(cells, "pts", down)


def shards(
    systems, features, task_ids, pattern, aggregate, coarse_inverse, task_cov, lengthscales, noise
):
    count, width = systems.shape
    blocks = width // BS
    coarse = coarse_inverse.shape[1]
    rows = count + coarse
    lanes = lanes_of(coarse)
    assert blocks == REACH
    ranks = lax.axis_size("pts")
    sides = lax.axis_size("probe")

    def shape(*dims, kind=f32):
        return jax.ShapeDtypeStruct(dims, kind)

    jac, pack, extra = call(
        invert_kernel,
        [shape(3, blocks, BS, BS, kind=bf16), shape(SYS + count, width), shape(TASKS + FEAT, width)],
        [features, task_ids, aggregate, systems, task_cov, coarse_inverse, pattern, lengthscales, noise],
        "invert",
        hbm=9,
        scratch=[
            pltpu.VMEM((blocks, BS, BS), f32),
            pltpu.VMEM(features.shape, f32),
            pltpu.VMEM(task_ids.shape, jnp.int32),
            pltpu.VMEM(aggregate.shape, jnp.int32),
            pltpu.VMEM(systems.shape, f32),
            pltpu.VMEM(task_cov.shape, f32),
            pltpu.VMEM(coarse_inverse.shape, f32),
            pltpu.SMEM(pattern.shape, jnp.int32),
            pltpu.SMEM(lengthscales.shape, f32),
            pltpu.SMEM(noise.shape, f32),
            pltpu.SemaphoreType.DMA((9,)),
        ],
        flops=10**10,
    )
    pack_l, pack_r = both_sides(pack)

    def build(places, deep, cells, name):
        return call(
            functools.partial(build_kernel, places=places, sides=len(cells)),
            [
                shape(blocks, deep, BS, kind=bf16),
                shape(blocks, deep, BS, kind=bf16),
                shape(blocks, deep, BS),
            ],
            cells + [pack, extra],
            name,
            flops=10**9,
        )

    own_hi, own_lo, own_sim = build(own_places, width, [pack], "build_own")
    halo_hi, halo_lo, halo_sim = build(
        halo_places, BAND - width, [pack_l, pack_r], "build_halo"
    )
    kernel = [own_hi, own_lo, halo_hi, halo_lo]
    v0, d1 = call(
        first_kernel,
        [shape(rows, width), shape(rows, width)],
        [pack, pack_l, pack_r, extra] + kernel + [jac],
        "first",
        flops=10**9,
    )
    d1_l, d1_r = both_sides(d1)
    cells = [own_hi, own_lo, own_sim, halo_hi, halo_lo, halo_sim]
    early, *stashed = call(
        early_moments_kernel,
        [shape(rows, lanes)] + [shape(*a.shape, kind=a.dtype) for a in cells],
        [pack, systems, d1, v0] + cells,
        "early",
        far_outs=len(cells),
        scratch=[pltpu.SemaphoreType.DMA((len(cells),))],
        flops=10**9,
    )
    v1, d2 = call(
        second_kernel,
        [shape(rows, width), shape(rows, width)],
        [extra, d1, d1_l, d1_r, early] + kernel + [jac],
        "second",
        flops=10**9,
    )
    d2_l, d2_r = both_sides(d2)
    (late,) = call(
        functools.partial(late_moments_kernel, count=count),
        [shape(rows, lanes)],
        [early, d1, d2, v1],
        "late",
        flops=10**9,
    )
    place = lax.axis_index("pts").astype(jnp.int32)[None]
    probe = lax.axis_index("probe").astype(jnp.int32)[None]
    others = [pack, pack_l, pack_r, d1, d1_l, d1_r]
    gram, *vectors = call(
        functools.partial(third_kernel, count=count, held=coarse_inverse.shape[0]),
        [shape(ranks, rows, lanes)] + [shape(*a.shape) for a in others + [d2] * 3],
        [place, extra, late, d2, d2_l, d2_r] + kernel + others,
        "third",
        smem=1,
        far_outs=9,
        scratch=[pltpu.SemaphoreType.DMA((9,))],
        flops=10**9,
    )
    gram = lax.all_to_all(gram, "pts", 0, 0, tiled=True)
    stored = [systems] + vectors + stashed
    answer, grads = call(
        functools.partial(final_kernel, sides=sides * count, points=ranks * width),
        [shape(count, width), shape(ranks * sides, FEAT, LANES)],
        [probe, gram] + stored,
        "final",
        smem=1,
        hbm=len(stored),
        scratch=[pltpu.VMEM(a.shape, a.dtype) for a in stored]
        + [pltpu.SemaphoreType.DMA((len(stored),))],
        flops=10**9,
        limit=32,
    )
    grads = lax.all_to_all(grads, ("pts", "probe"), 0, 0, tiled=True)
    lengths, tasks = call(
        tail_kernel, [shape(FEAT), shape(TASKS, TASKS)], [grads], "tail", flops=10**5
    )
    return answer, lengths, tasks


def solution(mesh):
    return jax.shard_map(
        shards,
        mesh=mesh,
        in_specs=(
            P("probe", ("groups", "pts")),
            P(None, ("groups", "pts")),
            P(("groups", "pts")),
            P(("groups", "pts"), None),
            P(("groups", "pts")),
            P(("groups", "pts"), None),
            P("groups", None),
            P("groups"),
            P("groups"),
        ),
        out_specs=(P("probe", ("groups", "pts")), P("groups"), P("groups", None)),
        check_vma=False,
    )
```

```python
import functools

import jax
import jax.numpy as jnp
from jax import lax
from jax.experimental import pallas as pl
from jax.experimental.pallas import tpu as pltpu
from jax.sharding import PartitionSpec as P

BS = 256
REACH = 3
FEAT = 8
TASKS = 16
ITERS = 3
SLOTS = 2 * REACH + 1
BAND = SLOTS * BS
BASE = 32
GROUP = 4
LANES = 128
SYS = 2 * FEAT

highest = lax.Precision.HIGHEST
f32 = jnp.float32
bf16 = jnp.bfloat16
NN = (((1,), (0,)), ((), ()))
NT = (((1,), (1,)), ((), ()))
TN = (((0,), (0,)), ((), ()))


def dot(a, b, dims=NN, precision=None):
    return lax.dot_general(a, b, dims, precision=precision, preferred_element_type=f32)


def iota(shape, dim):
    return lax.broadcasted_iota(jnp.int32, shape, dim)


def split(x, parts):
    out = []
    for _ in range(parts - 1):
        head = x.astype(bf16).astype(f32)
        out.append(head)
        x = x - head
    out.append(x.astype(bf16).astype(f32))
    return out


def column(ref, size):
    rows = iota((size, 1), 0)
    out = jnp.zeros((size, 1), f32)
    for i in range(size):
        out = jnp.where(rows == i, ref[i], out)
    return out


def one_hot(ids, size):
    return (iota((size, ids.shape[1]), 0).astype(f32) == ids).astype(f32)


def noise_row(noise_ref, ids):
    out = jnp.zeros(ids.shape, f32)
    for t in range(TASKS):
        out = jnp.where(ids == float(t), noise_ref[t], out)
    return out


def weight(pat_ref, block, offset):
    if offset != REACH:
        return pat_ref[block, offset].astype(f32)
    total = pat_ref[block, 0]
    for o in range(1, SLOTS):
        total = total + pat_ref[block, o]
    return total.astype(f32)


def near_stack(scaled, table):
    s0, s1, s2 = split(scaled, 3)
    n0, n1, n2 = split(-0.5 * jnp.sum(scaled * scaled, axis=0, keepdims=True), 3)
    rows = iota(scaled.shape, 0)
    norms = jnp.where(rows == 0, n0, jnp.where(rows == 1, n1, jnp.where(rows == 2, n2, 0.0)))
    pad = jnp.zeros((LANES - 7 * FEAT - 3 * TASKS, scaled.shape[1]), f32)
    stack = jnp.concatenate([s0, s0, s1, s1, s0, s2, norms, table, table, table, pad], axis=0)
    return stack.T.astype(bf16)


def own_stack(scaled, picked):
    s0, s1, s2 = split(scaled, 3)
    rows = iota(scaled.shape, 0)
    ones = jnp.where(rows < 3, 1.0, 0.0)
    count = scaled.shape[1]
    tail = LANES - 7 * FEAT - 3 * TASKS
    left = jnp.concatenate(
        [s0, s1, s0, s1, s2, s0, ones, jnp.zeros((3 * TASKS + tail, count), f32)], axis=0
    ).astype(bf16)
    right = jnp.concatenate(
        [jnp.zeros((7 * FEAT, count), f32)] + split(picked, 3) + [jnp.zeros((tail, count), f32)],
        axis=0,
    ).astype(bf16)
    sides = [
        jnp.concatenate([left[:, i : i + BS], right[:, i : i + BS]], axis=1)
        for i in range(0, count, BS)
    ]
    return sides, -0.5 * jnp.sum(scaled * scaled, axis=0, keepdims=True)


def small_inverse(p):
    n = len(p)
    if n == 1:
        return [[1.0 / p[0][0]]]
    if n == 2:
        a, b, d = p[0][0], p[0][1], p[1][1]
        r = 1.0 / (a * d - b * b)
        off = -b * r
        return [[d * r, off], [off, a * r]]
    h = n // 2
    ainv = small_inverse([row[:h] for row in p[:h]])
    b = [row[h:] for row in p[:h]]
    t = [[sum(ainv[i][k] * b[k][j] for k in range(h)) for j in range(h)] for i in range(h)]
    s = [[None] * h for _ in range(h)]
    for i in range(h):
        for j in range(i, h):
            s[i][j] = s[j][i] = p[h + i][h + j] - sum(b[k][i] * t[k][j] for k in range(h))
    sinv = small_inverse(s)
    u = [[sum(t[i][k] * sinv[k][j] for k in range(h)) for j in range(h)] for i in range(h)]
    out = [[None] * n for _ in range(n)]
    for i in range(h):
        for j in range(h):
            out[h + i][h + j] = sinv[i][j]
            out[i][h + j] = out[h + j][i] = -u[i][j]
    for i in range(h):
        for j in range(i, h):
            out[i][j] = out[j][i] = ainv[i][j] + sum(u[i][k] * t[j][k] for k in range(h))
    return out


def with_rows(cells, first, rows):
    top = first - first % 8
    part = cells[top : top + 8]
    sub = iota((8, 1), 0)
    for t, row in enumerate(rows):
        part = jnp.where(sub == first - top + t, row, part)
    pieces = [cells[:top], part, cells[top + 8 :]]
    return jnp.concatenate([p for p in pieces if p.shape[0]], axis=0)


def sweep_base(cells):
    lane = iota((BASE, LANES), 1)
    start = lane - lane % BASE
    inner = iota((1, LANES), 1) % BASE

    def columns(first):
        return [
            jnp.take_along_axis(cells, start + (first + t), axis=1, mode="promise_in_bounds")
            for t in range(GROUP)
        ]

    cols = columns(0)
    for first in range(0, BASE, GROUP):
        ahead = columns(first + GROUP) if first + GROUP < BASE else []
        pivots = [[cols[u][first + t : first + t + 1, :] for u in range(GROUP)] for t in range(GROUP)]
        inv = small_inverse(pivots)
        coming = []
        for col in ahead:
            head = [col[first + t : first + t + 1, :] for t in range(GROUP)]
            factor = [sum(inv[t][u] * head[u] for u in range(GROUP)) for t in range(GROUP)]
            for t in range(GROUP):
                col = col - cols[t] * factor[t]
            coming.append(with_rows(col, first, factor))
        rows = [cells[first + t : first + t + 1, :] for t in range(GROUP)]
        group = (inner >= first) & (inner < first + GROUP)
        for t in range(GROUP):
            rows[t] = jnp.where(inner == first + t, -1.0, jnp.where(group, 0.0, rows[t]))
        new = [sum(inv[t][u] * rows[u] for u in range(GROUP)) for t in range(GROUP)]
        cells = jnp.where(group, 0.0, cells)
        for t in range(GROUP):
            cells = cells - cols[t] * new[t]
        cells = with_rows(cells, first, new)
        cols = coming
    return cells


def fetch(pairs, sems):
    copies = [pltpu.make_async_copy(a, b, sems.at[i]) for i, (a, b) in enumerate(pairs)]
    for copy in copies:
        copy.start()
    return copies


def invert_kernel(
    place_ref, probe_ref, feat_hbm, ids_hbm, agg_hbm, sys_hbm, cov_hbm, coarse_hbm, pat_hbm, len_hbm, noise_hbm,
    jac_ref, pack_ref, extra_ref,
    work, feat_ref, ids_ref, agg_ref, sys_ref, cov_ref, coarse_ref, pat_ref, len_ref, noise_ref, sems,
):
    blocks = work.shape[0]
    width = blocks * BS
    pairs = [
        (feat_hbm, feat_ref), (ids_hbm, ids_ref), (agg_hbm, agg_ref), (cov_hbm, cov_ref),
        (pat_hbm, pat_ref), (len_hbm, len_ref), (noise_hbm, noise_ref), (coarse_hbm, coarse_ref),
        (sys_hbm, sys_ref),
    ]
    for copy in fetch(pairs, sems):
        copy.wait()
    scaled = feat_ref[...] / column(len_ref, FEAT)
    ids = ids_ref[...].astype(f32).reshape(1, width)
    which = agg_ref[...].astype(f32).reshape(1, width)
    table = one_hot(ids, TASKS)
    noise = noise_row(noise_ref, ids)
    c0, c1, c2 = split(cov_ref[...], 3)
    tab = table.astype(bf16)
    picked = (dot(c2.astype(bf16), tab) + dot(c1.astype(bf16), tab)) + dot(c0.astype(bf16), tab)
    rows = iota((FEAT, width), 0)
    weights = jnp.zeros((1, width), f32)
    places = iota((1, width), 1)
    for m in range(blocks):
        for o in range(SLOTS):
            weights = jnp.where(places == m * SLOTS + o, weight(pat_ref, m, o), weights)
    pack_ref[0:FEAT, :] = scaled
    pack_ref[FEAT : 2 * FEAT, :] = jnp.where(
        rows == 0,
        ids,
        jnp.where(rows == 1, which, jnp.where(rows == 2, probe_ref[0].astype(f32), 0.0)),
    )
    extra_ref[0:TASKS, :] = picked
    tail = jnp.where(rows == 0, noise, jnp.where(rows == 1, weights, 0.0))
    held = coarse_ref.shape[0]
    inverse = jnp.concatenate(
        [coarse_ref[...], jnp.zeros((held, width - coarse_ref.shape[1]), f32)], axis=1
    )
    tail = jnp.where(rows == 2, place_ref[0].astype(f32), tail)
    for r in range(held):
        tail = jnp.where(rows == 3 + r, inverse[r : r + 1], tail)
    extra_ref[TASKS : TASKS + FEAT, :] = tail
    near = near_stack(scaled, table)
    mates, norm = own_stack(scaled, picked)
    eye = iota((BS, BS), 0) == iota((BS, BS), 1)
    for m in range(blocks):
        at = slice(m * BS, (m + 1) * BS)
        both = dot(near[at], mates[m])
        block = weight(pat_ref, m, REACH) * jnp.exp(both[:, :BS] + norm[:, at]) * both[:, BS:]
        work[m] = block + jnp.where(eye, noise[:, at], 0.0)
    seg = iota((BASE, LANES), 1) // BASE
    wide = iota((BASE, BS), 1)
    deep = iota((BASE, BS), 0)
    strips = [work[m, 0:BASE, :] for m in range(blocks)]
    for k in range(BS // BASE):
        first = k * BASE
        tile, inside = first // LANES, first % LANES
        cells = jnp.where(iota((BASE, LANES), 1) % BASE == iota((BASE, LANES), 0), 1.0, 0.0)
        for m in range(blocks):
            piece = strips[m][:, tile * LANES : (tile + 1) * LANES]
            shift = (BASE * m - inside) % LANES
            if shift:
                piece = pltpu.roll(piece, shift, axis=1)
            cells = jnp.where(seg == m, piece, cells)
        inv = -sweep_base(cells)
        held = (wide >= first) & (wide < first + BASE)
        minus = jnp.where(wide - first == deep, -1.0, 0.0)
        stack = jnp.concatenate(
            [jnp.where(held, minus, s) for s in strips]
            + [jnp.zeros((LANES - blocks * BASE, BS), f32)],
            axis=0,
        )
        spread = jnp.concatenate([jnp.where(seg == m, inv, 0.0) for m in range(blocks)], axis=0)
        new = dot(spread, stack, precision=highest)
        gone = (iota((1, BS), 1) >= first) & (iota((1, BS), 1) < first + BASE)
        coming = []
        for m in range(blocks):
            row = new[m * BASE : (m + 1) * BASE, :]
            r0, r1, r2 = split(strips[m], 3)
            p0, p1, p2 = split(row, 3)
            a = jnp.concatenate([r0, r0, r1, r1, r0, r2], axis=0).astype(bf16)
            b = jnp.concatenate([p0, p1, p0, p1, p2, p0], axis=0).astype(bf16)
            value = jnp.where(gone, 0.0, work[m]) - dot(a, b, TN)
            coming.append(value[first + BASE : first + 2 * BASE])
            work[m] = value
            work[m, first : first + BASE, :] = row
        strips = coming
    for m in range(blocks):
        inv = -work[m]
        for i, part in enumerate(split(inv, 3)):
            jac_ref[i, m] = part.astype(bf16)
    pack_ref[SYS:, :] = smooth(sys_ref[...], jac_ref)


def own_places(m):
    return [(j, j, REACH + j - m) for j in range(REACH)]


def halo_places(m):
    lefts = [(j - m, j, j - m) for j in range(m, REACH)]
    return lefts + [(REACH - m + j, REACH + j, 2 * REACH - m + j) for j in range(m + 1)]


def build_kernel(*refs, places, sides):
    cells, (own_ref, extra_ref) = refs[:sides], refs[sides : sides + 2]
    hi_ref, lo_ref, sim_ref = refs[sides + 2 :]
    blocks = hi_ref.shape[0]
    near = []
    for ref in cells:
        near.append(near_stack(ref[0:FEAT, :], one_hot(ref[FEAT : FEAT + 1, :], TASKS)))
    mates, norm = own_stack(own_ref[0:FEAT, :], extra_ref[0:TASKS, :])
    weights = extra_ref[TASKS + 1 : TASKS + 2, :]
    for m in range(blocks):
        for row, j, o in places(m):
            part = near[j // REACH][(j % REACH) * BS : (j % REACH + 1) * BS]
            both = dot(part, mates[m])
            place = m * SLOTS + o
            exponent = both[:, :BS] + norm[:, m * BS : (m + 1) * BS]
            similar = weights[:, place : place + 1] * jnp.exp(exponent)
            kernel = similar * both[:, BS:]
            head = kernel.astype(bf16)
            rows = slice(row * BS, (row + 1) * BS)
            sim_ref[m, rows, :] = similar
            hi_ref[m, rows, :] = head
            lo_ref[m, rows, :] = (kernel - head.astype(f32)).astype(bf16)


def operate(own, left, right, noise, own_hi, own_lo, halo_hi, halo_lo):
    rows = own.shape[0]
    width = own.shape[1]

    def pieces(vectors):
        head, tail = split(vectors, 2)
        return jnp.concatenate([head, tail], axis=0).astype(bf16)

    mine, lefts, rights = pieces(own), pieces(left), pieces(right)
    out = []
    for m in range(REACH):
        beyond = jnp.concatenate([lefts[:, m * BS :], rights[:, : (m + 1) * BS]], axis=1)
        first = dot(mine, own_hi[m]) + dot(beyond, halo_hi[m])
        second = dot(mine[:rows], own_lo[m]) + dot(beyond[:rows], halo_lo[m])
        out.append(first[:rows] + first[rows:] + second)
    return jnp.concatenate(out, axis=1) + noise * own


def smooth(image, jac_ref):
    rows = image.shape[0]
    out = []
    for m in range(jac_ref.shape[1]):
        pieces = jnp.concatenate(split(image[:, m * BS : (m + 1) * BS], 3), axis=0).astype(bf16)
        a = dot(pieces, jac_ref[0, m])
        b = dot(pieces[: 2 * rows], jac_ref[1, m])
        c = dot(pieces[:rows], jac_ref[2, m])
        out.append(a[:rows] + (a[rows : 2 * rows] + b[:rows] + (a[2 * rows :] + b[rows:] + c)))
    return jnp.concatenate(out, axis=1)


def first_kernel(own_ref, left_ref, right_ref, extra_ref, *refs):
    kernel, (jac_ref, image_ref, next_ref) = refs[:4], refs[4:]
    count = own_ref.shape[0] - SYS
    coarse = image_ref.shape[0] - count

    def basis(ref):
        z = one_hot(ref[FEAT + 1 : FEAT + 2, :], coarse)
        return jnp.concatenate([ref[SYS:, :], z], axis=0)

    noise = extra_ref[TASKS : TASKS + 1, :]
    image = operate(basis(own_ref), basis(left_ref), basis(right_ref), noise, *kernel)
    image_ref[...] = image
    next_ref[...] = smooth(image, jac_ref)


def second_kernel(extra_ref, vec_ref, left_ref, right_ref, early_ref, *refs):
    kernel, (jac_ref, image_ref, next_ref) = refs[:4], refs[4:]
    noise = extra_ref[TASKS : TASKS + 1, :]
    image = operate(vec_ref[...], left_ref[...], right_ref[...], noise, *kernel)
    image_ref[...] = image
    next_ref[...] = smooth(image, jac_ref)


def pitch_of(coarse):
    return coarse + 1


def lanes_of(coarse):
    return -(-5 * pitch_of(coarse) // LANES) * LANES


def moment(vectors, images, pairs):
    count = pairs.shape[0]
    table = dot(images, vectors, NT, lax.Precision.HIGH)
    own = jnp.sum(pairs, axis=1, keepdims=True)
    if images.shape[0] > count:
        own = jnp.concatenate([own, jnp.zeros((images.shape[0] - count, 1), f32)], axis=0)
    return jnp.concatenate([table, own], axis=1)


def spread_out(parts, lanes):
    rows, pitch = next(iter(parts.values())).shape
    cells = [parts.get(k, jnp.zeros((rows, pitch), f32)) for k in range(5)]
    if lanes > 5 * pitch:
        cells.append(jnp.zeros((rows, lanes - 5 * pitch), f32))
    return jnp.concatenate(cells, axis=1)


def folded(low, high):
    order = low.shape[0]
    row, col = iota((order, order), 0), iota((order, order), 1)
    diagonal = jnp.sum(jnp.where(row == col, high, 0.0), axis=1, keepdims=True)
    return jnp.concatenate([jnp.where(row >= col, low, high), diagonal], axis=1)


def unfolded(cells):
    order = cells.shape[0]
    row, col = iota((order, order), 0), iota((order, order), 1)
    square = cells[:, :order]
    turned = dot(square, jnp.where(row == col, 1.0, 0.0), TN, highest)
    low = jnp.where(row >= col, square, turned)
    high = jnp.where(row < col, square, jnp.where(row > col, turned, cells[:, order:]))
    return low, high


def early_moments_kernel(own_ref, sys_ref, d1_ref, v0_ref, *refs):
    sources, (out_ref, *stashes), sems = refs[:6], refs[6:13], refs[13]
    copies = fetch(list(zip(sources, stashes)), sems)
    count = own_ref.shape[0] - SYS
    coarse = d1_ref.shape[0] - count
    lanes = out_ref.shape[1]
    pitch = pitch_of(coarse)
    systems = sys_ref[...]
    pre = own_ref[SYS:, :]
    z = one_hot(own_ref[FEAT + 1 : FEAT + 2, :], coarse)
    d1, v0 = d1_ref[...], v0_ref[...]
    m0 = moment(z, v0, pre * v0[:count])
    m1 = moment(d1[count:], v0, d1[:count] * v0[:count])
    out_ref[0:count, :] = spread_out({0: m0[:count], 1: m1[:count]}, lanes)
    start = moment(z, systems, systems * pre)
    if coarse > count:
        start = jnp.concatenate([start, jnp.zeros((coarse - count, pitch), f32)], axis=0)
    fold = folded(m0[count:, :coarse], m1[count:, :coarse])
    out_ref[count:, :] = spread_out({0: fold, 3: start}, lanes)
    for copy in copies:
        copy.wait()


def late_moments_kernel(before_ref, d1_ref, d2_ref, v1_ref, out_ref, *, count):
    lanes = out_ref.shape[1]
    d1, d2, v1 = d1_ref[...], d2_ref[...], v1_ref[...]
    coarse = d1.shape[0] - count
    m2 = moment(d1[count:], v1, d1[:count] * v1[:count])
    m3 = moment(d2[count:], v1, d2[:count] * v1[:count])
    out_ref[0:count, :] = before_ref[0:count, :] + spread_out({2: m2[:count], 3: m3[:count]}, lanes)
    fold = folded(m2[count:, :coarse], m3[count:, :coarse])
    out_ref[count:, :] = before_ref[count:, :] + spread_out({1: fold}, lanes)


def third_kernel(
    extra_ref, before_ref, vec_ref, left_ref, right_ref, *refs, count, held
):
    kernel, others, (out_hbm, *stashes) = refs[:4], refs[4:10], refs[10:20]
    out_ref, sems, out_sems = refs[20:]
    copies = fetch(list(zip([*others, vec_ref, left_ref, right_ref], stashes)), sems)
    coarse = vec_ref.shape[0] - count
    lanes = out_ref.shape[1]
    pitch = pitch_of(coarse)
    d2 = vec_ref[...]
    noise = extra_ref[TASKS : TASKS + 1, :]
    v2 = operate(d2, left_ref[...], right_ref[...], noise, *kernel)
    m4 = moment(d2[count:], v2, d2[:count] * v2[:count])
    row = iota((coarse, 1), 0).astype(f32)
    start = extra_ref[TASKS + 2 : TASKS + 3, 0:1] * held
    inverse = jnp.zeros((coarse, pitch), f32)
    for r in range(held):
        line = extra_ref[TASKS + 3 + r : TASKS + 4 + r, 0:pitch]
        inverse = jnp.where(row == start + r, line, inverse)
    top = before_ref[0:count, :] + spread_out({4: m4[:count]}, lanes)
    bottom = before_ref[count:, :] + spread_out({2: m4[count:], 4: inverse}, lanes)
    out_ref[0:count, :] = top
    out_ref[count:, :] = bottom
    pairs = [(out_ref, out_hbm.at[c]) for c in range(out_hbm.shape[0])]
    for copy in copies + fetch(pairs, out_sems):
        copy.wait()


def final_kernel(
    gram_ref, *refs, sides, points,
):
    far, (sol_ref, grad_ref), near_refs, sems = refs[:16], refs[16:18], refs[18:34], refs[34]
    copies = fetch(list(zip(far, near_refs)), sems)
    (
        sys_ref, own_ref, left_ref, right_ref, d1_ref, d1l_ref, d1r_ref, d2_ref, d2l_ref, d2r_ref,
        *kernel_refs,
    ) = near_refs
    width = own_ref.shape[1]
    count = own_ref.shape[0] - SYS
    rows = d1_ref.shape[0]
    coarse = rows - count
    pitch = pitch_of(coarse)
    wide = -(-3 * pitch // LANES) * LANES
    blocks = width // BS
    edge = width - REACH * BS
    gram = gram_ref[0]
    for c in range(1, gram_ref.shape[0]):
        gram = gram + gram_ref[c]
    bottom = gram[count:]
    gram = jnp.concatenate([gram[:count], jnp.zeros((count, wide), f32)], axis=1)
    squares = list(unfolded(bottom[:, :pitch])) + list(unfolded(bottom[:, pitch : 2 * pitch]))
    squares.append(bottom[:, 2 * pitch : 2 * pitch + coarse])
    lane = iota((1, wide), 1)
    slot, inside = lane // pitch, lane % pitch
    live = lane < 3 * pitch
    is_vec = live & (inside < coarse)
    is_one = live & (inside == coarse)

    def shifted(j):
        return jnp.where(live, gram[:, j * pitch : j * pitch + wide], 0.0)

    own = [shifted(j) for j in range(3)]
    gap = jnp.zeros((coarse, 1), f32)
    rest = jnp.zeros((coarse, wide - 3 * pitch), f32)
    hankel = []
    for i in range(3):
        line = [squares[i], gap, squares[i + 1], gap, squares[i + 2], gap]
        hankel.append(jnp.concatenate(line + ([rest] if wide > 3 * pitch else []), axis=1))
        hankel.append(jnp.zeros((1, wide), f32))
    if wide > 3 * pitch:
        hankel.append(jnp.zeros((wide - 3 * pitch, wide), f32))
    hankel = jnp.concatenate(hankel, axis=0)
    block0 = lane < pitch
    inverse = bottom[:, 4 * pitch : 4 * pitch + coarse]
    inverse = jnp.concatenate([inverse, jnp.zeros((coarse, wide - coarse), f32)], axis=1)
    inverse = jnp.concatenate([inverse, jnp.zeros((wide - coarse, wide), f32)], axis=0)
    start = bottom[:count, 3 * pitch : 4 * pitch]
    start = jnp.concatenate([start, jnp.zeros((count, wide - pitch), f32)], axis=1)
    against = jnp.where(
        block0, start, jnp.where(live, pltpu.roll(jnp.where(live, own[0], 0.0), pitch, axis=1), 0.0)
    )

    def total(x):
        return jnp.sum(x, axis=1, keepdims=True)

    def scalars(u, i):
        return total(jnp.where(lane == i * pitch + coarse, u, 0.0))

    def metric(u):
        out = dot(jnp.where(is_vec, u, 0.0), hankel, precision=highest)
        for j in range(3):
            out = out + scalars(u, j) * own[j]
        out = jnp.where(is_vec, out, 0.0)
        for i in range(3):
            out = jnp.where(lane == i * pitch + coarse, total(u * own[i]), out)
        return out

    def corrected(w):
        return dot(jnp.where(lane < coarse, w, 0.0), inverse, precision=highest)

    pre = corrected(against) + jnp.where(lane == coarse, 1.0, 0.0)
    direction = pre
    gamma = total(pre * against)
    answer = jnp.zeros_like(pre)
    image_sum = jnp.zeros_like(pre)
    for step in range(ITERS):
        image = metric(direction)
        alpha = gamma / total(direction * image)
        answer = answer + alpha * direction
        if step + 1 < ITERS:
            image_sum = image_sum + alpha * image
            moved_on = jnp.where(live & (slot > 0), pltpu.roll(direction, pitch, axis=1), 0.0)
            pre = pre - alpha * (moved_on + corrected(image))
            gamma_new = total(pre * (against - image_sum))
            direction = pre + (gamma_new / gamma) * direction
            gamma = gamma_new

    for copy in copies[:10]:
        copy.wait()
    pack = jnp.concatenate(
        [left_ref[:, edge:], own_ref[...], right_ref[:, : width - edge]], axis=1
    )
    z = one_hot(pack[FEAT + 1 : FEAT + 2], coarse)
    q0 = pack[SYS:]
    d1 = jnp.concatenate([d1l_ref[:, edge:], d1_ref[...], d1r_ref[:, : width - edge]], axis=1)
    d2 = jnp.concatenate([d2l_ref[:, edge:], d2_ref[...], d2r_ref[:, : width - edge]], axis=1)
    span = q0.shape[1]
    step = -(-coarse // FEAT) * FEAT
    deep = -(-3 * step // LANES) * LANES
    parts, basis = [], []
    for i, rest in enumerate((z, d1[count:], d2[count:])):
        parts.append(answer[:, i * pitch : i * pitch + coarse])
        basis.append(rest)
        if step > coarse:
            parts.append(jnp.zeros((count, step - coarse), f32))
            basis.append(jnp.zeros((step - coarse, span), f32))
    if deep > 3 * step:
        parts.append(jnp.zeros((count, deep - 3 * step), f32))
        basis.append(jnp.zeros((deep - 3 * step, span), f32))
    x = dot(
        jnp.concatenate(parts, axis=1), jnp.concatenate(basis, axis=0), precision=highest
    )
    x = x + scalars(answer, 0) * q0 + scalars(answer, 1) * d1[:count]
    x = x + scalars(answer, 2) * d2[:count]
    mine = slice(REACH * BS, REACH * BS + width)
    sol_ref[...] = x[:, mine]

    probe = own_ref[FEAT + 2 : FEAT + 3, 0:1]
    line = iota((count, 1), 0).astype(f32) + probe * count
    right = jnp.where(line == 0, x[:, mine], sys_ref[...])
    coef = jnp.where(line == 0, 0.5 / points, -0.5 / (sides - 1) / points)
    r0, r1 = split(right, 2)
    w0, w1 = split(x * coef, 2)
    rest = LANES - 3 * count
    near = jnp.concatenate([w0, w1, w0, jnp.zeros((rest, span), f32)], axis=0).T.astype(bf16)
    mate = jnp.concatenate([r0, r0, r1, jnp.zeros((rest, width), f32)], axis=0).astype(bf16)
    scaled = pack[0:FEAT]
    table = one_hot(pack[FEAT : FEAT + 1], TASKS)
    ones = jnp.ones((8, span), f32)
    terms = jnp.concatenate([scaled, ones, scaled * scaled], axis=0)
    t0, t1 = split(terms, 2)
    pad8 = jnp.zeros((8, span), f32)
    both = jnp.concatenate([t0, pad8, t1, pad8], axis=0).astype(bf16)
    heads = jnp.concatenate([t0, pad8], axis=0).astype(bf16)
    tables = table.astype(bf16)
    high = 32
    for copy in copies[10:]:
        copy.wait()
    length_total = jnp.zeros((FEAT, 1), f32)
    task_total = jnp.zeros((TASKS, TASKS), f32)
    for m in range(blocks):
        at = slice(m * BS, (m + 1) * BS)
        sums = jnp.zeros((high, BS), f32)
        held_sums = jnp.zeros((TASKS, BS), f32)
        places = [(0, row, j + REACH) for row, j, _ in own_places(m)]
        places += [(1, row, j if j < REACH else j + REACH) for row, j, _ in halo_places(m)]
        for side, row, block in places:
            hi_ref, lo_ref, sim_ref = kernel_refs[3 * side : 3 * side + 3]
            j = slice(block * BS, (block + 1) * BS)
            rows_at = slice(row * BS, (row + 1) * BS)
            outer = dot(near[j], mate[:, at])
            kernel = hi_ref[m, rows_at, :].astype(f32) + lo_ref[m, rows_at, :].astype(f32)
            energy = outer * kernel
            held = outer * sim_ref[m, rows_at, :]
            e0, e1 = (part.astype(bf16) for part in split(energy, 2))
            h0, h1 = (part.astype(bf16) for part in split(held, 2))
            first = dot(both[:, j], e0)
            sums = sums + first[:high] + first[high:] + dot(heads[:, j], e1)
            held_sums = held_sums + dot(tables[:, j], h0) + dot(tables[:, j], h1)
        mid = slice((REACH + m) * BS, (REACH + m + 1) * BS)
        left = scaled[:, mid]
        value = left * left * sums[FEAT : FEAT + 1] + sums[2 * FEAT : 3 * FEAT]
        value = value - 2.0 * left * sums[:FEAT]
        length_total = length_total + jnp.sum(value, axis=1, keepdims=True)
        task_total = task_total + dot(held_sums, table[:, mid], NT, highest)
    half = TASKS // 2
    value = jnp.concatenate(
        [
            task_total[:half],
            task_total[half:],
            jnp.where(iota((half, FEAT), 0) == iota((half, FEAT), 1), length_total, 0.0),
            jnp.zeros((half, LANES - 2 * TASKS - FEAT), f32),
        ],
        axis=1,
    )
    for c in range(grad_ref.shape[0]):
        grad_ref[c] = value


def tail_kernel(parts_ref, length_ref, task_ref):
    total = parts_ref[0]
    for c in range(1, parts_ref.shape[0]):
        total = total + parts_ref[c]
    half = TASKS // 2
    task_ref[0:half, :] = total[:, :TASKS]
    task_ref[half:, :] = total[:, TASKS : 2 * TASKS]
    length_ref[...] = jnp.sum(total[:, 2 * TASKS : 2 * TASKS + FEAT], axis=0)


MIB = 1024 * 1024


def call(body, outs, args, name, smem=0, hbm=0, far_outs=0, scratch=(), flops=0, limit=16):
    if hbm:
        args = args[:-hbm] + [pltpu.with_memory_space_constraint(a, pltpu.HBM) for a in args[-hbm:]]
    if far_outs:
        outs = outs[:-far_outs] + [pltpu.HBM(o.shape, o.dtype) for o in outs[-far_outs:]]
    vm = pl.BlockSpec(memory_space=pltpu.VMEM)
    sm = pl.BlockSpec(memory_space=pltpu.SMEM)
    far = pl.BlockSpec(memory_space=pltpu.HBM)
    return pl.pallas_call(
        body,
        out_shape=outs,
        in_specs=[sm] * smem + [vm] * (len(args) - smem - hbm) + [far] * hbm,
        out_specs=[vm] * (len(outs) - far_outs) + [far] * far_outs,
        scratch_shapes=scratch,
        compiler_params=pltpu.CompilerParams(vmem_limit_bytes=limit * MIB),
        cost_estimate=pl.CostEstimate(flops=flops, bytes_accessed=1 << 20, transcendentals=0),
        name=name,
    )(*args)


def both_sides(cells):
    count = lax.axis_size("pts")
    up = [(i, i + 1) for i in range(count - 1)]
    down = [(i + 1, i) for i in range(count - 1)]
    return lax.ppermute(cells, "pts", up), lax.ppermute(cells, "pts", down)


def shards(
    systems, features, task_ids, pattern, aggregate, coarse_inverse, task_cov, lengthscales, noise
):
    count, width = systems.shape
    blocks = width // BS
    coarse = coarse_inverse.shape[1]
    rows = count + coarse
    lanes = lanes_of(coarse)
    assert blocks == REACH
    place = lax.axis_index("pts").astype(jnp.int32)[None]
    probe = lax.axis_index("probe").astype(jnp.int32)[None]
    ranks = lax.axis_size("pts")
    sides = lax.axis_size("probe")

    def shape(*dims, kind=f32):
        return jax.ShapeDtypeStruct(dims, kind)

    jac, pack, extra = call(
        invert_kernel,
        [shape(3, blocks, BS, BS, kind=bf16), shape(SYS + count, width), shape(TASKS + FEAT, width)],
        [place, probe, features, task_ids, aggregate, systems, task_cov, coarse_inverse, pattern, lengthscales, noise],
        "invert",
        smem=2,
        hbm=9,
        scratch=[
            pltpu.VMEM((blocks, BS, BS), f32),
            pltpu.VMEM(features.shape, f32),
            pltpu.VMEM(task_ids.shape, jnp.int32),
            pltpu.VMEM(aggregate.shape, jnp.int32),
            pltpu.VMEM(systems.shape, f32),
            pltpu.VMEM(task_cov.shape, f32),
            pltpu.VMEM(coarse_inverse.shape, f32),
            pltpu.SMEM(pattern.shape, jnp.int32),
            pltpu.SMEM(lengthscales.shape, f32),
            pltpu.SMEM(noise.shape, f32),
            pltpu.SemaphoreType.DMA((9,)),
        ],
        flops=10**10,
    )
    pack_l, pack_r = both_sides(pack)

    def build(places, deep, cells, name):
        return call(
            functools.partial(build_kernel, places=places, sides=len(cells)),
            [
                shape(blocks, deep, BS, kind=bf16),
                shape(blocks, deep, BS, kind=bf16),
                shape(blocks, deep, BS),
            ],
            cells + [pack, extra],
            name,
            flops=10**9,
        )

    own_hi, own_lo, own_sim = build(own_places, width, [pack], "build_own")
    halo_hi, halo_lo, halo_sim = build(
        halo_places, BAND - width, [pack_l, pack_r], "build_halo"
    )
    kernel = [own_hi, own_lo, halo_hi, halo_lo]
    v0, d1 = call(
        first_kernel,
        [shape(rows, width), shape(rows, width)],
        [pack, pack_l, pack_r, extra] + kernel + [jac],
        "first",
        flops=10**9,
    )
    d1_l, d1_r = both_sides(d1)
    cells = [own_hi, own_lo, own_sim, halo_hi, halo_lo, halo_sim]
    early, *stashed = call(
        early_moments_kernel,
        [shape(rows, lanes)] + [shape(*a.shape, kind=a.dtype) for a in cells],
        [pack, systems, d1, v0] + cells,
        "early",
        far_outs=len(cells),
        scratch=[pltpu.SemaphoreType.DMA((len(cells),))],
        flops=10**9,
    )
    v1, d2 = call(
        second_kernel,
        [shape(rows, width), shape(rows, width)],
        [extra, d1, d1_l, d1_r, early] + kernel + [jac],
        "second",
        flops=10**9,
    )
    d2_l, d2_r = both_sides(d2)
    (late,) = call(
        functools.partial(late_moments_kernel, count=count),
        [shape(rows, lanes)],
        [early, d1, d2, v1],
        "late",
        flops=10**9,
    )
    others = [pack, pack_l, pack_r, d1, d1_l, d1_r]
    gram, *vectors = call(
        functools.partial(third_kernel, count=count, held=coarse_inverse.shape[0]),
        [shape(ranks, rows, lanes)] + [shape(*a.shape) for a in others + [d2] * 3],
        [extra, late, d2, d2_l, d2_r] + kernel + others,
        "third",
        far_outs=10,
        scratch=[
            pltpu.VMEM((rows, lanes), f32),
            pltpu.SemaphoreType.DMA((9,)),
            pltpu.SemaphoreType.DMA((ranks,)),
        ],
        flops=10**9,
    )
    gram = lax.all_to_all(gram, "pts", 0, 0, tiled=True)
    stored = [systems] + vectors + stashed
    answer, grads = call(
        functools.partial(final_kernel, sides=sides * count, points=ranks * width),
        [shape(count, width), shape(ranks * sides, FEAT, LANES)],
        [gram] + stored,
        "final",
        hbm=len(stored),
        scratch=[pltpu.VMEM(a.shape, a.dtype) for a in stored]
        + [pltpu.SemaphoreType.DMA((len(stored),))],
        flops=10**9,
        limit=32,
    )
    grads = lax.all_to_all(grads, ("pts", "probe"), 0, 0, tiled=True)
    lengths, tasks = call(
        tail_kernel, [shape(FEAT), shape(TASKS, TASKS)], [grads], "tail", flops=10**5
    )
    return answer, lengths, tasks


def solution(mesh):
    return jax.shard_map(
        shards,
        mesh=mesh,
        in_specs=(
            P("probe", ("groups", "pts")),
            P(None, ("groups", "pts")),
            P(("groups", "pts")),
            P(("groups", "pts"), None),
            P(("groups", "pts")),
            P(("groups", "pts"), None),
            P("groups", None),
            P("groups"),
            P("groups"),
        ),
        out_specs=(P("probe", ("groups", "pts")), P("groups"), P("groups", None)),
        check_vma=False,
    )
```

```python
import functools

import jax
import jax.numpy as jnp
from jax import lax
from jax.experimental import pallas as pl
from jax.experimental.pallas import tpu as pltpu
from jax.sharding import PartitionSpec as P

BS = 256
REACH = 3
FEAT = 8
TASKS = 16
ITERS = 3
SLOTS = 2 * REACH + 1
BAND = SLOTS * BS
BASE = 32
GROUP = 4
LANES = 128
SYS = 2 * FEAT

highest = lax.Precision.HIGHEST
f32 = jnp.float32
bf16 = jnp.bfloat16
NN = (((1,), (0,)), ((), ()))
NT = (((1,), (1,)), ((), ()))
TN = (((0,), (0,)), ((), ()))


def dot(a, b, dims=NN, precision=None):
    return lax.dot_general(a, b, dims, precision=precision, preferred_element_type=f32)


def iota(shape, dim):
    return lax.broadcasted_iota(jnp.int32, shape, dim)


def split(x, parts):
    out = []
    for _ in range(parts - 1):
        head = x.astype(bf16).astype(f32)
        out.append(head)
        x = x - head
    out.append(x.astype(bf16).astype(f32))
    return out


def column(ref, size):
    rows = iota((size, 1), 0)
    out = jnp.zeros((size, 1), f32)
    for i in range(size):
        out = jnp.where(rows == i, ref[i], out)
    return out


def one_hot(ids, size):
    return (iota((size, ids.shape[1]), 0).astype(f32) == ids).astype(f32)


def noise_row(noise_ref, ids):
    out = jnp.zeros(ids.shape, f32)
    for t in range(TASKS):
        out = jnp.where(ids == float(t), noise_ref[t], out)
    return out


def weight(pat_ref, block, offset):
    if offset != REACH:
        return pat_ref[block, offset].astype(f32)
    total = pat_ref[block, 0]
    for o in range(1, SLOTS):
        total = total + pat_ref[block, o]
    return total.astype(f32)


def near_stack(scaled, table):
    s0, s1, s2 = split(scaled, 3)
    n0, n1, n2 = split(-0.5 * jnp.sum(scaled * scaled, axis=0, keepdims=True), 3)
    rows = iota(scaled.shape, 0)
    norms = jnp.where(rows == 0, n0, jnp.where(rows == 1, n1, jnp.where(rows == 2, n2, 0.0)))
    pad = jnp.zeros((LANES - 7 * FEAT - 3 * TASKS, scaled.shape[1]), f32)
    stack = jnp.concatenate([s0, s0, s1, s1, s0, s2, norms, table, table, table, pad], axis=0)
    return stack.T.astype(bf16)


def own_stack(scaled, picked):
    s0, s1, s2 = split(scaled, 3)
    rows = iota(scaled.shape, 0)
    ones = jnp.where(rows < 3, 1.0, 0.0)
    count = scaled.shape[1]
    tail = LANES - 7 * FEAT - 3 * TASKS
    left = jnp.concatenate(
        [s0, s1, s0, s1, s2, s0, ones, jnp.zeros((3 * TASKS + tail, count), f32)], axis=0
    ).astype(bf16)
    right = jnp.concatenate(
        [jnp.zeros((7 * FEAT, count), f32)] + split(picked, 3) + [jnp.zeros((tail, count), f32)],
        axis=0,
    ).astype(bf16)
    sides = [
        jnp.concatenate([left[:, i : i + BS], right[:, i : i + BS]], axis=1)
        for i in range(0, count, BS)
    ]
    return sides, -0.5 * jnp.sum(scaled * scaled, axis=0, keepdims=True)


def small_inverse(p):
    n = len(p)
    if n == 1:
        return [[1.0 / p[0][0]]]
    if n == 2:
        a, b, d = p[0][0], p[0][1], p[1][1]
        r = 1.0 / (a * d - b * b)
        off = -b * r
        return [[d * r, off], [off, a * r]]
    h = n // 2
    ainv = small_inverse([row[:h] for row in p[:h]])
    b = [row[h:] for row in p[:h]]
    t = [[sum(ainv[i][k] * b[k][j] for k in range(h)) for j in range(h)] for i in range(h)]
    s = [[None] * h for _ in range(h)]
    for i in range(h):
        for j in range(i, h):
            s[i][j] = s[j][i] = p[h + i][h + j] - sum(b[k][i] * t[k][j] for k in range(h))
    sinv = small_inverse(s)
    u = [[sum(t[i][k] * sinv[k][j] for k in range(h)) for j in range(h)] for i in range(h)]
    out = [[None] * n for _ in range(n)]
    for i in range(h):
        for j in range(h):
            out[h + i][h + j] = sinv[i][j]
            out[i][h + j] = out[h + j][i] = -u[i][j]
    for i in range(h):
        for j in range(i, h):
            out[i][j] = out[j][i] = ainv[i][j] + sum(u[i][k] * t[j][k] for k in range(h))
    return out


def with_rows(cells, first, rows):
    top = first - first % 8
    part = cells[top : top + 8]
    sub = iota((8, 1), 0)
    for t, row in enumerate(rows):
        part = jnp.where(sub == first - top + t, row, part)
    pieces = [cells[:top], part, cells[top + 8 :]]
    return jnp.concatenate([p for p in pieces if p.shape[0]], axis=0)


def sweep_base(cells):
    lane = iota((BASE, LANES), 1)
    start = lane - lane % BASE
    inner = iota((1, LANES), 1) % BASE

    def columns(first):
        return [
            jnp.take_along_axis(cells, start + (first + t), axis=1, mode="promise_in_bounds")
            for t in range(GROUP)
        ]

    cols = columns(0)
    for first in range(0, BASE, GROUP):
        ahead = columns(first + GROUP) if first + GROUP < BASE else []
        pivots = [[cols[u][first + t : first + t + 1, :] for u in range(GROUP)] for t in range(GROUP)]
        inv = small_inverse(pivots)
        coming = []
        for col in ahead:
            head = [col[first + t : first + t + 1, :] for t in range(GROUP)]
            factor = [sum(inv[t][u] * head[u] for u in range(GROUP)) for t in range(GROUP)]
            for t in range(GROUP):
                col = col - cols[t] * factor[t]
            coming.append(with_rows(col, first, factor))
        rows = [cells[first + t : first + t + 1, :] for t in range(GROUP)]
        group = (inner >= first) & (inner < first + GROUP)
        for t in range(GROUP):
            rows[t] = jnp.where(inner == first + t, -1.0, jnp.where(group, 0.0, rows[t]))
        new = [sum(inv[t][u] * rows[u] for u in range(GROUP)) for t in range(GROUP)]
        cells = jnp.where(group, 0.0, cells)
        for t in range(GROUP):
            cells = cells - cols[t] * new[t]
        cells = with_rows(cells, first, new)
        cols = coming
    return cells


def fetch(pairs, sems):
    copies = [pltpu.make_async_copy(a, b, sems.at[i]) for i, (a, b) in enumerate(pairs)]
    for copy in copies:
        copy.start()
    return copies


def invert_kernel(
    place_ref, probe_ref, feat_hbm, ids_hbm, agg_hbm, sys_hbm, cov_hbm, coarse_hbm, pat_hbm, len_hbm, noise_hbm,
    jac_ref, pack_ref, extra_ref,
    work, feat_ref, ids_ref, agg_ref, sys_ref, cov_ref, coarse_ref, pat_ref, len_ref, noise_ref, sems,
):
    blocks = work.shape[0]
    width = blocks * BS
    pairs = [
        (feat_hbm, feat_ref), (ids_hbm, ids_ref), (agg_hbm, agg_ref), (cov_hbm, cov_ref),
        (pat_hbm, pat_ref), (len_hbm, len_ref), (noise_hbm, noise_ref), (coarse_hbm, coarse_ref),
        (sys_hbm, sys_ref),
    ]
    for copy in fetch(pairs, sems):
        copy.wait()
    scaled = feat_ref[...] / column(len_ref, FEAT)
    ids = ids_ref[...].astype(f32).reshape(1, width)
    which = agg_ref[...].astype(f32).reshape(1, width)
    table = one_hot(ids, TASKS)
    noise = noise_row(noise_ref, ids)
    c0, c1, c2 = split(cov_ref[...], 3)
    tab = table.astype(bf16)
    picked = (dot(c2.astype(bf16), tab) + dot(c1.astype(bf16), tab)) + dot(c0.astype(bf16), tab)
    rows = iota((FEAT, width), 0)
    weights = jnp.zeros((1, width), f32)
    places = iota((1, width), 1)
    for m in range(blocks):
        for o in range(SLOTS):
            weights = jnp.where(places == m * SLOTS + o, weight(pat_ref, m, o), weights)
    pack_ref[0:FEAT, :] = scaled
    pack_ref[FEAT : 2 * FEAT, :] = jnp.where(
        rows == 0,
        ids,
        jnp.where(rows == 1, which, jnp.where(rows == 2, probe_ref[0].astype(f32), 0.0)),
    )
    extra_ref[0:TASKS, :] = picked
    tail = jnp.where(rows == 0, noise, jnp.where(rows == 1, weights, 0.0))
    held = coarse_ref.shape[0]
    inverse = jnp.concatenate(
        [coarse_ref[...], jnp.zeros((held, width - coarse_ref.shape[1]), f32)], axis=1
    )
    tail = jnp.where(rows == 2, place_ref[0].astype(f32), tail)
    for r in range(held):
        tail = jnp.where(rows == 3 + r, inverse[r : r + 1], tail)
    extra_ref[TASKS : TASKS + FEAT, :] = tail
    near = near_stack(scaled, table)
    mates, norm = own_stack(scaled, picked)
    eye = iota((BS, BS), 0) == iota((BS, BS), 1)
    for m in range(blocks):
        at = slice(m * BS, (m + 1) * BS)
        both = dot(near[at], mates[m])
        block = weight(pat_ref, m, REACH) * jnp.exp(both[:, :BS] + norm[:, at]) * both[:, BS:]
        work[m] = block + jnp.where(eye, noise[:, at], 0.0)
    seg = iota((BASE, LANES), 1) // BASE
    wide = iota((BASE, BS), 1)
    deep = iota((BASE, BS), 0)
    strips = [work[m, 0:BASE, :] for m in range(blocks)]
    for k in range(BS // BASE):
        first = k * BASE
        tile, inside = first // LANES, first % LANES
        cells = jnp.where(iota((BASE, LANES), 1) % BASE == iota((BASE, LANES), 0), 1.0, 0.0)
        for m in range(blocks):
            piece = strips[m][:, tile * LANES : (tile + 1) * LANES]
            shift = (BASE * m - inside) % LANES
            if shift:
                piece = pltpu.roll(piece, shift, axis=1)
            cells = jnp.where(seg == m, piece, cells)
        inv = -sweep_base(cells)
        held = (wide >= first) & (wide < first + BASE)
        minus = jnp.where(wide - first == deep, -1.0, 0.0)
        stack = jnp.concatenate(
            [jnp.where(held, minus, s) for s in strips]
            + [jnp.zeros((LANES - blocks * BASE, BS), f32)],
            axis=0,
        )
        spread = jnp.concatenate([jnp.where(seg == m, inv, 0.0) for m in range(blocks)], axis=0)
        new = dot(spread, stack, precision=highest)
        gone = (iota((1, BS), 1) >= first) & (iota((1, BS), 1) < first + BASE)
        coming = []
        for m in range(blocks):
            row = new[m * BASE : (m + 1) * BASE, :]
            r0, r1, r2 = split(strips[m], 3)
            p0, p1, p2 = split(row, 3)
            a = jnp.concatenate([r0, r0, r1, r1, r0, r2], axis=0).astype(bf16)
            b = jnp.concatenate([p0, p1, p0, p1, p2, p0], axis=0).astype(bf16)
            value = jnp.where(gone, 0.0, work[m]) - dot(a, b, TN)
            coming.append(value[first + BASE : first + 2 * BASE])
            work[m] = value
            work[m, first : first + BASE, :] = row
        strips = coming
    for m in range(blocks):
        inv = -work[m]
        for i, part in enumerate(split(inv, 3)):
            jac_ref[i, m] = part.astype(bf16)
    pack_ref[SYS:, :] = smooth(sys_ref[...], jac_ref)


def own_places(m):
    return [(j, j, REACH + j - m) for j in range(REACH)]


def halo_places(m):
    lefts = [(j - m, j, j - m) for j in range(m, REACH)]
    return lefts + [(REACH - m + j, REACH + j, 2 * REACH - m + j) for j in range(m + 1)]


def build_kernel(*refs, places, sides):
    cells, (own_ref, extra_ref) = refs[:sides], refs[sides : sides + 2]
    hi_ref, lo_ref, sim_ref = refs[sides + 2 :]
    blocks = hi_ref.shape[0]
    near = []
    for ref in cells:
        near.append(near_stack(ref[0:FEAT, :], one_hot(ref[FEAT : FEAT + 1, :], TASKS)))
    mates, norm = own_stack(own_ref[0:FEAT, :], extra_ref[0:TASKS, :])
    weights = extra_ref[TASKS + 1 : TASKS + 2, :]
    for m in range(blocks):
        for row, j, o in places(m):
            part = near[j // REACH][(j % REACH) * BS : (j % REACH + 1) * BS]
            both = dot(part, mates[m])
            place = m * SLOTS + o
            exponent = both[:, :BS] + norm[:, m * BS : (m + 1) * BS]
            similar = weights[:, place : place + 1] * jnp.exp(exponent)
            kernel = similar * both[:, BS:]
            head = kernel.astype(bf16)
            rows = slice(row * BS, (row + 1) * BS)
            sim_ref[m, rows, :] = similar
            hi_ref[m, rows, :] = head
            lo_ref[m, rows, :] = (kernel - head.astype(f32)).astype(bf16)


def operate(own, left, right, noise, own_hi, own_lo, halo_hi, halo_lo):
    rows = own.shape[0]
    width = own.shape[1]

    def pieces(vectors):
        head, tail = split(vectors, 2)
        return jnp.concatenate([head, tail], axis=0).astype(bf16)

    mine, lefts, rights = pieces(own), pieces(left), pieces(right)
    out = []
    for m in range(REACH):
        beyond = jnp.concatenate([lefts[:, m * BS :], rights[:, : (m + 1) * BS]], axis=1)
        first = dot(mine, own_hi[m]) + dot(beyond, halo_hi[m])
        second = dot(mine[:rows], own_lo[m]) + dot(beyond[:rows], halo_lo[m])
        out.append(first[:rows] + first[rows:] + second)
    return jnp.concatenate(out, axis=1) + noise * own


def smooth(image, jac_ref):
    rows = image.shape[0]
    out = []
    for m in range(jac_ref.shape[1]):
        pieces = jnp.concatenate(split(image[:, m * BS : (m + 1) * BS], 3), axis=0).astype(bf16)
        a = dot(pieces, jac_ref[0, m])
        b = dot(pieces[: 2 * rows], jac_ref[1, m])
        c = dot(pieces[:rows], jac_ref[2, m])
        out.append(a[:rows] + (a[rows : 2 * rows] + b[:rows] + (a[2 * rows :] + b[rows:] + c)))
    return jnp.concatenate(out, axis=1)


def first_kernel(own_ref, left_ref, right_ref, extra_ref, *refs):
    kernel, (jac_ref, image_ref, next_ref) = refs[:4], refs[4:]
    count = own_ref.shape[0] - SYS
    coarse = image_ref.shape[0] - count

    def basis(ref):
        z = one_hot(ref[FEAT + 1 : FEAT + 2, :], coarse)
        return jnp.concatenate([ref[SYS:, :], z], axis=0)

    noise = extra_ref[TASKS : TASKS + 1, :]
    image = operate(basis(own_ref), basis(left_ref), basis(right_ref), noise, *kernel)
    image_ref[...] = image
    next_ref[...] = smooth(image, jac_ref)


def second_kernel(extra_ref, vec_ref, left_ref, right_ref, early_ref, *refs):
    kernel, (jac_ref, image_ref, next_ref) = refs[:4], refs[4:]
    noise = extra_ref[TASKS : TASKS + 1, :]
    image = operate(vec_ref[...], left_ref[...], right_ref[...], noise, *kernel)
    image_ref[...] = image
    next_ref[...] = smooth(image, jac_ref)


def pitch_of(coarse):
    return coarse + 1


def lanes_of(coarse):
    return -(-5 * pitch_of(coarse) // LANES) * LANES


def moment(vectors, images, pairs):
    count = pairs.shape[0]
    table = dot(images, vectors, NT, lax.Precision.HIGH)
    own = jnp.sum(pairs, axis=1, keepdims=True)
    if images.shape[0] > count:
        own = jnp.concatenate([own, jnp.zeros((images.shape[0] - count, 1), f32)], axis=0)
    return jnp.concatenate([table, own], axis=1)


def spread_out(parts, lanes):
    rows, pitch = next(iter(parts.values())).shape
    cells = [parts.get(k, jnp.zeros((rows, pitch), f32)) for k in range(5)]
    if lanes > 5 * pitch:
        cells.append(jnp.zeros((rows, lanes - 5 * pitch), f32))
    return jnp.concatenate(cells, axis=1)


def folded(low, high):
    order = low.shape[0]
    row, col = iota((order, order), 0), iota((order, order), 1)
    diagonal = jnp.sum(jnp.where(row == col, high, 0.0), axis=1, keepdims=True)
    return jnp.concatenate([jnp.where(row >= col, low, high), diagonal], axis=1)


def unfolded(cells):
    order = cells.shape[0]
    row, col = iota((order, order), 0), iota((order, order), 1)
    square = cells[:, :order]
    turned = dot(square, jnp.where(row == col, 1.0, 0.0), TN, highest)
    low = jnp.where(row >= col, square, turned)
    high = jnp.where(row < col, square, jnp.where(row > col, turned, cells[:, order:]))
    return low, high


def early_moments_kernel(own_ref, sys_ref, d1_ref, v0_ref, out_ref):
    count = own_ref.shape[0] - SYS
    coarse = d1_ref.shape[0] - count
    lanes = out_ref.shape[1]
    pitch = pitch_of(coarse)
    systems = sys_ref[...]
    pre = own_ref[SYS:, :]
    z = one_hot(own_ref[FEAT + 1 : FEAT + 2, :], coarse)
    d1, v0 = d1_ref[...], v0_ref[...]
    m0 = moment(z, v0, pre * v0[:count])
    m1 = moment(d1[count:], v0, d1[:count] * v0[:count])
    out_ref[0:count, :] = spread_out({0: m0[:count], 1: m1[:count]}, lanes)
    start = moment(z, systems, systems * pre)
    if coarse > count:
        start = jnp.concatenate([start, jnp.zeros((coarse - count, pitch), f32)], axis=0)
    fold = folded(m0[count:, :coarse], m1[count:, :coarse])
    out_ref[count:, :] = spread_out({0: fold, 3: start}, lanes)


def late_moments_kernel(before_ref, d1_ref, d2_ref, v1_ref, out_ref, *, count):
    lanes = out_ref.shape[1]
    d1, d2, v1 = d1_ref[...], d2_ref[...], v1_ref[...]
    coarse = d1.shape[0] - count
    m2 = moment(d1[count:], v1, d1[:count] * v1[:count])
    m3 = moment(d2[count:], v1, d2[:count] * v1[:count])
    out_ref[0:count, :] = before_ref[0:count, :] + spread_out({2: m2[:count], 3: m3[:count]}, lanes)
    fold = folded(m2[count:, :coarse], m3[count:, :coarse])
    out_ref[count:, :] = before_ref[count:, :] + spread_out({1: fold}, lanes)


def third_kernel(
    extra_ref, before_ref, vec_ref, left_ref, right_ref, *refs, count, held
):
    kernel, out_ref = refs[:4], refs[4]
    coarse = vec_ref.shape[0] - count
    lanes = out_ref.shape[2]
    pitch = pitch_of(coarse)
    d2 = vec_ref[...]
    noise = extra_ref[TASKS : TASKS + 1, :]
    v2 = operate(d2, left_ref[...], right_ref[...], noise, *kernel)
    m4 = moment(d2[count:], v2, d2[:count] * v2[:count])
    row = iota((coarse, 1), 0).astype(f32)
    start = extra_ref[TASKS + 2 : TASKS + 3, 0:1] * held
    inverse = jnp.zeros((coarse, pitch), f32)
    for r in range(held):
        line = extra_ref[TASKS + 3 + r : TASKS + 4 + r, 0:pitch]
        inverse = jnp.where(row == start + r, line, inverse)
    top = before_ref[0:count, :] + spread_out({4: m4[:count]}, lanes)
    bottom = before_ref[count:, :] + spread_out({2: m4[count:], 4: inverse}, lanes)
    for c in range(out_ref.shape[0]):
        out_ref[c, 0:count, :] = top
        out_ref[c, count:, :] = bottom


def final_kernel(
    gram_ref, sys_ref, own_ref, left_ref, right_ref, d1_ref, d1l_ref, d1r_ref, d2_ref, d2l_ref,
    d2r_ref, *refs, sides, points,
):
    kernel_refs, (sol_ref, grad_ref) = refs[:6], refs[6:]
    width = own_ref.shape[1]
    count = own_ref.shape[0] - SYS
    rows = d1_ref.shape[0]
    coarse = rows - count
    pitch = pitch_of(coarse)
    wide = -(-3 * pitch // LANES) * LANES
    blocks = width // BS
    edge = width - REACH * BS
    gram = gram_ref[0]
    for c in range(1, gram_ref.shape[0]):
        gram = gram + gram_ref[c]
    bottom = gram[count:]
    gram = jnp.concatenate([gram[:count], jnp.zeros((count, wide), f32)], axis=1)
    squares = list(unfolded(bottom[:, :pitch])) + list(unfolded(bottom[:, pitch : 2 * pitch]))
    squares.append(bottom[:, 2 * pitch : 2 * pitch + coarse])
    lane = iota((1, wide), 1)
    slot, inside = lane // pitch, lane % pitch
    live = lane < 3 * pitch
    is_vec = live & (inside < coarse)
    is_one = live & (inside == coarse)

    def shifted(j):
        return jnp.where(live, gram[:, j * pitch : j * pitch + wide], 0.0)

    own = [shifted(j) for j in range(3)]
    gap = jnp.zeros((coarse, 1), f32)
    rest = jnp.zeros((coarse, wide - 3 * pitch), f32)
    hankel = []
    for i in range(3):
        line = [squares[i], gap, squares[i + 1], gap, squares[i + 2], gap]
        hankel.append(jnp.concatenate(line + ([rest] if wide > 3 * pitch else []), axis=1))
        hankel.append(jnp.zeros((1, wide), f32))
    if wide > 3 * pitch:
        hankel.append(jnp.zeros((wide - 3 * pitch, wide), f32))
    hankel = jnp.concatenate(hankel, axis=0)
    block0 = lane < pitch
    inverse = bottom[:, 4 * pitch : 4 * pitch + coarse]
    inverse = jnp.concatenate([inverse, jnp.zeros((coarse, wide - coarse), f32)], axis=1)
    inverse = jnp.concatenate([inverse, jnp.zeros((wide - coarse, wide), f32)], axis=0)
    start = bottom[:count, 3 * pitch : 4 * pitch]
    start = jnp.concatenate([start, jnp.zeros((count, wide - pitch), f32)], axis=1)
    against = jnp.where(
        block0, start, jnp.where(live, pltpu.roll(jnp.where(live, own[0], 0.0), pitch, axis=1), 0.0)
    )

    def total(x):
        return jnp.sum(x, axis=1, keepdims=True)

    def scalars(u, i):
        return total(jnp.where(lane == i * pitch + coarse, u, 0.0))

    def metric(u):
        out = dot(jnp.where(is_vec, u, 0.0), hankel, precision=highest)
        for j in range(3):
            out = out + scalars(u, j) * own[j]
        out = jnp.where(is_vec, out, 0.0)
        for i in range(3):
            out = jnp.where(lane == i * pitch + coarse, total(u * own[i]), out)
        return out

    def corrected(w):
        return dot(jnp.where(lane < coarse, w, 0.0), inverse, precision=highest)

    pre = corrected(against) + jnp.where(lane == coarse, 1.0, 0.0)
    direction = pre
    gamma = total(pre * against)
    answer = jnp.zeros_like(pre)
    image_sum = jnp.zeros_like(pre)
    for step in range(ITERS):
        image = metric(direction)
        alpha = gamma / total(direction * image)
        answer = answer + alpha * direction
        if step + 1 < ITERS:
            image_sum = image_sum + alpha * image
            moved_on = jnp.where(live & (slot > 0), pltpu.roll(direction, pitch, axis=1), 0.0)
            pre = pre - alpha * (moved_on + corrected(image))
            gamma_new = total(pre * (against - image_sum))
            direction = pre + (gamma_new / gamma) * direction
            gamma = gamma_new

    pack = jnp.concatenate(
        [left_ref[:, edge:], own_ref[...], right_ref[:, : width - edge]], axis=1
    )
    z = one_hot(pack[FEAT + 1 : FEAT + 2], coarse)
    q0 = pack[SYS:]
    d1 = jnp.concatenate([d1l_ref[:, edge:], d1_ref[...], d1r_ref[:, : width - edge]], axis=1)
    d2 = jnp.concatenate([d2l_ref[:, edge:], d2_ref[...], d2r_ref[:, : width - edge]], axis=1)
    span = q0.shape[1]
    step = -(-coarse // FEAT) * FEAT
    deep = -(-3 * step // LANES) * LANES
    parts, basis = [], []
    for i, rest in enumerate((z, d1[count:], d2[count:])):
        parts.append(answer[:, i * pitch : i * pitch + coarse])
        basis.append(rest)
        if step > coarse:
            parts.append(jnp.zeros((count, step - coarse), f32))
            basis.append(jnp.zeros((step - coarse, span), f32))
    if deep > 3 * step:
        parts.append(jnp.zeros((count, deep - 3 * step), f32))
        basis.append(jnp.zeros((deep - 3 * step, span), f32))
    x = dot(
        jnp.concatenate(parts, axis=1), jnp.concatenate(basis, axis=0), precision=highest
    )
    x = x + scalars(answer, 0) * q0 + scalars(answer, 1) * d1[:count]
    x = x + scalars(answer, 2) * d2[:count]
    mine = slice(REACH * BS, REACH * BS + width)
    sol_ref[...] = x[:, mine]

    probe = own_ref[FEAT + 2 : FEAT + 3, 0:1]
    line = iota((count, 1), 0).astype(f32) + probe * count
    right = jnp.where(line == 0, x[:, mine], sys_ref[...])
    coef = jnp.where(line == 0, 0.5 / points, -0.5 / (sides - 1) / points)
    r0, r1 = split(right, 2)
    w0, w1 = split(x * coef, 2)
    rest = LANES - 3 * count
    near = jnp.concatenate([w0, w1, w0, jnp.zeros((rest, span), f32)], axis=0).T.astype(bf16)
    mate = jnp.concatenate([r0, r0, r1, jnp.zeros((rest, width), f32)], axis=0).astype(bf16)
    scaled = pack[0:FEAT]
    table = one_hot(pack[FEAT : FEAT + 1], TASKS)
    ones = jnp.ones((8, span), f32)
    terms = jnp.concatenate([scaled, ones, scaled * scaled], axis=0)
    t0, t1 = split(terms, 2)
    pad8 = jnp.zeros((8, span), f32)
    both = jnp.concatenate([t0, pad8, t1, pad8], axis=0).astype(bf16)
    heads = jnp.concatenate([t0, pad8], axis=0).astype(bf16)
    tables = table.astype(bf16)
    high = 32
    length_total = jnp.zeros((FEAT, 1), f32)
    task_total = jnp.zeros((TASKS, TASKS), f32)
    for m in range(blocks):
        at = slice(m * BS, (m + 1) * BS)
        sums = jnp.zeros((high, BS), f32)
        held_sums = jnp.zeros((TASKS, BS), f32)
        places = [(0, row, j + REACH) for row, j, _ in own_places(m)]
        places += [(1, row, j if j < REACH else j + REACH) for row, j, _ in halo_places(m)]
        for side, row, block in places:
            hi_ref, lo_ref, sim_ref = kernel_refs[3 * side : 3 * side + 3]
            j = slice(block * BS, (block + 1) * BS)
            rows_at = slice(row * BS, (row + 1) * BS)
            outer = dot(near[j], mate[:, at])
            kernel = hi_ref[m, rows_at, :].astype(f32) + lo_ref[m, rows_at, :].astype(f32)
            energy = outer * kernel
            held = outer * sim_ref[m, rows_at, :]
            e0, e1 = (part.astype(bf16) for part in split(energy, 2))
            h0, h1 = (part.astype(bf16) for part in split(held, 2))
            first = dot(both[:, j], e0)
            sums = sums + first[:high] + first[high:] + dot(heads[:, j], e1)
            held_sums = held_sums + dot(tables[:, j], h0) + dot(tables[:, j], h1)
        mid = slice((REACH + m) * BS, (REACH + m + 1) * BS)
        left = scaled[:, mid]
        value = left * left * sums[FEAT : FEAT + 1] + sums[2 * FEAT : 3 * FEAT]
        value = value - 2.0 * left * sums[:FEAT]
        length_total = length_total + jnp.sum(value, axis=1, keepdims=True)
        task_total = task_total + dot(held_sums, table[:, mid], NT, highest)
    half = TASKS // 2
    value = jnp.concatenate(
        [
            task_total[:half],
            task_total[half:],
            jnp.where(iota((half, FEAT), 0) == iota((half, FEAT), 1), length_total, 0.0),
            jnp.zeros((half, LANES - 2 * TASKS - FEAT), f32),
        ],
        axis=1,
    )
    for c in range(grad_ref.shape[0]):
        grad_ref[c] = value


def tail_kernel(parts_ref, length_ref, task_ref):
    total = parts_ref[0]
    for c in range(1, parts_ref.shape[0]):
        total = total + parts_ref[c]
    half = TASKS // 2
    task_ref[0:half, :] = total[:, :TASKS]
    task_ref[half:, :] = total[:, TASKS : 2 * TASKS]
    length_ref[...] = jnp.sum(total[:, 2 * TASKS : 2 * TASKS + FEAT], axis=0)


MIB = 1024 * 1024


def call(body, outs, args, name, smem=0, hbm=0, far_outs=0, scratch=(), flops=0, limit=16):
    if hbm:
        args = args[:-hbm] + [pltpu.with_memory_space_constraint(a, pltpu.HBM) for a in args[-hbm:]]
    if far_outs:
        outs = outs[:-far_outs] + [pltpu.HBM(o.shape, o.dtype) for o in outs[-far_outs:]]
    vm = pl.BlockSpec(memory_space=pltpu.VMEM)
    sm = pl.BlockSpec(memory_space=pltpu.SMEM)
    far = pl.BlockSpec(memory_space=pltpu.HBM)
    return pl.pallas_call(
        body,
        out_shape=outs,
        in_specs=[sm] * smem + [vm] * (len(args) - smem - hbm) + [far] * hbm,
        out_specs=[vm] * (len(outs) - far_outs) + [far] * far_outs,
        scratch_shapes=scratch,
        compiler_params=pltpu.CompilerParams(vmem_limit_bytes=limit * MIB),
        cost_estimate=pl.CostEstimate(flops=flops, bytes_accessed=1 << 20, transcendentals=0),
        name=name,
    )(*args)


def both_sides(cells):
    count = lax.axis_size("pts")
    up = [(i, i + 1) for i in range(count - 1)]
    down = [(i + 1, i) for i in range(count - 1)]
    return lax.ppermute(cells, "pts", up), lax.ppermute(cells, "pts", down)


def shards(
    systems, features, task_ids, pattern, aggregate, coarse_inverse, task_cov, lengthscales, noise
):
    count, width = systems.shape
    blocks = width // BS
    coarse = coarse_inverse.shape[1]
    rows = count + coarse
    lanes = lanes_of(coarse)
    assert blocks == REACH
    place = lax.axis_index("pts").astype(jnp.int32)[None]
    probe = lax.axis_index("probe").astype(jnp.int32)[None]
    ranks = lax.axis_size("pts")
    sides = lax.axis_size("probe")

    def shape(*dims, kind=f32):
        return jax.ShapeDtypeStruct(dims, kind)

    jac, pack, extra = call(
        invert_kernel,
        [shape(3, blocks, BS, BS, kind=bf16), shape(SYS + count, width), shape(TASKS + FEAT, width)],
        [place, probe, features, task_ids, aggregate, systems, task_cov, coarse_inverse, pattern, lengthscales, noise],
        "invert",
        smem=2,
        hbm=9,
        scratch=[
            pltpu.VMEM((blocks, BS, BS), f32),
            pltpu.VMEM(features.shape, f32),
            pltpu.VMEM(task_ids.shape, jnp.int32),
            pltpu.VMEM(aggregate.shape, jnp.int32),
            pltpu.VMEM(systems.shape, f32),
            pltpu.VMEM(task_cov.shape, f32),
            pltpu.VMEM(coarse_inverse.shape, f32),
            pltpu.SMEM(pattern.shape, jnp.int32),
            pltpu.SMEM(lengthscales.shape, f32),
            pltpu.SMEM(noise.shape, f32),
            pltpu.SemaphoreType.DMA((9,)),
        ],
        flops=10**10,
    )
    pack_l, pack_r = both_sides(pack)

    def build(places, deep, cells, name):
        return call(
            functools.partial(build_kernel, places=places, sides=len(cells)),
            [
                shape(blocks, deep, BS, kind=bf16),
                shape(blocks, deep, BS, kind=bf16),
                shape(blocks, deep, BS),
            ],
            cells + [pack, extra],
            name,
            flops=10**9,
        )

    own_hi, own_lo, own_sim = build(own_places, width, [pack], "build_own")
    halo_hi, halo_lo, halo_sim = build(
        halo_places, BAND - width, [pack_l, pack_r], "build_halo"
    )
    kernel = [own_hi, own_lo, halo_hi, halo_lo]
    v0, d1 = call(
        first_kernel,
        [shape(rows, width), shape(rows, width)],
        [pack, pack_l, pack_r, extra] + kernel + [jac],
        "first",
        flops=10**9,
    )
    d1_l, d1_r = both_sides(d1)
    (early,) = call(
        early_moments_kernel, [shape(rows, lanes)], [pack, systems, d1, v0], "early", flops=10**9
    )
    v1, d2 = call(
        second_kernel,
        [shape(rows, width), shape(rows, width)],
        [extra, d1, d1_l, d1_r, early] + kernel + [jac],
        "second",
        flops=10**9,
    )
    d2_l, d2_r = both_sides(d2)
    (late,) = call(
        functools.partial(late_moments_kernel, count=count),
        [shape(rows, lanes)],
        [early, d1, d2, v1],
        "late",
        flops=10**9,
    )
    (gram,) = call(
        functools.partial(third_kernel, count=count, held=coarse_inverse.shape[0]),
        [shape(ranks, rows, lanes)],
        [extra, late, d2, d2_l, d2_r] + kernel,
        "third",
        flops=10**9,
    )
    gram = lax.all_to_all(gram, "pts", 0, 0, tiled=True)
    cells = [own_hi, own_lo, own_sim, halo_hi, halo_lo, halo_sim]
    answer, grads = call(
        functools.partial(final_kernel, sides=sides * count, points=ranks * width),
        [shape(count, width), shape(ranks * sides, FEAT, LANES)],
        [gram, systems, pack, pack_l, pack_r, d1, d1_l, d1_r, d2, d2_l, d2_r] + cells,
        "final",
        flops=10**9,
    )
    grads = lax.all_to_all(grads, ("pts", "probe"), 0, 0, tiled=True)
    lengths, tasks = call(
        tail_kernel, [shape(FEAT), shape(TASKS, TASKS)], [grads], "tail", flops=10**5
    )
    return answer, lengths, tasks


def solution(mesh):
    return jax.shard_map(
        shards,
        mesh=mesh,
        in_specs=(
            P("probe", ("groups", "pts")),
            P(None, ("groups", "pts")),
            P(("groups", "pts")),
            P(("groups", "pts"), None),
            P(("groups", "pts")),
            P(("groups", "pts"), None),
            P("groups", None),
            P("groups"),
            P("groups"),
        ),
        out_specs=(P("probe", ("groups", "pts")), P("groups"), P("groups", None)),
        check_vma=False,
    )
```

```python
import functools

import jax
import jax.numpy as jnp
from jax import lax
from jax.experimental import pallas as pl
from jax.experimental.pallas import tpu as pltpu
from jax.sharding import PartitionSpec as P

BS = 256
REACH = 3
FEAT = 8
TASKS = 16
ITERS = 3
SLOTS = 2 * REACH + 1
BAND = SLOTS * BS
BASE = 32
GROUP = 4
LANES = 128
SYS = 2 * FEAT

highest = lax.Precision.HIGHEST
f32 = jnp.float32
bf16 = jnp.bfloat16
NN = (((1,), (0,)), ((), ()))
NT = (((1,), (1,)), ((), ()))
TN = (((0,), (0,)), ((), ()))


def dot(a, b, dims=NN, precision=None):
    return lax.dot_general(a, b, dims, precision=precision, preferred_element_type=f32)


def iota(shape, dim):
    return lax.broadcasted_iota(jnp.int32, shape, dim)


def split(x, parts):
    out = []
    for _ in range(parts - 1):
        head = x.astype(bf16).astype(f32)
        out.append(head)
        x = x - head
    out.append(x.astype(bf16).astype(f32))
    return out


def column(ref, size):
    rows = iota((size, 1), 0)
    out = jnp.zeros((size, 1), f32)
    for i in range(size):
        out = jnp.where(rows == i, ref[i], out)
    return out


def one_hot(ids, size):
    return (iota((size, ids.shape[1]), 0).astype(f32) == ids).astype(f32)


def noise_row(noise_ref, ids):
    out = jnp.zeros(ids.shape, f32)
    for t in range(TASKS):
        out = jnp.where(ids == float(t), noise_ref[t], out)
    return out


def weight(pat_ref, block, offset):
    if offset != REACH:
        return pat_ref[block, offset].astype(f32)
    total = pat_ref[block, 0]
    for o in range(1, SLOTS):
        total = total + pat_ref[block, o]
    return total.astype(f32)


def near_stack(scaled, table):
    s0, s1, s2 = split(scaled, 3)
    n0, n1, n2 = split(-0.5 * jnp.sum(scaled * scaled, axis=0, keepdims=True), 3)
    rows = iota(scaled.shape, 0)
    norms = jnp.where(rows == 0, n0, jnp.where(rows == 1, n1, jnp.where(rows == 2, n2, 0.0)))
    pad = jnp.zeros((LANES - 7 * FEAT - 3 * TASKS, scaled.shape[1]), f32)
    stack = jnp.concatenate([s0, s0, s1, s1, s0, s2, norms, table, table, table, pad], axis=0)
    return stack.T.astype(bf16)


def own_stack(scaled, picked):
    s0, s1, s2 = split(scaled, 3)
    rows = iota(scaled.shape, 0)
    ones = jnp.where(rows < 3, 1.0, 0.0)
    count = scaled.shape[1]
    tail = LANES - 7 * FEAT - 3 * TASKS
    left = jnp.concatenate(
        [s0, s1, s0, s1, s2, s0, ones, jnp.zeros((3 * TASKS + tail, count), f32)], axis=0
    ).astype(bf16)
    right = jnp.concatenate(
        [jnp.zeros((7 * FEAT, count), f32)] + split(picked, 3) + [jnp.zeros((tail, count), f32)],
        axis=0,
    ).astype(bf16)
    sides = [
        jnp.concatenate([left[:, i : i + BS], right[:, i : i + BS]], axis=1)
        for i in range(0, count, BS)
    ]
    return sides, -0.5 * jnp.sum(scaled * scaled, axis=0, keepdims=True)


def small_inverse(p):
    n = len(p)
    if n == 1:
        return [[1.0 / p[0][0]]]
    if n == 2:
        a, b, d = p[0][0], p[0][1], p[1][1]
        r = 1.0 / (a * d - b * b)
        off = -b * r
        return [[d * r, off], [off, a * r]]
    h = n // 2
    ainv = small_inverse([row[:h] for row in p[:h]])
    b = [row[h:] for row in p[:h]]
    t = [[sum(ainv[i][k] * b[k][j] for k in range(h)) for j in range(h)] for i in range(h)]
    s = [[None] * h for _ in range(h)]
    for i in range(h):
        for j in range(i, h):
            s[i][j] = s[j][i] = p[h + i][h + j] - sum(b[k][i] * t[k][j] for k in range(h))
    sinv = small_inverse(s)
    u = [[sum(t[i][k] * sinv[k][j] for k in range(h)) for j in range(h)] for i in range(h)]
    out = [[None] * n for _ in range(n)]
    for i in range(h):
        for j in range(h):
            out[h + i][h + j] = sinv[i][j]
            out[i][h + j] = out[h + j][i] = -u[i][j]
    for i in range(h):
        for j in range(i, h):
            out[i][j] = out[j][i] = ainv[i][j] + sum(u[i][k] * t[j][k] for k in range(h))
    return out


def with_rows(cells, first, rows):
    top = first - first % 8
    part = cells[top : top + 8]
    sub = iota((8, 1), 0)
    for t, row in enumerate(rows):
        part = jnp.where(sub == first - top + t, row, part)
    pieces = [cells[:top], part, cells[top + 8 :]]
    return jnp.concatenate([p for p in pieces if p.shape[0]], axis=0)


def sweep_base(cells):
    lane = iota((BASE, LANES), 1)
    start = lane - lane % BASE
    inner = iota((1, LANES), 1) % BASE

    def columns(first):
        return [
            jnp.take_along_axis(cells, start + (first + t), axis=1, mode="promise_in_bounds")
            for t in range(GROUP)
        ]

    cols = columns(0)
    for first in range(0, BASE, GROUP):
        ahead = columns(first + GROUP) if first + GROUP < BASE else []
        pivots = [[cols[u][first + t : first + t + 1, :] for u in range(GROUP)] for t in range(GROUP)]
        inv = small_inverse(pivots)
        coming = []
        for col in ahead:
            head = [col[first + t : first + t + 1, :] for t in range(GROUP)]
            factor = [sum(inv[t][u] * head[u] for u in range(GROUP)) for t in range(GROUP)]
            for t in range(GROUP):
                col = col - cols[t] * factor[t]
            coming.append(with_rows(col, first, factor))
        rows = [cells[first + t : first + t + 1, :] for t in range(GROUP)]
        group = (inner >= first) & (inner < first + GROUP)
        for t in range(GROUP):
            rows[t] = jnp.where(inner == first + t, -1.0, jnp.where(group, 0.0, rows[t]))
        new = [sum(inv[t][u] * rows[u] for u in range(GROUP)) for t in range(GROUP)]
        cells = jnp.where(group, 0.0, cells)
        for t in range(GROUP):
            cells = cells - cols[t] * new[t]
        cells = with_rows(cells, first, new)
        cols = coming
    return cells


def fetch(pairs, sems):
    copies = [pltpu.make_async_copy(a, b, sems.at[i]) for i, (a, b) in enumerate(pairs)]
    for copy in copies:
        copy.start()
    return copies


def invert_kernel(
    place_ref, probe_ref, feat_hbm, ids_hbm, agg_hbm, sys_hbm, cov_hbm, coarse_hbm, pat_hbm, len_hbm, noise_hbm,
    jac_ref, pack_ref, extra_ref,
    work, feat_ref, ids_ref, agg_ref, sys_ref, cov_ref, coarse_ref, pat_ref, len_ref, noise_ref, sems,
):
    blocks = work.shape[0]
    width = blocks * BS
    pairs = [
        (feat_hbm, feat_ref), (ids_hbm, ids_ref), (agg_hbm, agg_ref), (cov_hbm, cov_ref),
        (pat_hbm, pat_ref), (len_hbm, len_ref), (noise_hbm, noise_ref), (coarse_hbm, coarse_ref),
        (sys_hbm, sys_ref),
    ]
    for copy in fetch(pairs, sems):
        copy.wait()
    scaled = feat_ref[...] / column(len_ref, FEAT)
    ids = ids_ref[...].astype(f32).reshape(1, width)
    which = agg_ref[...].astype(f32).reshape(1, width)
    table = one_hot(ids, TASKS)
    noise = noise_row(noise_ref, ids)
    c0, c1, c2 = split(cov_ref[...], 3)
    tab = table.astype(bf16)
    picked = (dot(c2.astype(bf16), tab) + dot(c1.astype(bf16), tab)) + dot(c0.astype(bf16), tab)
    rows = iota((FEAT, width), 0)
    weights = jnp.zeros((1, width), f32)
    places = iota((1, width), 1)
    for m in range(blocks):
        for o in range(SLOTS):
            weights = jnp.where(places == m * SLOTS + o, weight(pat_ref, m, o), weights)
    pack_ref[0:FEAT, :] = scaled
    pack_ref[FEAT : 2 * FEAT, :] = jnp.where(
        rows == 0,
        ids,
        jnp.where(rows == 1, which, jnp.where(rows == 2, probe_ref[0].astype(f32), 0.0)),
    )
    extra_ref[0:TASKS, :] = picked
    tail = jnp.where(rows == 0, noise, jnp.where(rows == 1, weights, 0.0))
    held = coarse_ref.shape[0]
    inverse = jnp.concatenate(
        [coarse_ref[...], jnp.zeros((held, width - coarse_ref.shape[1]), f32)], axis=1
    )
    tail = jnp.where(rows == 2, place_ref[0].astype(f32), tail)
    for r in range(held):
        tail = jnp.where(rows == 3 + r, inverse[r : r + 1], tail)
    extra_ref[TASKS : TASKS + FEAT, :] = tail
    near = near_stack(scaled, table)
    mates, norm = own_stack(scaled, picked)
    eye = iota((BS, BS), 0) == iota((BS, BS), 1)
    for m in range(blocks):
        at = slice(m * BS, (m + 1) * BS)
        both = dot(near[at], mates[m])
        block = weight(pat_ref, m, REACH) * jnp.exp(both[:, :BS] + norm[:, at]) * both[:, BS:]
        work[m] = block + jnp.where(eye, noise[:, at], 0.0)
    seg = iota((BASE, LANES), 1) // BASE
    wide = iota((BASE, BS), 1)
    deep = iota((BASE, BS), 0)
    strips = [work[m, 0:BASE, :] for m in range(blocks)]
    for k in range(BS // BASE):
        first = k * BASE
        tile, inside = first // LANES, first % LANES
        cells = jnp.where(iota((BASE, LANES), 1) % BASE == iota((BASE, LANES), 0), 1.0, 0.0)
        for m in range(blocks):
            piece = strips[m][:, tile * LANES : (tile + 1) * LANES]
            shift = (BASE * m - inside) % LANES
            if shift:
                piece = pltpu.roll(piece, shift, axis=1)
            cells = jnp.where(seg == m, piece, cells)
        inv = -sweep_base(cells)
        held = (wide >= first) & (wide < first + BASE)
        minus = jnp.where(wide - first == deep, -1.0, 0.0)
        stack = jnp.concatenate(
            [jnp.where(held, minus, s) for s in strips]
            + [jnp.zeros((LANES - blocks * BASE, BS), f32)],
            axis=0,
        )
        spread = jnp.concatenate([jnp.where(seg == m, inv, 0.0) for m in range(blocks)], axis=0)
        new = dot(spread, stack, precision=highest)
        gone = (iota((1, BS), 1) >= first) & (iota((1, BS), 1) < first + BASE)
        coming = []
        for m in range(blocks):
            row = new[m * BASE : (m + 1) * BASE, :]
            r0, r1, r2 = split(strips[m], 3)
            p0, p1, p2 = split(row, 3)
            a = jnp.concatenate([r0, r0, r1, r1, r0, r2], axis=0).astype(bf16)
            b = jnp.concatenate([p0, p1, p0, p1, p2, p0], axis=0).astype(bf16)
            value = jnp.where(gone, 0.0, work[m]) - dot(a, b, TN)
            coming.append(value[first + BASE : first + 2 * BASE])
            work[m] = value
            work[m, first : first + BASE, :] = row
        strips = coming
    for m in range(blocks):
        inv = -work[m]
        for i, part in enumerate(split(inv, 3)):
            jac_ref[i, m] = part.astype(bf16)
    pack_ref[SYS:, :] = smooth(sys_ref[...], jac_ref)


def own_places(m):
    return [(j, j, REACH + j - m) for j in range(REACH)]


def halo_places(m):
    lefts = [(j - m, j, j - m) for j in range(m, REACH)]
    return lefts + [(REACH - m + j, REACH + j, 2 * REACH - m + j) for j in range(m + 1)]


def build_kernel(*refs, places, sides):
    cells, (own_ref, extra_ref) = refs[:sides], refs[sides : sides + 2]
    hi_ref, lo_ref, sim_ref = refs[sides + 2 :]
    blocks = hi_ref.shape[0]
    near = []
    for ref in cells:
        near.append(near_stack(ref[0:FEAT, :], one_hot(ref[FEAT : FEAT + 1, :], TASKS)))
    mates, norm = own_stack(own_ref[0:FEAT, :], extra_ref[0:TASKS, :])
    weights = extra_ref[TASKS + 1 : TASKS + 2, :]
    for m in range(blocks):
        for row, j, o in places(m):
            part = near[j // REACH][(j % REACH) * BS : (j % REACH + 1) * BS]
            both = dot(part, mates[m])
            place = m * SLOTS + o
            exponent = both[:, :BS] + norm[:, m * BS : (m + 1) * BS]
            similar = weights[:, place : place + 1] * jnp.exp(exponent)
            kernel = similar * both[:, BS:]
            head = kernel.astype(bf16)
            rows = slice(row * BS, (row + 1) * BS)
            if o <= REACH or sides == 1:
                sim_ref[m, rows, :] = similar
            hi_ref[m, rows, :] = head
            lo_ref[m, rows, :] = (kernel - head.astype(f32)).astype(bf16)


def pieces(vectors):
    return jnp.concatenate(split(vectors, 2), axis=0).astype(bf16)


def apply(cells, hi, lo):
    rows = cells.shape[0] // 2
    first = dot(cells, hi)
    return first[:rows] + first[rows:] + dot(cells[:rows], lo)


def operate_own(own, noise, own_hi, own_lo):
    mine = pieces(own)
    out = [apply(mine, own_hi[m], own_lo[m]) for m in range(REACH)]
    return jnp.concatenate(out, axis=1) + noise * own


def operate_left(left, halo_hi, halo_lo):
    cells = pieces(left)
    out = []
    for m in range(REACH):
        part = slice(0, (REACH - m) * BS)
        out.append(apply(cells[:, m * BS :], halo_hi[m, part, :], halo_lo[m, part, :]))
    return jnp.concatenate(out, axis=1)


def operate(own, left, right, noise, own_hi, own_lo, halo_hi, halo_lo):
    lefts, rights = pieces(left), pieces(right)
    out = []
    for m in range(REACH):
        beyond = jnp.concatenate([lefts[:, m * BS :], rights[:, : (m + 1) * BS]], axis=1)
        out.append(apply(beyond, halo_hi[m], halo_lo[m]))
    return operate_own(own, noise, own_hi, own_lo) + jnp.concatenate(out, axis=1)


def smooth(image, jac_ref):
    rows = image.shape[0]
    out = []
    for m in range(jac_ref.shape[1]):
        pieces = jnp.concatenate(split(image[:, m * BS : (m + 1) * BS], 3), axis=0).astype(bf16)
        a = dot(pieces, jac_ref[0, m])
        b = dot(pieces[: 2 * rows], jac_ref[1, m])
        c = dot(pieces[:rows], jac_ref[2, m])
        out.append(a[:rows] + (a[rows : 2 * rows] + b[:rows] + (a[2 * rows :] + b[rows:] + c)))
    return jnp.concatenate(out, axis=1)


def first_kernel(own_ref, left_ref, right_ref, extra_ref, *refs):
    kernel, (jac_ref, image_ref, next_ref) = refs[:4], refs[4:]
    count = own_ref.shape[0] - SYS
    coarse = image_ref.shape[0] - count

    def basis(ref):
        z = one_hot(ref[FEAT + 1 : FEAT + 2, :], coarse)
        return jnp.concatenate([ref[SYS:, :], z], axis=0)

    noise = extra_ref[TASKS : TASKS + 1, :]
    image = operate(basis(own_ref), basis(left_ref), basis(right_ref), noise, *kernel)
    image_ref[...] = image
    next_ref[...] = smooth(image, jac_ref)


def second_kernel(extra_ref, vec_ref, left_ref, right_ref, early_ref, sys_ref, *refs):
    kernel, (jac_ref, image_ref, cargo_ref) = refs[:4], refs[4:]
    rows = vec_ref.shape[0]
    noise = extra_ref[TASKS : TASKS + 1, :]
    image = operate(vec_ref[...], left_ref[...], right_ref[...], noise, *kernel)
    image_ref[...] = image
    cargo_ref[0:rows, :] = smooth(image, jac_ref)
    cargo_ref[rows:, :] = sys_ref[...]


def pitch_of(coarse):
    return coarse + 1


def lanes_of(coarse):
    return -(-5 * pitch_of(coarse) // LANES) * LANES


def moment(vectors, images, pairs):
    count = pairs.shape[0]
    table = dot(images, vectors, NT, lax.Precision.HIGH)
    own = jnp.sum(pairs, axis=1, keepdims=True)
    if images.shape[0] > count:
        own = jnp.concatenate([own, jnp.zeros((images.shape[0] - count, 1), f32)], axis=0)
    return jnp.concatenate([table, own], axis=1)


def spread_out(parts, lanes):
    rows, pitch = next(iter(parts.values())).shape
    cells = [parts.get(k, jnp.zeros((rows, pitch), f32)) for k in range(5)]
    if lanes > 5 * pitch:
        cells.append(jnp.zeros((rows, lanes - 5 * pitch), f32))
    return jnp.concatenate(cells, axis=1)


def folded(low, high):
    order = low.shape[0]
    row, col = iota((order, order), 0), iota((order, order), 1)
    diagonal = jnp.sum(jnp.where(row == col, high, 0.0), axis=1, keepdims=True)
    return jnp.concatenate([jnp.where(row >= col, low, high), diagonal], axis=1)


def unfolded(cells):
    order = cells.shape[0]
    row, col = iota((order, order), 0), iota((order, order), 1)
    square = cells[:, :order]
    turned = dot(square, jnp.where(row == col, 1.0, 0.0), TN, highest)
    low = jnp.where(row >= col, square, turned)
    high = jnp.where(row < col, square, jnp.where(row > col, turned, cells[:, order:]))
    return low, high


def early_moments_kernel(own_ref, sys_ref, d1_ref, v0_ref, out_ref):
    count = own_ref.shape[0] - SYS
    coarse = d1_ref.shape[0] - count
    lanes = out_ref.shape[1]
    pitch = pitch_of(coarse)
    systems = sys_ref[...]
    pre = own_ref[SYS:, :]
    z = one_hot(own_ref[FEAT + 1 : FEAT + 2, :], coarse)
    d1, v0 = d1_ref[...], v0_ref[...]
    m0 = moment(z, v0, pre * v0[:count])
    m1 = moment(d1[count:], v0, d1[:count] * v0[:count])
    out_ref[0:count, :] = spread_out({0: m0[:count], 1: m1[:count]}, lanes)
    start = moment(z, systems, systems * pre)
    if coarse > count:
        start = jnp.concatenate([start, jnp.zeros((coarse - count, pitch), f32)], axis=0)
    fold = folded(m0[count:, :coarse], m1[count:, :coarse])
    out_ref[count:, :] = spread_out({0: fold, 3: start}, lanes)


def late_moments_kernel(before_ref, d1_ref, cargo_ref, v1_ref, out_ref, *, count):
    lanes = out_ref.shape[1]
    d1, d2, v1 = d1_ref[...], cargo_ref[0 : d1_ref.shape[0], :], v1_ref[...]
    coarse = d1.shape[0] - count
    m2 = moment(d1[count:], v1, d1[:count] * v1[:count])
    m3 = moment(d2[count:], v1, d2[:count] * v1[:count])
    out_ref[0:count, :] = before_ref[0:count, :] + spread_out({2: m2[:count], 3: m3[:count]}, lanes)
    fold = folded(m2[count:, :coarse], m3[count:, :coarse])
    out_ref[count:, :] = before_ref[count:, :] + spread_out({1: fold}, lanes)


def third_kernel(
    extra_ref, before_ref, cargo_ref, left_ref, *refs, count, held
):
    kernel, out_ref = refs[:4], refs[4]
    rows = cargo_ref.shape[0] - count
    coarse = rows - count
    lanes = out_ref.shape[2]
    pitch = pitch_of(coarse)
    d2 = cargo_ref[0:rows, :]
    noise = extra_ref[TASKS : TASKS + 1, :]
    inner = operate_own(d2, noise, *kernel[:2])
    cross = operate_left(left_ref[0:rows, :], *kernel[2:])
    m4 = moment(d2[count:], inner + cross, d2[:count] * (inner + 2.0 * cross)[:count])
    mirror = dot(d2, cross[count:], NT, lax.Precision.HIGH)
    m4 = m4 + jnp.concatenate([mirror, jnp.zeros((rows, 1), f32)], axis=1)
    row = iota((coarse, 1), 0).astype(f32)
    start = extra_ref[TASKS + 2 : TASKS + 3, 0:1] * held
    inverse = jnp.zeros((coarse, pitch), f32)
    for r in range(held):
        line = extra_ref[TASKS + 3 + r : TASKS + 4 + r, 0:pitch]
        inverse = jnp.where(row == start + r, line, inverse)
    top = before_ref[0:count, :] + spread_out({4: m4[:count]}, lanes)
    bottom = before_ref[count:, :] + spread_out({2: m4[count:], 4: inverse}, lanes)
    for c in range(out_ref.shape[0]):
        out_ref[c, 0:count, :] = top
        out_ref[c, count:, :] = bottom


def final_kernel(
    gram_ref, own_ref, left_ref, d1_ref, d1l_ref, cargo_ref, cargol_ref, *refs, sides, points,
):
    kernel_refs, (sol_ref, grad_ref) = refs[:6], refs[6:]
    width = own_ref.shape[1]
    count = own_ref.shape[0] - SYS
    rows = d1_ref.shape[0]
    coarse = rows - count
    pitch = pitch_of(coarse)
    wide = -(-3 * pitch // LANES) * LANES
    blocks = width // BS
    gram = gram_ref[0]
    for c in range(1, gram_ref.shape[0]):
        gram = gram + gram_ref[c]
    bottom = gram[count:]
    gram = jnp.concatenate([gram[:count], jnp.zeros((count, wide), f32)], axis=1)
    squares = list(unfolded(bottom[:, :pitch])) + list(unfolded(bottom[:, pitch : 2 * pitch]))
    squares.append(bottom[:, 2 * pitch : 2 * pitch + coarse])
    lane = iota((1, wide), 1)
    slot, inside = lane // pitch, lane % pitch
    live = lane < 3 * pitch
    is_vec = live & (inside < coarse)
    is_one = live & (inside == coarse)

    def shifted(j):
        return jnp.where(live, gram[:, j * pitch : j * pitch + wide], 0.0)

    own = [shifted(j) for j in range(3)]
    gap = jnp.zeros((coarse, 1), f32)
    rest = jnp.zeros((coarse, wide - 3 * pitch), f32)
    hankel = []
    for i in range(3):
        line = [squares[i], gap, squares[i + 1], gap, squares[i + 2], gap]
        hankel.append(jnp.concatenate(line + ([rest] if wide > 3 * pitch else []), axis=1))
        hankel.append(jnp.zeros((1, wide), f32))
    if wide > 3 * pitch:
        hankel.append(jnp.zeros((wide - 3 * pitch, wide), f32))
    hankel = jnp.concatenate(hankel, axis=0)
    block0 = lane < pitch
    inverse = bottom[:, 4 * pitch : 4 * pitch + coarse]
    inverse = jnp.concatenate([inverse, jnp.zeros((coarse, wide - coarse), f32)], axis=1)
    inverse = jnp.concatenate([inverse, jnp.zeros((wide - coarse, wide), f32)], axis=0)
    start = bottom[:count, 3 * pitch : 4 * pitch]
    start = jnp.concatenate([start, jnp.zeros((count, wide - pitch), f32)], axis=1)
    against = jnp.where(
        block0, start, jnp.where(live, pltpu.roll(jnp.where(live, own[0], 0.0), pitch, axis=1), 0.0)
    )

    def total(x):
        return jnp.sum(x, axis=1, keepdims=True)

    def scalars(u, i):
        return total(jnp.where(lane == i * pitch + coarse, u, 0.0))

    def metric(u):
        out = dot(jnp.where(is_vec, u, 0.0), hankel, precision=highest)
        for j in range(3):
            out = out + scalars(u, j) * own[j]
        out = jnp.where(is_vec, out, 0.0)
        for i in range(3):
            out = jnp.where(lane == i * pitch + coarse, total(u * own[i]), out)
        return out

    def corrected(w):
        return dot(jnp.where(lane < coarse, w, 0.0), inverse, precision=highest)

    pre = corrected(against) + jnp.where(lane == coarse, 1.0, 0.0)
    direction = pre
    gamma = total(pre * against)
    answer = jnp.zeros_like(pre)
    image_sum = jnp.zeros_like(pre)
    for step in range(ITERS):
        image = metric(direction)
        alpha = gamma / total(direction * image)
        answer = answer + alpha * direction
        if step + 1 < ITERS:
            image_sum = image_sum + alpha * image
            moved_on = jnp.where(live & (slot > 0), pltpu.roll(direction, pitch, axis=1), 0.0)
            pre = pre - alpha * (moved_on + corrected(image))
            gamma_new = total(pre * (against - image_sum))
            direction = pre + (gamma_new / gamma) * direction
            gamma = gamma_new

    pack = jnp.concatenate([left_ref[...], own_ref[...]], axis=1)
    z = one_hot(pack[FEAT + 1 : FEAT + 2], coarse)
    q0 = pack[SYS:]
    d1 = jnp.concatenate([d1l_ref[...], d1_ref[...]], axis=1)
    cargo = jnp.concatenate([cargol_ref[...], cargo_ref[...]], axis=1)
    d2 = cargo[:rows]
    span = q0.shape[1]
    step = -(-coarse // FEAT) * FEAT
    deep = -(-3 * step // LANES) * LANES
    parts, basis = [], []
    for i, rest in enumerate((z, d1[count:], d2[count:])):
        parts.append(answer[:, i * pitch : i * pitch + coarse])
        basis.append(rest)
        if step > coarse:
            parts.append(jnp.zeros((count, step - coarse), f32))
            basis.append(jnp.zeros((step - coarse, span), f32))
    if deep > 3 * step:
        parts.append(jnp.zeros((count, deep - 3 * step), f32))
        basis.append(jnp.zeros((deep - 3 * step, span), f32))
    x = dot(
        jnp.concatenate(parts, axis=1), jnp.concatenate(basis, axis=0), precision=highest
    )
    x = x + scalars(answer, 0) * q0 + scalars(answer, 1) * d1[:count]
    x = x + scalars(answer, 2) * d2[:count]
    mine = slice(width, 2 * width)
    sol_ref[...] = x[:, mine]

    probe = own_ref[FEAT + 2 : FEAT + 3, 0:1]
    line = iota((count, 1), 0).astype(f32) + probe * count
    right = jnp.where(line == 0, x, cargo[rows:])
    coef = jnp.where(line == 0, 0.5 / points, -0.5 / (sides - 1) / points)
    r0, r1 = split(right, 2)
    w0, w1 = split(x * coef, 2)
    rest = jnp.zeros((LANES - 6 * count, span), f32)
    near = jnp.concatenate([w0, w1, w0, r0, r1, r0, rest], axis=0).T.astype(bf16)
    none = jnp.zeros((3 * count, width), f32)
    rest = rest[:, mine]
    ahead = jnp.concatenate([r0, r0, r1], axis=0)[:, mine]
    back = jnp.concatenate([w0, w0, w1], axis=0)[:, mine]
    mates = [
        jnp.concatenate([ahead, none, rest], axis=0).astype(bf16),
        jnp.concatenate([none, back, rest], axis=0).astype(bf16),
    ]
    scaled = pack[0:FEAT]
    table = one_hot(pack[FEAT : FEAT + 1], TASKS)
    ones = jnp.ones((8, span), f32)
    terms = jnp.concatenate([scaled, ones, scaled * scaled], axis=0)
    t0, t1 = split(terms, 2)
    pad8 = jnp.zeros((8, span), f32)
    both = jnp.concatenate([t0, pad8, t1, pad8], axis=0).astype(bf16)
    heads = jnp.concatenate([t0, pad8], axis=0).astype(bf16)
    tables = table.astype(bf16)
    high = 32
    length_total = jnp.zeros((FEAT, 1), f32)
    task_total = jnp.zeros((TASKS, TASKS), f32)
    for m in range(blocks):
        at = slice(m * BS, (m + 1) * BS)
        sums = jnp.zeros((high, BS), f32)
        held_sums = [jnp.zeros((TASKS, BS), f32) for _ in mates]
        places = [(1, row, j + REACH) for row, j, _ in own_places(m)]
        places += [(2, row, j) for row, j, _ in halo_places(m) if j < REACH]
        for orders, row, block in places:
            hi_ref, lo_ref, sim_ref = kernel_refs[3 * orders - 3 : 3 * orders]
            j = slice(block * BS, (block + 1) * BS)
            rows_at = slice(row * BS, (row + 1) * BS)
            outers = [dot(near[j], mate[:, at]) for mate in mates[:orders]]
            kernel = hi_ref[m, rows_at, :].astype(f32) + lo_ref[m, rows_at, :].astype(f32)
            similar = sim_ref[m, rows_at, :]
            energy = sum(outers) * kernel
            e0, e1 = (part.astype(bf16) for part in split(energy, 2))
            first = dot(both[:, j], e0)
            sums = sums + first[:high] + first[high:] + dot(heads[:, j], e1)
            for k in range(orders):
                h0, h1 = (part.astype(bf16) for part in split(outers[k] * similar, 2))
                held_sums[k] = held_sums[k] + dot(tables[:, j], h0) + dot(tables[:, j], h1)
        mid = slice(width + m * BS, width + (m + 1) * BS)
        left = scaled[:, mid]
        value = left * left * sums[FEAT : FEAT + 1] + sums[2 * FEAT : 3 * FEAT]
        value = value - 2.0 * left * sums[:FEAT]
        length_total = length_total + jnp.sum(value, axis=1, keepdims=True)
        task_total = task_total + dot(held_sums[0], table[:, mid], NT, highest)
        task_total = task_total + dot(table[:, mid], held_sums[1], NT, highest)
    half = TASKS // 2
    value = jnp.concatenate(
        [
            task_total[:half],
            task_total[half:],
            jnp.where(iota((half, FEAT), 0) == iota((half, FEAT), 1), length_total, 0.0),
            jnp.zeros((half, LANES - 2 * TASKS - FEAT), f32),
        ],
        axis=1,
    )
    for c in range(grad_ref.shape[0]):
        grad_ref[c] = value


def tail_kernel(parts_ref, length_ref, task_ref):
    total = parts_ref[0]
    for c in range(1, parts_ref.shape[0]):
        total = total + parts_ref[c]
    half = TASKS // 2
    task_ref[0:half, :] = total[:, :TASKS]
    task_ref[half:, :] = total[:, TASKS : 2 * TASKS]
    length_ref[...] = jnp.sum(total[:, 2 * TASKS : 2 * TASKS + FEAT], axis=0)


MIB = 1024 * 1024


def call(body, outs, args, name, smem=0, hbm=0, far_outs=0, scratch=(), flops=0, limit=16):
    if hbm:
        args = args[:-hbm] + [pltpu.with_memory_space_constraint(a, pltpu.HBM) for a in args[-hbm:]]
    if far_outs:
        outs = outs[:-far_outs] + [pltpu.HBM(o.shape, o.dtype) for o in outs[-far_outs:]]
    vm = pl.BlockSpec(memory_space=pltpu.VMEM)
    sm = pl.BlockSpec(memory_space=pltpu.SMEM)
    far = pl.BlockSpec(memory_space=pltpu.HBM)
    return pl.pallas_call(
        body,
        out_shape=outs,
        in_specs=[sm] * smem + [vm] * (len(args) - smem - hbm) + [far] * hbm,
        out_specs=[vm] * (len(outs) - far_outs) + [far] * far_outs,
        scratch_shapes=scratch,
        compiler_params=pltpu.CompilerParams(vmem_limit_bytes=limit * MIB),
        cost_estimate=pl.CostEstimate(flops=flops, bytes_accessed=1 << 20, transcendentals=0),
        name=name,
    )(*args)


def both_sides(cells):
    count = lax.axis_size("pts")
    up = [(i, i + 1) for i in range(count - 1)]
    down = [(i + 1, i) for i in range(count - 1)]
    return lax.ppermute(cells, "pts", up), lax.ppermute(cells, "pts", down)


def from_left(cells):
    count = lax.axis_size("pts")
    return lax.ppermute(cells, "pts", [(i, i + 1) for i in range(count - 1)])


def shards(
    systems, features, task_ids, pattern, aggregate, coarse_inverse, task_cov, lengthscales, noise
):
    count, width = systems.shape
    blocks = width // BS
    coarse = coarse_inverse.shape[1]
    rows = count + coarse
    lanes = lanes_of(coarse)
    assert blocks == REACH
    place = lax.axis_index("pts").astype(jnp.int32)[None]
    probe = lax.axis_index("probe").astype(jnp.int32)[None]
    ranks = lax.axis_size("pts")
    sides = lax.axis_size("probe")

    def shape(*dims, kind=f32):
        return jax.ShapeDtypeStruct(dims, kind)

    jac, pack, extra = call(
        invert_kernel,
        [shape(3, blocks, BS, BS, kind=bf16), shape(SYS + count, width), shape(TASKS + FEAT, width)],
        [place, probe, features, task_ids, aggregate, systems, task_cov, coarse_inverse, pattern, lengthscales, noise],
        "invert",
        smem=2,
        hbm=9,
        scratch=[
            pltpu.VMEM((blocks, BS, BS), f32),
            pltpu.VMEM(features.shape, f32),
            pltpu.VMEM(task_ids.shape, jnp.int32),
            pltpu.VMEM(aggregate.shape, jnp.int32),
            pltpu.VMEM(systems.shape, f32),
            pltpu.VMEM(task_cov.shape, f32),
            pltpu.VMEM(coarse_inverse.shape, f32),
            pltpu.SMEM(pattern.shape, jnp.int32),
            pltpu.SMEM(lengthscales.shape, f32),
            pltpu.SMEM(noise.shape, f32),
            pltpu.SemaphoreType.DMA((9,)),
        ],
        flops=10**10,
    )
    pack_l, pack_r = both_sides(pack)

    def build(places, deep, cells, name):
        return call(
            functools.partial(build_kernel, places=places, sides=len(cells)),
            [
                shape(blocks, deep, BS, kind=bf16),
                shape(blocks, deep, BS, kind=bf16),
                shape(blocks, deep, BS),
            ],
            cells + [pack, extra],
            name,
            flops=10**9,
        )

    own_hi, own_lo, own_sim = build(own_places, width, [pack], "build_own")
    halo_hi, halo_lo, halo_sim = build(
        halo_places, BAND - width, [pack_l, pack_r], "build_halo"
    )
    kernel = [own_hi, own_lo, halo_hi, halo_lo]
    v0, d1 = call(
        first_kernel,
        [shape(rows, width), shape(rows, width)],
        [pack, pack_l, pack_r, extra] + kernel + [jac],
        "first",
        flops=10**9,
    )
    d1_l, d1_r = both_sides(d1)
    (early,) = call(
        early_moments_kernel, [shape(rows, lanes)], [pack, systems, d1, v0], "early", flops=10**9
    )
    v1, cargo = call(
        second_kernel,
        [shape(rows, width), shape(rows + count, width)],
        [extra, d1, d1_l, d1_r, early, systems] + kernel + [jac],
        "second",
        flops=10**9,
    )
    cargo_l = from_left(cargo)
    (late,) = call(
        functools.partial(late_moments_kernel, count=count),
        [shape(rows, lanes)],
        [early, d1, cargo, v1],
        "late",
        flops=10**9,
    )
    (gram,) = call(
        functools.partial(third_kernel, count=count, held=coarse_inverse.shape[0]),
        [shape(ranks, rows, lanes)],
        [extra, late, cargo, cargo_l] + kernel,
        "third",
        flops=10**9,
    )
    gram = lax.all_to_all(gram, "pts", 0, 0, tiled=True)
    cells = [own_hi, own_lo, own_sim, halo_hi, halo_lo, halo_sim]
    answer, grads = call(
        functools.partial(final_kernel, sides=sides * count, points=ranks * width),
        [shape(count, width), shape(ranks * sides, FEAT, LANES)],
        [gram, pack, pack_l, d1, d1_l, cargo, cargo_l] + cells,
        "final",
        flops=10**9,
    )
    grads = lax.all_to_all(grads, ("pts", "probe"), 0, 0, tiled=True)
    lengths, tasks = call(
        tail_kernel, [shape(FEAT), shape(TASKS, TASKS)], [grads], "tail", flops=10**5
    )
    return answer, lengths, tasks


def solution(mesh):
    return jax.shard_map(
        shards,
        mesh=mesh,
        in_specs=(
            P("probe", ("groups", "pts")),
            P(None, ("groups", "pts")),
            P(("groups", "pts")),
            P(("groups", "pts"), None),
            P(("groups", "pts")),
            P(("groups", "pts"), None),
            P("groups", None),
            P("groups"),
            P("groups"),
        ),
        out_specs=(P("probe", ("groups", "pts")), P("groups"), P("groups", None)),
        check_vma=False,
    )
```

```python
import functools

import jax
import jax.numpy as jnp
from jax import lax
from jax.experimental import pallas as pl
from jax.experimental.pallas import tpu as pltpu
from jax.sharding import PartitionSpec as P

BS = 256
REACH = 3
FEAT = 8
TASKS = 16
ITERS = 3
SLOTS = 2 * REACH + 1
BAND = SLOTS * BS
BASE = 32
GROUP = 4
LANES = 128
SYS = 2 * FEAT

highest = lax.Precision.HIGHEST
f32 = jnp.float32
bf16 = jnp.bfloat16
NN = (((1,), (0,)), ((), ()))
NT = (((1,), (1,)), ((), ()))
TN = (((0,), (0,)), ((), ()))


def dot(a, b, dims=NN, precision=None):
    return lax.dot_general(a, b, dims, precision=precision, preferred_element_type=f32)


def iota(shape, dim):
    return lax.broadcasted_iota(jnp.int32, shape, dim)


def split(x, parts):
    out = []
    for _ in range(parts - 1):
        head = x.astype(bf16).astype(f32)
        out.append(head)
        x = x - head
    out.append(x.astype(bf16).astype(f32))
    return out


def column(ref, size):
    rows = iota((size, 1), 0)
    out = jnp.zeros((size, 1), f32)
    for i in range(size):
        out = jnp.where(rows == i, ref[i], out)
    return out


def one_hot(ids, size):
    return (iota((size, ids.shape[1]), 0).astype(f32) == ids).astype(f32)


def noise_row(noise_ref, ids):
    out = jnp.zeros(ids.shape, f32)
    for t in range(TASKS):
        out = jnp.where(ids == float(t), noise_ref[t], out)
    return out


def weight(pat_ref, block, offset):
    if offset != REACH:
        return pat_ref[block, offset].astype(f32)
    total = pat_ref[block, 0]
    for o in range(1, SLOTS):
        total = total + pat_ref[block, o]
    return total.astype(f32)


def near_stack(scaled, table):
    s0, s1, s2 = split(scaled, 3)
    n0, n1, n2 = split(-0.5 * jnp.sum(scaled * scaled, axis=0, keepdims=True), 3)
    rows = iota(scaled.shape, 0)
    norms = jnp.where(rows == 0, n0, jnp.where(rows == 1, n1, jnp.where(rows == 2, n2, 0.0)))
    pad = jnp.zeros((LANES - 7 * FEAT - 3 * TASKS, scaled.shape[1]), f32)
    stack = jnp.concatenate([s0, s0, s1, s1, s0, s2, norms, table, table, table, pad], axis=0)
    return stack.T.astype(bf16)


def own_stack(scaled, picked):
    s0, s1, s2 = split(scaled, 3)
    rows = iota(scaled.shape, 0)
    ones = jnp.where(rows < 3, 1.0, 0.0)
    count = scaled.shape[1]
    tail = LANES - 7 * FEAT - 3 * TASKS
    left = jnp.concatenate(
        [s0, s1, s0, s1, s2, s0, ones, jnp.zeros((3 * TASKS + tail, count), f32)], axis=0
    ).astype(bf16)
    right = jnp.concatenate(
        [jnp.zeros((7 * FEAT, count), f32)] + split(picked, 3) + [jnp.zeros((tail, count), f32)],
        axis=0,
    ).astype(bf16)
    sides = [
        jnp.concatenate([left[:, i : i + BS], right[:, i : i + BS]], axis=1)
        for i in range(0, count, BS)
    ]
    return sides, -0.5 * jnp.sum(scaled * scaled, axis=0, keepdims=True)


def small_inverse(p):
    n = len(p)
    if n == 1:
        return [[pltpu.reciprocal(p[0][0], approx=True)]]
    if n == 2:
        a, b, d = p[0][0], p[0][1], p[1][1]
        r = pltpu.reciprocal(a * d - b * b, approx=True)
        off = -b * r
        return [[d * r, off], [off, a * r]]
    h = n // 2
    ainv = small_inverse([row[:h] for row in p[:h]])
    b = [row[h:] for row in p[:h]]
    t = [[sum(ainv[i][k] * b[k][j] for k in range(h)) for j in range(h)] for i in range(h)]
    s = [[None] * h for _ in range(h)]
    for i in range(h):
        for j in range(i, h):
            s[i][j] = s[j][i] = p[h + i][h + j] - sum(b[k][i] * t[k][j] for k in range(h))
    sinv = small_inverse(s)
    u = [[sum(t[i][k] * sinv[k][j] for k in range(h)) for j in range(h)] for i in range(h)]
    out = [[None] * n for _ in range(n)]
    for i in range(h):
        for j in range(h):
            out[h + i][h + j] = sinv[i][j]
            out[i][h + j] = out[h + j][i] = -u[i][j]
    for i in range(h):
        for j in range(i, h):
            out[i][j] = out[j][i] = ainv[i][j] + sum(u[i][k] * t[j][k] for k in range(h))
    return out


def with_rows(cells, first, rows):
    top = first - first % 8
    part = cells[top : top + 8]
    sub = iota((8, 1), 0)
    for t, row in enumerate(rows):
        part = jnp.where(sub == first - top + t, row, part)
    pieces = [cells[:top], part, cells[top + 8 :]]
    return jnp.concatenate([p for p in pieces if p.shape[0]], axis=0)


def sweep_base(cells):
    lane = iota((BASE, LANES), 1)
    start = lane - lane % BASE
    inner = iota((1, LANES), 1) % BASE

    def columns(first):
        return [
            jnp.take_along_axis(cells, start + (first + t), axis=1, mode="promise_in_bounds")
            for t in range(GROUP)
        ]

    cols = columns(0)
    for first in range(0, BASE, GROUP):
        ahead = columns(first + GROUP) if first + GROUP < BASE else []
        pivots = [[cols[u][first + t : first + t + 1, :] for u in range(GROUP)] for t in range(GROUP)]
        inv = small_inverse(pivots)
        coming = []
        for col in ahead:
            head = [col[first + t : first + t + 1, :] for t in range(GROUP)]
            factor = [sum(inv[t][u] * head[u] for u in range(GROUP)) for t in range(GROUP)]
            for t in range(GROUP):
                col = col - cols[t] * factor[t]
            coming.append(with_rows(col, first, factor))
        rows = [cells[first + t : first + t + 1, :] for t in range(GROUP)]
        group = (inner >= first) & (inner < first + GROUP)
        for t in range(GROUP):
            rows[t] = jnp.where(inner == first + t, -1.0, jnp.where(group, 0.0, rows[t]))
        new = [sum(inv[t][u] * rows[u] for u in range(GROUP)) for t in range(GROUP)]
        cells = jnp.where(group, 0.0, cells)
        for t in range(GROUP):
            cells = cells - cols[t] * new[t]
        cells = with_rows(cells, first, new)
        cols = coming
    return cells


def fetch(pairs, sems):
    copies = [pltpu.make_async_copy(a, b, sems.at[i]) for i, (a, b) in enumerate(pairs)]
    for copy in copies:
        copy.start()
    return copies


def invert_kernel(
    place_ref, probe_ref, feat_hbm, ids_hbm, agg_hbm, sys_hbm, cov_hbm, coarse_hbm, pat_hbm, len_hbm, noise_hbm,
    jac_ref, pack_ref, extra_ref,
    work, feat_ref, ids_ref, agg_ref, sys_ref, cov_ref, coarse_ref, pat_ref, len_ref, noise_ref, sems,
):
    blocks = work.shape[0]
    width = blocks * BS
    pairs = [
        (feat_hbm, feat_ref), (ids_hbm, ids_ref), (agg_hbm, agg_ref), (cov_hbm, cov_ref),
        (pat_hbm, pat_ref), (len_hbm, len_ref), (noise_hbm, noise_ref), (coarse_hbm, coarse_ref),
        (sys_hbm, sys_ref),
    ]
    for copy in fetch(pairs, sems):
        copy.wait()
    scaled = feat_ref[...] / column(len_ref, FEAT)
    ids = ids_ref[...].astype(f32).reshape(1, width)
    which = agg_ref[...].astype(f32).reshape(1, width)
    table = one_hot(ids, TASKS)
    noise = noise_row(noise_ref, ids)
    c0, c1, c2 = split(cov_ref[...], 3)
    tab = table.astype(bf16)
    picked = (dot(c2.astype(bf16), tab) + dot(c1.astype(bf16), tab)) + dot(c0.astype(bf16), tab)
    rows = iota((FEAT, width), 0)
    weights = jnp.zeros((1, width), f32)
    places = iota((1, width), 1)
    for m in range(blocks):
        for o in range(SLOTS):
            weights = jnp.where(places == m * SLOTS + o, weight(pat_ref, m, o), weights)
    pack_ref[0:FEAT, :] = scaled
    pack_ref[FEAT : 2 * FEAT, :] = jnp.where(
        rows == 0,
        ids,
        jnp.where(rows == 1, which, jnp.where(rows == 2, probe_ref[0].astype(f32), 0.0)),
    )
    extra_ref[0:TASKS, :] = picked
    tail = jnp.where(rows == 0, noise, jnp.where(rows == 1, weights, 0.0))
    held = coarse_ref.shape[0]
    inverse = jnp.concatenate(
        [coarse_ref[...], jnp.zeros((held, width - coarse_ref.shape[1]), f32)], axis=1
    )
    tail = jnp.where(rows == 2, place_ref[0].astype(f32), tail)
    for r in range(held):
        tail = jnp.where(rows == 3 + r, inverse[r : r + 1], tail)
    extra_ref[TASKS : TASKS + FEAT, :] = tail
    near = near_stack(scaled, table)
    mates, norm = own_stack(scaled, picked)
    eye = iota((BS, BS), 0) == iota((BS, BS), 1)
    for m in range(blocks):
        at = slice(m * BS, (m + 1) * BS)
        both = dot(near[at], mates[m])
        block = weight(pat_ref, m, REACH) * jnp.exp(both[:, :BS] + norm[:, at]) * both[:, BS:]
        work[m] = block + jnp.where(eye, noise[:, at], 0.0)
    seg = iota((BASE, LANES), 1) // BASE
    wide = iota((BASE, BS), 1)
    deep = iota((BASE, BS), 0)

    def packed(strips, first):
        tile, inside = first // LANES, first % LANES
        cells = jnp.zeros((BASE, LANES), f32)
        for m in range(blocks):
            piece = strips[m][:, tile * LANES : (tile + 1) * LANES]
            shift = (BASE * m - inside) % LANES
            if shift:
                piece = pltpu.roll(piece, shift, axis=1)
            cells = jnp.where(seg == m, piece, cells)
        return cells

    def diagonal(cells):
        parts = [jnp.where(seg == m, cells, 0.0) for m in range(LANES // BASE)]
        return jnp.concatenate(parts, axis=0)

    eye = jnp.where(iota((BASE, LANES), 1) % BASE == iota((BASE, LANES), 0), 1.0, 0.0)
    strips = [work[m, 0:BASE, :] for m in range(blocks)]
    after = [work[m, BASE : 2 * BASE, :] for m in range(blocks)]
    cells = jnp.where(seg < blocks, packed(strips, 0), eye)
    for k in range(BS // BASE):
        first = k * BASE
        inv = -sweep_base(cells)
        if first + BASE < BS:
            half = dot(inv, diagonal(packed(strips, first + BASE)), precision=highest)
            drop = dot(packed(after, first), diagonal(half), precision=highest)
            cells = jnp.where(seg < blocks, packed(after, first + BASE) - drop, eye)
        held = (wide >= first) & (wide < first + BASE)
        minus = jnp.where(wide - first == deep, -1.0, 0.0)
        stack = jnp.concatenate(
            [jnp.where(held, minus, s) for s in strips]
            + [jnp.zeros((LANES - blocks * BASE, BS), f32)],
            axis=0,
        )
        spread = jnp.concatenate([jnp.where(seg == m, inv, 0.0) for m in range(blocks)], axis=0)
        new = dot(spread, stack, precision=highest)
        gone = (iota((1, BS), 1) >= first) & (iota((1, BS), 1) < first + BASE)
        coming, then = [], []
        for m in range(blocks):
            row = new[m * BASE : (m + 1) * BASE, :]
            r0, r1, r2 = split(strips[m], 3)
            p0, p1, p2 = split(row, 3)
            a = jnp.concatenate([r0, r0, r1, r1, r0, r2], axis=0).astype(bf16)
            b = jnp.concatenate([p0, p1, p0, p1, p2, p0], axis=0).astype(bf16)
            value = jnp.where(gone, 0.0, work[m]) - dot(a, b, TN)
            coming.append(value[first + BASE : first + 2 * BASE])
            then.append(value[first + 2 * BASE : first + 3 * BASE])
            work[m] = value
            work[m, first : first + BASE, :] = row
        strips, after = coming, then
    for m in range(blocks):
        inv = -work[m]
        for i, part in enumerate(split(inv, 3)):
            jac_ref[i, m] = part.astype(bf16)
    pack_ref[SYS:, :] = smooth(sys_ref[...], jac_ref)


def own_places(m):
    return [(j, j, REACH + j - m) for j in range(REACH)]


def halo_places(m):
    lefts = [(j - m, j, j - m) for j in range(m, REACH)]
    return lefts + [(REACH - m + j, REACH + j, 2 * REACH - m + j) for j in range(m + 1)]


def build_kernel(*refs, places, sides):
    cells, (own_ref, extra_ref) = refs[:sides], refs[sides : sides + 2]
    hi_ref, lo_ref, sim_ref = refs[sides + 2 :]
    blocks = hi_ref.shape[0]
    near = []
    for ref in cells:
        near.append(near_stack(ref[0:FEAT, :], one_hot(ref[FEAT : FEAT + 1, :], TASKS)))
    mates, norm = own_stack(own_ref[0:FEAT, :], extra_ref[0:TASKS, :])
    weights = extra_ref[TASKS + 1 : TASKS + 2, :]
    for m in range(blocks):
        for row, j, o in places(m):
            part = near[j // REACH][(j % REACH) * BS : (j % REACH + 1) * BS]
            both = dot(part, mates[m])
            place = m * SLOTS + o
            exponent = both[:, :BS] + norm[:, m * BS : (m + 1) * BS]
            similar = weights[:, place : place + 1] * jnp.exp(exponent)
            kernel = similar * both[:, BS:]
            head = kernel.astype(bf16)
            rows = slice(row * BS, (row + 1) * BS)
            if o <= REACH or sides == 1:
                sim_ref[m, rows, :] = similar
            hi_ref[m, rows, :] = head
            lo_ref[m, rows, :] = (kernel - head.astype(f32)).astype(bf16)


def pieces(vectors):
    return jnp.concatenate(split(vectors, 2), axis=0).astype(bf16)


def apply(cells, hi, lo):
    rows = cells.shape[0] // 2
    first = dot(cells, hi)
    return first[:rows] + first[rows:] + dot(cells[:rows], lo)


def operate_own(own, noise, own_hi, own_lo):
    mine = pieces(own)
    out = [apply(mine, own_hi[m], own_lo[m]) for m in range(REACH)]
    return jnp.concatenate(out, axis=1) + noise * own


def operate_left(left, halo_hi, halo_lo):
    cells = pieces(left)
    out = []
    for m in range(REACH):
        part = slice(0, (REACH - m) * BS)
        out.append(apply(cells[:, m * BS :], halo_hi[m, part, :], halo_lo[m, part, :]))
    return jnp.concatenate(out, axis=1)


def operate(own, left, right, noise, own_hi, own_lo, halo_hi, halo_lo):
    lefts, rights = pieces(left), pieces(right)
    out = []
    for m in range(REACH):
        beyond = jnp.concatenate([lefts[:, m * BS :], rights[:, : (m + 1) * BS]], axis=1)
        out.append(apply(beyond, halo_hi[m], halo_lo[m]))
    return operate_own(own, noise, own_hi, own_lo) + jnp.concatenate(out, axis=1)


def smooth(image, jac_ref):
    rows = image.shape[0]
    out = []
    for m in range(jac_ref.shape[1]):
        pieces = jnp.concatenate(split(image[:, m * BS : (m + 1) * BS], 3), axis=0).astype(bf16)
        a = dot(pieces, jac_ref[0, m])
        b = dot(pieces[: 2 * rows], jac_ref[1, m])
        c = dot(pieces[:rows], jac_ref[2, m])
        out.append(a[:rows] + (a[rows : 2 * rows] + b[:rows] + (a[2 * rows :] + b[rows:] + c)))
    return jnp.concatenate(out, axis=1)


def first_kernel(own_ref, left_ref, right_ref, extra_ref, *refs):
    kernel, (jac_ref, image_ref, next_ref) = refs[:4], refs[4:]
    count = own_ref.shape[0] - SYS
    coarse = image_ref.shape[0] - count

    def basis(ref):
        z = one_hot(ref[FEAT + 1 : FEAT + 2, :], coarse)
        return jnp.concatenate([ref[SYS:, :], z], axis=0)

    noise = extra_ref[TASKS : TASKS + 1, :]
    image = operate(basis(own_ref), basis(left_ref), basis(right_ref), noise, *kernel)
    image_ref[...] = image
    next_ref[...] = smooth(image, jac_ref)


def second_kernel(extra_ref, vec_ref, left_ref, right_ref, early_ref, sys_ref, *refs):
    kernel, (jac_ref, image_ref, cargo_ref) = refs[:4], refs[4:]
    rows = vec_ref.shape[0]
    noise = extra_ref[TASKS : TASKS + 1, :]
    image = operate(vec_ref[...], left_ref[...], right_ref[...], noise, *kernel)
    image_ref[...] = image
    cargo_ref[0:rows, :] = smooth(image, jac_ref)
    cargo_ref[rows:, :] = sys_ref[...]


def pitch_of(coarse):
    return coarse + 1


def lanes_of(coarse):
    return -(-5 * pitch_of(coarse) // LANES) * LANES


def moment(vectors, images, pairs):
    count = pairs.shape[0]
    table = dot(images, vectors, NT, lax.Precision.HIGH)
    own = jnp.sum(pairs, axis=1, keepdims=True)
    if images.shape[0] > count:
        own = jnp.concatenate([own, jnp.zeros((images.shape[0] - count, 1), f32)], axis=0)
    return jnp.concatenate([table, own], axis=1)


def spread_out(parts, lanes):
    rows, pitch = next(iter(parts.values())).shape
    cells = [parts.get(k, jnp.zeros((rows, pitch), f32)) for k in range(5)]
    if lanes > 5 * pitch:
        cells.append(jnp.zeros((rows, lanes - 5 * pitch), f32))
    return jnp.concatenate(cells, axis=1)


def folded(low, high):
    order = low.shape[0]
    row, col = iota((order, order), 0), iota((order, order), 1)
    diagonal = jnp.sum(jnp.where(row == col, high, 0.0), axis=1, keepdims=True)
    return jnp.concatenate([jnp.where(row >= col, low, high), diagonal], axis=1)


def unfolded(cells):
    order = cells.shape[0]
    row, col = iota((order, order), 0), iota((order, order), 1)
    square = cells[:, :order]
    turned = dot(square, jnp.where(row == col, 1.0, 0.0), TN, highest)
    low = jnp.where(row >= col, square, turned)
    high = jnp.where(row < col, square, jnp.where(row > col, turned, cells[:, order:]))
    return low, high


def early_moments_kernel(own_ref, sys_ref, d1_ref, v0_ref, out_ref):
    count = own_ref.shape[0] - SYS
    coarse = d1_ref.shape[0] - count
    lanes = out_ref.shape[1]
    pitch = pitch_of(coarse)
    systems = sys_ref[...]
    pre = own_ref[SYS:, :]
    z = one_hot(own_ref[FEAT + 1 : FEAT + 2, :], coarse)
    d1, v0 = d1_ref[...], v0_ref[...]
    m0 = moment(z, v0, pre * v0[:count])
    m1 = moment(d1[count:], v0, d1[:count] * v0[:count])
    out_ref[0:count, :] = spread_out({0: m0[:count], 1: m1[:count]}, lanes)
    start = moment(z, systems, systems * pre)
    if coarse > count:
        start = jnp.concatenate([start, jnp.zeros((coarse - count, pitch), f32)], axis=0)
    fold = folded(m0[count:, :coarse], m1[count:, :coarse])
    out_ref[count:, :] = spread_out({0: fold, 3: start}, lanes)


def late_moments_kernel(before_ref, d1_ref, cargo_ref, v1_ref, out_ref, *, count):
    lanes = out_ref.shape[1]
    d1, d2, v1 = d1_ref[...], cargo_ref[0 : d1_ref.shape[0], :], v1_ref[...]
    coarse = d1.shape[0] - count
    m2 = moment(d1[count:], v1, d1[:count] * v1[:count])
    m3 = moment(d2[count:], v1, d2[:count] * v1[:count])
    out_ref[0:count, :] = before_ref[0:count, :] + spread_out({2: m2[:count], 3: m3[:count]}, lanes)
    fold = folded(m2[count:, :coarse], m3[count:, :coarse])
    out_ref[count:, :] = before_ref[count:, :] + spread_out({1: fold}, lanes)


def third_kernel(
    extra_ref, before_ref, cargo_ref, left_ref, *refs, count, held
):
    kernel, out_ref = refs[:4], refs[4]
    rows = cargo_ref.shape[0] - count
    coarse = rows - count
    lanes = out_ref.shape[2]
    pitch = pitch_of(coarse)
    d2 = cargo_ref[0:rows, :]
    noise = extra_ref[TASKS : TASKS + 1, :]
    inner = operate_own(d2, noise, *kernel[:2])
    cross = operate_left(left_ref[0:rows, :], *kernel[2:])
    m4 = moment(d2[count:], inner + cross, d2[:count] * (inner + 2.0 * cross)[:count])
    mirror = dot(d2, cross[count:], NT, lax.Precision.HIGH)
    m4 = m4 + jnp.concatenate([mirror, jnp.zeros((rows, 1), f32)], axis=1)
    row = iota((coarse, 1), 0).astype(f32)
    start = extra_ref[TASKS + 2 : TASKS + 3, 0:1] * held
    inverse = jnp.zeros((coarse, pitch), f32)
    for r in range(held):
        line = extra_ref[TASKS + 3 + r : TASKS + 4 + r, 0:pitch]
        inverse = jnp.where(row == start + r, line, inverse)
    top = before_ref[0:count, :] + spread_out({4: m4[:count]}, lanes)
    bottom = before_ref[count:, :] + spread_out({2: m4[count:], 4: inverse}, lanes)
    for c in range(out_ref.shape[0]):
        out_ref[c, 0:count, :] = top
        out_ref[c, count:, :] = bottom


def final_kernel(
    gram_ref, own_ref, left_ref, d1_ref, d1l_ref, cargo_ref, cargol_ref, *refs, sides, points,
):
    kernel_refs, (sol_ref, grad_ref) = refs[:6], refs[6:]
    width = own_ref.shape[1]
    count = own_ref.shape[0] - SYS
    rows = d1_ref.shape[0]
    coarse = rows - count
    pitch = pitch_of(coarse)
    wide = -(-3 * pitch // LANES) * LANES
    blocks = width // BS
    gram = gram_ref[0]
    for c in range(1, gram_ref.shape[0]):
        gram = gram + gram_ref[c]
    bottom = gram[count:]
    gram = jnp.concatenate([gram[:count], jnp.zeros((count, wide), f32)], axis=1)
    squares = list(unfolded(bottom[:, :pitch])) + list(unfolded(bottom[:, pitch : 2 * pitch]))
    squares.append(bottom[:, 2 * pitch : 2 * pitch + coarse])
    lane = iota((1, wide), 1)
    slot, inside = lane // pitch, lane % pitch
    live = lane < 3 * pitch
    is_vec = live & (inside < coarse)
    is_one = live & (inside == coarse)

    def shifted(j):
        return jnp.where(live, gram[:, j * pitch : j * pitch + wide], 0.0)

    own = [shifted(j) for j in range(3)]
    gap = jnp.zeros((coarse, 1), f32)
    rest = jnp.zeros((coarse, wide - 3 * pitch), f32)
    hankel = []
    for i in range(3):
        line = [squares[i], gap, squares[i + 1], gap, squares[i + 2], gap]
        hankel.append(jnp.concatenate(line + ([rest] if wide > 3 * pitch else []), axis=1))
        hankel.append(jnp.zeros((1, wide), f32))
    if wide > 3 * pitch:
        hankel.append(jnp.zeros((wide - 3 * pitch, wide), f32))
    hankel = jnp.concatenate(hankel, axis=0)
    block0 = lane < pitch
    inverse = bottom[:, 4 * pitch : 4 * pitch + coarse]
    inverse = jnp.concatenate([inverse, jnp.zeros((coarse, wide - coarse), f32)], axis=1)
    inverse = jnp.concatenate([inverse, jnp.zeros((wide - coarse, wide), f32)], axis=0)
    start = bottom[:count, 3 * pitch : 4 * pitch]
    start = jnp.concatenate([start, jnp.zeros((count, wide - pitch), f32)], axis=1)
    against = jnp.where(
        block0, start, jnp.where(live, pltpu.roll(jnp.where(live, own[0], 0.0), pitch, axis=1), 0.0)
    )

    def total(x):
        return jnp.sum(x, axis=1, keepdims=True)

    def scalars(u, i):
        return total(jnp.where(lane == i * pitch + coarse, u, 0.0))

    def metric(u):
        out = dot(jnp.where(is_vec, u, 0.0), hankel, precision=highest)
        for j in range(3):
            out = out + scalars(u, j) * own[j]
        out = jnp.where(is_vec, out, 0.0)
        for i in range(3):
            out = jnp.where(lane == i * pitch + coarse, total(u * own[i]), out)
        return out

    def corrected(w):
        return dot(jnp.where(lane < coarse, w, 0.0), inverse, precision=highest)

    pre = corrected(against) + jnp.where(lane == coarse, 1.0, 0.0)
    direction = pre
    gamma = total(pre * against)
    answer = jnp.zeros_like(pre)
    image_sum = jnp.zeros_like(pre)
    for step in range(ITERS):
        image = metric(direction)
        alpha = gamma / total(direction * image)
        answer = answer + alpha * direction
        if step + 1 < ITERS:
            image_sum = image_sum + alpha * image
            moved_on = jnp.where(live & (slot > 0), pltpu.roll(direction, pitch, axis=1), 0.0)
            pre = pre - alpha * (moved_on + corrected(image))
            gamma_new = total(pre * (against - image_sum))
            direction = pre + (gamma_new / gamma) * direction
            gamma = gamma_new

    pack = jnp.concatenate([left_ref[...], own_ref[...]], axis=1)
    z = one_hot(pack[FEAT + 1 : FEAT + 2], coarse)
    q0 = pack[SYS:]
    d1 = jnp.concatenate([d1l_ref[...], d1_ref[...]], axis=1)
    cargo = jnp.concatenate([cargol_ref[...], cargo_ref[...]], axis=1)
    d2 = cargo[:rows]
    span = q0.shape[1]
    step = -(-coarse // FEAT) * FEAT
    deep = -(-3 * step // LANES) * LANES
    parts, basis = [], []
    for i, rest in enumerate((z, d1[count:], d2[count:])):
        parts.append(answer[:, i * pitch : i * pitch + coarse])
        basis.append(rest)
        if step > coarse:
            parts.append(jnp.zeros((count, step - coarse), f32))
            basis.append(jnp.zeros((step - coarse, span), f32))
    if deep > 3 * step:
        parts.append(jnp.zeros((count, deep - 3 * step), f32))
        basis.append(jnp.zeros((deep - 3 * step, span), f32))
    x = dot(
        jnp.concatenate(parts, axis=1), jnp.concatenate(basis, axis=0), precision=highest
    )
    x = x + scalars(answer, 0) * q0 + scalars(answer, 1) * d1[:count]
    x = x + scalars(answer, 2) * d2[:count]
    mine = slice(width, 2 * width)
    sol_ref[...] = x[:, mine]

    probe = own_ref[FEAT + 2 : FEAT + 3, 0:1]
    line = iota((count, 1), 0).astype(f32) + probe * count
    right = jnp.where(line == 0, x, cargo[rows:])
    coef = jnp.where(line == 0, 0.5 / points, -0.5 / (sides - 1) / points)
    r0, r1 = split(right, 2)
    w0, w1 = split(x * coef, 2)
    rest = jnp.zeros((LANES - 6 * count, span), f32)
    near = jnp.concatenate([w0, w1, w0, r0, r1, r0, rest], axis=0).T.astype(bf16)
    none = jnp.zeros((3 * count, width), f32)
    rest = rest[:, mine]
    ahead = jnp.concatenate([r0, r0, r1], axis=0)[:, mine]
    back = jnp.concatenate([w0, w0, w1], axis=0)[:, mine]
    mates = [
        jnp.concatenate([ahead, none, rest], axis=0).astype(bf16),
        jnp.concatenate([none, back, rest], axis=0).astype(bf16),
    ]
    scaled = pack[0:FEAT]
    table = one_hot(pack[FEAT : FEAT + 1], TASKS)
    ones = jnp.ones((8, span), f32)
    terms = jnp.concatenate([scaled, ones, scaled * scaled], axis=0)
    t0, t1 = split(terms, 2)
    pad8 = jnp.zeros((8, span), f32)
    both = jnp.concatenate([t0, pad8, t1, pad8], axis=0).astype(bf16)
    heads = jnp.concatenate([t0, pad8], axis=0).astype(bf16)
    tables = table.astype(bf16)
    high = 32
    length_total = jnp.zeros((FEAT, 1), f32)
    task_total = jnp.zeros((TASKS, TASKS), f32)
    for m in range(blocks):
        at = slice(m * BS, (m + 1) * BS)
        sums = jnp.zeros((high, BS), f32)
        held_sums = [jnp.zeros((TASKS, BS), f32) for _ in mates]
        places = [(1, row, j + REACH) for row, j, _ in own_places(m)]
        places += [(2, row, j) for row, j, _ in halo_places(m) if j < REACH]
        for orders, row, block in places:
            hi_ref, lo_ref, sim_ref = kernel_refs[3 * orders - 3 : 3 * orders]
            j = slice(block * BS, (block + 1) * BS)
            rows_at = slice(row * BS, (row + 1) * BS)
            outers = [dot(near[j], mate[:, at]) for mate in mates[:orders]]
            kernel = hi_ref[m, rows_at, :].astype(f32) + lo_ref[m, rows_at, :].astype(f32)
            similar = sim_ref[m, rows_at, :]
            energy = sum(outers) * kernel
            e0, e1 = (part.astype(bf16) for part in split(energy, 2))
            first = dot(both[:, j], e0)
            sums = sums + first[:high] + first[high:] + dot(heads[:, j], e1)
            for k in range(orders):
                h0, h1 = (part.astype(bf16) for part in split(outers[k] * similar, 2))
                held_sums[k] = held_sums[k] + dot(tables[:, j], h0) + dot(tables[:, j], h1)
        mid = slice(width + m * BS, width + (m + 1) * BS)
        left = scaled[:, mid]
        value = left * left * sums[FEAT : FEAT + 1] + sums[2 * FEAT : 3 * FEAT]
        value = value - 2.0 * left * sums[:FEAT]
        length_total = length_total + jnp.sum(value, axis=1, keepdims=True)
        task_total = task_total + dot(held_sums[0], table[:, mid], NT, highest)
        task_total = task_total + dot(table[:, mid], held_sums[1], NT, highest)
    half = TASKS // 2
    value = jnp.concatenate(
        [
            task_total[:half],
            task_total[half:],
            jnp.where(iota((half, FEAT), 0) == iota((half, FEAT), 1), length_total, 0.0),
            jnp.zeros((half, LANES - 2 * TASKS - FEAT), f32),
        ],
        axis=1,
    )
    for c in range(grad_ref.shape[0]):
        grad_ref[c] = value


def tail_kernel(parts_ref, length_ref, task_ref):
    total = parts_ref[0]
    for c in range(1, parts_ref.shape[0]):
        total = total + parts_ref[c]
    half = TASKS // 2
    task_ref[0:half, :] = total[:, :TASKS]
    task_ref[half:, :] = total[:, TASKS : 2 * TASKS]
    length_ref[...] = jnp.sum(total[:, 2 * TASKS : 2 * TASKS + FEAT], axis=0)


MIB = 1024 * 1024


def call(body, outs, args, name, smem=0, hbm=0, far_outs=0, scratch=(), flops=0, limit=16):
    if hbm:
        args = args[:-hbm] + [pltpu.with_memory_space_constraint(a, pltpu.HBM) for a in args[-hbm:]]
    if far_outs:
        outs = outs[:-far_outs] + [pltpu.HBM(o.shape, o.dtype) for o in outs[-far_outs:]]
    vm = pl.BlockSpec(memory_space=pltpu.VMEM)
    sm = pl.BlockSpec(memory_space=pltpu.SMEM)
    far = pl.BlockSpec(memory_space=pltpu.HBM)
    return pl.pallas_call(
        body,
        out_shape=outs,
        in_specs=[sm] * smem + [vm] * (len(args) - smem - hbm) + [far] * hbm,
        out_specs=[vm] * (len(outs) - far_outs) + [far] * far_outs,
        scratch_shapes=scratch,
        compiler_params=pltpu.CompilerParams(vmem_limit_bytes=limit * MIB),
        cost_estimate=pl.CostEstimate(flops=flops, bytes_accessed=1 << 20, transcendentals=0),
        name=name,
    )(*args)


def both_sides(cells):
    count = lax.axis_size("pts")
    up = [(i, i + 1) for i in range(count - 1)]
    down = [(i + 1, i) for i in range(count - 1)]
    return lax.ppermute(cells, "pts", up), lax.ppermute(cells, "pts", down)


def from_left(cells):
    count = lax.axis_size("pts")
    return lax.ppermute(cells, "pts", [(i, i + 1) for i in range(count - 1)])


def shards(
    systems, features, task_ids, pattern, aggregate, coarse_inverse, task_cov, lengthscales, noise
):
    count, width = systems.shape
    blocks = width // BS
    coarse = coarse_inverse.shape[1]
    rows = count + coarse
    lanes = lanes_of(coarse)
    assert blocks == REACH
    place = lax.axis_index("pts").astype(jnp.int32)[None]
    probe = lax.axis_index("probe").astype(jnp.int32)[None]
    ranks = lax.axis_size("pts")
    sides = lax.axis_size("probe")

    def shape(*dims, kind=f32):
        return jax.ShapeDtypeStruct(dims, kind)

    jac, pack, extra = call(
        invert_kernel,
        [shape(3, blocks, BS, BS, kind=bf16), shape(SYS + count, width), shape(TASKS + FEAT, width)],
        [place, probe, features, task_ids, aggregate, systems, task_cov, coarse_inverse, pattern, lengthscales, noise],
        "invert",
        smem=2,
        hbm=9,
        scratch=[
            pltpu.VMEM((blocks, BS, BS), f32),
            pltpu.VMEM(features.shape, f32),
            pltpu.VMEM(task_ids.shape, jnp.int32),
            pltpu.VMEM(aggregate.shape, jnp.int32),
            pltpu.VMEM(systems.shape, f32),
            pltpu.VMEM(task_cov.shape, f32),
            pltpu.VMEM(coarse_inverse.shape, f32),
            pltpu.SMEM(pattern.shape, jnp.int32),
            pltpu.SMEM(lengthscales.shape, f32),
            pltpu.SMEM(noise.shape, f32),
            pltpu.SemaphoreType.DMA((9,)),
        ],
        flops=10**10,
    )
    pack_l, pack_r = both_sides(pack)

    def build(places, deep, cells, name):
        return call(
            functools.partial(build_kernel, places=places, sides=len(cells)),
            [
                shape(blocks, deep, BS, kind=bf16),
                shape(blocks, deep, BS, kind=bf16),
                shape(blocks, deep, BS),
            ],
            cells + [pack, extra],
            name,
            flops=10**9,
        )

    own_hi, own_lo, own_sim = build(own_places, width, [pack], "build_own")
    halo_hi, halo_lo, halo_sim = build(
        halo_places, BAND - width, [pack_l, pack_r], "build_halo"
    )
    kernel = [own_hi, own_lo, halo_hi, halo_lo]
    v0, d1 = call(
        first_kernel,
        [shape(rows, width), shape(rows, width)],
        [pack, pack_l, pack_r, extra] + kernel + [jac],
        "first",
        flops=10**9,
    )
    d1_l, d1_r = both_sides(d1)
    (early,) = call(
        early_moments_kernel, [shape(rows, lanes)], [pack, systems, d1, v0], "early", flops=10**9
    )
    v1, cargo = call(
        second_kernel,
        [shape(rows, width), shape(rows + count, width)],
        [extra, d1, d1_l, d1_r, early, systems] + kernel + [jac],
        "second",
        flops=10**9,
    )
    cargo_l = from_left(cargo)
    (late,) = call(
        functools.partial(late_moments_kernel, count=count),
        [shape(rows, lanes)],
        [early, d1, cargo, v1],
        "late",
        flops=10**9,
    )
    (gram,) = call(
        functools.partial(third_kernel, count=count, held=coarse_inverse.shape[0]),
        [shape(ranks, rows, lanes)],
        [extra, late, cargo, cargo_l] + kernel,
        "third",
        flops=10**9,
    )
    gram = lax.all_to_all(gram, "pts", 0, 0, tiled=True)
    cells = [own_hi, own_lo, own_sim, halo_hi, halo_lo, halo_sim]
    answer, grads = call(
        functools.partial(final_kernel, sides=sides * count, points=ranks * width),
        [shape(count, width), shape(ranks * sides, FEAT, LANES)],
        [gram, pack, pack_l, d1, d1_l, cargo, cargo_l] + cells,
        "final",
        flops=10**9,
    )
    grads = lax.all_to_all(grads, ("pts", "probe"), 0, 0, tiled=True)
    lengths, tasks = call(
        tail_kernel, [shape(FEAT), shape(TASKS, TASKS)], [grads], "tail", flops=10**5
    )
    return answer, lengths, tasks


def solution(mesh):
    return jax.shard_map(
        shards,
        mesh=mesh,
        in_specs=(
            P("probe", ("groups", "pts")),
            P(None, ("groups", "pts")),
            P(("groups", "pts")),
            P(("groups", "pts"), None),
            P(("groups", "pts")),
            P(("groups", "pts"), None),
            P("groups", None),
            P("groups"),
            P("groups"),
        ),
        out_specs=(P("probe", ("groups", "pts")), P("groups"), P("groups", None)),
        check_vma=False,
    )
```

```python
import functools

import jax
import jax.numpy as jnp
from jax import lax
from jax.experimental import pallas as pl
from jax.experimental.pallas import tpu as pltpu
from jax.sharding import PartitionSpec as P

BS = 256
REACH = 3
FEAT = 8
TASKS = 16
ITERS = 3
SLOTS = 2 * REACH + 1
BAND = SLOTS * BS
BASE = 32
GROUP = 4
LANES = 128
SYS = 2 * FEAT

highest = lax.Precision.HIGHEST
f32 = jnp.float32
bf16 = jnp.bfloat16
NN = (((1,), (0,)), ((), ()))
NT = (((1,), (1,)), ((), ()))
TN = (((0,), (0,)), ((), ()))


def dot(a, b, dims=NN, precision=None):
    return lax.dot_general(a, b, dims, precision=precision, preferred_element_type=f32)


def iota(shape, dim):
    return lax.broadcasted_iota(jnp.int32, shape, dim)


def split(x, parts):
    out = []
    for _ in range(parts - 1):
        head = x.astype(bf16).astype(f32)
        out.append(head)
        x = x - head
    out.append(x.astype(bf16).astype(f32))
    return out


def column(ref, size):
    rows = iota((size, 1), 0)
    out = jnp.zeros((size, 1), f32)
    for i in range(size):
        out = jnp.where(rows == i, ref[i], out)
    return out


def one_hot(ids, size):
    return (iota((size, ids.shape[1]), 0).astype(f32) == ids).astype(f32)


def noise_row(noise_ref, ids):
    out = jnp.zeros(ids.shape, f32)
    for t in range(TASKS):
        out = jnp.where(ids == float(t), noise_ref[t], out)
    return out


def weight(pat_ref, block, offset):
    if offset != REACH:
        return pat_ref[block, offset].astype(f32)
    total = pat_ref[block, 0]
    for o in range(1, SLOTS):
        total = total + pat_ref[block, o]
    return total.astype(f32)


def near_stack(scaled, table):
    s0, s1, s2 = split(scaled, 3)
    n0, n1, n2 = split(-0.5 * jnp.sum(scaled * scaled, axis=0, keepdims=True), 3)
    rows = iota(scaled.shape, 0)
    norms = jnp.where(rows == 0, n0, jnp.where(rows == 1, n1, jnp.where(rows == 2, n2, 0.0)))
    pad = jnp.zeros((LANES - 7 * FEAT - 3 * TASKS, scaled.shape[1]), f32)
    stack = jnp.concatenate([s0, s0, s1, s1, s0, s2, norms, table, table, table, pad], axis=0)
    return stack.T.astype(bf16)


def own_stack(scaled, picked):
    s0, s1, s2 = split(scaled, 3)
    rows = iota(scaled.shape, 0)
    ones = jnp.where(rows < 3, 1.0, 0.0)
    count = scaled.shape[1]
    tail = LANES - 7 * FEAT - 3 * TASKS
    left = jnp.concatenate(
        [s0, s1, s0, s1, s2, s0, ones, jnp.zeros((3 * TASKS + tail, count), f32)], axis=0
    ).astype(bf16)
    right = jnp.concatenate(
        [jnp.zeros((7 * FEAT, count), f32)] + split(picked, 3) + [jnp.zeros((tail, count), f32)],
        axis=0,
    ).astype(bf16)
    sides = [
        jnp.concatenate([left[:, i : i + BS], right[:, i : i + BS]], axis=1)
        for i in range(0, count, BS)
    ]
    return sides, -0.5 * jnp.sum(scaled * scaled, axis=0, keepdims=True)


def small_inverse(p):
    n = len(p)
    if n == 1:
        return [[pltpu.reciprocal(p[0][0], approx=True)]]
    if n == 2:
        a, b, d = p[0][0], p[0][1], p[1][1]
        r = pltpu.reciprocal(a * d - b * b, approx=True)
        off = -b * r
        return [[d * r, off], [off, a * r]]
    h = n // 2
    ainv = small_inverse([row[:h] for row in p[:h]])
    b = [row[h:] for row in p[:h]]
    t = [[sum(ainv[i][k] * b[k][j] for k in range(h)) for j in range(h)] for i in range(h)]
    s = [[None] * h for _ in range(h)]
    for i in range(h):
        for j in range(i, h):
            s[i][j] = s[j][i] = p[h + i][h + j] - sum(b[k][i] * t[k][j] for k in range(h))
    sinv = small_inverse(s)
    u = [[sum(t[i][k] * sinv[k][j] for k in range(h)) for j in range(h)] for i in range(h)]
    out = [[None] * n for _ in range(n)]
    for i in range(h):
        for j in range(h):
            out[h + i][h + j] = sinv[i][j]
            out[i][h + j] = out[h + j][i] = -u[i][j]
    for i in range(h):
        for j in range(i, h):
            out[i][j] = out[j][i] = ainv[i][j] + sum(u[i][k] * t[j][k] for k in range(h))
    return out


def with_rows(cells, first, rows):
    top = first - first % 8
    part = cells[top : top + 8]
    sub = iota((8, 1), 0)
    for t, row in enumerate(rows):
        part = jnp.where(sub == first - top + t, row, part)
    pieces = [cells[:top], part, cells[top + 8 :]]
    return jnp.concatenate([p for p in pieces if p.shape[0]], axis=0)


def sweep_base(cells, beside):
    lane = iota((BASE, LANES), 1)
    start = lane - lane % BASE
    inner = iota((1, LANES), 1) % BASE

    def columns(first):
        return [
            jnp.take_along_axis(cells, start + (first + t), axis=1, mode="promise_in_bounds")
            for t in range(GROUP)
        ]

    cols = columns(0)
    for first in range(0, BASE, GROUP):
        ahead = columns(first + GROUP) if first + GROUP < BASE else []
        pivots = [[cols[u][first + t : first + t + 1, :] for u in range(GROUP)] for t in range(GROUP)]
        inv = small_inverse(pivots)
        coming = []
        for col in ahead:
            head = [col[first + t : first + t + 1, :] for t in range(GROUP)]
            factor = [sum(inv[t][u] * head[u] for u in range(GROUP)) for t in range(GROUP)]
            for t in range(GROUP):
                col = col - cols[t] * factor[t]
            coming.append(with_rows(col, first, factor))
        rows = [cells[first + t : first + t + 1, :] for t in range(GROUP)]
        group = (inner >= first) & (inner < first + GROUP)
        for t in range(GROUP):
            rows[t] = jnp.where(inner == first + t, -1.0, jnp.where(group, 0.0, rows[t]))
        new = [sum(inv[t][u] * rows[u] for u in range(GROUP)) for t in range(GROUP)]
        cells = jnp.where(group, 0.0, cells)
        for t in range(GROUP):
            cells = cells - cols[t] * new[t]
        cells = with_rows(cells, first, new)
        cols = coming
        if beside:
            beside.pop(0)()
    assert not beside
    return cells


def fetch(pairs, sems):
    copies = [pltpu.make_async_copy(a, b, sems.at[i]) for i, (a, b) in enumerate(pairs)]
    for copy in copies:
        copy.start()
    return copies


def invert_kernel(
    place_ref, probe_ref, feat_hbm, ids_hbm, agg_hbm, sys_hbm, cov_hbm, coarse_hbm, pat_hbm, len_hbm, noise_hbm,
    jac_ref, pack_ref, extra_ref,
    work, feat_ref, ids_ref, agg_ref, sys_ref, cov_ref, coarse_ref, pat_ref, len_ref, noise_ref, sems,
):
    blocks = work.shape[0]
    width = blocks * BS
    pairs = [
        (feat_hbm, feat_ref), (ids_hbm, ids_ref), (agg_hbm, agg_ref), (cov_hbm, cov_ref),
        (pat_hbm, pat_ref), (len_hbm, len_ref), (noise_hbm, noise_ref), (coarse_hbm, coarse_ref),
        (sys_hbm, sys_ref),
    ]
    for copy in fetch(pairs, sems):
        copy.wait()
    scaled = feat_ref[...] / column(len_ref, FEAT)
    ids = ids_ref[...].astype(f32).reshape(1, width)
    which = agg_ref[...].astype(f32).reshape(1, width)
    table = one_hot(ids, TASKS)
    noise = noise_row(noise_ref, ids)
    c0, c1, c2 = split(cov_ref[...], 3)
    tab = table.astype(bf16)
    picked = (dot(c2.astype(bf16), tab) + dot(c1.astype(bf16), tab)) + dot(c0.astype(bf16), tab)
    rows = iota((FEAT, width), 0)
    weights = jnp.zeros((1, width), f32)
    places = iota((1, width), 1)
    for m in range(blocks):
        for o in range(SLOTS):
            weights = jnp.where(places == m * SLOTS + o, weight(pat_ref, m, o), weights)
    pack_ref[0:FEAT, :] = scaled
    pack_ref[FEAT : 2 * FEAT, :] = jnp.where(
        rows == 0,
        ids,
        jnp.where(rows == 1, which, jnp.where(rows == 2, probe_ref[0].astype(f32), 0.0)),
    )
    extra_ref[0:TASKS, :] = picked
    tail = jnp.where(rows == 0, noise, jnp.where(rows == 1, weights, 0.0))
    held = coarse_ref.shape[0]
    inverse = jnp.concatenate(
        [coarse_ref[...], jnp.zeros((held, width - coarse_ref.shape[1]), f32)], axis=1
    )
    tail = jnp.where(rows == 2, place_ref[0].astype(f32), tail)
    for r in range(held):
        tail = jnp.where(rows == 3 + r, inverse[r : r + 1], tail)
    extra_ref[TASKS : TASKS + FEAT, :] = tail
    near = near_stack(scaled, table)
    mates, norm = own_stack(scaled, picked)
    eye = iota((BS, BS), 0) == iota((BS, BS), 1)
    for m in range(blocks):
        at = slice(m * BS, (m + 1) * BS)
        both = dot(near[at], mates[m])
        block = weight(pat_ref, m, REACH) * jnp.exp(both[:, :BS] + norm[:, at]) * both[:, BS:]
        work[m] = block + jnp.where(eye, noise[:, at], 0.0)
    seg = iota((BASE, LANES), 1) // BASE
    wide = iota((BASE, BS), 1)
    deep = iota((BASE, BS), 0)

    def packed(strips, first):
        tile, inside = first // LANES, first % LANES
        cells = jnp.zeros((BASE, LANES), f32)
        for m in range(blocks):
            piece = strips[m][:, tile * LANES : (tile + 1) * LANES]
            shift = (BASE * m - inside) % LANES
            if shift:
                piece = pltpu.roll(piece, shift, axis=1)
            cells = jnp.where(seg == m, piece, cells)
        return cells

    def diagonal(cells):
        parts = [jnp.where(seg == m, cells, 0.0) for m in range(LANES // BASE)]
        return jnp.concatenate(parts, axis=0)

    eye = jnp.where(iota((BASE, LANES), 1) % BASE == iota((BASE, LANES), 0), 1.0, 0.0)

    def updates(first, inv, strips):
        state = {}

        def product():
            held = (wide >= first) & (wide < first + BASE)
            minus = jnp.where(wide - first == deep, -1.0, 0.0)
            stack = jnp.concatenate(
                [jnp.where(held, minus, s) for s in strips]
                + [jnp.zeros((LANES - blocks * BASE, BS), f32)],
                axis=0,
            )
            spread = diagonal(inv)[: blocks * BASE]
            new = dot(spread, stack, precision=highest)
            for m in range(blocks):
                state[m] = new[m * BASE : (m + 1) * BASE, :]

        def rows_of(m, low, high):
            def piece():
                r0, r1, r2 = split(strips[m][:, low:high], 3)
                p0, p1, p2 = split(state[m], 3)
                a = jnp.concatenate([r0, r0, r1, r1, r0, r2], axis=0).astype(bf16)
                b = jnp.concatenate([p0, p1, p0, p1, p2, p0], axis=0).astype(bf16)
                gone = (iota((1, BS), 1) >= first) & (iota((1, BS), 1) < first + BASE)
                work[m, low:high, :] = jnp.where(gone, 0.0, work[m, low:high, :]) - dot(a, b, TN)
                if low <= first < high:
                    work[m, first : first + BASE, :] = state[m]

            return piece

        half = BS // 2
        return [product] + [
            rows_of(m, low, low + half) for m in range(blocks) for low in range(0, BS, half)
        ]

    def strips_at(first):
        return [work[m, first : first + BASE, :] for m in range(blocks)]

    cells = jnp.where(seg < blocks, packed(strips_at(0), 0), eye)
    pending = []
    for first in range(0, BS, BASE):
        inv = -sweep_base(cells, pending)
        strips = strips_at(first)
        if first + BASE < BS:
            after = strips_at(first + BASE)
            half = dot(inv, diagonal(packed(strips, first + BASE)), precision=highest)
            drop = dot(packed(after, first), diagonal(half), precision=highest)
            cells = jnp.where(seg < blocks, packed(after, first + BASE) - drop, eye)
        pending = updates(first, inv, strips)
    for piece in pending:
        piece()
    for m in range(blocks):
        inv = -work[m]
        for i, part in enumerate(split(inv, 3)):
            jac_ref[i, m] = part.astype(bf16)
    pack_ref[SYS:, :] = smooth(sys_ref[...], jac_ref)


def own_places(m):
    return [(j, j, REACH + j - m) for j in range(REACH)]


def halo_places(m):
    lefts = [(j - m, j, j - m) for j in range(m, REACH)]
    return lefts + [(REACH - m + j, REACH + j, 2 * REACH - m + j) for j in range(m + 1)]


def build_kernel(*refs, places, sides):
    cells, (own_ref, extra_ref) = refs[:sides], refs[sides : sides + 2]
    hi_ref, lo_ref, sim_ref = refs[sides + 2 :]
    blocks = hi_ref.shape[0]
    near = []
    for ref in cells:
        near.append(near_stack(ref[0:FEAT, :], one_hot(ref[FEAT : FEAT + 1, :], TASKS)))
    mates, norm = own_stack(own_ref[0:FEAT, :], extra_ref[0:TASKS, :])
    weights = extra_ref[TASKS + 1 : TASKS + 2, :]
    for m in range(blocks):
        for row, j, o in places(m):
            part = near[j // REACH][(j % REACH) * BS : (j % REACH + 1) * BS]
            both = dot(part, mates[m])
            place = m * SLOTS + o
            exponent = both[:, :BS] + norm[:, m * BS : (m + 1) * BS]
            similar = weights[:, place : place + 1] * jnp.exp(exponent)
            kernel = similar * both[:, BS:]
            head = kernel.astype(bf16)
            rows = slice(row * BS, (row + 1) * BS)
            if o <= REACH or sides == 1:
                sim_ref[m, rows, :] = similar
            hi_ref[m, rows, :] = head
            lo_ref[m, rows, :] = (kernel - head.astype(f32)).astype(bf16)


def pieces(vectors):
    return jnp.concatenate(split(vectors, 2), axis=0).astype(bf16)


def apply(cells, hi, lo):
    rows = cells.shape[0] // 2
    first = dot(cells, hi)
    return first[:rows] + first[rows:] + dot(cells[:rows], lo)


def operate_own(own, noise, own_hi, own_lo):
    mine = pieces(own)
    out = [apply(mine, own_hi[m], own_lo[m]) for m in range(REACH)]
    return jnp.concatenate(out, axis=1) + noise * own


def operate_left(left, halo_hi, halo_lo):
    cells = pieces(left)
    out = []
    for m in range(REACH):
        part = slice(0, (REACH - m) * BS)
        out.append(apply(cells[:, m * BS :], halo_hi[m, part, :], halo_lo[m, part, :]))
    return jnp.concatenate(out, axis=1)


def operate(own, left, right, noise, own_hi, own_lo, halo_hi, halo_lo):
    lefts, rights = pieces(left), pieces(right)
    out = []
    for m in range(REACH):
        beyond = jnp.concatenate([lefts[:, m * BS :], rights[:, : (m + 1) * BS]], axis=1)
        out.append(apply(beyond, halo_hi[m], halo_lo[m]))
    return operate_own(own, noise, own_hi, own_lo) + jnp.concatenate(out, axis=1)


def smooth(image, jac_ref):
    rows = image.shape[0]
    out = []
    for m in range(jac_ref.shape[1]):
        pieces = jnp.concatenate(split(image[:, m * BS : (m + 1) * BS], 3), axis=0).astype(bf16)
        a = dot(pieces, jac_ref[0, m])
        b = dot(pieces[: 2 * rows], jac_ref[1, m])
        c = dot(pieces[:rows], jac_ref[2, m])
        out.append(a[:rows] + (a[rows : 2 * rows] + b[:rows] + (a[2 * rows :] + b[rows:] + c)))
    return jnp.concatenate(out, axis=1)


def first_kernel(own_ref, left_ref, right_ref, extra_ref, *refs):
    kernel, (jac_ref, image_ref, next_ref) = refs[:4], refs[4:]
    count = own_ref.shape[0] - SYS
    coarse = image_ref.shape[0] - count

    def basis(ref):
        z = one_hot(ref[FEAT + 1 : FEAT + 2, :], coarse)
        return jnp.concatenate([ref[SYS:, :], z], axis=0)

    noise = extra_ref[TASKS : TASKS + 1, :]
    image = operate(basis(own_ref), basis(left_ref), basis(right_ref), noise, *kernel)
    image_ref[...] = image
    next_ref[...] = smooth(image, jac_ref)


def second_kernel(extra_ref, vec_ref, left_ref, right_ref, early_ref, sys_ref, *refs):
    kernel, (jac_ref, image_ref, cargo_ref) = refs[:4], refs[4:]
    rows = vec_ref.shape[0]
    noise = extra_ref[TASKS : TASKS + 1, :]
    image = operate(vec_ref[...], left_ref[...], right_ref[...], noise, *kernel)
    image_ref[...] = image
    cargo_ref[0:rows, :] = smooth(image, jac_ref)
    cargo_ref[rows:, :] = sys_ref[...]


def pitch_of(coarse):
    return coarse + 1


def lanes_of(coarse):
    return -(-5 * pitch_of(coarse) // LANES) * LANES


def moment(vectors, images, pairs):
    count = pairs.shape[0]
    table = dot(images, vectors, NT, lax.Precision.HIGH)
    own = jnp.sum(pairs, axis=1, keepdims=True)
    if images.shape[0] > count:
        own = jnp.concatenate([own, jnp.zeros((images.shape[0] - count, 1), f32)], axis=0)
    return jnp.concatenate([table, own], axis=1)


def spread_out(parts, lanes):
    rows, pitch = next(iter(parts.values())).shape
    cells = [parts.get(k, jnp.zeros((rows, pitch), f32)) for k in range(5)]
    if lanes > 5 * pitch:
        cells.append(jnp.zeros((rows, lanes - 5 * pitch), f32))
    return jnp.concatenate(cells, axis=1)


def folded(low, high):
    order = low.shape[0]
    row, col = iota((order, order), 0), iota((order, order), 1)
    diagonal = jnp.sum(jnp.where(row == col, high, 0.0), axis=1, keepdims=True)
    return jnp.concatenate([jnp.where(row >= col, low, high), diagonal], axis=1)


def unfolded(cells):
    order = cells.shape[0]
    row, col = iota((order, order), 0), iota((order, order), 1)
    square = cells[:, :order]
    turned = dot(square, jnp.where(row == col, 1.0, 0.0), TN, highest)
    low = jnp.where(row >= col, square, turned)
    high = jnp.where(row < col, square, jnp.where(row > col, turned, cells[:, order:]))
    return low, high


def early_moments_kernel(own_ref, sys_ref, d1_ref, v0_ref, out_ref):
    count = own_ref.shape[0] - SYS
    coarse = d1_ref.shape[0] - count
    lanes = out_ref.shape[1]
    pitch = pitch_of(coarse)
    systems = sys_ref[...]
    pre = own_ref[SYS:, :]
    z = one_hot(own_ref[FEAT + 1 : FEAT + 2, :], coarse)
    d1, v0 = d1_ref[...], v0_ref[...]
    m0 = moment(z, v0, pre * v0[:count])
    m1 = moment(d1[count:], v0, d1[:count] * v0[:count])
    out_ref[0:count, :] = spread_out({0: m0[:count], 1: m1[:count]}, lanes)
    start = moment(z, systems, systems * pre)
    if coarse > count:
        start = jnp.concatenate([start, jnp.zeros((coarse - count, pitch), f32)], axis=0)
    fold = folded(m0[count:, :coarse], m1[count:, :coarse])
    out_ref[count:, :] = spread_out({0: fold, 3: start}, lanes)


def late_moments_kernel(before_ref, d1_ref, cargo_ref, v1_ref, out_ref, *, count):
    lanes = out_ref.shape[1]
    d1, d2, v1 = d1_ref[...], cargo_ref[0 : d1_ref.shape[0], :], v1_ref[...]
    coarse = d1.shape[0] - count
    m2 = moment(d1[count:], v1, d1[:count] * v1[:count])
    m3 = moment(d2[count:], v1, d2[:count] * v1[:count])
    out_ref[0:count, :] = before_ref[0:count, :] + spread_out({2: m2[:count], 3: m3[:count]}, lanes)
    fold = folded(m2[count:, :coarse], m3[count:, :coarse])
    out_ref[count:, :] = before_ref[count:, :] + spread_out({1: fold}, lanes)


def third_kernel(
    extra_ref, before_ref, cargo_ref, left_ref, *refs, count, held
):
    kernel, out_ref = refs[:4], refs[4]
    rows = cargo_ref.shape[0] - count
    coarse = rows - count
    lanes = out_ref.shape[2]
    pitch = pitch_of(coarse)
    d2 = cargo_ref[0:rows, :]
    noise = extra_ref[TASKS : TASKS + 1, :]
    inner = operate_own(d2, noise, *kernel[:2])
    cross = operate_left(left_ref[0:rows, :], *kernel[2:])
    m4 = moment(d2[count:], inner + cross, d2[:count] * (inner + 2.0 * cross)[:count])
    mirror = dot(d2, cross[count:], NT, lax.Precision.HIGH)
    m4 = m4 + jnp.concatenate([mirror, jnp.zeros((rows, 1), f32)], axis=1)
    row = iota((coarse, 1), 0).astype(f32)
    start = extra_ref[TASKS + 2 : TASKS + 3, 0:1] * held
    inverse = jnp.zeros((coarse, pitch), f32)
    for r in range(held):
        line = extra_ref[TASKS + 3 + r : TASKS + 4 + r, 0:pitch]
        inverse = jnp.where(row == start + r, line, inverse)
    top = before_ref[0:count, :] + spread_out({4: m4[:count]}, lanes)
    bottom = before_ref[count:, :] + spread_out({2: m4[count:], 4: inverse}, lanes)
    for c in range(out_ref.shape[0]):
        out_ref[c, 0:count, :] = top
        out_ref[c, count:, :] = bottom


def final_kernel(
    gram_ref, own_ref, left_ref, d1_ref, d1l_ref, cargo_ref, cargol_ref, *refs, sides, points,
):
    kernel_refs, (sol_ref, grad_ref) = refs[:6], refs[6:]
    width = own_ref.shape[1]
    count = own_ref.shape[0] - SYS
    rows = d1_ref.shape[0]
    coarse = rows - count
    pitch = pitch_of(coarse)
    wide = -(-3 * pitch // LANES) * LANES
    blocks = width // BS
    gram = gram_ref[0]
    for c in range(1, gram_ref.shape[0]):
        gram = gram + gram_ref[c]
    bottom = gram[count:]
    gram = jnp.concatenate([gram[:count], jnp.zeros((count, wide), f32)], axis=1)
    squares = list(unfolded(bottom[:, :pitch])) + list(unfolded(bottom[:, pitch : 2 * pitch]))
    squares.append(bottom[:, 2 * pitch : 2 * pitch + coarse])
    lane = iota((1, wide), 1)
    slot, inside = lane // pitch, lane % pitch
    live = lane < 3 * pitch
    is_vec = live & (inside < coarse)
    is_one = live & (inside == coarse)

    def shifted(j):
        return jnp.where(live, gram[:, j * pitch : j * pitch + wide], 0.0)

    own = [shifted(j) for j in range(3)]
    gap = jnp.zeros((coarse, 1), f32)
    rest = jnp.zeros((coarse, wide - 3 * pitch), f32)
    hankel = []
    for i in range(3):
        line = [squares[i], gap, squares[i + 1], gap, squares[i + 2], gap]
        hankel.append(jnp.concatenate(line + ([rest] if wide > 3 * pitch else []), axis=1))
        hankel.append(jnp.zeros((1, wide), f32))
    if wide > 3 * pitch:
        hankel.append(jnp.zeros((wide - 3 * pitch, wide), f32))
    hankel = jnp.concatenate(hankel, axis=0)
    block0 = lane < pitch
    inverse = bottom[:, 4 * pitch : 4 * pitch + coarse]
    inverse = jnp.concatenate([inverse, jnp.zeros((coarse, wide - coarse), f32)], axis=1)
    inverse = jnp.concatenate([inverse, jnp.zeros((wide - coarse, wide), f32)], axis=0)
    start = bottom[:count, 3 * pitch : 4 * pitch]
    start = jnp.concatenate([start, jnp.zeros((count, wide - pitch), f32)], axis=1)
    against = jnp.where(
        block0, start, jnp.where(live, pltpu.roll(jnp.where(live, own[0], 0.0), pitch, axis=1), 0.0)
    )

    def total(x):
        return jnp.sum(x, axis=1, keepdims=True)

    def scalars(u, i):
        return total(jnp.where(lane == i * pitch + coarse, u, 0.0))

    def metric(u):
        out = dot(jnp.where(is_vec, u, 0.0), hankel, precision=highest)
        for j in range(3):
            out = out + scalars(u, j) * own[j]
        out = jnp.where(is_vec, out, 0.0)
        for i in range(3):
            out = jnp.where(lane == i * pitch + coarse, total(u * own[i]), out)
        return out

    def corrected(w):
        return dot(jnp.where(lane < coarse, w, 0.0), inverse, precision=highest)

    pre = corrected(against) + jnp.where(lane == coarse, 1.0, 0.0)
    direction = pre
    gamma = total(pre * against)
    answer = jnp.zeros_like(pre)
    image_sum = jnp.zeros_like(pre)
    for step in range(ITERS):
        image = metric(direction)
        alpha = gamma / total(direction * image)
        answer = answer + alpha * direction
        if step + 1 < ITERS:
            image_sum = image_sum + alpha * image
            moved_on = jnp.where(live & (slot > 0), pltpu.roll(direction, pitch, axis=1), 0.0)
            pre = pre - alpha * (moved_on + corrected(image))
            gamma_new = total(pre * (against - image_sum))
            direction = pre + (gamma_new / gamma) * direction
            gamma = gamma_new

    pack = jnp.concatenate([left_ref[...], own_ref[...]], axis=1)
    z = one_hot(pack[FEAT + 1 : FEAT + 2], coarse)
    q0 = pack[SYS:]
    d1 = jnp.concatenate([d1l_ref[...], d1_ref[...]], axis=1)
    cargo = jnp.concatenate([cargol_ref[...], cargo_ref[...]], axis=1)
    d2 = cargo[:rows]
    span = q0.shape[1]
    step = -(-coarse // FEAT) * FEAT
    deep = -(-3 * step // LANES) * LANES
    parts, basis = [], []
    for i, rest in enumerate((z, d1[count:], d2[count:])):
        parts.append(answer[:, i * pitch : i * pitch + coarse])
        basis.append(rest)
        if step > coarse:
            parts.append(jnp.zeros((count, step - coarse), f32))
            basis.append(jnp.zeros((step - coarse, span), f32))
    if deep > 3 * step:
        parts.append(jnp.zeros((count, deep - 3 * step), f32))
        basis.append(jnp.zeros((deep - 3 * step, span), f32))
    x = dot(
        jnp.concatenate(parts, axis=1), jnp.concatenate(basis, axis=0), precision=highest
    )
    x = x + scalars(answer, 0) * q0 + scalars(answer, 1) * d1[:count]
    x = x + scalars(answer, 2) * d2[:count]
    mine = slice(width, 2 * width)
    sol_ref[...] = x[:, mine]

    probe = own_ref[FEAT + 2 : FEAT + 3, 0:1]
    line = iota((count, 1), 0).astype(f32) + probe * count
    right = jnp.where(line == 0, x, cargo[rows:])
    coef = jnp.where(line == 0, 0.5 / points, -0.5 / (sides - 1) / points)
    r0, r1 = split(right, 2)
    w0, w1 = split(x * coef, 2)
    rest = jnp.zeros((LANES - 6 * count, span), f32)
    near = jnp.concatenate([w0, w1, w0, r0, r1, r0, rest], axis=0).T.astype(bf16)
    none = jnp.zeros((3 * count, width), f32)
    rest = rest[:, mine]
    ahead = jnp.concatenate([r0, r0, r1], axis=0)[:, mine]
    back = jnp.concatenate([w0, w0, w1], axis=0)[:, mine]
    mates = [
        jnp.concatenate([ahead, none, rest], axis=0).astype(bf16),
        jnp.concatenate([none, back, rest], axis=0).astype(bf16),
    ]
    scaled = pack[0:FEAT]
    table = one_hot(pack[FEAT : FEAT + 1], TASKS)
    ones = jnp.ones((8, span), f32)
    terms = jnp.concatenate([scaled, ones, scaled * scaled], axis=0)
    t0, t1 = split(terms, 2)
    pad8 = jnp.zeros((8, span), f32)
    both = jnp.concatenate([t0, pad8, t1, pad8], axis=0).astype(bf16)
    heads = jnp.concatenate([t0, pad8], axis=0).astype(bf16)
    tables = table.astype(bf16)
    high = 32
    length_total = jnp.zeros((FEAT, 1), f32)
    task_total = jnp.zeros((TASKS, TASKS), f32)
    for m in range(blocks):
        at = slice(m * BS, (m + 1) * BS)
        sums = jnp.zeros((high, BS), f32)
        held_sums = [jnp.zeros((TASKS, BS), f32) for _ in mates]
        places = [(1, row, j + REACH) for row, j, _ in own_places(m)]
        places += [(2, row, j) for row, j, _ in halo_places(m) if j < REACH]
        for orders, row, block in places:
            hi_ref, lo_ref, sim_ref = kernel_refs[3 * orders - 3 : 3 * orders]
            j = slice(block * BS, (block + 1) * BS)
            rows_at = slice(row * BS, (row + 1) * BS)
            outers = [dot(near[j], mate[:, at]) for mate in mates[:orders]]
            kernel = hi_ref[m, rows_at, :].astype(f32) + lo_ref[m, rows_at, :].astype(f32)
            similar = sim_ref[m, rows_at, :]
            energy = sum(outers) * kernel
            e0, e1 = (part.astype(bf16) for part in split(energy, 2))
            first = dot(both[:, j], e0)
            sums = sums + first[:high] + first[high:] + dot(heads[:, j], e1)
            for k in range(orders):
                h0, h1 = (part.astype(bf16) for part in split(outers[k] * similar, 2))
                held_sums[k] = held_sums[k] + dot(tables[:, j], h0) + dot(tables[:, j], h1)
        mid = slice(width + m * BS, width + (m + 1) * BS)
        left = scaled[:, mid]
        value = left * left * sums[FEAT : FEAT + 1] + sums[2 * FEAT : 3 * FEAT]
        value = value - 2.0 * left * sums[:FEAT]
        length_total = length_total + jnp.sum(value, axis=1, keepdims=True)
        task_total = task_total + dot(held_sums[0], table[:, mid], NT, highest)
        task_total = task_total + dot(table[:, mid], held_sums[1], NT, highest)
    half = TASKS // 2
    value = jnp.concatenate(
        [
            task_total[:half],
            task_total[half:],
            jnp.where(iota((half, FEAT), 0) == iota((half, FEAT), 1), length_total, 0.0),
            jnp.zeros((half, LANES - 2 * TASKS - FEAT), f32),
        ],
        axis=1,
    )
    for c in range(grad_ref.shape[0]):
        grad_ref[c] = value


def tail_kernel(parts_ref, length_ref, task_ref):
    total = parts_ref[0]
    for c in range(1, parts_ref.shape[0]):
        total = total + parts_ref[c]
    half = TASKS // 2
    task_ref[0:half, :] = total[:, :TASKS]
    task_ref[half:, :] = total[:, TASKS : 2 * TASKS]
    length_ref[...] = jnp.sum(total[:, 2 * TASKS : 2 * TASKS + FEAT], axis=0)


MIB = 1024 * 1024


def call(body, outs, args, name, smem=0, hbm=0, far_outs=0, scratch=(), flops=0, limit=16):
    if hbm:
        args = args[:-hbm] + [pltpu.with_memory_space_constraint(a, pltpu.HBM) for a in args[-hbm:]]
    if far_outs:
        outs = outs[:-far_outs] + [pltpu.HBM(o.shape, o.dtype) for o in outs[-far_outs:]]
    vm = pl.BlockSpec(memory_space=pltpu.VMEM)
    sm = pl.BlockSpec(memory_space=pltpu.SMEM)
    far = pl.BlockSpec(memory_space=pltpu.HBM)
    return pl.pallas_call(
        body,
        out_shape=outs,
        in_specs=[sm] * smem + [vm] * (len(args) - smem - hbm) + [far] * hbm,
        out_specs=[vm] * (len(outs) - far_outs) + [far] * far_outs,
        scratch_shapes=scratch,
        compiler_params=pltpu.CompilerParams(vmem_limit_bytes=limit * MIB),
        cost_estimate=pl.CostEstimate(flops=flops, bytes_accessed=1 << 20, transcendentals=0),
        name=name,
    )(*args)


def both_sides(cells):
    count = lax.axis_size("pts")
    up = [(i, i + 1) for i in range(count - 1)]
    down = [(i + 1, i) for i in range(count - 1)]
    return lax.ppermute(cells, "pts", up), lax.ppermute(cells, "pts", down)


def from_left(cells):
    count = lax.axis_size("pts")
    return lax.ppermute(cells, "pts", [(i, i + 1) for i in range(count - 1)])


def shards(
    systems, features, task_ids, pattern, aggregate, coarse_inverse, task_cov, lengthscales, noise
):
    count, width = systems.shape
    blocks = width // BS
    coarse = coarse_inverse.shape[1]
    rows = count + coarse
    lanes = lanes_of(coarse)
    assert blocks == REACH
    place = lax.axis_index("pts").astype(jnp.int32)[None]
    probe = lax.axis_index("probe").astype(jnp.int32)[None]
    ranks = lax.axis_size("pts")
    sides = lax.axis_size("probe")

    def shape(*dims, kind=f32):
        return jax.ShapeDtypeStruct(dims, kind)

    jac, pack, extra = call(
        invert_kernel,
        [shape(3, blocks, BS, BS, kind=bf16), shape(SYS + count, width), shape(TASKS + FEAT, width)],
        [place, probe, features, task_ids, aggregate, systems, task_cov, coarse_inverse, pattern, lengthscales, noise],
        "invert",
        smem=2,
        hbm=9,
        scratch=[
            pltpu.VMEM((blocks, BS, BS), f32),
            pltpu.VMEM(features.shape, f32),
            pltpu.VMEM(task_ids.shape, jnp.int32),
            pltpu.VMEM(aggregate.shape, jnp.int32),
            pltpu.VMEM(systems.shape, f32),
            pltpu.VMEM(task_cov.shape, f32),
            pltpu.VMEM(coarse_inverse.shape, f32),
            pltpu.SMEM(pattern.shape, jnp.int32),
            pltpu.SMEM(lengthscales.shape, f32),
            pltpu.SMEM(noise.shape, f32),
            pltpu.SemaphoreType.DMA((9,)),
        ],
        flops=10**10,
    )
    pack_l, pack_r = both_sides(pack)

    def build(places, deep, cells, name):
        return call(
            functools.partial(build_kernel, places=places, sides=len(cells)),
            [
                shape(blocks, deep, BS, kind=bf16),
                shape(blocks, deep, BS, kind=bf16),
                shape(blocks, deep, BS),
            ],
            cells + [pack, extra],
            name,
            flops=10**9,
        )

    own_hi, own_lo, own_sim = build(own_places, width, [pack], "build_own")
    halo_hi, halo_lo, halo_sim = build(
        halo_places, BAND - width, [pack_l, pack_r], "build_halo"
    )
    kernel = [own_hi, own_lo, halo_hi, halo_lo]
    v0, d1 = call(
        first_kernel,
        [shape(rows, width), shape(rows, width)],
        [pack, pack_l, pack_r, extra] + kernel + [jac],
        "first",
        flops=10**9,
    )
    d1_l, d1_r = both_sides(d1)
    (early,) = call(
        early_moments_kernel, [shape(rows, lanes)], [pack, systems, d1, v0], "early", flops=10**9
    )
    v1, cargo = call(
        second_kernel,
        [shape(rows, width), shape(rows + count, width)],
        [extra, d1, d1_l, d1_r, early, systems] + kernel + [jac],
        "second",
        flops=10**9,
    )
    cargo_l = from_left(cargo)
    (late,) = call(
        functools.partial(late_moments_kernel, count=count),
        [shape(rows, lanes)],
        [early, d1, cargo, v1],
        "late",
        flops=10**9,
    )
    (gram,) = call(
        functools.partial(third_kernel, count=count, held=coarse_inverse.shape[0]),
        [shape(ranks, rows, lanes)],
        [extra, late, cargo, cargo_l] + kernel,
        "third",
        flops=10**9,
    )
    gram = lax.all_to_all(gram, "pts", 0, 0, tiled=True)
    cells = [own_hi, own_lo, own_sim, halo_hi, halo_lo, halo_sim]
    answer, grads = call(
        functools.partial(final_kernel, sides=sides * count, points=ranks * width),
        [shape(count, width), shape(ranks * sides, FEAT, LANES)],
        [gram, pack, pack_l, d1, d1_l, cargo, cargo_l] + cells,
        "final",
        flops=10**9,
    )
    grads = lax.all_to_all(grads, ("pts", "probe"), 0, 0, tiled=True)
    lengths, tasks = call(
        tail_kernel, [shape(FEAT), shape(TASKS, TASKS)], [grads], "tail", flops=10**5
    )
    return answer, lengths, tasks


def solution(mesh):
    return jax.shard_map(
        shards,
        mesh=mesh,
        in_specs=(
            P("probe", ("groups", "pts")),
            P(None, ("groups", "pts")),
            P(("groups", "pts")),
            P(("groups", "pts"), None),
            P(("groups", "pts")),
            P(("groups", "pts"), None),
            P("groups", None),
            P("groups"),
            P("groups"),
        ),
        out_specs=(P("probe", ("groups", "pts")), P("groups"), P("groups", None)),
        check_vma=False,
    )
```

```python
import functools

import jax
import jax.numpy as jnp
from jax import lax
from jax.experimental import pallas as pl
from jax.experimental.pallas import tpu as pltpu
from jax.sharding import PartitionSpec as P

BS = 256
REACH = 3
FEAT = 8
TASKS = 16
ITERS = 3
SLOTS = 2 * REACH + 1
BAND = SLOTS * BS
BASE = 32
GROUP = 4
LANES = 128
SYS = 2 * FEAT

highest = lax.Precision.HIGHEST
f32 = jnp.float32
bf16 = jnp.bfloat16
NN = (((1,), (0,)), ((), ()))
NT = (((1,), (1,)), ((), ()))
TN = (((0,), (0,)), ((), ()))


def dot(a, b, dims=NN, precision=None):
    return lax.dot_general(a, b, dims, precision=precision, preferred_element_type=f32)


def iota(shape, dim):
    return lax.broadcasted_iota(jnp.int32, shape, dim)


def split(x, parts):
    out = []
    for _ in range(parts - 1):
        head = x.astype(bf16).astype(f32)
        out.append(head)
        x = x - head
    out.append(x.astype(bf16).astype(f32))
    return out


def column(ref, size):
    rows = iota((size, 1), 0)
    out = jnp.zeros((size, 1), f32)
    for i in range(size):
        out = jnp.where(rows == i, ref[i], out)
    return out


def one_hot(ids, size):
    return (iota((size, ids.shape[1]), 0).astype(f32) == ids).astype(f32)


def noise_row(noise_ref, ids):
    out = jnp.zeros(ids.shape, f32)
    for t in range(TASKS):
        out = jnp.where(ids == float(t), noise_ref[t], out)
    return out


def weight(pat_ref, block, offset):
    if offset != REACH:
        return pat_ref[block, offset].astype(f32)
    total = pat_ref[block, 0]
    for o in range(1, SLOTS):
        total = total + pat_ref[block, o]
    return total.astype(f32)


def near_stack(scaled, table):
    s0, s1, s2 = split(scaled, 3)
    n0, n1, n2 = split(-0.5 * jnp.sum(scaled * scaled, axis=0, keepdims=True), 3)
    rows = iota(scaled.shape, 0)
    norms = jnp.where(rows == 0, n0, jnp.where(rows == 1, n1, jnp.where(rows == 2, n2, 0.0)))
    pad = jnp.zeros((LANES - 7 * FEAT - 3 * TASKS, scaled.shape[1]), f32)
    stack = jnp.concatenate([s0, s0, s1, s1, s0, s2, norms, table, table, table, pad], axis=0)
    return stack.T.astype(bf16)


def own_stack(scaled, picked):
    s0, s1, s2 = split(scaled, 3)
    rows = iota(scaled.shape, 0)
    ones = jnp.where(rows < 3, 1.0, 0.0)
    count = scaled.shape[1]
    tail = LANES - 7 * FEAT - 3 * TASKS
    left = jnp.concatenate(
        [s0, s1, s0, s1, s2, s0, ones, jnp.zeros((3 * TASKS + tail, count), f32)], axis=0
    ).astype(bf16)
    right = jnp.concatenate(
        [jnp.zeros((7 * FEAT, count), f32)] + split(picked, 3) + [jnp.zeros((tail, count), f32)],
        axis=0,
    ).astype(bf16)
    sides = [
        jnp.concatenate([left[:, i : i + BS], right[:, i : i + BS]], axis=1)
        for i in range(0, count, BS)
    ]
    return sides, -0.5 * jnp.sum(scaled * scaled, axis=0, keepdims=True)


def small_inverse(p):
    n = len(p)
    if n == 1:
        return [[pltpu.reciprocal(p[0][0], approx=True)]]
    if n == 2:
        a, b, d = p[0][0], p[0][1], p[1][1]
        r = pltpu.reciprocal(a * d - b * b, approx=True)
        off = -b * r
        return [[d * r, off], [off, a * r]]
    h = n // 2
    ainv = small_inverse([row[:h] for row in p[:h]])
    b = [row[h:] for row in p[:h]]
    t = [[sum(ainv[i][k] * b[k][j] for k in range(h)) for j in range(h)] for i in range(h)]
    s = [[None] * h for _ in range(h)]
    for i in range(h):
        for j in range(i, h):
            s[i][j] = s[j][i] = p[h + i][h + j] - sum(b[k][i] * t[k][j] for k in range(h))
    sinv = small_inverse(s)
    u = [[sum(t[i][k] * sinv[k][j] for k in range(h)) for j in range(h)] for i in range(h)]
    out = [[None] * n for _ in range(n)]
    for i in range(h):
        for j in range(h):
            out[h + i][h + j] = sinv[i][j]
            out[i][h + j] = out[h + j][i] = -u[i][j]
    for i in range(h):
        for j in range(i, h):
            out[i][j] = out[j][i] = ainv[i][j] + sum(u[i][k] * t[j][k] for k in range(h))
    return out


def sweep_base(cells, beside):
    tall = range(BASE // 8)
    tiles = [cells[8 * i : 8 * i + 8] for i in tall]
    lane = iota((8, LANES), 1)
    start = lane - lane % BASE
    inner = lane % BASE
    sub = iota((8, LANES), 0)

    def columns(first):
        return [
            [
                jnp.take_along_axis(tile, start + (first + t), axis=1, mode="promise_in_bounds")
                for tile in tiles
            ]
            for t in range(GROUP)
        ]

    def row(parts, r):
        return jnp.broadcast_to(parts[r // 8][r % 8 : r % 8 + 1, :], (8, LANES))

    def with_rows(parts, first, rows):
        part = parts[first // 8]
        for t, value in enumerate(rows):
            part = jnp.where(sub == first % 8 + t, value, part)
        return [part if i == first // 8 else parts[i] for i in tall]

    def less(parts, factor):
        out = []
        for i in tall:
            part = parts[i]
            for t in range(GROUP):
                part = part - cols[t][i] * factor[t]
            out.append(part)
        return out

    cols = columns(0)
    for first in range(0, BASE, GROUP):
        ahead = columns(first + GROUP) if first + GROUP < BASE else []
        pivots = [[None] * GROUP for _ in range(GROUP)]
        for t in range(GROUP):
            for u in range(t, GROUP):
                pivots[t][u] = pivots[u][t] = row(cols[u], first + t)
        inv = small_inverse(pivots)
        coming = []
        for col in ahead:
            head = [row(col, first + t) for t in range(GROUP)]
            factor = [sum(inv[t][u] * head[u] for u in range(GROUP)) for t in range(GROUP)]
            coming.append(with_rows(less(col, factor), first, factor))
        group = (inner >= first) & (inner < first + GROUP)
        rows = []
        for t in range(GROUP):
            value = jnp.where(group, 0.0, row(tiles, first + t))
            rows.append(jnp.where(inner == first + t, -1.0, value))
        new = [sum(inv[t][u] * rows[u] for u in range(GROUP)) for t in range(GROUP)]
        tiles = [jnp.where(group, 0.0, tile) for tile in tiles]
        tiles = with_rows(less(tiles, new), first, new)
        cols = coming
        if beside:
            beside.pop(0)()
    while beside:
        beside.pop(0)()
    return jnp.concatenate(tiles, axis=0)


def fetch(pairs, sems):
    copies = [pltpu.make_async_copy(a, b, sems.at[i]) for i, (a, b) in enumerate(pairs)]
    for copy in copies:
        copy.start()
    return copies


def invert_kernel(
    place_ref, probe_ref, feat_hbm, ids_hbm, agg_hbm, sys_hbm, cov_hbm, coarse_hbm, pat_hbm, len_hbm, noise_hbm,
    jac_ref, pack_ref, extra_ref,
    work, feat_ref, ids_ref, agg_ref, sys_ref, cov_ref, coarse_ref, pat_ref, len_ref, noise_ref, sems,
):
    blocks = work.shape[0]
    width = blocks * BS
    pairs = [
        (feat_hbm, feat_ref), (ids_hbm, ids_ref), (agg_hbm, agg_ref), (cov_hbm, cov_ref),
        (pat_hbm, pat_ref), (len_hbm, len_ref), (noise_hbm, noise_ref), (coarse_hbm, coarse_ref),
        (sys_hbm, sys_ref),
    ]
    for copy in fetch(pairs, sems):
        copy.wait()
    scaled = feat_ref[...] / column(len_ref, FEAT)
    ids = ids_ref[...].astype(f32).reshape(1, width)
    which = agg_ref[...].astype(f32).reshape(1, width)
    table = one_hot(ids, TASKS)
    noise = noise_row(noise_ref, ids)
    c0, c1, c2 = split(cov_ref[...], 3)
    tab = table.astype(bf16)
    picked = (dot(c2.astype(bf16), tab) + dot(c1.astype(bf16), tab)) + dot(c0.astype(bf16), tab)
    rows = iota((FEAT, width), 0)
    weights = jnp.zeros((1, width), f32)
    places = iota((1, width), 1)
    for m in range(blocks):
        for o in range(SLOTS):
            weights = jnp.where(places == m * SLOTS + o, weight(pat_ref, m, o), weights)
    pack_ref[0:FEAT, :] = scaled
    pack_ref[FEAT : 2 * FEAT, :] = jnp.where(
        rows == 0,
        ids,
        jnp.where(rows == 1, which, jnp.where(rows == 2, probe_ref[0].astype(f32), 0.0)),
    )
    extra_ref[0:TASKS, :] = picked
    tail = jnp.where(rows == 0, noise, jnp.where(rows == 1, weights, 0.0))
    held = coarse_ref.shape[0]
    inverse = jnp.concatenate(
        [coarse_ref[...], jnp.zeros((held, width - coarse_ref.shape[1]), f32)], axis=1
    )
    tail = jnp.where(rows == 2, place_ref[0].astype(f32), tail)
    for r in range(held):
        tail = jnp.where(rows == 3 + r, inverse[r : r + 1], tail)
    extra_ref[TASKS : TASKS + FEAT, :] = tail
    near = near_stack(scaled, table)
    mates, norm = own_stack(scaled, picked)
    eye = iota((BS, BS), 0) == iota((BS, BS), 1)
    for m in range(blocks):
        at = slice(m * BS, (m + 1) * BS)
        both = dot(near[at], mates[m])
        block = weight(pat_ref, m, REACH) * jnp.exp(both[:, :BS] + norm[:, at]) * both[:, BS:]
        work[m] = block + jnp.where(eye, noise[:, at], 0.0)
    seg = iota((BASE, LANES), 1) // BASE
    wide = iota((BASE, BS), 1)
    deep = iota((BASE, BS), 0)

    def packed(strips, first):
        tile, inside = first // LANES, first % LANES
        cells = jnp.zeros((BASE, LANES), f32)
        for m in range(blocks):
            piece = strips[m][:, tile * LANES : (tile + 1) * LANES]
            shift = (BASE * m - inside) % LANES
            if shift:
                piece = pltpu.roll(piece, shift, axis=1)
            cells = jnp.where(seg == m, piece, cells)
        return cells

    def diagonal(cells):
        parts = [jnp.where(seg == m, cells, 0.0) for m in range(LANES // BASE)]
        return jnp.concatenate(parts, axis=0)

    eye = jnp.where(iota((BASE, LANES), 1) % BASE == iota((BASE, LANES), 0), 1.0, 0.0)

    def updates(first, inv, strips):
        state = {}

        def product():
            held = (wide >= first) & (wide < first + BASE)
            minus = jnp.where(wide - first == deep, -1.0, 0.0)
            stack = jnp.concatenate(
                [jnp.where(held, minus, s) for s in strips]
                + [jnp.zeros((LANES - blocks * BASE, BS), f32)],
                axis=0,
            )
            spread = diagonal(inv)[: blocks * BASE]
            new = dot(spread, stack, precision=highest)
            for m in range(blocks):
                state[m] = new[m * BASE : (m + 1) * BASE, :]

        def rows_of(m, low, high):
            def piece():
                r0, r1, r2 = split(strips[m][:, low:high], 3)
                p0, p1, p2 = split(state[m], 3)
                a = jnp.concatenate([r0, r0, r1, r1, r0, r2], axis=0).astype(bf16)
                b = jnp.concatenate([p0, p1, p0, p1, p2, p0], axis=0).astype(bf16)
                gone = (iota((1, BS), 1) >= first) & (iota((1, BS), 1) < first + BASE)
                work[m, low:high, :] = jnp.where(gone, 0.0, work[m, low:high, :]) - dot(a, b, TN)
                if low <= first < high:
                    work[m, first : first + BASE, :] = state[m]

            return piece

        half = BS // 2
        return [product] + [
            rows_of(m, low, low + half) for m in range(blocks) for low in range(0, BS, half)
        ]

    def strips_at(first):
        return [work[m, first : first + BASE, :] for m in range(blocks)]

    cells = jnp.where(seg < blocks, packed(strips_at(0), 0), eye)
    pending = []
    for first in range(0, BS, BASE):
        inv = -sweep_base(cells, pending)
        strips = strips_at(first)
        if first + BASE < BS:
            after = strips_at(first + BASE)
            half = dot(inv, diagonal(packed(strips, first + BASE)), precision=highest)
            drop = dot(packed(after, first), diagonal(half), precision=highest)
            cells = jnp.where(seg < blocks, packed(after, first + BASE) - drop, eye)
        pending = updates(first, inv, strips)
    for piece in pending:
        piece()
    for m in range(blocks):
        inv = -work[m]
        for i, part in enumerate(split(inv, 3)):
            jac_ref[i, m] = part.astype(bf16)
    pack_ref[SYS:, :] = smooth(sys_ref[...], jac_ref)


def own_places(m):
    return [(j, j, REACH + j - m) for j in range(REACH)]


def halo_places(m):
    lefts = [(j - m, j, j - m) for j in range(m, REACH)]
    return lefts + [(REACH - m + j, REACH + j, 2 * REACH - m + j) for j in range(m + 1)]


def build_kernel(*refs, places, sides):
    cells, (own_ref, extra_ref) = refs[:sides], refs[sides : sides + 2]
    hi_ref, lo_ref, sim_ref = refs[sides + 2 :]
    blocks = hi_ref.shape[0]
    near = []
    for ref in cells:
        near.append(near_stack(ref[0:FEAT, :], one_hot(ref[FEAT : FEAT + 1, :], TASKS)))
    mates, norm = own_stack(own_ref[0:FEAT, :], extra_ref[0:TASKS, :])
    weights = extra_ref[TASKS + 1 : TASKS + 2, :]
    for m in range(blocks):
        for row, j, o in places(m):
            part = near[j // REACH][(j % REACH) * BS : (j % REACH + 1) * BS]
            both = dot(part, mates[m])
            place = m * SLOTS + o
            exponent = both[:, :BS] + norm[:, m * BS : (m + 1) * BS]
            similar = weights[:, place : place + 1] * jnp.exp(exponent)
            kernel = similar * both[:, BS:]
            head = kernel.astype(bf16)
            rows = slice(row * BS, (row + 1) * BS)
            if o <= REACH or sides == 1:
                sim_ref[m, rows, :] = similar
            hi_ref[m, rows, :] = head
            lo_ref[m, rows, :] = (kernel - head.astype(f32)).astype(bf16)


def pieces(vectors):
    return jnp.concatenate(split(vectors, 2), axis=0).astype(bf16)


def apply(cells, hi, lo):
    rows = cells.shape[0] // 2
    first = dot(cells, hi)
    return first[:rows] + first[rows:] + dot(cells[:rows], lo)


def operate_own(own, noise, own_hi, own_lo):
    mine = pieces(own)
    out = [apply(mine, own_hi[m], own_lo[m]) for m in range(REACH)]
    return jnp.concatenate(out, axis=1) + noise * own


def operate_left(left, halo_hi, halo_lo):
    cells = pieces(left)
    out = []
    for m in range(REACH):
        part = slice(0, (REACH - m) * BS)
        out.append(apply(cells[:, m * BS :], halo_hi[m, part, :], halo_lo[m, part, :]))
    return jnp.concatenate(out, axis=1)


def operate(own, left, right, noise, own_hi, own_lo, halo_hi, halo_lo):
    lefts, rights = pieces(left), pieces(right)
    out = []
    for m in range(REACH):
        beyond = jnp.concatenate([lefts[:, m * BS :], rights[:, : (m + 1) * BS]], axis=1)
        out.append(apply(beyond, halo_hi[m], halo_lo[m]))
    return operate_own(own, noise, own_hi, own_lo) + jnp.concatenate(out, axis=1)


def smooth(image, jac_ref):
    rows = image.shape[0]
    out = []
    for m in range(jac_ref.shape[1]):
        pieces = jnp.concatenate(split(image[:, m * BS : (m + 1) * BS], 3), axis=0).astype(bf16)
        a = dot(pieces, jac_ref[0, m])
        b = dot(pieces[: 2 * rows], jac_ref[1, m])
        c = dot(pieces[:rows], jac_ref[2, m])
        out.append(a[:rows] + (a[rows : 2 * rows] + b[:rows] + (a[2 * rows :] + b[rows:] + c)))
    return jnp.concatenate(out, axis=1)


def first_kernel(own_ref, left_ref, right_ref, extra_ref, *refs):
    kernel, (jac_ref, image_ref, next_ref) = refs[:4], refs[4:]
    count = own_ref.shape[0] - SYS
    coarse = image_ref.shape[0] - count

    def basis(ref):
        z = one_hot(ref[FEAT + 1 : FEAT + 2, :], coarse)
        return jnp.concatenate([ref[SYS:, :], z], axis=0)

    noise = extra_ref[TASKS : TASKS + 1, :]
    image = operate(basis(own_ref), basis(left_ref), basis(right_ref), noise, *kernel)
    image_ref[...] = image
    next_ref[...] = smooth(image, jac_ref)


def second_kernel(extra_ref, vec_ref, left_ref, right_ref, early_ref, sys_ref, *refs):
    kernel, (jac_ref, image_ref, cargo_ref) = refs[:4], refs[4:]
    rows = vec_ref.shape[0]
    noise = extra_ref[TASKS : TASKS + 1, :]
    image = operate(vec_ref[...], left_ref[...], right_ref[...], noise, *kernel)
    image_ref[...] = image
    cargo_ref[0:rows, :] = smooth(image, jac_ref)
    cargo_ref[rows:, :] = sys_ref[...]


def pitch_of(coarse):
    return coarse + 1


def lanes_of(coarse):
    return -(-5 * pitch_of(coarse) // LANES) * LANES


def moment(vectors, images, pairs):
    count = pairs.shape[0]
    table = dot(images, vectors, NT, lax.Precision.HIGH)
    own = jnp.sum(pairs, axis=1, keepdims=True)
    if images.shape[0] > count:
        own = jnp.concatenate([own, jnp.zeros((images.shape[0] - count, 1), f32)], axis=0)
    return jnp.concatenate([table, own], axis=1)


def spread_out(parts, lanes):
    rows, pitch = next(iter(parts.values())).shape
    cells = [parts.get(k, jnp.zeros((rows, pitch), f32)) for k in range(5)]
    if lanes > 5 * pitch:
        cells.append(jnp.zeros((rows, lanes - 5 * pitch), f32))
    return jnp.concatenate(cells, axis=1)


def folded(low, high):
    order = low.shape[0]
    row, col = iota((order, order), 0), iota((order, order), 1)
    diagonal = jnp.sum(jnp.where(row == col, high, 0.0), axis=1, keepdims=True)
    return jnp.concatenate([jnp.where(row >= col, low, high), diagonal], axis=1)


def unfolded(cells):
    order = cells.shape[0]
    row, col = iota((order, order), 0), iota((order, order), 1)
    square = cells[:, :order]
    turned = dot(square, jnp.where(row == col, 1.0, 0.0), TN, highest)
    low = jnp.where(row >= col, square, turned)
    high = jnp.where(row < col, square, jnp.where(row > col, turned, cells[:, order:]))
    return low, high


def early_moments_kernel(own_ref, sys_ref, d1_ref, v0_ref, out_ref):
    count = own_ref.shape[0] - SYS
    coarse = d1_ref.shape[0] - count
    lanes = out_ref.shape[1]
    pitch = pitch_of(coarse)
    systems = sys_ref[...]
    pre = own_ref[SYS:, :]
    z = one_hot(own_ref[FEAT + 1 : FEAT + 2, :], coarse)
    d1, v0 = d1_ref[...], v0_ref[...]
    m0 = moment(z, v0, pre * v0[:count])
    m1 = moment(d1[count:], v0, d1[:count] * v0[:count])
    out_ref[0:count, :] = spread_out({0: m0[:count], 1: m1[:count]}, lanes)
    start = moment(z, systems, systems * pre)
    if coarse > count:
        start = jnp.concatenate([start, jnp.zeros((coarse - count, pitch), f32)], axis=0)
    fold = folded(m0[count:, :coarse], m1[count:, :coarse])
    out_ref[count:, :] = spread_out({0: fold, 3: start}, lanes)


def late_moments_kernel(before_ref, d1_ref, cargo_ref, v1_ref, out_ref, *, count):
    lanes = out_ref.shape[1]
    d1, d2, v1 = d1_ref[...], cargo_ref[0 : d1_ref.shape[0], :], v1_ref[...]
    coarse = d1.shape[0] - count
    m2 = moment(d1[count:], v1, d1[:count] * v1[:count])
    m3 = moment(d2[count:], v1, d2[:count] * v1[:count])
    out_ref[0:count, :] = before_ref[0:count, :] + spread_out({2: m2[:count], 3: m3[:count]}, lanes)
    fold = folded(m2[count:, :coarse], m3[count:, :coarse])
    out_ref[count:, :] = before_ref[count:, :] + spread_out({1: fold}, lanes)


def third_kernel(
    extra_ref, before_ref, cargo_ref, left_ref, *refs, count, held
):
    kernel, out_ref = refs[:4], refs[4]
    rows = cargo_ref.shape[0] - count
    coarse = rows - count
    lanes = out_ref.shape[2]
    pitch = pitch_of(coarse)
    d2 = cargo_ref[0:rows, :]
    noise = extra_ref[TASKS : TASKS + 1, :]
    inner = operate_own(d2, noise, *kernel[:2])
    cross = operate_left(left_ref[0:rows, :], *kernel[2:])
    m4 = moment(d2[count:], inner + cross, d2[:count] * (inner + 2.0 * cross)[:count])
    mirror = dot(d2, cross[count:], NT, lax.Precision.HIGH)
    m4 = m4 + jnp.concatenate([mirror, jnp.zeros((rows, 1), f32)], axis=1)
    row = iota((coarse, 1), 0).astype(f32)
    start = extra_ref[TASKS + 2 : TASKS + 3, 0:1] * held
    inverse = jnp.zeros((coarse, pitch), f32)
    for r in range(held):
        line = extra_ref[TASKS + 3 + r : TASKS + 4 + r, 0:pitch]
        inverse = jnp.where(row == start + r, line, inverse)
    top = before_ref[0:count, :] + spread_out({4: m4[:count]}, lanes)
    bottom = before_ref[count:, :] + spread_out({2: m4[count:], 4: inverse}, lanes)
    for c in range(out_ref.shape[0]):
        out_ref[c, 0:count, :] = top
        out_ref[c, count:, :] = bottom


def final_kernel(
    gram_ref, own_ref, left_ref, d1_ref, d1l_ref, cargo_ref, cargol_ref, *refs, sides, points,
):
    kernel_refs, (sol_ref, grad_ref) = refs[:6], refs[6:]
    width = own_ref.shape[1]
    count = own_ref.shape[0] - SYS
    rows = d1_ref.shape[0]
    coarse = rows - count
    pitch = pitch_of(coarse)
    wide = -(-3 * pitch // LANES) * LANES
    blocks = width // BS
    gram = gram_ref[0]
    for c in range(1, gram_ref.shape[0]):
        gram = gram + gram_ref[c]
    bottom = gram[count:]
    gram = jnp.concatenate([gram[:count], jnp.zeros((count, wide), f32)], axis=1)
    squares = list(unfolded(bottom[:, :pitch])) + list(unfolded(bottom[:, pitch : 2 * pitch]))
    squares.append(bottom[:, 2 * pitch : 2 * pitch + coarse])
    lane = iota((1, wide), 1)
    slot, inside = lane // pitch, lane % pitch
    live = lane < 3 * pitch
    is_vec = live & (inside < coarse)
    is_one = live & (inside == coarse)

    def shifted(j):
        return jnp.where(live, gram[:, j * pitch : j * pitch + wide], 0.0)

    own = [shifted(j) for j in range(3)]
    gap = jnp.zeros((coarse, 1), f32)
    rest = jnp.zeros((coarse, wide - 3 * pitch), f32)
    hankel = []
    for i in range(3):
        line = [squares[i], gap, squares[i + 1], gap, squares[i + 2], gap]
        hankel.append(jnp.concatenate(line + ([rest] if wide > 3 * pitch else []), axis=1))
        hankel.append(jnp.zeros((1, wide), f32))
    if wide > 3 * pitch:
        hankel.append(jnp.zeros((wide - 3 * pitch, wide), f32))
    hankel = jnp.concatenate(hankel, axis=0)
    block0 = lane < pitch
    inverse = bottom[:, 4 * pitch : 4 * pitch + coarse]
    inverse = jnp.concatenate([inverse, jnp.zeros((coarse, wide - coarse), f32)], axis=1)
    inverse = jnp.concatenate([inverse, jnp.zeros((wide - coarse, wide), f32)], axis=0)
    start = bottom[:count, 3 * pitch : 4 * pitch]
    start = jnp.concatenate([start, jnp.zeros((count, wide - pitch), f32)], axis=1)
    against = jnp.where(
        block0, start, jnp.where(live, pltpu.roll(jnp.where(live, own[0], 0.0), pitch, axis=1), 0.0)
    )

    def total(x):
        return jnp.sum(x, axis=1, keepdims=True)

    def scalars(u, i):
        return total(jnp.where(lane == i * pitch + coarse, u, 0.0))

    def metric(u):
        out = dot(jnp.where(is_vec, u, 0.0), hankel, precision=highest)
        for j in range(3):
            out = out + scalars(u, j) * own[j]
        out = jnp.where(is_vec, out, 0.0)
        for i in range(3):
            out = jnp.where(lane == i * pitch + coarse, total(u * own[i]), out)
        return out

    def corrected(w):
        return dot(jnp.where(lane < coarse, w, 0.0), inverse, precision=highest)

    pre = corrected(against) + jnp.where(lane == coarse, 1.0, 0.0)
    direction = pre
    gamma = total(pre * against)
    answer = jnp.zeros_like(pre)
    image_sum = jnp.zeros_like(pre)
    for step in range(ITERS):
        image = metric(direction)
        alpha = gamma / total(direction * image)
        answer = answer + alpha * direction
        if step + 1 < ITERS:
            image_sum = image_sum + alpha * image
            moved_on = jnp.where(live & (slot > 0), pltpu.roll(direction, pitch, axis=1), 0.0)
            pre = pre - alpha * (moved_on + corrected(image))
            gamma_new = total(pre * (against - image_sum))
            direction = pre + (gamma_new / gamma) * direction
            gamma = gamma_new

    pack = jnp.concatenate([left_ref[...], own_ref[...]], axis=1)
    z = one_hot(pack[FEAT + 1 : FEAT + 2], coarse)
    q0 = pack[SYS:]
    d1 = jnp.concatenate([d1l_ref[...], d1_ref[...]], axis=1)
    cargo = jnp.concatenate([cargol_ref[...], cargo_ref[...]], axis=1)
    d2 = cargo[:rows]
    span = q0.shape[1]
    step = -(-coarse // FEAT) * FEAT
    deep = -(-3 * step // LANES) * LANES
    parts, basis = [], []
    for i, rest in enumerate((z, d1[count:], d2[count:])):
        parts.append(answer[:, i * pitch : i * pitch + coarse])
        basis.append(rest)
        if step > coarse:
            parts.append(jnp.zeros((count, step - coarse), f32))
            basis.append(jnp.zeros((step - coarse, span), f32))
    if deep > 3 * step:
        parts.append(jnp.zeros((count, deep - 3 * step), f32))
        basis.append(jnp.zeros((deep - 3 * step, span), f32))
    x = dot(
        jnp.concatenate(parts, axis=1), jnp.concatenate(basis, axis=0), precision=highest
    )
    x = x + scalars(answer, 0) * q0 + scalars(answer, 1) * d1[:count]
    x = x + scalars(answer, 2) * d2[:count]
    mine = slice(width, 2 * width)
    sol_ref[...] = x[:, mine]

    probe = own_ref[FEAT + 2 : FEAT + 3, 0:1]
    line = iota((count, 1), 0).astype(f32) + probe * count
    right = jnp.where(line == 0, x, cargo[rows:])
    coef = jnp.where(line == 0, 0.5 / points, -0.5 / (sides - 1) / points)
    r0, r1 = split(right, 2)
    w0, w1 = split(x * coef, 2)
    rest = jnp.zeros((LANES - 6 * count, span), f32)
    near = jnp.concatenate([w0, w1, w0, r0, r1, r0, rest], axis=0).T.astype(bf16)
    none = jnp.zeros((3 * count, width), f32)
    rest = rest[:, mine]
    ahead = jnp.concatenate([r0, r0, r1], axis=0)[:, mine]
    back = jnp.concatenate([w0, w0, w1], axis=0)[:, mine]
    mates = [
        jnp.concatenate([ahead, none, rest], axis=0).astype(bf16),
        jnp.concatenate([none, back, rest], axis=0).astype(bf16),
    ]
    scaled = pack[0:FEAT]
    table = one_hot(pack[FEAT : FEAT + 1], TASKS)
    ones = jnp.ones((8, span), f32)
    terms = jnp.concatenate([scaled, ones, scaled * scaled], axis=0)
    t0, t1 = split(terms, 2)
    pad8 = jnp.zeros((8, span), f32)
    both = jnp.concatenate([t0, pad8, t1, pad8], axis=0).astype(bf16)
    heads = jnp.concatenate([t0, pad8], axis=0).astype(bf16)
    tables = table.astype(bf16)
    high = 32
    length_total = jnp.zeros((FEAT, 1), f32)
    task_total = jnp.zeros((TASKS, TASKS), f32)
    for m in range(blocks):
        at = slice(m * BS, (m + 1) * BS)
        sums = jnp.zeros((high, BS), f32)
        held_sums = [jnp.zeros((TASKS, BS), f32) for _ in mates]
        places = [(1, row, j + REACH) for row, j, _ in own_places(m)]
        places += [(2, row, j) for row, j, _ in halo_places(m) if j < REACH]
        for orders, row, block in places:
            hi_ref, lo_ref, sim_ref = kernel_refs[3 * orders - 3 : 3 * orders]
            j = slice(block * BS, (block + 1) * BS)
            rows_at = slice(row * BS, (row + 1) * BS)
            outers = [dot(near[j], mate[:, at]) for mate in mates[:orders]]
            kernel = hi_ref[m, rows_at, :].astype(f32) + lo_ref[m, rows_at, :].astype(f32)
            similar = sim_ref[m, rows_at, :]
            energy = sum(outers) * kernel
            e0, e1 = (part.astype(bf16) for part in split(energy, 2))
            first = dot(both[:, j], e0)
            sums = sums + first[:high] + first[high:] + dot(heads[:, j], e1)
            for k in range(orders):
                h0, h1 = (part.astype(bf16) for part in split(outers[k] * similar, 2))
                held_sums[k] = held_sums[k] + dot(tables[:, j], h0) + dot(tables[:, j], h1)
        mid = slice(width + m * BS, width + (m + 1) * BS)
        left = scaled[:, mid]
        value = left * left * sums[FEAT : FEAT + 1] + sums[2 * FEAT : 3 * FEAT]
        value = value - 2.0 * left * sums[:FEAT]
        length_total = length_total + jnp.sum(value, axis=1, keepdims=True)
        task_total = task_total + dot(held_sums[0], table[:, mid], NT, highest)
        task_total = task_total + dot(table[:, mid], held_sums[1], NT, highest)
    half = TASKS // 2
    value = jnp.concatenate(
        [
            task_total[:half],
            task_total[half:],
            jnp.where(iota((half, FEAT), 0) == iota((half, FEAT), 1), length_total, 0.0),
            jnp.zeros((half, LANES - 2 * TASKS - FEAT), f32),
        ],
        axis=1,
    )
    for c in range(grad_ref.shape[0]):
        grad_ref[c] = value


def tail_kernel(parts_ref, length_ref, task_ref):
    total = parts_ref[0]
    for c in range(1, parts_ref.shape[0]):
        total = total + parts_ref[c]
    half = TASKS // 2
    task_ref[0:half, :] = total[:, :TASKS]
    task_ref[half:, :] = total[:, TASKS : 2 * TASKS]
    length_ref[...] = jnp.sum(total[:, 2 * TASKS : 2 * TASKS + FEAT], axis=0)


MIB = 1024 * 1024


def call(body, outs, args, name, smem=0, hbm=0, far_outs=0, scratch=(), flops=0, limit=16):
    if hbm:
        args = args[:-hbm] + [pltpu.with_memory_space_constraint(a, pltpu.HBM) for a in args[-hbm:]]
    if far_outs:
        outs = outs[:-far_outs] + [pltpu.HBM(o.shape, o.dtype) for o in outs[-far_outs:]]
    vm = pl.BlockSpec(memory_space=pltpu.VMEM)
    sm = pl.BlockSpec(memory_space=pltpu.SMEM)
    far = pl.BlockSpec(memory_space=pltpu.HBM)
    return pl.pallas_call(
        body,
        out_shape=outs,
        in_specs=[sm] * smem + [vm] * (len(args) - smem - hbm) + [far] * hbm,
        out_specs=[vm] * (len(outs) - far_outs) + [far] * far_outs,
        scratch_shapes=scratch,
        compiler_params=pltpu.CompilerParams(vmem_limit_bytes=limit * MIB),
        cost_estimate=pl.CostEstimate(flops=flops, bytes_accessed=1 << 20, transcendentals=0),
        name=name,
    )(*args)


def both_sides(cells):
    count = lax.axis_size("pts")
    up = [(i, i + 1) for i in range(count - 1)]
    down = [(i + 1, i) for i in range(count - 1)]
    return lax.ppermute(cells, "pts", up), lax.ppermute(cells, "pts", down)


def from_left(cells):
    count = lax.axis_size("pts")
    return lax.ppermute(cells, "pts", [(i, i + 1) for i in range(count - 1)])


def shards(
    systems, features, task_ids, pattern, aggregate, coarse_inverse, task_cov, lengthscales, noise
):
    count, width = systems.shape
    blocks = width // BS
    coarse = coarse_inverse.shape[1]
    rows = count + coarse
    lanes = lanes_of(coarse)
    assert blocks == REACH
    place = lax.axis_index("pts").astype(jnp.int32)[None]
    probe = lax.axis_index("probe").astype(jnp.int32)[None]
    ranks = lax.axis_size("pts")
    sides = lax.axis_size("probe")

    def shape(*dims, kind=f32):
        return jax.ShapeDtypeStruct(dims, kind)

    jac, pack, extra = call(
        invert_kernel,
        [shape(3, blocks, BS, BS, kind=bf16), shape(SYS + count, width), shape(TASKS + FEAT, width)],
        [place, probe, features, task_ids, aggregate, systems, task_cov, coarse_inverse, pattern, lengthscales, noise],
        "invert",
        smem=2,
        hbm=9,
        scratch=[
            pltpu.VMEM((blocks, BS, BS), f32),
            pltpu.VMEM(features.shape, f32),
            pltpu.VMEM(task_ids.shape, jnp.int32),
            pltpu.VMEM(aggregate.shape, jnp.int32),
            pltpu.VMEM(systems.shape, f32),
            pltpu.VMEM(task_cov.shape, f32),
            pltpu.VMEM(coarse_inverse.shape, f32),
            pltpu.SMEM(pattern.shape, jnp.int32),
            pltpu.SMEM(lengthscales.shape, f32),
            pltpu.SMEM(noise.shape, f32),
            pltpu.SemaphoreType.DMA((9,)),
        ],
        flops=10**10,
    )
    pack_l, pack_r = both_sides(pack)

    def build(places, deep, cells, name):
        return call(
            functools.partial(build_kernel, places=places, sides=len(cells)),
            [
                shape(blocks, deep, BS, kind=bf16),
                shape(blocks, deep, BS, kind=bf16),
                shape(blocks, deep, BS),
            ],
            cells + [pack, extra],
            name,
            flops=10**9,
        )

    own_hi, own_lo, own_sim = build(own_places, width, [pack], "build_own")
    halo_hi, halo_lo, halo_sim = build(
        halo_places, BAND - width, [pack_l, pack_r], "build_halo"
    )
    kernel = [own_hi, own_lo, halo_hi, halo_lo]
    v0, d1 = call(
        first_kernel,
        [shape(rows, width), shape(rows, width)],
        [pack, pack_l, pack_r, extra] + kernel + [jac],
        "first",
        flops=10**9,
    )
    d1_l, d1_r = both_sides(d1)
    (early,) = call(
        early_moments_kernel, [shape(rows, lanes)], [pack, systems, d1, v0], "early", flops=10**9
    )
    v1, cargo = call(
        second_kernel,
        [shape(rows, width), shape(rows + count, width)],
        [extra, d1, d1_l, d1_r, early, systems] + kernel + [jac],
        "second",
        flops=10**9,
    )
    cargo_l = from_left(cargo)
    (late,) = call(
        functools.partial(late_moments_kernel, count=count),
        [shape(rows, lanes)],
        [early, d1, cargo, v1],
        "late",
        flops=10**9,
    )
    (gram,) = call(
        functools.partial(third_kernel, count=count, held=coarse_inverse.shape[0]),
        [shape(ranks, rows, lanes)],
        [extra, late, cargo, cargo_l] + kernel,
        "third",
        flops=10**9,
    )
    gram = lax.all_to_all(gram, "pts", 0, 0, tiled=True)
    cells = [own_hi, own_lo, own_sim, halo_hi, halo_lo, halo_sim]
    answer, grads = call(
        functools.partial(final_kernel, sides=sides * count, points=ranks * width),
        [shape(count, width), shape(ranks * sides, FEAT, LANES)],
        [gram, pack, pack_l, d1, d1_l, cargo, cargo_l] + cells,
        "final",
        flops=10**9,
    )
    grads = lax.all_to_all(grads, ("pts", "probe"), 0, 0, tiled=True)
    lengths, tasks = call(
        tail_kernel, [shape(FEAT), shape(TASKS, TASKS)], [grads], "tail", flops=10**5
    )
    return answer, lengths, tasks


def solution(mesh):
    return jax.shard_map(
        shards,
        mesh=mesh,
        in_specs=(
            P("probe", ("groups", "pts")),
            P(None, ("groups", "pts")),
            P(("groups", "pts")),
            P(("groups", "pts"), None),
            P(("groups", "pts")),
            P(("groups", "pts"), None),
            P("groups", None),
            P("groups"),
            P("groups"),
        ),
        out_specs=(P("probe", ("groups", "pts")), P("groups"), P("groups", None)),
        check_vma=False,
    )
```

```python
import functools

import jax
import jax.numpy as jnp
from jax import lax
from jax.experimental import pallas as pl
from jax.experimental.pallas import tpu as pltpu
from jax.sharding import PartitionSpec as P

BS = 256
REACH = 3
FEAT = 8
TASKS = 16
ITERS = 3
SLOTS = 2 * REACH + 1
BAND = SLOTS * BS
BASE = 32
GROUP = 2
LANES = 128
SYS = 2 * FEAT

highest = lax.Precision.HIGHEST
f32 = jnp.float32
bf16 = jnp.bfloat16
NN = (((1,), (0,)), ((), ()))
NT = (((1,), (1,)), ((), ()))
TN = (((0,), (0,)), ((), ()))


def dot(a, b, dims=NN, precision=None):
    return lax.dot_general(a, b, dims, precision=precision, preferred_element_type=f32)


def iota(shape, dim):
    return lax.broadcasted_iota(jnp.int32, shape, dim)


def split(x, parts):
    out = []
    for _ in range(parts - 1):
        head = x.astype(bf16).astype(f32)
        out.append(head)
        x = x - head
    out.append(x.astype(bf16).astype(f32))
    return out


def column(ref, size):
    rows = iota((size, 1), 0)
    out = jnp.zeros((size, 1), f32)
    for i in range(size):
        out = jnp.where(rows == i, ref[i], out)
    return out


def one_hot(ids, size):
    return (iota((size, ids.shape[1]), 0).astype(f32) == ids).astype(f32)


def noise_row(noise_ref, ids):
    out = jnp.zeros(ids.shape, f32)
    for t in range(TASKS):
        out = jnp.where(ids == float(t), noise_ref[t], out)
    return out


def weight(pat_ref, block, offset):
    if offset != REACH:
        return pat_ref[block, offset].astype(f32)
    total = pat_ref[block, 0]
    for o in range(1, SLOTS):
        total = total + pat_ref[block, o]
    return total.astype(f32)


def near_stack(scaled, table):
    s0, s1, s2 = split(scaled, 3)
    n0, n1, n2 = split(-0.5 * jnp.sum(scaled * scaled, axis=0, keepdims=True), 3)
    rows = iota(scaled.shape, 0)
    norms = jnp.where(rows == 0, n0, jnp.where(rows == 1, n1, jnp.where(rows == 2, n2, 0.0)))
    pad = jnp.zeros((LANES - 7 * FEAT - 3 * TASKS, scaled.shape[1]), f32)
    stack = jnp.concatenate([s0, s0, s1, s1, s0, s2, norms, table, table, table, pad], axis=0)
    return stack.T.astype(bf16)


def own_stack(scaled, picked):
    s0, s1, s2 = split(scaled, 3)
    rows = iota(scaled.shape, 0)
    ones = jnp.where(rows < 3, 1.0, 0.0)
    count = scaled.shape[1]
    tail = LANES - 7 * FEAT - 3 * TASKS
    left = jnp.concatenate(
        [s0, s1, s0, s1, s2, s0, ones, jnp.zeros((3 * TASKS + tail, count), f32)], axis=0
    ).astype(bf16)
    right = jnp.concatenate(
        [jnp.zeros((7 * FEAT, count), f32)] + split(picked, 3) + [jnp.zeros((tail, count), f32)],
        axis=0,
    ).astype(bf16)
    sides = [
        jnp.concatenate([left[:, i : i + BS], right[:, i : i + BS]], axis=1)
        for i in range(0, count, BS)
    ]
    return sides, -0.5 * jnp.sum(scaled * scaled, axis=0, keepdims=True)


def small_inverse(p):
    n = len(p)
    if n == 1:
        return [[pltpu.reciprocal(p[0][0], approx=True)]]
    if n == 2:
        a, b, d = p[0][0], p[0][1], p[1][1]
        r = pltpu.reciprocal(a * d - b * b, approx=True)
        off = -b * r
        return [[d * r, off], [off, a * r]]
    h = n // 2
    ainv = small_inverse([row[:h] for row in p[:h]])
    b = [row[h:] for row in p[:h]]
    t = [[sum(ainv[i][k] * b[k][j] for k in range(h)) for j in range(h)] for i in range(h)]
    s = [[None] * h for _ in range(h)]
    for i in range(h):
        for j in range(i, h):
            s[i][j] = s[j][i] = p[h + i][h + j] - sum(b[k][i] * t[k][j] for k in range(h))
    sinv = small_inverse(s)
    u = [[sum(t[i][k] * sinv[k][j] for k in range(h)) for j in range(h)] for i in range(h)]
    out = [[None] * n for _ in range(n)]
    for i in range(h):
        for j in range(h):
            out[h + i][h + j] = sinv[i][j]
            out[i][h + j] = out[h + j][i] = -u[i][j]
    for i in range(h):
        for j in range(i, h):
            out[i][j] = out[j][i] = ainv[i][j] + sum(u[i][k] * t[j][k] for k in range(h))
    return out


def sweep_base(cells, beside):
    tall = range(BASE // 8)
    tiles = [cells[8 * i : 8 * i + 8] for i in tall]
    lane = iota((8, LANES), 1)
    start = lane - lane % BASE
    inner = lane % BASE
    sub = iota((8, LANES), 0)

    def columns(first):
        return [
            [
                jnp.take_along_axis(tile, start + (first + t), axis=1, mode="promise_in_bounds")
                for tile in tiles
            ]
            for t in range(GROUP)
        ]

    def row(parts, r):
        return jnp.broadcast_to(parts[r // 8][r % 8 : r % 8 + 1, :], (8, LANES))

    def with_rows(parts, first, rows):
        part = parts[first // 8]
        for t, value in enumerate(rows):
            part = jnp.where(sub == first % 8 + t, value, part)
        return [part if i == first // 8 else parts[i] for i in tall]

    def less(parts, factor):
        out = []
        for i in tall:
            part = parts[i]
            for t in range(GROUP):
                part = part - cols[t][i] * factor[t]
            out.append(part)
        return out

    cols = columns(0)
    for first in range(0, BASE, GROUP):
        ahead = columns(first + GROUP) if first + GROUP < BASE else []
        pivots = [[None] * GROUP for _ in range(GROUP)]
        for t in range(GROUP):
            for u in range(t, GROUP):
                pivots[t][u] = pivots[u][t] = row(cols[u], first + t)
        inv = small_inverse(pivots)
        coming = []
        for col in ahead:
            head = [row(col, first + t) for t in range(GROUP)]
            factor = [sum(inv[t][u] * head[u] for u in range(GROUP)) for t in range(GROUP)]
            coming.append(with_rows(less(col, factor), first, factor))
        group = (inner >= first) & (inner < first + GROUP)
        rows = []
        for t in range(GROUP):
            value = jnp.where(group, 0.0, row(tiles, first + t))
            rows.append(jnp.where(inner == first + t, -1.0, value))
        new = [sum(inv[t][u] * rows[u] for u in range(GROUP)) for t in range(GROUP)]
        tiles = [jnp.where(group, 0.0, tile) for tile in tiles]
        tiles = with_rows(less(tiles, new), first, new)
        cols = coming
        if beside:
            beside.pop(0)()
    while beside:
        beside.pop(0)()
    return jnp.concatenate(tiles, axis=0)


def fetch(pairs, sems):
    copies = [pltpu.make_async_copy(a, b, sems.at[i]) for i, (a, b) in enumerate(pairs)]
    for copy in copies:
        copy.start()
    return copies


def invert_kernel(
    place_ref, probe_ref, feat_hbm, ids_hbm, agg_hbm, sys_hbm, cov_hbm, coarse_hbm, pat_hbm, len_hbm, noise_hbm,
    jac_ref, pack_ref, extra_ref,
    work, feat_ref, ids_ref, agg_ref, sys_ref, cov_ref, coarse_ref, pat_ref, len_ref, noise_ref, sems,
):
    blocks = work.shape[0]
    width = blocks * BS
    pairs = [
        (feat_hbm, feat_ref), (ids_hbm, ids_ref), (agg_hbm, agg_ref), (cov_hbm, cov_ref),
        (pat_hbm, pat_ref), (len_hbm, len_ref), (noise_hbm, noise_ref), (coarse_hbm, coarse_ref),
        (sys_hbm, sys_ref),
    ]
    for copy in fetch(pairs, sems):
        copy.wait()
    scaled = feat_ref[...] / column(len_ref, FEAT)
    ids = ids_ref[...].astype(f32).reshape(1, width)
    which = agg_ref[...].astype(f32).reshape(1, width)
    table = one_hot(ids, TASKS)
    noise = noise_row(noise_ref, ids)
    c0, c1, c2 = split(cov_ref[...], 3)
    tab = table.astype(bf16)
    picked = (dot(c2.astype(bf16), tab) + dot(c1.astype(bf16), tab)) + dot(c0.astype(bf16), tab)
    rows = iota((FEAT, width), 0)
    weights = jnp.zeros((1, width), f32)
    places = iota((1, width), 1)
    for m in range(blocks):
        for o in range(SLOTS):
            weights = jnp.where(places == m * SLOTS + o, weight(pat_ref, m, o), weights)
    pack_ref[0:FEAT, :] = scaled
    pack_ref[FEAT : 2 * FEAT, :] = jnp.where(
        rows == 0,
        ids,
        jnp.where(rows == 1, which, jnp.where(rows == 2, probe_ref[0].astype(f32), 0.0)),
    )
    extra_ref[0:TASKS, :] = picked
    tail = jnp.where(rows == 0, noise, jnp.where(rows == 1, weights, 0.0))
    held = coarse_ref.shape[0]
    inverse = jnp.concatenate(
        [coarse_ref[...], jnp.zeros((held, width - coarse_ref.shape[1]), f32)], axis=1
    )
    tail = jnp.where(rows == 2, place_ref[0].astype(f32), tail)
    for r in range(held):
        tail = jnp.where(rows == 3 + r, inverse[r : r + 1], tail)
    extra_ref[TASKS : TASKS + FEAT, :] = tail
    near = near_stack(scaled, table)
    mates, norm = own_stack(scaled, picked)
    eye = iota((BS, BS), 0) == iota((BS, BS), 1)
    for m in range(blocks):
        at = slice(m * BS, (m + 1) * BS)
        both = dot(near[at], mates[m])
        block = weight(pat_ref, m, REACH) * jnp.exp(both[:, :BS] + norm[:, at]) * both[:, BS:]
        work[m] = block + jnp.where(eye, noise[:, at], 0.0)
    seg = iota((BASE, LANES), 1) // BASE
    wide = iota((BASE, BS), 1)
    deep = iota((BASE, BS), 0)

    def packed(strips, first):
        tile, inside = first // LANES, first % LANES
        cells = jnp.zeros((BASE, LANES), f32)
        for m in range(blocks):
            piece = strips[m][:, tile * LANES : (tile + 1) * LANES]
            shift = (BASE * m - inside) % LANES
            if shift:
                piece = pltpu.roll(piece, shift, axis=1)
            cells = jnp.where(seg == m, piece, cells)
        return cells

    def diagonal(cells):
        parts = [jnp.where(seg == m, cells, 0.0) for m in range(LANES // BASE)]
        return jnp.concatenate(parts, axis=0)

    eye = jnp.where(iota((BASE, LANES), 1) % BASE == iota((BASE, LANES), 0), 1.0, 0.0)

    def updates(first, inv, strips):
        state = {}

        def product():
            held = (wide >= first) & (wide < first + BASE)
            minus = jnp.where(wide - first == deep, -1.0, 0.0)
            stack = jnp.concatenate(
                [jnp.where(held, minus, s) for s in strips]
                + [jnp.zeros((LANES - blocks * BASE, BS), f32)],
                axis=0,
            )
            spread = diagonal(inv)[: blocks * BASE]
            new = dot(spread, stack, precision=highest)
            for m in range(blocks):
                state[m] = new[m * BASE : (m + 1) * BASE, :]

        def rows_of(m, low, high):
            def piece():
                r0, r1, r2 = split(strips[m][:, low:high], 3)
                p0, p1, p2 = split(state[m], 3)
                a = jnp.concatenate([r0, r0, r1, r1, r0, r2], axis=0).astype(bf16)
                b = jnp.concatenate([p0, p1, p0, p1, p2, p0], axis=0).astype(bf16)
                gone = (iota((1, BS), 1) >= first) & (iota((1, BS), 1) < first + BASE)
                work[m, low:high, :] = jnp.where(gone, 0.0, work[m, low:high, :]) - dot(a, b, TN)
                if low <= first < high:
                    work[m, first : first + BASE, :] = state[m]

            return piece

        half = BS // 2
        return [product] + [
            rows_of(m, low, low + half) for m in range(blocks) for low in range(0, BS, half)
        ]

    def strips_at(first):
        return [work[m, first : first + BASE, :] for m in range(blocks)]

    cells = jnp.where(seg < blocks, packed(strips_at(0), 0), eye)
    pending = []
    for first in range(0, BS, BASE):
        inv = -sweep_base(cells, pending)
        strips = strips_at(first)
        if first + BASE < BS:
            after = strips_at(first + BASE)
            half = dot(inv, diagonal(packed(strips, first + BASE)), precision=highest)
            drop = dot(packed(after, first), diagonal(half), precision=highest)
            cells = jnp.where(seg < blocks, packed(after, first + BASE) - drop, eye)
        pending = updates(first, inv, strips)
    for piece in pending:
        piece()
    for m in range(blocks):
        inv = -work[m]
        for i, part in enumerate(split(inv, 3)):
            jac_ref[i, m] = part.astype(bf16)
    pack_ref[SYS:, :] = smooth(sys_ref[...], jac_ref)


def own_places(m):
    return [(j, j, REACH + j - m) for j in range(REACH)]


def halo_places(m):
    lefts = [(j - m, j, j - m) for j in range(m, REACH)]
    return lefts + [(REACH - m + j, REACH + j, 2 * REACH - m + j) for j in range(m + 1)]


def build_kernel(*refs, places, sides):
    cells, (own_ref, extra_ref) = refs[:sides], refs[sides : sides + 2]
    hi_ref, lo_ref, sim_ref = refs[sides + 2 :]
    blocks = hi_ref.shape[0]
    near = []
    for ref in cells:
        near.append(near_stack(ref[0:FEAT, :], one_hot(ref[FEAT : FEAT + 1, :], TASKS)))
    mates, norm = own_stack(own_ref[0:FEAT, :], extra_ref[0:TASKS, :])
    weights = extra_ref[TASKS + 1 : TASKS + 2, :]
    for m in range(blocks):
        for row, j, o in places(m):
            part = near[j // REACH][(j % REACH) * BS : (j % REACH + 1) * BS]
            both = dot(part, mates[m])
            place = m * SLOTS + o
            exponent = both[:, :BS] + norm[:, m * BS : (m + 1) * BS]
            similar = weights[:, place : place + 1] * jnp.exp(exponent)
            kernel = similar * both[:, BS:]
            head = kernel.astype(bf16)
            rows = slice(row * BS, (row + 1) * BS)
            if o <= REACH or sides == 1:
                sim_ref[m, rows, :] = similar
            hi_ref[m, rows, :] = head
            lo_ref[m, rows, :] = (kernel - head.astype(f32)).astype(bf16)


def pieces(vectors):
    return jnp.concatenate(split(vectors, 2), axis=0).astype(bf16)


def apply(cells, hi, lo):
    rows = cells.shape[0] // 2
    first = dot(cells, hi)
    return first[:rows] + first[rows:] + dot(cells[:rows], lo)


def operate_own(own, noise, own_hi, own_lo):
    mine = pieces(own)
    out = [apply(mine, own_hi[m], own_lo[m]) for m in range(REACH)]
    return jnp.concatenate(out, axis=1) + noise * own


def operate_left(left, halo_hi, halo_lo):
    cells = pieces(left)
    out = []
    for m in range(REACH):
        part = slice(0, (REACH - m) * BS)
        out.append(apply(cells[:, m * BS :], halo_hi[m, part, :], halo_lo[m, part, :]))
    return jnp.concatenate(out, axis=1)


def operate(own, left, right, noise, own_hi, own_lo, halo_hi, halo_lo):
    lefts, rights = pieces(left), pieces(right)
    out = []
    for m in range(REACH):
        beyond = jnp.concatenate([lefts[:, m * BS :], rights[:, : (m + 1) * BS]], axis=1)
        out.append(apply(beyond, halo_hi[m], halo_lo[m]))
    return operate_own(own, noise, own_hi, own_lo) + jnp.concatenate(out, axis=1)


def smooth(image, jac_ref):
    rows = image.shape[0]
    out = []
    for m in range(jac_ref.shape[1]):
        pieces = jnp.concatenate(split(image[:, m * BS : (m + 1) * BS], 3), axis=0).astype(bf16)
        a = dot(pieces, jac_ref[0, m])
        b = dot(pieces[: 2 * rows], jac_ref[1, m])
        c = dot(pieces[:rows], jac_ref[2, m])
        out.append(a[:rows] + (a[rows : 2 * rows] + b[:rows] + (a[2 * rows :] + b[rows:] + c)))
    return jnp.concatenate(out, axis=1)


def first_kernel(own_ref, left_ref, right_ref, extra_ref, *refs):
    kernel, (jac_ref, image_ref, next_ref) = refs[:4], refs[4:]
    count = own_ref.shape[0] - SYS
    coarse = image_ref.shape[0] - count

    def basis(ref):
        z = one_hot(ref[FEAT + 1 : FEAT + 2, :], coarse)
        return jnp.concatenate([ref[SYS:, :], z], axis=0)

    noise = extra_ref[TASKS : TASKS + 1, :]
    image = operate(basis(own_ref), basis(left_ref), basis(right_ref), noise, *kernel)
    image_ref[...] = image
    next_ref[...] = smooth(image, jac_ref)


def second_kernel(extra_ref, vec_ref, left_ref, right_ref, early_ref, sys_ref, *refs):
    kernel, (jac_ref, image_ref, cargo_ref) = refs[:4], refs[4:]
    rows = vec_ref.shape[0]
    noise = extra_ref[TASKS : TASKS + 1, :]
    image = operate(vec_ref[...], left_ref[...], right_ref[...], noise, *kernel)
    image_ref[...] = image
    cargo_ref[0:rows, :] = smooth(image, jac_ref)
    cargo_ref[rows:, :] = sys_ref[...]


def pitch_of(coarse):
    return coarse + 1


def lanes_of(coarse):
    return -(-5 * pitch_of(coarse) // LANES) * LANES


def moment(vectors, images, pairs):
    count = pairs.shape[0]
    table = dot(images, vectors, NT, lax.Precision.HIGH)
    own = jnp.sum(pairs, axis=1, keepdims=True)
    if images.shape[0] > count:
        own = jnp.concatenate([own, jnp.zeros((images.shape[0] - count, 1), f32)], axis=0)
    return jnp.concatenate([table, own], axis=1)


def spread_out(parts, lanes):
    rows, pitch = next(iter(parts.values())).shape
    cells = [parts.get(k, jnp.zeros((rows, pitch), f32)) for k in range(5)]
    if lanes > 5 * pitch:
        cells.append(jnp.zeros((rows, lanes - 5 * pitch), f32))
    return jnp.concatenate(cells, axis=1)


def folded(low, high):
    order = low.shape[0]
    row, col = iota((order, order), 0), iota((order, order), 1)
    diagonal = jnp.sum(jnp.where(row == col, high, 0.0), axis=1, keepdims=True)
    return jnp.concatenate([jnp.where(row >= col, low, high), diagonal], axis=1)


def unfolded(cells):
    order = cells.shape[0]
    row, col = iota((order, order), 0), iota((order, order), 1)
    square = cells[:, :order]
    turned = dot(square, jnp.where(row == col, 1.0, 0.0), TN, highest)
    low = jnp.where(row >= col, square, turned)
    high = jnp.where(row < col, square, jnp.where(row > col, turned, cells[:, order:]))
    return low, high


def early_moments_kernel(own_ref, sys_ref, d1_ref, v0_ref, out_ref):
    count = own_ref.shape[0] - SYS
    coarse = d1_ref.shape[0] - count
    lanes = out_ref.shape[1]
    pitch = pitch_of(coarse)
    systems = sys_ref[...]
    pre = own_ref[SYS:, :]
    z = one_hot(own_ref[FEAT + 1 : FEAT + 2, :], coarse)
    d1, v0 = d1_ref[...], v0_ref[...]
    m0 = moment(z, v0, pre * v0[:count])
    m1 = moment(d1[count:], v0, d1[:count] * v0[:count])
    out_ref[0:count, :] = spread_out({0: m0[:count], 1: m1[:count]}, lanes)
    start = moment(z, systems, systems * pre)
    if coarse > count:
        start = jnp.concatenate([start, jnp.zeros((coarse - count, pitch), f32)], axis=0)
    fold = folded(m0[count:, :coarse], m1[count:, :coarse])
    out_ref[count:, :] = spread_out({0: fold, 3: start}, lanes)


def late_moments_kernel(before_ref, d1_ref, cargo_ref, v1_ref, out_ref, *, count):
    lanes = out_ref.shape[1]
    d1, d2, v1 = d1_ref[...], cargo_ref[0 : d1_ref.shape[0], :], v1_ref[...]
    coarse = d1.shape[0] - count
    m2 = moment(d1[count:], v1, d1[:count] * v1[:count])
    m3 = moment(d2[count:], v1, d2[:count] * v1[:count])
    out_ref[0:count, :] = before_ref[0:count, :] + spread_out({2: m2[:count], 3: m3[:count]}, lanes)
    fold = folded(m2[count:, :coarse], m3[count:, :coarse])
    out_ref[count:, :] = before_ref[count:, :] + spread_out({1: fold}, lanes)


def third_kernel(
    extra_ref, before_ref, cargo_ref, left_ref, *refs, count, held
):
    kernel, out_ref = refs[:4], refs[4]
    rows = cargo_ref.shape[0] - count
    coarse = rows - count
    lanes = out_ref.shape[2]
    pitch = pitch_of(coarse)
    d2 = cargo_ref[0:rows, :]
    noise = extra_ref[TASKS : TASKS + 1, :]
    inner = operate_own(d2, noise, *kernel[:2])
    cross = operate_left(left_ref[0:rows, :], *kernel[2:])
    m4 = moment(d2[count:], inner + cross, d2[:count] * (inner + 2.0 * cross)[:count])
    mirror = dot(d2, cross[count:], NT, lax.Precision.HIGH)
    m4 = m4 + jnp.concatenate([mirror, jnp.zeros((rows, 1), f32)], axis=1)
    row = iota((coarse, 1), 0).astype(f32)
    start = extra_ref[TASKS + 2 : TASKS + 3, 0:1] * held
    inverse = jnp.zeros((coarse, pitch), f32)
    for r in range(held):
        line = extra_ref[TASKS + 3 + r : TASKS + 4 + r, 0:pitch]
        inverse = jnp.where(row == start + r, line, inverse)
    top = before_ref[0:count, :] + spread_out({4: m4[:count]}, lanes)
    bottom = before_ref[count:, :] + spread_out({2: m4[count:], 4: inverse}, lanes)
    for c in range(out_ref.shape[0]):
        out_ref[c, 0:count, :] = top
        out_ref[c, count:, :] = bottom


def final_kernel(
    gram_ref, own_ref, left_ref, d1_ref, d1l_ref, cargo_ref, cargol_ref, *refs, sides, points,
):
    kernel_refs, (sol_ref, grad_ref) = refs[:6], refs[6:]
    width = own_ref.shape[1]
    count = own_ref.shape[0] - SYS
    rows = d1_ref.shape[0]
    coarse = rows - count
    pitch = pitch_of(coarse)
    wide = -(-3 * pitch // LANES) * LANES
    blocks = width // BS
    gram = gram_ref[0]
    for c in range(1, gram_ref.shape[0]):
        gram = gram + gram_ref[c]
    bottom = gram[count:]
    gram = jnp.concatenate([gram[:count], jnp.zeros((count, wide), f32)], axis=1)
    squares = list(unfolded(bottom[:, :pitch])) + list(unfolded(bottom[:, pitch : 2 * pitch]))
    squares.append(bottom[:, 2 * pitch : 2 * pitch + coarse])
    lane = iota((1, wide), 1)
    slot, inside = lane // pitch, lane % pitch
    live = lane < 3 * pitch
    is_vec = live & (inside < coarse)
    is_one = live & (inside == coarse)

    def shifted(j):
        return jnp.where(live, gram[:, j * pitch : j * pitch + wide], 0.0)

    own = [shifted(j) for j in range(3)]
    gap = jnp.zeros((coarse, 1), f32)
    rest = jnp.zeros((coarse, wide - 3 * pitch), f32)
    hankel = []
    for i in range(3):
        line = [squares[i], gap, squares[i + 1], gap, squares[i + 2], gap]
        hankel.append(jnp.concatenate(line + ([rest] if wide > 3 * pitch else []), axis=1))
        hankel.append(jnp.zeros((1, wide), f32))
    if wide > 3 * pitch:
        hankel.append(jnp.zeros((wide - 3 * pitch, wide), f32))
    hankel = jnp.concatenate(hankel, axis=0)
    block0 = lane < pitch
    inverse = bottom[:, 4 * pitch : 4 * pitch + coarse]
    inverse = jnp.concatenate([inverse, jnp.zeros((coarse, wide - coarse), f32)], axis=1)
    inverse = jnp.concatenate([inverse, jnp.zeros((wide - coarse, wide), f32)], axis=0)
    start = bottom[:count, 3 * pitch : 4 * pitch]
    start = jnp.concatenate([start, jnp.zeros((count, wide - pitch), f32)], axis=1)
    against = jnp.where(
        block0, start, jnp.where(live, pltpu.roll(jnp.where(live, own[0], 0.0), pitch, axis=1), 0.0)
    )

    def total(x):
        return jnp.sum(x, axis=1, keepdims=True)

    def scalars(u, i):
        return total(jnp.where(lane == i * pitch + coarse, u, 0.0))

    def metric(u):
        out = dot(jnp.where(is_vec, u, 0.0), hankel, precision=highest)
        for j in range(3):
            out = out + scalars(u, j) * own[j]
        out = jnp.where(is_vec, out, 0.0)
        for i in range(3):
            out = jnp.where(lane == i * pitch + coarse, total(u * own[i]), out)
        return out

    def corrected(w):
        return dot(jnp.where(lane < coarse, w, 0.0), inverse, precision=highest)

    pre = corrected(against) + jnp.where(lane == coarse, 1.0, 0.0)
    direction = pre
    gamma = total(pre * against)
    answer = jnp.zeros_like(pre)
    image_sum = jnp.zeros_like(pre)
    for step in range(ITERS):
        image = metric(direction)
        alpha = gamma / total(direction * image)
        answer = answer + alpha * direction
        if step + 1 < ITERS:
            image_sum = image_sum + alpha * image
            moved_on = jnp.where(live & (slot > 0), pltpu.roll(direction, pitch, axis=1), 0.0)
            pre = pre - alpha * (moved_on + corrected(image))
            gamma_new = total(pre * (against - image_sum))
            direction = pre + (gamma_new / gamma) * direction
            gamma = gamma_new

    pack = jnp.concatenate([left_ref[...], own_ref[...]], axis=1)
    z = one_hot(pack[FEAT + 1 : FEAT + 2], coarse)
    q0 = pack[SYS:]
    d1 = jnp.concatenate([d1l_ref[...], d1_ref[...]], axis=1)
    cargo = jnp.concatenate([cargol_ref[...], cargo_ref[...]], axis=1)
    d2 = cargo[:rows]
    span = q0.shape[1]
    step = -(-coarse // FEAT) * FEAT
    deep = -(-3 * step // LANES) * LANES
    parts, basis = [], []
    for i, rest in enumerate((z, d1[count:], d2[count:])):
        parts.append(answer[:, i * pitch : i * pitch + coarse])
        basis.append(rest)
        if step > coarse:
            parts.append(jnp.zeros((count, step - coarse), f32))
            basis.append(jnp.zeros((step - coarse, span), f32))
    if deep > 3 * step:
        parts.append(jnp.zeros((count, deep - 3 * step), f32))
        basis.append(jnp.zeros((deep - 3 * step, span), f32))
    x = dot(
        jnp.concatenate(parts, axis=1), jnp.concatenate(basis, axis=0), precision=highest
    )
    x = x + scalars(answer, 0) * q0 + scalars(answer, 1) * d1[:count]
    x = x + scalars(answer, 2) * d2[:count]
    mine = slice(width, 2 * width)
    sol_ref[...] = x[:, mine]

    probe = own_ref[FEAT + 2 : FEAT + 3, 0:1]
    line = iota((count, 1), 0).astype(f32) + probe * count
    right = jnp.where(line == 0, x, cargo[rows:])
    coef = jnp.where(line == 0, 0.5 / points, -0.5 / (sides - 1) / points)
    r0, r1 = split(right, 2)
    w0, w1 = split(x * coef, 2)
    rest = jnp.zeros((LANES - 6 * count, span), f32)
    near = jnp.concatenate([w0, w1, w0, r0, r1, r0, rest], axis=0).T.astype(bf16)
    none = jnp.zeros((3 * count, width), f32)
    rest = rest[:, mine]
    ahead = jnp.concatenate([r0, r0, r1], axis=0)[:, mine]
    back = jnp.concatenate([w0, w0, w1], axis=0)[:, mine]
    mates = [
        jnp.concatenate([ahead, none, rest], axis=0).astype(bf16),
        jnp.concatenate([none, back, rest], axis=0).astype(bf16),
    ]
    scaled = pack[0:FEAT]
    table = one_hot(pack[FEAT : FEAT + 1], TASKS)
    ones = jnp.ones((8, span), f32)
    terms = jnp.concatenate([scaled, ones, scaled * scaled], axis=0)
    t0, t1 = split(terms, 2)
    pad8 = jnp.zeros((8, span), f32)
    both = jnp.concatenate([t0, pad8, t1, pad8], axis=0).astype(bf16)
    heads = jnp.concatenate([t0, pad8], axis=0).astype(bf16)
    tables = table.astype(bf16)
    high = 32
    length_total = jnp.zeros((FEAT, 1), f32)
    task_total = jnp.zeros((TASKS, TASKS), f32)
    for m in range(blocks):
        at = slice(m * BS, (m + 1) * BS)
        sums = jnp.zeros((high, BS), f32)
        held_sums = [jnp.zeros((TASKS, BS), f32) for _ in mates]
        places = [(1, row, j + REACH) for row, j, _ in own_places(m)]
        places += [(2, row, j) for row, j, _ in halo_places(m) if j < REACH]
        for orders, row, block in places:
            hi_ref, lo_ref, sim_ref = kernel_refs[3 * orders - 3 : 3 * orders]
            j = slice(block * BS, (block + 1) * BS)
            rows_at = slice(row * BS, (row + 1) * BS)
            outers = [dot(near[j], mate[:, at]) for mate in mates[:orders]]
            kernel = hi_ref[m, rows_at, :].astype(f32) + lo_ref[m, rows_at, :].astype(f32)
            similar = sim_ref[m, rows_at, :]
            energy = sum(outers) * kernel
            e0, e1 = (part.astype(bf16) for part in split(energy, 2))
            first = dot(both[:, j], e0)
            sums = sums + first[:high] + first[high:] + dot(heads[:, j], e1)
            for k in range(orders):
                h0, h1 = (part.astype(bf16) for part in split(outers[k] * similar, 2))
                held_sums[k] = held_sums[k] + dot(tables[:, j], h0) + dot(tables[:, j], h1)
        mid = slice(width + m * BS, width + (m + 1) * BS)
        left = scaled[:, mid]
        value = left * left * sums[FEAT : FEAT + 1] + sums[2 * FEAT : 3 * FEAT]
        value = value - 2.0 * left * sums[:FEAT]
        length_total = length_total + jnp.sum(value, axis=1, keepdims=True)
        task_total = task_total + dot(held_sums[0], table[:, mid], NT, highest)
        task_total = task_total + dot(table[:, mid], held_sums[1], NT, highest)
    half = TASKS // 2
    value = jnp.concatenate(
        [
            task_total[:half],
            task_total[half:],
            jnp.where(iota((half, FEAT), 0) == iota((half, FEAT), 1), length_total, 0.0),
            jnp.zeros((half, LANES - 2 * TASKS - FEAT), f32),
        ],
        axis=1,
    )
    for c in range(grad_ref.shape[0]):
        grad_ref[c] = value


def tail_kernel(parts_ref, length_ref, task_ref):
    total = parts_ref[0]
    for c in range(1, parts_ref.shape[0]):
        total = total + parts_ref[c]
    half = TASKS // 2
    task_ref[0:half, :] = total[:, :TASKS]
    task_ref[half:, :] = total[:, TASKS : 2 * TASKS]
    length_ref[...] = jnp.sum(total[:, 2 * TASKS : 2 * TASKS + FEAT], axis=0)


MIB = 1024 * 1024


def call(body, outs, args, name, smem=0, hbm=0, far_outs=0, scratch=(), flops=0, limit=16):
    if hbm:
        args = args[:-hbm] + [pltpu.with_memory_space_constraint(a, pltpu.HBM) for a in args[-hbm:]]
    if far_outs:
        outs = outs[:-far_outs] + [pltpu.HBM(o.shape, o.dtype) for o in outs[-far_outs:]]
    vm = pl.BlockSpec(memory_space=pltpu.VMEM)
    sm = pl.BlockSpec(memory_space=pltpu.SMEM)
    far = pl.BlockSpec(memory_space=pltpu.HBM)
    return pl.pallas_call(
        body,
        out_shape=outs,
        in_specs=[sm] * smem + [vm] * (len(args) - smem - hbm) + [far] * hbm,
        out_specs=[vm] * (len(outs) - far_outs) + [far] * far_outs,
        scratch_shapes=scratch,
        compiler_params=pltpu.CompilerParams(vmem_limit_bytes=limit * MIB),
        cost_estimate=pl.CostEstimate(flops=flops, bytes_accessed=1 << 20, transcendentals=0),
        name=name,
    )(*args)


def both_sides(cells):
    count = lax.axis_size("pts")
    up = [(i, i + 1) for i in range(count - 1)]
    down = [(i + 1, i) for i in range(count - 1)]
    return lax.ppermute(cells, "pts", up), lax.ppermute(cells, "pts", down)


def from_left(cells):
    count = lax.axis_size("pts")
    return lax.ppermute(cells, "pts", [(i, i + 1) for i in range(count - 1)])


def shards(
    systems, features, task_ids, pattern, aggregate, coarse_inverse, task_cov, lengthscales, noise
):
    count, width = systems.shape
    blocks = width // BS
    coarse = coarse_inverse.shape[1]
    rows = count + coarse
    lanes = lanes_of(coarse)
    assert blocks == REACH
    place = lax.axis_index("pts").astype(jnp.int32)[None]
    probe = lax.axis_index("probe").astype(jnp.int32)[None]
    ranks = lax.axis_size("pts")
    sides = lax.axis_size("probe")

    def shape(*dims, kind=f32):
        return jax.ShapeDtypeStruct(dims, kind)

    jac, pack, extra = call(
        invert_kernel,
        [shape(3, blocks, BS, BS, kind=bf16), shape(SYS + count, width), shape(TASKS + FEAT, width)],
        [place, probe, features, task_ids, aggregate, systems, task_cov, coarse_inverse, pattern, lengthscales, noise],
        "invert",
        smem=2,
        hbm=9,
        scratch=[
            pltpu.VMEM((blocks, BS, BS), f32),
            pltpu.VMEM(features.shape, f32),
            pltpu.VMEM(task_ids.shape, jnp.int32),
            pltpu.VMEM(aggregate.shape, jnp.int32),
            pltpu.VMEM(systems.shape, f32),
            pltpu.VMEM(task_cov.shape, f32),
            pltpu.VMEM(coarse_inverse.shape, f32),
            pltpu.SMEM(pattern.shape, jnp.int32),
            pltpu.SMEM(lengthscales.shape, f32),
            pltpu.SMEM(noise.shape, f32),
            pltpu.SemaphoreType.DMA((9,)),
        ],
        flops=10**10,
    )
    pack_l, pack_r = both_sides(pack)

    def build(places, deep, cells, name):
        return call(
            functools.partial(build_kernel, places=places, sides=len(cells)),
            [
                shape(blocks, deep, BS, kind=bf16),
                shape(blocks, deep, BS, kind=bf16),
                shape(blocks, deep, BS),
            ],
            cells + [pack, extra],
            name,
            flops=10**9,
        )

    own_hi, own_lo, own_sim = build(own_places, width, [pack], "build_own")
    halo_hi, halo_lo, halo_sim = build(
        halo_places, BAND - width, [pack_l, pack_r], "build_halo"
    )
    kernel = [own_hi, own_lo, halo_hi, halo_lo]
    v0, d1 = call(
        first_kernel,
        [shape(rows, width), shape(rows, width)],
        [pack, pack_l, pack_r, extra] + kernel + [jac],
        "first",
        flops=10**9,
    )
    d1_l, d1_r = both_sides(d1)
    (early,) = call(
        early_moments_kernel, [shape(rows, lanes)], [pack, systems, d1, v0], "early", flops=10**9
    )
    v1, cargo = call(
        second_kernel,
        [shape(rows, width), shape(rows + count, width)],
        [extra, d1, d1_l, d1_r, early, systems] + kernel + [jac],
        "second",
        flops=10**9,
    )
    cargo_l = from_left(cargo)
    (late,) = call(
        functools.partial(late_moments_kernel, count=count),
        [shape(rows, lanes)],
        [early, d1, cargo, v1],
        "late",
        flops=10**9,
    )
    (gram,) = call(
        functools.partial(third_kernel, count=count, held=coarse_inverse.shape[0]),
        [shape(ranks, rows, lanes)],
        [extra, late, cargo, cargo_l] + kernel,
        "third",
        flops=10**9,
    )
    gram = lax.all_to_all(gram, "pts", 0, 0, tiled=True)
    cells = [own_hi, own_lo, own_sim, halo_hi, halo_lo, halo_sim]
    answer, grads = call(
        functools.partial(final_kernel, sides=sides * count, points=ranks * width),
        [shape(count, width), shape(ranks * sides, FEAT, LANES)],
        [gram, pack, pack_l, d1, d1_l, cargo, cargo_l] + cells,
        "final",
        flops=10**9,
    )
    grads = lax.all_to_all(grads, ("pts", "probe"), 0, 0, tiled=True)
    lengths, tasks = call(
        tail_kernel, [shape(FEAT), shape(TASKS, TASKS)], [grads], "tail", flops=10**5
    )
    return answer, lengths, tasks


def solution(mesh):
    return jax.shard_map(
        shards,
        mesh=mesh,
        in_specs=(
            P("probe", ("groups", "pts")),
            P(None, ("groups", "pts")),
            P(("groups", "pts")),
            P(("groups", "pts"), None),
            P(("groups", "pts")),
            P(("groups", "pts"), None),
            P("groups", None),
            P("groups"),
            P("groups"),
        ),
        out_specs=(P("probe", ("groups", "pts")), P("groups"), P("groups", None)),
        check_vma=False,
    )
```

```python
import functools

import jax
import jax.numpy as jnp
from jax import lax
from jax.experimental import pallas as pl
from jax.experimental.pallas import tpu as pltpu
from jax.sharding import PartitionSpec as P

BS = 256
REACH = 3
FEAT = 8
TASKS = 16
ITERS = 3
SLOTS = 2 * REACH + 1
BAND = SLOTS * BS
BASE = 32
GROUP = 4
LANES = 128
SYS = 2 * FEAT

highest = lax.Precision.HIGHEST
f32 = jnp.float32
bf16 = jnp.bfloat16
NN = (((1,), (0,)), ((), ()))
NT = (((1,), (1,)), ((), ()))
TN = (((0,), (0,)), ((), ()))


def dot(a, b, dims=NN, precision=None):
    return lax.dot_general(a, b, dims, precision=precision, preferred_element_type=f32)


def iota(shape, dim):
    return lax.broadcasted_iota(jnp.int32, shape, dim)


def split(x, parts):
    out = []
    for _ in range(parts - 1):
        head = x.astype(bf16).astype(f32)
        out.append(head)
        x = x - head
    out.append(x.astype(bf16).astype(f32))
    return out


def column(ref, size):
    rows = iota((size, 1), 0)
    out = jnp.zeros((size, 1), f32)
    for i in range(size):
        out = jnp.where(rows == i, ref[i], out)
    return out


def one_hot(ids, size):
    return (iota((size, ids.shape[1]), 0).astype(f32) == ids).astype(f32)


def noise_row(noise_ref, ids):
    out = jnp.zeros(ids.shape, f32)
    for t in range(TASKS):
        out = jnp.where(ids == float(t), noise_ref[t], out)
    return out


def weight(pat_ref, block, offset):
    if offset != REACH:
        return pat_ref[block, offset].astype(f32)
    total = pat_ref[block, 0]
    for o in range(1, SLOTS):
        total = total + pat_ref[block, o]
    return total.astype(f32)


def near_stack(scaled, table):
    s0, s1, s2 = split(scaled, 3)
    n0, n1, n2 = split(-0.5 * jnp.sum(scaled * scaled, axis=0, keepdims=True), 3)
    rows = iota(scaled.shape, 0)
    norms = jnp.where(rows == 0, n0, jnp.where(rows == 1, n1, jnp.where(rows == 2, n2, 0.0)))
    pad = jnp.zeros((LANES - 7 * FEAT - 3 * TASKS, scaled.shape[1]), f32)
    stack = jnp.concatenate([s0, s0, s1, s1, s0, s2, norms, table, table, table, pad], axis=0)
    return stack.T.astype(bf16)


def own_stack(scaled, picked):
    s0, s1, s2 = split(scaled, 3)
    rows = iota(scaled.shape, 0)
    ones = jnp.where(rows < 3, 1.0, 0.0)
    count = scaled.shape[1]
    tail = LANES - 7 * FEAT - 3 * TASKS
    left = jnp.concatenate(
        [s0, s1, s0, s1, s2, s0, ones, jnp.zeros((3 * TASKS + tail, count), f32)], axis=0
    ).astype(bf16)
    right = jnp.concatenate(
        [jnp.zeros((7 * FEAT, count), f32)] + split(picked, 3) + [jnp.zeros((tail, count), f32)],
        axis=0,
    ).astype(bf16)
    sides = [
        jnp.concatenate([left[:, i : i + BS], right[:, i : i + BS]], axis=1)
        for i in range(0, count, BS)
    ]
    return sides, -0.5 * jnp.sum(scaled * scaled, axis=0, keepdims=True)


def small_inverse(p):
    n = len(p)
    if n == 1:
        return [[pltpu.reciprocal(p[0][0], approx=True)]]
    if n == 2:
        a, b, d = p[0][0], p[0][1], p[1][1]
        r = pltpu.reciprocal(a * d - b * b, approx=True)
        off = -b * r
        return [[d * r, off], [off, a * r]]
    h = n // 2
    ainv = small_inverse([row[:h] for row in p[:h]])
    b = [row[h:] for row in p[:h]]
    t = [[sum(ainv[i][k] * b[k][j] for k in range(h)) for j in range(h)] for i in range(h)]
    s = [[None] * h for _ in range(h)]
    for i in range(h):
        for j in range(i, h):
            s[i][j] = s[j][i] = p[h + i][h + j] - sum(b[k][i] * t[k][j] for k in range(h))
    sinv = small_inverse(s)
    u = [[sum(t[i][k] * sinv[k][j] for k in range(h)) for j in range(h)] for i in range(h)]
    out = [[None] * n for _ in range(n)]
    for i in range(h):
        for j in range(h):
            out[h + i][h + j] = sinv[i][j]
            out[i][h + j] = out[h + j][i] = -u[i][j]
    for i in range(h):
        for j in range(i, h):
            out[i][j] = out[j][i] = ainv[i][j] + sum(u[i][k] * t[j][k] for k in range(h))
    return out


def sweep_base(cells, beside):
    tall = range(BASE // 8)
    tiles = [cells[8 * i : 8 * i + 8] for i in tall]
    lane = iota((8, LANES), 1)
    start = lane - lane % BASE
    inner = lane % BASE
    sub = iota((8, LANES), 0)

    def columns(first):
        return [
            [
                jnp.take_along_axis(tile, start + (first + t), axis=1, mode="promise_in_bounds")
                for tile in tiles
            ]
            for t in range(GROUP)
        ]

    def row(parts, r):
        return jnp.broadcast_to(parts[r // 8][r % 8 : r % 8 + 1, :], (8, LANES))

    def with_rows(parts, first, rows):
        part = parts[first // 8]
        for t, value in enumerate(rows):
            part = jnp.where(sub == first % 8 + t, value, part)
        return [part if i == first // 8 else parts[i] for i in tall]

    def less(parts, cols, factor):
        out = []
        for i in tall:
            part = parts[i]
            for t in range(GROUP):
                part = part - cols[t][i] * factor[t]
            out.append(part)
        return out

    def symmetric(entry):
        out = [[None] * GROUP for _ in range(GROUP)]
        for t in range(GROUP):
            for u in range(t, GROUP):
                out[t][u] = out[u][t] = entry(t, u)
        return out

    cols, ahead = columns(0), columns(GROUP)
    pivots = symmetric(lambda t, u: row(cols[u], t))
    for first in range(0, BASE, GROUP):
        then = first + GROUP
        far = columns(first + 2 * GROUP) if first + 2 * GROUP < BASE else []
        heads = [[row(col, first + t) for t in range(GROUP)] for col in ahead + far]
        inv = small_inverse(pivots)
        factors = [
            [sum(inv[t][u] * head[u] for u in range(GROUP)) for t in range(GROUP)]
            for head in heads
        ]
        if ahead:
            pivots = symmetric(
                lambda t, u: row(ahead[u], then + t)
                - sum(heads[t][i] * factors[u][i] for i in range(GROUP))
            )
        coming = [
            with_rows(less(col, cols, factor), first, factor)
            for col, factor in zip(ahead + far, factors)
        ]
        group = (inner >= first) & (inner < first + GROUP)
        rows = []
        for t in range(GROUP):
            value = jnp.where(group, 0.0, row(tiles, first + t))
            rows.append(jnp.where(inner == first + t, -1.0, value))
        new = [sum(inv[t][u] * rows[u] for u in range(GROUP)) for t in range(GROUP)]
        tiles = [jnp.where(group, 0.0, tile) for tile in tiles]
        tiles = with_rows(less(tiles, cols, new), first, new)
        cols, ahead = coming[:GROUP], coming[GROUP:]
        if beside:
            beside.pop(0)()
    while beside:
        beside.pop(0)()
    return jnp.concatenate(tiles, axis=0)


def fetch(pairs, sems):
    copies = [pltpu.make_async_copy(a, b, sems.at[i]) for i, (a, b) in enumerate(pairs)]
    for copy in copies:
        copy.start()
    return copies


def invert_kernel(
    place_ref, probe_ref, feat_hbm, ids_hbm, agg_hbm, sys_hbm, cov_hbm, coarse_hbm, pat_hbm, len_hbm, noise_hbm,
    jac_ref, pack_ref, extra_ref,
    work, feat_ref, ids_ref, agg_ref, sys_ref, cov_ref, coarse_ref, pat_ref, len_ref, noise_ref, sems,
):
    blocks = work.shape[0]
    width = blocks * BS
    pairs = [
        (feat_hbm, feat_ref), (ids_hbm, ids_ref), (agg_hbm, agg_ref), (cov_hbm, cov_ref),
        (pat_hbm, pat_ref), (len_hbm, len_ref), (noise_hbm, noise_ref), (coarse_hbm, coarse_ref),
        (sys_hbm, sys_ref),
    ]
    for copy in fetch(pairs, sems):
        copy.wait()
    scaled = feat_ref[...] / column(len_ref, FEAT)
    ids = ids_ref[...].astype(f32).reshape(1, width)
    which = agg_ref[...].astype(f32).reshape(1, width)
    table = one_hot(ids, TASKS)
    noise = noise_row(noise_ref, ids)
    c0, c1, c2 = split(cov_ref[...], 3)
    tab = table.astype(bf16)
    picked = (dot(c2.astype(bf16), tab) + dot(c1.astype(bf16), tab)) + dot(c0.astype(bf16), tab)
    rows = iota((FEAT, width), 0)
    weights = jnp.zeros((1, width), f32)
    places = iota((1, width), 1)
    for m in range(blocks):
        for o in range(SLOTS):
            weights = jnp.where(places == m * SLOTS + o, weight(pat_ref, m, o), weights)
    pack_ref[0:FEAT, :] = scaled
    pack_ref[FEAT : 2 * FEAT, :] = jnp.where(
        rows == 0,
        ids,
        jnp.where(rows == 1, which, jnp.where(rows == 2, probe_ref[0].astype(f32), 0.0)),
    )
    extra_ref[0:TASKS, :] = picked
    tail = jnp.where(rows == 0, noise, jnp.where(rows == 1, weights, 0.0))
    held = coarse_ref.shape[0]
    inverse = jnp.concatenate(
        [coarse_ref[...], jnp.zeros((held, width - coarse_ref.shape[1]), f32)], axis=1
    )
    tail = jnp.where(rows == 2, place_ref[0].astype(f32), tail)
    for r in range(held):
        tail = jnp.where(rows == 3 + r, inverse[r : r + 1], tail)
    extra_ref[TASKS : TASKS + FEAT, :] = tail
    near = near_stack(scaled, table)
    mates, norm = own_stack(scaled, picked)
    eye = iota((BS, BS), 0) == iota((BS, BS), 1)
    for m in range(blocks):
        at = slice(m * BS, (m + 1) * BS)
        both = dot(near[at], mates[m])
        block = weight(pat_ref, m, REACH) * jnp.exp(both[:, :BS] + norm[:, at]) * both[:, BS:]
        work[m] = block + jnp.where(eye, noise[:, at], 0.0)
    seg = iota((BASE, LANES), 1) // BASE
    wide = iota((BASE, BS), 1)
    deep = iota((BASE, BS), 0)

    def packed(strips, first):
        tile, inside = first // LANES, first % LANES
        cells = jnp.zeros((BASE, LANES), f32)
        for m in range(blocks):
            piece = strips[m][:, tile * LANES : (tile + 1) * LANES]
            shift = (BASE * m - inside) % LANES
            if shift:
                piece = pltpu.roll(piece, shift, axis=1)
            cells = jnp.where(seg == m, piece, cells)
        return cells

    def diagonal(cells):
        parts = [jnp.where(seg == m, cells, 0.0) for m in range(LANES // BASE)]
        return jnp.concatenate(parts, axis=0)

    eye = jnp.where(iota((BASE, LANES), 1) % BASE == iota((BASE, LANES), 0), 1.0, 0.0)

    def updates(first, inv, strips):
        state = {}

        def product():
            held = (wide >= first) & (wide < first + BASE)
            minus = jnp.where(wide - first == deep, -1.0, 0.0)
            stack = jnp.concatenate(
                [jnp.where(held, minus, s) for s in strips]
                + [jnp.zeros((LANES - blocks * BASE, BS), f32)],
                axis=0,
            )
            spread = diagonal(inv)[: blocks * BASE]
            new = dot(spread, stack, precision=highest)
            for m in range(blocks):
                state[m] = new[m * BASE : (m + 1) * BASE, :]

        def rows_of(m, low, high):
            def piece():
                r0, r1, r2 = split(strips[m][:, low:high], 3)
                p0, p1, p2 = split(state[m], 3)
                a = jnp.concatenate([r0, r0, r1, r1, r0, r2], axis=0).astype(bf16)
                b = jnp.concatenate([p0, p1, p0, p1, p2, p0], axis=0).astype(bf16)
                gone = (iota((1, BS), 1) >= first) & (iota((1, BS), 1) < first + BASE)
                work[m, low:high, :] = jnp.where(gone, 0.0, work[m, low:high, :]) - dot(a, b, TN)
                if low <= first < high:
                    work[m, first : first + BASE, :] = state[m]

            return piece

        half = BS // 2
        return [product] + [
            rows_of(m, low, low + half) for m in range(blocks) for low in range(0, BS, half)
        ]

    def strips_at(first):
        return [work[m, first : first + BASE, :] for m in range(blocks)]

    cells = jnp.where(seg < blocks, packed(strips_at(0), 0), eye)
    pending = []
    for first in range(0, BS, BASE):
        inv = -sweep_base(cells, pending)
        strips = strips_at(first)
        if first + BASE < BS:
            after = strips_at(first + BASE)
            half = dot(inv, diagonal(packed(strips, first + BASE)), precision=highest)
            drop = dot(packed(after, first), diagonal(half), precision=highest)
            cells = jnp.where(seg < blocks, packed(after, first + BASE) - drop, eye)
        pending = updates(first, inv, strips)
    for piece in pending:
        piece()
    for m in range(blocks):
        inv = -work[m]
        for i, part in enumerate(split(inv, 3)):
            jac_ref[i, m] = part.astype(bf16)
    pack_ref[SYS:, :] = smooth(sys_ref[...], jac_ref)


def own_places(m):
    return [(j, j, REACH + j - m) for j in range(REACH)]


def halo_places(m):
    lefts = [(j - m, j, j - m) for j in range(m, REACH)]
    return lefts + [(REACH - m + j, REACH + j, 2 * REACH - m + j) for j in range(m + 1)]


def build_kernel(*refs, places, sides):
    cells, (own_ref, extra_ref) = refs[:sides], refs[sides : sides + 2]
    hi_ref, lo_ref, sim_ref = refs[sides + 2 :]
    blocks = hi_ref.shape[0]
    near = []
    for ref in cells:
        near.append(near_stack(ref[0:FEAT, :], one_hot(ref[FEAT : FEAT + 1, :], TASKS)))
    mates, norm = own_stack(own_ref[0:FEAT, :], extra_ref[0:TASKS, :])
    weights = extra_ref[TASKS + 1 : TASKS + 2, :]
    for m in range(blocks):
        for row, j, o in places(m):
            part = near[j // REACH][(j % REACH) * BS : (j % REACH + 1) * BS]
            both = dot(part, mates[m])
            place = m * SLOTS + o
            exponent = both[:, :BS] + norm[:, m * BS : (m + 1) * BS]
            similar = weights[:, place : place + 1] * jnp.exp(exponent)
            kernel = similar * both[:, BS:]
            head = kernel.astype(bf16)
            rows = slice(row * BS, (row + 1) * BS)
            if o <= REACH or sides == 1:
                sim_ref[m, rows, :] = similar
            hi_ref[m, rows, :] = head
            lo_ref[m, rows, :] = (kernel - head.astype(f32)).astype(bf16)


def pieces(vectors):
    return jnp.concatenate(split(vectors, 2), axis=0).astype(bf16)


def apply(cells, hi, lo):
    rows = cells.shape[0] // 2
    first = dot(cells, hi)
    return first[:rows] + first[rows:] + dot(cells[:rows], lo)


def operate_own(own, noise, own_hi, own_lo):
    mine = pieces(own)
    out = [apply(mine, own_hi[m], own_lo[m]) for m in range(REACH)]
    return jnp.concatenate(out, axis=1) + noise * own


def operate_left(left, halo_hi, halo_lo):
    cells = pieces(left)
    out = []
    for m in range(REACH):
        part = slice(0, (REACH - m) * BS)
        out.append(apply(cells[:, m * BS :], halo_hi[m, part, :], halo_lo[m, part, :]))
    return jnp.concatenate(out, axis=1)


def operate(own, left, right, noise, own_hi, own_lo, halo_hi, halo_lo):
    lefts, rights = pieces(left), pieces(right)
    out = []
    for m in range(REACH):
        beyond = jnp.concatenate([lefts[:, m * BS :], rights[:, : (m + 1) * BS]], axis=1)
        out.append(apply(beyond, halo_hi[m], halo_lo[m]))
    return operate_own(own, noise, own_hi, own_lo) + jnp.concatenate(out, axis=1)


def smooth(image, jac_ref):
    rows = image.shape[0]
    out = []
    for m in range(jac_ref.shape[1]):
        pieces = jnp.concatenate(split(image[:, m * BS : (m + 1) * BS], 3), axis=0).astype(bf16)
        a = dot(pieces, jac_ref[0, m])
        b = dot(pieces[: 2 * rows], jac_ref[1, m])
        c = dot(pieces[:rows], jac_ref[2, m])
        out.append(a[:rows] + (a[rows : 2 * rows] + b[:rows] + (a[2 * rows :] + b[rows:] + c)))
    return jnp.concatenate(out, axis=1)


def first_kernel(own_ref, left_ref, right_ref, extra_ref, *refs):
    kernel, (jac_ref, image_ref, next_ref) = refs[:4], refs[4:]
    count = own_ref.shape[0] - SYS
    coarse = image_ref.shape[0] - count

    def basis(ref):
        z = one_hot(ref[FEAT + 1 : FEAT + 2, :], coarse)
        return jnp.concatenate([ref[SYS:, :], z], axis=0)

    noise = extra_ref[TASKS : TASKS + 1, :]
    image = operate(basis(own_ref), basis(left_ref), basis(right_ref), noise, *kernel)
    image_ref[...] = image
    next_ref[...] = smooth(image, jac_ref)


def second_kernel(extra_ref, vec_ref, left_ref, right_ref, early_ref, sys_ref, *refs):
    kernel, (jac_ref, image_ref, cargo_ref) = refs[:4], refs[4:]
    rows = vec_ref.shape[0]
    noise = extra_ref[TASKS : TASKS + 1, :]
    image = operate(vec_ref[...], left_ref[...], right_ref[...], noise, *kernel)
    image_ref[...] = image
    cargo_ref[0:rows, :] = smooth(image, jac_ref)
    cargo_ref[rows:, :] = sys_ref[...]


def pitch_of(coarse):
    return coarse + 1


def lanes_of(coarse):
    return -(-5 * pitch_of(coarse) // LANES) * LANES


def moment(vectors, images, pairs):
    count = pairs.shape[0]
    table = dot(images, vectors, NT, lax.Precision.HIGH)
    own = jnp.sum(pairs, axis=1, keepdims=True)
    if images.shape[0] > count:
        own = jnp.concatenate([own, jnp.zeros((images.shape[0] - count, 1), f32)], axis=0)
    return jnp.concatenate([table, own], axis=1)


def spread_out(parts, lanes):
    rows, pitch = next(iter(parts.values())).shape
    cells = [parts.get(k, jnp.zeros((rows, pitch), f32)) for k in range(5)]
    if lanes > 5 * pitch:
        cells.append(jnp.zeros((rows, lanes - 5 * pitch), f32))
    return jnp.concatenate(cells, axis=1)


def folded(low, high):
    order = low.shape[0]
    row, col = iota((order, order), 0), iota((order, order), 1)
    diagonal = jnp.sum(jnp.where(row == col, high, 0.0), axis=1, keepdims=True)
    return jnp.concatenate([jnp.where(row >= col, low, high), diagonal], axis=1)


def unfolded(cells):
    order = cells.shape[0]
    row, col = iota((order, order), 0), iota((order, order), 1)
    square = cells[:, :order]
    turned = dot(square, jnp.where(row == col, 1.0, 0.0), TN, highest)
    low = jnp.where(row >= col, square, turned)
    high = jnp.where(row < col, square, jnp.where(row > col, turned, cells[:, order:]))
    return low, high


def early_moments_kernel(own_ref, sys_ref, d1_ref, v0_ref, out_ref):
    count = own_ref.shape[0] - SYS
    coarse = d1_ref.shape[0] - count
    lanes = out_ref.shape[1]
    pitch = pitch_of(coarse)
    systems = sys_ref[...]
    pre = own_ref[SYS:, :]
    z = one_hot(own_ref[FEAT + 1 : FEAT + 2, :], coarse)
    d1, v0 = d1_ref[...], v0_ref[...]
    m0 = moment(z, v0, pre * v0[:count])
    m1 = moment(d1[count:], v0, d1[:count] * v0[:count])
    out_ref[0:count, :] = spread_out({0: m0[:count], 1: m1[:count]}, lanes)
    start = moment(z, systems, systems * pre)
    if coarse > count:
        start = jnp.concatenate([start, jnp.zeros((coarse - count, pitch), f32)], axis=0)
    fold = folded(m0[count:, :coarse], m1[count:, :coarse])
    out_ref[count:, :] = spread_out({0: fold, 3: start}, lanes)


def late_moments_kernel(before_ref, d1_ref, cargo_ref, v1_ref, out_ref, *, count):
    lanes = out_ref.shape[1]
    d1, d2, v1 = d1_ref[...], cargo_ref[0 : d1_ref.shape[0], :], v1_ref[...]
    coarse = d1.shape[0] - count
    m2 = moment(d1[count:], v1, d1[:count] * v1[:count])
    m3 = moment(d2[count:], v1, d2[:count] * v1[:count])
    out_ref[0:count, :] = before_ref[0:count, :] + spread_out({2: m2[:count], 3: m3[:count]}, lanes)
    fold = folded(m2[count:, :coarse], m3[count:, :coarse])
    out_ref[count:, :] = before_ref[count:, :] + spread_out({1: fold}, lanes)


def third_kernel(
    extra_ref, before_ref, cargo_ref, left_ref, *refs, count, held
):
    kernel, out_ref = refs[:4], refs[4]
    rows = cargo_ref.shape[0] - count
    coarse = rows - count
    lanes = out_ref.shape[2]
    pitch = pitch_of(coarse)
    d2 = cargo_ref[0:rows, :]
    noise = extra_ref[TASKS : TASKS + 1, :]
    inner = operate_own(d2, noise, *kernel[:2])
    cross = operate_left(left_ref[0:rows, :], *kernel[2:])
    m4 = moment(d2[count:], inner + cross, d2[:count] * (inner + 2.0 * cross)[:count])
    mirror = dot(d2, cross[count:], NT, lax.Precision.HIGH)
    m4 = m4 + jnp.concatenate([mirror, jnp.zeros((rows, 1), f32)], axis=1)
    row = iota((coarse, 1), 0).astype(f32)
    start = extra_ref[TASKS + 2 : TASKS + 3, 0:1] * held
    inverse = jnp.zeros((coarse, pitch), f32)
    for r in range(held):
        line = extra_ref[TASKS + 3 + r : TASKS + 4 + r, 0:pitch]
        inverse = jnp.where(row == start + r, line, inverse)
    top = before_ref[0:count, :] + spread_out({4: m4[:count]}, lanes)
    bottom = before_ref[count:, :] + spread_out({2: m4[count:], 4: inverse}, lanes)
    for c in range(out_ref.shape[0]):
        out_ref[c, 0:count, :] = top
        out_ref[c, count:, :] = bottom


def final_kernel(
    gram_ref, own_ref, left_ref, d1_ref, d1l_ref, cargo_ref, cargol_ref, *refs, sides, points,
):
    kernel_refs, (sol_ref, grad_ref) = refs[:6], refs[6:]
    width = own_ref.shape[1]
    count = own_ref.shape[0] - SYS
    rows = d1_ref.shape[0]
    coarse = rows - count
    pitch = pitch_of(coarse)
    wide = -(-3 * pitch // LANES) * LANES
    blocks = width // BS
    gram = gram_ref[0]
    for c in range(1, gram_ref.shape[0]):
        gram = gram + gram_ref[c]
    bottom = gram[count:]
    gram = jnp.concatenate([gram[:count], jnp.zeros((count, wide), f32)], axis=1)
    squares = list(unfolded(bottom[:, :pitch])) + list(unfolded(bottom[:, pitch : 2 * pitch]))
    squares.append(bottom[:, 2 * pitch : 2 * pitch + coarse])
    lane = iota((1, wide), 1)
    slot, inside = lane // pitch, lane % pitch
    live = lane < 3 * pitch
    is_vec = live & (inside < coarse)
    is_one = live & (inside == coarse)

    def shifted(j):
        return jnp.where(live, gram[:, j * pitch : j * pitch + wide], 0.0)

    own = [shifted(j) for j in range(3)]
    gap = jnp.zeros((coarse, 1), f32)
    rest = jnp.zeros((coarse, wide - 3 * pitch), f32)
    hankel = []
    for i in range(3):
        line = [squares[i], gap, squares[i + 1], gap, squares[i + 2], gap]
        hankel.append(jnp.concatenate(line + ([rest] if wide > 3 * pitch else []), axis=1))
        hankel.append(jnp.zeros((1, wide), f32))
    if wide > 3 * pitch:
        hankel.append(jnp.zeros((wide - 3 * pitch, wide), f32))
    hankel = jnp.concatenate(hankel, axis=0)
    block0 = lane < pitch
    inverse = bottom[:, 4 * pitch : 4 * pitch + coarse]
    inverse = jnp.concatenate([inverse, jnp.zeros((coarse, wide - coarse), f32)], axis=1)
    inverse = jnp.concatenate([inverse, jnp.zeros((wide - coarse, wide), f32)], axis=0)
    start = bottom[:count, 3 * pitch : 4 * pitch]
    start = jnp.concatenate([start, jnp.zeros((count, wide - pitch), f32)], axis=1)
    against = jnp.where(
        block0, start, jnp.where(live, pltpu.roll(jnp.where(live, own[0], 0.0), pitch, axis=1), 0.0)
    )

    def total(x):
        return jnp.sum(x, axis=1, keepdims=True)

    def scalars(u, i):
        return total(jnp.where(lane == i * pitch + coarse, u, 0.0))

    def metric(u):
        out = dot(jnp.where(is_vec, u, 0.0), hankel, precision=highest)
        for j in range(3):
            out = out + scalars(u, j) * own[j]
        out = jnp.where(is_vec, out, 0.0)
        for i in range(3):
            out = jnp.where(lane == i * pitch + coarse, total(u * own[i]), out)
        return out

    def corrected(w):
        return dot(jnp.where(lane < coarse, w, 0.0), inverse, precision=highest)

    pre = corrected(against) + jnp.where(lane == coarse, 1.0, 0.0)
    direction = pre
    gamma = total(pre * against)
    answer = jnp.zeros_like(pre)
    image_sum = jnp.zeros_like(pre)
    for step in range(ITERS):
        image = metric(direction)
        alpha = gamma / total(direction * image)
        answer = answer + alpha * direction
        if step + 1 < ITERS:
            image_sum = image_sum + alpha * image
            moved_on = jnp.where(live & (slot > 0), pltpu.roll(direction, pitch, axis=1), 0.0)
            pre = pre - alpha * (moved_on + corrected(image))
            gamma_new = total(pre * (against - image_sum))
            direction = pre + (gamma_new / gamma) * direction
            gamma = gamma_new

    pack = jnp.concatenate([left_ref[...], own_ref[...]], axis=1)
    z = one_hot(pack[FEAT + 1 : FEAT + 2], coarse)
    q0 = pack[SYS:]
    d1 = jnp.concatenate([d1l_ref[...], d1_ref[...]], axis=1)
    cargo = jnp.concatenate([cargol_ref[...], cargo_ref[...]], axis=1)
    d2 = cargo[:rows]
    span = q0.shape[1]
    step = -(-coarse // FEAT) * FEAT
    deep = -(-3 * step // LANES) * LANES
    parts, basis = [], []
    for i, rest in enumerate((z, d1[count:], d2[count:])):
        parts.append(answer[:, i * pitch : i * pitch + coarse])
        basis.append(rest)
        if step > coarse:
            parts.append(jnp.zeros((count, step - coarse), f32))
            basis.append(jnp.zeros((step - coarse, span), f32))
    if deep > 3 * step:
        parts.append(jnp.zeros((count, deep - 3 * step), f32))
        basis.append(jnp.zeros((deep - 3 * step, span), f32))
    x = dot(
        jnp.concatenate(parts, axis=1), jnp.concatenate(basis, axis=0), precision=highest
    )
    x = x + scalars(answer, 0) * q0 + scalars(answer, 1) * d1[:count]
    x = x + scalars(answer, 2) * d2[:count]
    mine = slice(width, 2 * width)
    sol_ref[...] = x[:, mine]

    probe = own_ref[FEAT + 2 : FEAT + 3, 0:1]
    line = iota((count, 1), 0).astype(f32) + probe * count
    right = jnp.where(line == 0, x, cargo[rows:])
    coef = jnp.where(line == 0, 0.5 / points, -0.5 / (sides - 1) / points)
    r0, r1 = split(right, 2)
    w0, w1 = split(x * coef, 2)
    rest = jnp.zeros((LANES - 6 * count, span), f32)
    near = jnp.concatenate([w0, w1, w0, r0, r1, r0, rest], axis=0).T.astype(bf16)
    none = jnp.zeros((3 * count, width), f32)
    rest = rest[:, mine]
    ahead = jnp.concatenate([r0, r0, r1], axis=0)[:, mine]
    back = jnp.concatenate([w0, w0, w1], axis=0)[:, mine]
    mates = [
        jnp.concatenate([ahead, none, rest], axis=0).astype(bf16),
        jnp.concatenate([none, back, rest], axis=0).astype(bf16),
    ]
    scaled = pack[0:FEAT]
    table = one_hot(pack[FEAT : FEAT + 1], TASKS)
    ones = jnp.ones((8, span), f32)
    terms = jnp.concatenate([scaled, ones, scaled * scaled], axis=0)
    t0, t1 = split(terms, 2)
    pad8 = jnp.zeros((8, span), f32)
    both = jnp.concatenate([t0, pad8, t1, pad8], axis=0).astype(bf16)
    heads = jnp.concatenate([t0, pad8], axis=0).astype(bf16)
    tables = table.astype(bf16)
    high = 32
    length_total = jnp.zeros((FEAT, 1), f32)
    task_total = jnp.zeros((TASKS, TASKS), f32)
    for m in range(blocks):
        at = slice(m * BS, (m + 1) * BS)
        sums = jnp.zeros((high, BS), f32)
        held_sums = [jnp.zeros((TASKS, BS), f32) for _ in mates]
        places = [(1, row, j + REACH) for row, j, _ in own_places(m)]
        places += [(2, row, j) for row, j, _ in halo_places(m) if j < REACH]
        for orders, row, block in places:
            hi_ref, lo_ref, sim_ref = kernel_refs[3 * orders - 3 : 3 * orders]
            j = slice(block * BS, (block + 1) * BS)
            rows_at = slice(row * BS, (row + 1) * BS)
            outers = [dot(near[j], mate[:, at]) for mate in mates[:orders]]
            kernel = hi_ref[m, rows_at, :].astype(f32) + lo_ref[m, rows_at, :].astype(f32)
            similar = sim_ref[m, rows_at, :]
            energy = sum(outers) * kernel
            e0, e1 = (part.astype(bf16) for part in split(energy, 2))
            first = dot(both[:, j], e0)
            sums = sums + first[:high] + first[high:] + dot(heads[:, j], e1)
            for k in range(orders):
                h0, h1 = (part.astype(bf16) for part in split(outers[k] * similar, 2))
                held_sums[k] = held_sums[k] + dot(tables[:, j], h0) + dot(tables[:, j], h1)
        mid = slice(width + m * BS, width + (m + 1) * BS)
        left = scaled[:, mid]
        value = left * left * sums[FEAT : FEAT + 1] + sums[2 * FEAT : 3 * FEAT]
        value = value - 2.0 * left * sums[:FEAT]
        length_total = length_total + jnp.sum(value, axis=1, keepdims=True)
        task_total = task_total + dot(held_sums[0], table[:, mid], NT, highest)
        task_total = task_total + dot(table[:, mid], held_sums[1], NT, highest)
    half = TASKS // 2
    value = jnp.concatenate(
        [
            task_total[:half],
            task_total[half:],
            jnp.where(iota((half, FEAT), 0) == iota((half, FEAT), 1), length_total, 0.0),
            jnp.zeros((half, LANES - 2 * TASKS - FEAT), f32),
        ],
        axis=1,
    )
    for c in range(grad_ref.shape[0]):
        grad_ref[c] = value


def tail_kernel(parts_ref, length_ref, task_ref):
    total = parts_ref[0]
    for c in range(1, parts_ref.shape[0]):
        total = total + parts_ref[c]
    half = TASKS // 2
    task_ref[0:half, :] = total[:, :TASKS]
    task_ref[half:, :] = total[:, TASKS : 2 * TASKS]
    length_ref[...] = jnp.sum(total[:, 2 * TASKS : 2 * TASKS + FEAT], axis=0)


MIB = 1024 * 1024


def call(body, outs, args, name, smem=0, hbm=0, far_outs=0, scratch=(), flops=0, limit=16):
    if hbm:
        args = args[:-hbm] + [pltpu.with_memory_space_constraint(a, pltpu.HBM) for a in args[-hbm:]]
    if far_outs:
        outs = outs[:-far_outs] + [pltpu.HBM(o.shape, o.dtype) for o in outs[-far_outs:]]
    vm = pl.BlockSpec(memory_space=pltpu.VMEM)
    sm = pl.BlockSpec(memory_space=pltpu.SMEM)
    far = pl.BlockSpec(memory_space=pltpu.HBM)
    return pl.pallas_call(
        body,
        out_shape=outs,
        in_specs=[sm] * smem + [vm] * (len(args) - smem - hbm) + [far] * hbm,
        out_specs=[vm] * (len(outs) - far_outs) + [far] * far_outs,
        scratch_shapes=scratch,
        compiler_params=pltpu.CompilerParams(vmem_limit_bytes=limit * MIB),
        cost_estimate=pl.CostEstimate(flops=flops, bytes_accessed=1 << 20, transcendentals=0),
        name=name,
    )(*args)


def both_sides(cells):
    count = lax.axis_size("pts")
    up = [(i, i + 1) for i in range(count - 1)]
    down = [(i + 1, i) for i in range(count - 1)]
    return lax.ppermute(cells, "pts", up), lax.ppermute(cells, "pts", down)


def from_left(cells):
    count = lax.axis_size("pts")
    return lax.ppermute(cells, "pts", [(i, i + 1) for i in range(count - 1)])


def shards(
    systems, features, task_ids, pattern, aggregate, coarse_inverse, task_cov, lengthscales, noise
):
    count, width = systems.shape
    blocks = width // BS
    coarse = coarse_inverse.shape[1]
    rows = count + coarse
    lanes = lanes_of(coarse)
    assert blocks == REACH
    place = lax.axis_index("pts").astype(jnp.int32)[None]
    probe = lax.axis_index("probe").astype(jnp.int32)[None]
    ranks = lax.axis_size("pts")
    sides = lax.axis_size("probe")

    def shape(*dims, kind=f32):
        return jax.ShapeDtypeStruct(dims, kind)

    jac, pack, extra = call(
        invert_kernel,
        [shape(3, blocks, BS, BS, kind=bf16), shape(SYS + count, width), shape(TASKS + FEAT, width)],
        [place, probe, features, task_ids, aggregate, systems, task_cov, coarse_inverse, pattern, lengthscales, noise],
        "invert",
        smem=2,
        hbm=9,
        scratch=[
            pltpu.VMEM((blocks, BS, BS), f32),
            pltpu.VMEM(features.shape, f32),
            pltpu.VMEM(task_ids.shape, jnp.int32),
            pltpu.VMEM(aggregate.shape, jnp.int32),
            pltpu.VMEM(systems.shape, f32),
            pltpu.VMEM(task_cov.shape, f32),
            pltpu.VMEM(coarse_inverse.shape, f32),
            pltpu.SMEM(pattern.shape, jnp.int32),
            pltpu.SMEM(lengthscales.shape, f32),
            pltpu.SMEM(noise.shape, f32),
            pltpu.SemaphoreType.DMA((9,)),
        ],
        flops=10**10,
    )
    pack_l, pack_r = both_sides(pack)

    def build(places, deep, cells, name):
        return call(
            functools.partial(build_kernel, places=places, sides=len(cells)),
            [
                shape(blocks, deep, BS, kind=bf16),
                shape(blocks, deep, BS, kind=bf16),
                shape(blocks, deep, BS),
            ],
            cells + [pack, extra],
            name,
            flops=10**9,
        )

    own_hi, own_lo, own_sim = build(own_places, width, [pack], "build_own")
    halo_hi, halo_lo, halo_sim = build(
        halo_places, BAND - width, [pack_l, pack_r], "build_halo"
    )
    kernel = [own_hi, own_lo, halo_hi, halo_lo]
    v0, d1 = call(
        first_kernel,
        [shape(rows, width), shape(rows, width)],
        [pack, pack_l, pack_r, extra] + kernel + [jac],
        "first",
        flops=10**9,
    )
    d1_l, d1_r = both_sides(d1)
    (early,) = call(
        early_moments_kernel, [shape(rows, lanes)], [pack, systems, d1, v0], "early", flops=10**9
    )
    v1, cargo = call(
        second_kernel,
        [shape(rows, width), shape(rows + count, width)],
        [extra, d1, d1_l, d1_r, early, systems] + kernel + [jac],
        "second",
        flops=10**9,
    )
    cargo_l = from_left(cargo)
    (late,) = call(
        functools.partial(late_moments_kernel, count=count),
        [shape(rows, lanes)],
        [early, d1, cargo, v1],
        "late",
        flops=10**9,
    )
    (gram,) = call(
        functools.partial(third_kernel, count=count, held=coarse_inverse.shape[0]),
        [shape(ranks, rows, lanes)],
        [extra, late, cargo, cargo_l] + kernel,
        "third",
        flops=10**9,
    )
    gram = lax.all_to_all(gram, "pts", 0, 0, tiled=True)
    cells = [own_hi, own_lo, own_sim, halo_hi, halo_lo, halo_sim]
    answer, grads = call(
        functools.partial(final_kernel, sides=sides * count, points=ranks * width),
        [shape(count, width), shape(ranks * sides, FEAT, LANES)],
        [gram, pack, pack_l, d1, d1_l, cargo, cargo_l] + cells,
        "final",
        flops=10**9,
    )
    grads = lax.all_to_all(grads, ("pts", "probe"), 0, 0, tiled=True)
    lengths, tasks = call(
        tail_kernel, [shape(FEAT), shape(TASKS, TASKS)], [grads], "tail", flops=10**5
    )
    return answer, lengths, tasks


def solution(mesh):
    return jax.shard_map(
        shards,
        mesh=mesh,
        in_specs=(
            P("probe", ("groups", "pts")),
            P(None, ("groups", "pts")),
            P(("groups", "pts")),
            P(("groups", "pts"), None),
            P(("groups", "pts")),
            P(("groups", "pts"), None),
            P("groups", None),
            P("groups"),
            P("groups"),
        ),
        out_specs=(P("probe", ("groups", "pts")), P("groups"), P("groups", None)),
        check_vma=False,
    )
```

```python
import functools

import jax
import jax.numpy as jnp
from jax import lax
from jax.experimental import pallas as pl
from jax.experimental.pallas import tpu as pltpu
from jax.sharding import PartitionSpec as P

BS = 256
REACH = 3
FEAT = 8
TASKS = 16
ITERS = 3
SLOTS = 2 * REACH + 1
BAND = SLOTS * BS
BASE = 32
GROUP = 4
LANES = 128
SYS = 2 * FEAT

highest = lax.Precision.HIGHEST
f32 = jnp.float32
bf16 = jnp.bfloat16
NN = (((1,), (0,)), ((), ()))
NT = (((1,), (1,)), ((), ()))
TN = (((0,), (0,)), ((), ()))


def dot(a, b, dims=NN, precision=None):
    return lax.dot_general(a, b, dims, precision=precision, preferred_element_type=f32)


def iota(shape, dim):
    return lax.broadcasted_iota(jnp.int32, shape, dim)


def split(x, parts):
    out = []
    for _ in range(parts - 1):
        head = x.astype(bf16).astype(f32)
        out.append(head)
        x = x - head
    out.append(x.astype(bf16).astype(f32))
    return out


def column(ref, size):
    rows = iota((size, 1), 0)
    out = jnp.zeros((size, 1), f32)
    for i in range(size):
        out = jnp.where(rows == i, ref[i], out)
    return out


def one_hot(ids, size):
    return (iota((size, ids.shape[1]), 0).astype(f32) == ids).astype(f32)


def noise_row(noise_ref, ids):
    out = jnp.zeros(ids.shape, f32)
    for t in range(TASKS):
        out = jnp.where(ids == float(t), noise_ref[t], out)
    return out


def weight(pat_ref, block, offset):
    if offset != REACH:
        return pat_ref[block, offset].astype(f32)
    total = pat_ref[block, 0]
    for o in range(1, SLOTS):
        total = total + pat_ref[block, o]
    return total.astype(f32)


def near_stack(scaled, table):
    s0, s1, s2 = split(scaled, 3)
    n0, n1, n2 = split(-0.5 * jnp.sum(scaled * scaled, axis=0, keepdims=True), 3)
    rows = iota(scaled.shape, 0)
    norms = jnp.where(rows == 0, n0, jnp.where(rows == 1, n1, jnp.where(rows == 2, n2, 0.0)))
    pad = jnp.zeros((LANES - 7 * FEAT - 3 * TASKS, scaled.shape[1]), f32)
    stack = jnp.concatenate([s0, s0, s1, s1, s0, s2, norms, table, table, table, pad], axis=0)
    return stack.T.astype(bf16)


def own_stack(scaled, picked):
    s0, s1, s2 = split(scaled, 3)
    rows = iota(scaled.shape, 0)
    ones = jnp.where(rows < 3, 1.0, 0.0)
    count = scaled.shape[1]
    tail = LANES - 7 * FEAT - 3 * TASKS
    left = jnp.concatenate(
        [s0, s1, s0, s1, s2, s0, ones, jnp.zeros((3 * TASKS + tail, count), f32)], axis=0
    ).astype(bf16)
    right = jnp.concatenate(
        [jnp.zeros((7 * FEAT, count), f32)] + split(picked, 3) + [jnp.zeros((tail, count), f32)],
        axis=0,
    ).astype(bf16)
    sides = [
        jnp.concatenate([left[:, i : i + BS], right[:, i : i + BS]], axis=1)
        for i in range(0, count, BS)
    ]
    return sides, -0.5 * jnp.sum(scaled * scaled, axis=0, keepdims=True)


def small_inverse(p):
    n = len(p)
    if n == 1:
        return [[pltpu.reciprocal(p[0][0], approx=True)]]
    if n == 2:
        a, b, d = p[0][0], p[0][1], p[1][1]
        r = pltpu.reciprocal(a * d - b * b, approx=True)
        off = -b * r
        return [[d * r, off], [off, a * r]]
    h = n // 2
    ainv = small_inverse([row[:h] for row in p[:h]])
    b = [row[h:] for row in p[:h]]
    t = [[sum(ainv[i][k] * b[k][j] for k in range(h)) for j in range(h)] for i in range(h)]
    s = [[None] * h for _ in range(h)]
    for i in range(h):
        for j in range(i, h):
            s[i][j] = s[j][i] = p[h + i][h + j] - sum(b[k][i] * t[k][j] for k in range(h))
    sinv = small_inverse(s)
    u = [[sum(t[i][k] * sinv[k][j] for k in range(h)) for j in range(h)] for i in range(h)]
    out = [[None] * n for _ in range(n)]
    for i in range(h):
        for j in range(h):
            out[h + i][h + j] = sinv[i][j]
            out[i][h + j] = out[h + j][i] = -u[i][j]
    for i in range(h):
        for j in range(i, h):
            out[i][j] = out[j][i] = ainv[i][j] + sum(u[i][k] * t[j][k] for k in range(h))
    return out


def sweep_base(cells, beside):
    tall = range(BASE // 8)
    tiles = [cells[8 * i : 8 * i + 8] for i in tall]
    lane = iota((8, LANES), 1)
    start = lane - lane % BASE
    inner = lane % BASE
    sub = iota((8, LANES), 0)

    def columns(first):
        return [
            [
                jnp.take_along_axis(tile, start + (first + t), axis=1, mode="promise_in_bounds")
                for tile in tiles
            ]
            for t in range(GROUP)
        ]

    def row(parts, r):
        return jnp.broadcast_to(parts[r // 8][r % 8 : r % 8 + 1, :], (8, LANES))

    def with_rows(parts, first, rows):
        part = parts[first // 8]
        for t, value in enumerate(rows):
            part = jnp.where(sub == first % 8 + t, value, part)
        return [part if i == first // 8 else parts[i] for i in tall]

    def less(parts, factor):
        out = []
        for i in tall:
            part = parts[i]
            for t in range(GROUP):
                part = part - cols[t][i] * factor[t]
            out.append(part)
        return out

    cols = columns(0)
    for first in range(0, BASE, GROUP):
        ahead = columns(first + GROUP) if first + GROUP < BASE else []
        pivots = [[None] * GROUP for _ in range(GROUP)]
        for t in range(GROUP):
            for u in range(t, GROUP):
                pivots[t][u] = pivots[u][t] = row(cols[u], first + t)
        inv = small_inverse(pivots)
        coming = []
        for col in ahead:
            head = [row(col, first + t) for t in range(GROUP)]
            factor = [sum(inv[t][u] * head[u] for u in range(GROUP)) for t in range(GROUP)]
            coming.append(with_rows(less(col, factor), first, factor))
        group = (inner >= first) & (inner < first + GROUP)
        rows = []
        for t in range(GROUP):
            value = jnp.where(group, 0.0, row(tiles, first + t))
            rows.append(jnp.where(inner == first + t, -1.0, value))
        new = [sum(inv[t][u] * rows[u] for u in range(GROUP)) for t in range(GROUP)]
        tiles = [jnp.where(group, 0.0, tile) for tile in tiles]
        tiles = with_rows(less(tiles, new), first, new)
        cols = coming
        if beside:
            beside.pop(0)()
    while beside:
        beside.pop(0)()
    return jnp.concatenate(tiles, axis=0)


def fetch(pairs, sems):
    copies = [pltpu.make_async_copy(a, b, sems.at[i]) for i, (a, b) in enumerate(pairs)]
    for copy in copies:
        copy.start()
    return copies


def invert_kernel(
    place_ref, probe_ref, feat_hbm, ids_hbm, agg_hbm, sys_hbm, cov_hbm, coarse_hbm, pat_hbm, len_hbm, noise_hbm,
    jac_ref, pack_ref, extra_ref,
    work, feat_ref, ids_ref, agg_ref, sys_ref, cov_ref, coarse_ref, pat_ref, len_ref, noise_ref, sems,
):
    blocks = work.shape[0]
    width = blocks * BS
    pairs = [
        (feat_hbm, feat_ref), (ids_hbm, ids_ref), (agg_hbm, agg_ref), (cov_hbm, cov_ref),
        (pat_hbm, pat_ref), (len_hbm, len_ref), (noise_hbm, noise_ref), (coarse_hbm, coarse_ref),
        (sys_hbm, sys_ref),
    ]
    for copy in fetch(pairs, sems):
        copy.wait()
    scaled = feat_ref[...] / column(len_ref, FEAT)
    ids = ids_ref[...].astype(f32).reshape(1, width)
    which = agg_ref[...].astype(f32).reshape(1, width)
    table = one_hot(ids, TASKS)
    noise = noise_row(noise_ref, ids)
    c0, c1, c2 = split(cov_ref[...], 3)
    tab = table.astype(bf16)
    picked = (dot(c2.astype(bf16), tab) + dot(c1.astype(bf16), tab)) + dot(c0.astype(bf16), tab)
    rows = iota((FEAT, width), 0)
    weights = jnp.zeros((1, width), f32)
    places = iota((1, width), 1)
    for m in range(blocks):
        for o in range(SLOTS):
            weights = jnp.where(places == m * SLOTS + o, weight(pat_ref, m, o), weights)
    pack_ref[0:FEAT, :] = scaled
    pack_ref[FEAT : 2 * FEAT, :] = jnp.where(
        rows == 0,
        ids,
        jnp.where(rows == 1, which, jnp.where(rows == 2, probe_ref[0].astype(f32), 0.0)),
    )
    extra_ref[0:TASKS, :] = picked
    tail = jnp.where(rows == 0, noise, jnp.where(rows == 1, weights, 0.0))
    held = coarse_ref.shape[0]
    inverse = jnp.concatenate(
        [coarse_ref[...], jnp.zeros((held, width - coarse_ref.shape[1]), f32)], axis=1
    )
    tail = jnp.where(rows == 2, place_ref[0].astype(f32), tail)
    for r in range(held):
        tail = jnp.where(rows == 3 + r, inverse[r : r + 1], tail)
    extra_ref[TASKS : TASKS + FEAT, :] = tail
    near = near_stack(scaled, table)
    mates, norm = own_stack(scaled, picked)
    eye = iota((BS, BS), 0) == iota((BS, BS), 1)
    for m in range(blocks):
        at = slice(m * BS, (m + 1) * BS)
        both = dot(near[at], mates[m])
        block = weight(pat_ref, m, REACH) * jnp.exp(both[:, :BS] + norm[:, at]) * both[:, BS:]
        work[m] = block + jnp.where(eye, noise[:, at], 0.0)
    seg = iota((BASE, LANES), 1) // BASE
    wide = iota((BASE, BS), 1)
    deep = iota((BASE, BS), 0)

    def packed(strips, first):
        tile, inside = first // LANES, first % LANES
        cells = jnp.zeros((BASE, LANES), f32)
        for m in range(blocks):
            piece = strips[m][:, tile * LANES : (tile + 1) * LANES]
            shift = (BASE * m - inside) % LANES
            if shift:
                piece = pltpu.roll(piece, shift, axis=1)
            cells = jnp.where(seg == m, piece, cells)
        return cells

    def diagonal(cells):
        parts = [jnp.where(seg == m, cells, 0.0) for m in range(LANES // BASE)]
        return jnp.concatenate(parts, axis=0)

    eye = jnp.where(iota((BASE, LANES), 1) % BASE == iota((BASE, LANES), 0), 1.0, 0.0)

    def updates(first, inv, strips):
        state = {}

        def product():
            held = (wide >= first) & (wide < first + BASE)
            minus = jnp.where(wide - first == deep, -1.0, 0.0)
            stack = jnp.concatenate(
                [jnp.where(held, minus, s) for s in strips]
                + [jnp.zeros((LANES - blocks * BASE, BS), f32)],
                axis=0,
            )
            spread = diagonal(inv)[: blocks * BASE]
            new = dot(spread, stack, precision=highest)
            for m in range(blocks):
                state[m] = new[m * BASE : (m + 1) * BASE, :]

        def rows_of(m, low, high):
            def piece():
                r0, r1, r2 = split(strips[m][:, low:high], 3)
                p0, p1, p2 = split(state[m], 3)
                a = jnp.concatenate([r0, r0, r1, r1, r0, r2], axis=0).astype(bf16)
                b = jnp.concatenate([p0, p1, p0, p1, p2, p0], axis=0).astype(bf16)
                gone = (iota((1, BS), 1) >= first) & (iota((1, BS), 1) < first + BASE)
                work[m, low:high, :] = jnp.where(gone, 0.0, work[m, low:high, :]) - dot(a, b, TN)
                if low <= first < high:
                    work[m, first : first + BASE, :] = state[m]

            return piece

        half = BS // 2
        return [product] + [
            rows_of(m, low, low + half) for m in range(blocks) for low in range(0, BS, half)
        ]

    def strips_at(first):
        return [work[m, first : first + BASE, :] for m in range(blocks)]

    cells = jnp.where(seg < blocks, packed(strips_at(0), 0), eye)
    pending = []
    for first in range(0, BS, BASE):
        inv = -sweep_base(cells, pending)
        strips = strips_at(first)
        if first + BASE < BS:
            after = strips_at(first + BASE)
            half = dot(inv, diagonal(packed(strips, first + BASE)), precision=highest)
            drop = dot(packed(after, first), diagonal(half), precision=highest)
            cells = jnp.where(seg < blocks, packed(after, first + BASE) - drop, eye)
        pending = updates(first, inv, strips)
    for piece in pending:
        piece()
    for m in range(blocks):
        inv = -work[m]
        for i, part in enumerate(split(inv, 3)):
            jac_ref[i, m] = part.astype(bf16)
    pack_ref[SYS:, :] = smooth(sys_ref[...], jac_ref)


def own_places(m):
    return [(j, j, REACH + j - m) for j in range(REACH)]


def halo_places(m):
    lefts = [(j - m, j, j - m) for j in range(m, REACH)]
    return lefts + [(REACH - m + j, REACH + j, 2 * REACH - m + j) for j in range(m + 1)]


def build_kernel(*refs, places, sides):
    cells, (own_ref, extra_ref) = refs[:sides], refs[sides : sides + 2]
    hi_ref, lo_ref, sim_ref = refs[sides + 2 :]
    blocks = hi_ref.shape[0]
    near = []
    for ref in cells:
        near.append(near_stack(ref[0:FEAT, :], one_hot(ref[FEAT : FEAT + 1, :], TASKS)))
    mates, norm = own_stack(own_ref[0:FEAT, :], extra_ref[0:TASKS, :])
    weights = extra_ref[TASKS + 1 : TASKS + 2, :]
    for m in range(blocks):
        for row, j, o in places(m):
            part = near[j // REACH][(j % REACH) * BS : (j % REACH + 1) * BS]
            both = dot(part, mates[m])
            place = m * SLOTS + o
            exponent = both[:, :BS] + norm[:, m * BS : (m + 1) * BS]
            similar = weights[:, place : place + 1] * jnp.exp(exponent)
            kernel = similar * both[:, BS:]
            head = kernel.astype(bf16)
            rows = slice(row * BS, (row + 1) * BS)
            if o <= REACH or sides == 1:
                sim_ref[m, rows, :] = similar
            hi_ref[m, rows, :] = head
            lo_ref[m, rows, :] = (kernel - head.astype(f32)).astype(bf16)


def pieces(vectors):
    return jnp.concatenate(split(vectors, 2), axis=0).astype(bf16)


def apply(cells, hi, lo):
    rows = cells.shape[0] // 2
    first = dot(cells, hi)
    return first[:rows] + first[rows:] + dot(cells[:rows], lo)


def operate_own(own, noise, own_hi, own_lo):
    mine = pieces(own)
    out = [apply(mine, own_hi[m], own_lo[m]) for m in range(REACH)]
    return jnp.concatenate(out, axis=1) + noise * own


def operate_left(left, halo_hi, halo_lo):
    cells = pieces(left)
    out = []
    for m in range(REACH):
        part = slice(0, (REACH - m) * BS)
        out.append(apply(cells[:, m * BS :], halo_hi[m, part, :], halo_lo[m, part, :]))
    return jnp.concatenate(out, axis=1)


def operate_halo(left, right, halo_hi, halo_lo):
    lefts, rights = pieces(left), pieces(right)
    out = []
    for m in range(REACH):
        beyond = jnp.concatenate([lefts[:, m * BS :], rights[:, : (m + 1) * BS]], axis=1)
        out.append(apply(beyond, halo_hi[m], halo_lo[m]))
    return jnp.concatenate(out, axis=1)


def smooth_pieces(vectors, parts):
    rows = vectors.shape[0]
    cells = jnp.concatenate(split(vectors, 3), axis=0).astype(bf16)
    a = dot(cells, parts[0])
    b = dot(cells[: 2 * rows], parts[1])
    c = dot(cells[:rows], parts[2])
    return a[:rows] + (a[rows : 2 * rows] + b[:rows] + (a[2 * rows :] + b[rows:] + c))


def smooth(image, jac_ref):
    return jnp.concatenate(
        [
            smooth_pieces(image[:, m * BS : (m + 1) * BS], [jac_ref[i, m] for i in range(3)])
            for m in range(REACH)
        ],
        axis=1,
    )


def basis(pack_ref, coarse):
    z = one_hot(pack_ref[FEAT + 1 : FEAT + 2, :], coarse)
    return jnp.concatenate([pack_ref[SYS:, :], z], axis=0)


def build_own_kernel(own_ref, extra_ref, hi_ref, lo_ref, sim_ref, part_ref):
    build_kernel(
        own_ref, own_ref, extra_ref, hi_ref, lo_ref, sim_ref, places=own_places, sides=1
    )
    coarse = part_ref.shape[0] - (own_ref.shape[0] - SYS)
    noise = extra_ref[TASKS : TASKS + 1, :]
    part_ref[...] = operate_own(basis(own_ref, coarse), noise, hi_ref, lo_ref)


def first_kernel(part_ref, left_ref, right_ref, hi_ref, lo_ref, jac_ref, image_ref, next_ref):
    coarse = part_ref.shape[0] - (left_ref.shape[0] - SYS)
    ends = [basis(ref, coarse) for ref in (left_ref, right_ref)]
    image = part_ref[...] + operate_halo(*ends, hi_ref, lo_ref)
    image_ref[...] = image
    next_ref[...] = smooth(image, jac_ref)


def second_kernel(
    part_ref, left_ref, right_ref, sys_ref, hi_ref, lo_ref, jac_ref, image_ref, cargo_ref
):
    rows = part_ref.shape[0]
    image = part_ref[...] + operate_halo(left_ref[...], right_ref[...], hi_ref, lo_ref)
    image_ref[...] = image
    cargo_ref[0:rows, :] = smooth(image, jac_ref)
    cargo_ref[rows:, :] = sys_ref[...]


def pitch_of(coarse):
    return coarse + 1


def lanes_of(coarse):
    return -(-5 * pitch_of(coarse) // LANES) * LANES


def moment(vectors, images, pairs):
    count = pairs.shape[0]
    table = dot(images, vectors, NT, lax.Precision.HIGH)
    own = jnp.sum(pairs, axis=1, keepdims=True)
    if images.shape[0] > count:
        own = jnp.concatenate([own, jnp.zeros((images.shape[0] - count, 1), f32)], axis=0)
    return jnp.concatenate([table, own], axis=1)


def spread_out(parts, lanes):
    rows, pitch = next(iter(parts.values())).shape
    cells = [parts.get(k, jnp.zeros((rows, pitch), f32)) for k in range(5)]
    if lanes > 5 * pitch:
        cells.append(jnp.zeros((rows, lanes - 5 * pitch), f32))
    return jnp.concatenate(cells, axis=1)


def folded(low, high):
    order = low.shape[0]
    row, col = iota((order, order), 0), iota((order, order), 1)
    diagonal = jnp.sum(jnp.where(row == col, high, 0.0), axis=1, keepdims=True)
    return jnp.concatenate([jnp.where(row >= col, low, high), diagonal], axis=1)


def unfolded(cells):
    order = cells.shape[0]
    row, col = iota((order, order), 0), iota((order, order), 1)
    square = cells[:, :order]
    turned = dot(square, jnp.where(row == col, 1.0, 0.0), TN, highest)
    low = jnp.where(row >= col, square, turned)
    high = jnp.where(row < col, square, jnp.where(row > col, turned, cells[:, order:]))
    return low, high


def early_moments_kernel(
    own_ref, sys_ref, d1_ref, v0_ref, extra_ref, hi_ref, lo_ref, out_ref, part_ref
):
    part_ref[...] = operate_own(d1_ref[...], extra_ref[TASKS : TASKS + 1, :], hi_ref, lo_ref)
    count = own_ref.shape[0] - SYS
    coarse = d1_ref.shape[0] - count
    lanes = out_ref.shape[1]
    pitch = pitch_of(coarse)
    systems = sys_ref[...]
    pre = own_ref[SYS:, :]
    z = one_hot(own_ref[FEAT + 1 : FEAT + 2, :], coarse)
    d1, v0 = d1_ref[...], v0_ref[...]
    m0 = moment(z, v0, pre * v0[:count])
    m1 = moment(d1[count:], v0, d1[:count] * v0[:count])
    out_ref[0:count, :] = spread_out({0: m0[:count], 1: m1[:count]}, lanes)
    start = moment(z, systems, systems * pre)
    if coarse > count:
        start = jnp.concatenate([start, jnp.zeros((coarse - count, pitch), f32)], axis=0)
    fold = folded(m0[count:, :coarse], m1[count:, :coarse])
    out_ref[count:, :] = spread_out({0: fold, 3: start}, lanes)


def late_moments_kernel(
    before_ref, d1_ref, cargo_ref, v1_ref, extra_ref, hi_ref, lo_ref, out_ref, part_ref, *, count
):
    lanes = out_ref.shape[1]
    d1, d2, v1 = d1_ref[...], cargo_ref[0 : d1_ref.shape[0], :], v1_ref[...]
    part_ref[...] = operate_own(d2, extra_ref[TASKS : TASKS + 1, :], hi_ref, lo_ref)
    coarse = d1.shape[0] - count
    m2 = moment(d1[count:], v1, d1[:count] * v1[:count])
    m3 = moment(d2[count:], v1, d2[:count] * v1[:count])
    out_ref[0:count, :] = before_ref[0:count, :] + spread_out({2: m2[:count], 3: m3[:count]}, lanes)
    fold = folded(m2[count:, :coarse], m3[count:, :coarse])
    out_ref[count:, :] = before_ref[count:, :] + spread_out({1: fold}, lanes)


def third_kernel(
    extra_ref, before_ref, cargo_ref, left_ref, part_ref, hi_ref, lo_ref, out_ref, *, count, held
):
    rows = cargo_ref.shape[0] - count
    coarse = rows - count
    lanes = out_ref.shape[2]
    pitch = pitch_of(coarse)
    d2 = cargo_ref[0:rows, :]
    inner = part_ref[...]
    cross = operate_left(left_ref[0:rows, :], hi_ref, lo_ref)
    m4 = moment(d2[count:], inner + cross, d2[:count] * (inner + 2.0 * cross)[:count])
    mirror = dot(d2, cross[count:], NT, lax.Precision.HIGH)
    m4 = m4 + jnp.concatenate([mirror, jnp.zeros((rows, 1), f32)], axis=1)
    row = iota((coarse, 1), 0).astype(f32)
    start = extra_ref[TASKS + 2 : TASKS + 3, 0:1] * held
    inverse = jnp.zeros((coarse, pitch), f32)
    for r in range(held):
        line = extra_ref[TASKS + 3 + r : TASKS + 4 + r, 0:pitch]
        inverse = jnp.where(row == start + r, line, inverse)
    top = before_ref[0:count, :] + spread_out({4: m4[:count]}, lanes)
    bottom = before_ref[count:, :] + spread_out({2: m4[count:], 4: inverse}, lanes)
    for c in range(out_ref.shape[0]):
        out_ref[c, 0:count, :] = top
        out_ref[c, count:, :] = bottom


def final_kernel(
    gram_ref, own_ref, left_ref, d1_ref, d1l_ref, cargo_ref, cargol_ref, *refs, sides, points,
):
    kernel_refs, (sol_ref, grad_ref) = refs[:6], refs[6:]
    width = own_ref.shape[1]
    count = own_ref.shape[0] - SYS
    rows = d1_ref.shape[0]
    coarse = rows - count
    pitch = pitch_of(coarse)
    wide = -(-3 * pitch // LANES) * LANES
    blocks = width // BS
    gram = gram_ref[0]
    for c in range(1, gram_ref.shape[0]):
        gram = gram + gram_ref[c]
    bottom = gram[count:]
    gram = jnp.concatenate([gram[:count], jnp.zeros((count, wide), f32)], axis=1)
    squares = list(unfolded(bottom[:, :pitch])) + list(unfolded(bottom[:, pitch : 2 * pitch]))
    squares.append(bottom[:, 2 * pitch : 2 * pitch + coarse])
    lane = iota((1, wide), 1)
    slot, inside = lane // pitch, lane % pitch
    live = lane < 3 * pitch
    is_vec = live & (inside < coarse)
    is_one = live & (inside == coarse)

    def shifted(j):
        return jnp.where(live, gram[:, j * pitch : j * pitch + wide], 0.0)

    own = [shifted(j) for j in range(3)]
    gap = jnp.zeros((coarse, 1), f32)
    rest = jnp.zeros((coarse, wide - 3 * pitch), f32)
    hankel = []
    for i in range(3):
        line = [squares[i], gap, squares[i + 1], gap, squares[i + 2], gap]
        hankel.append(jnp.concatenate(line + ([rest] if wide > 3 * pitch else []), axis=1))
        hankel.append(jnp.zeros((1, wide), f32))
    if wide > 3 * pitch:
        hankel.append(jnp.zeros((wide - 3 * pitch, wide), f32))
    hankel = jnp.concatenate(hankel, axis=0)
    block0 = lane < pitch
    inverse = bottom[:, 4 * pitch : 4 * pitch + coarse]
    inverse = jnp.concatenate([inverse, jnp.zeros((coarse, wide - coarse), f32)], axis=1)
    inverse = jnp.concatenate([inverse, jnp.zeros((wide - coarse, wide), f32)], axis=0)
    start = bottom[:count, 3 * pitch : 4 * pitch]
    start = jnp.concatenate([start, jnp.zeros((count, wide - pitch), f32)], axis=1)
    against = jnp.where(
        block0, start, jnp.where(live, pltpu.roll(jnp.where(live, own[0], 0.0), pitch, axis=1), 0.0)
    )

    def total(x):
        return jnp.sum(x, axis=1, keepdims=True)

    def scalars(u, i):
        return total(jnp.where(lane == i * pitch + coarse, u, 0.0))

    def metric(u):
        out = dot(jnp.where(is_vec, u, 0.0), hankel, precision=highest)
        for j in range(3):
            out = out + scalars(u, j) * own[j]
        out = jnp.where(is_vec, out, 0.0)
        for i in range(3):
            out = jnp.where(lane == i * pitch + coarse, total(u * own[i]), out)
        return out

    def corrected(w):
        return dot(jnp.where(lane < coarse, w, 0.0), inverse, precision=highest)

    pre = corrected(against) + jnp.where(lane == coarse, 1.0, 0.0)
    direction = pre
    gamma = total(pre * against)
    answer = jnp.zeros_like(pre)
    image_sum = jnp.zeros_like(pre)
    for step in range(ITERS):
        image = metric(direction)
        alpha = gamma / total(direction * image)
        answer = answer + alpha * direction
        if step + 1 < ITERS:
            image_sum = image_sum + alpha * image
            moved_on = jnp.where(live & (slot > 0), pltpu.roll(direction, pitch, axis=1), 0.0)
            pre = pre - alpha * (moved_on + corrected(image))
            gamma_new = total(pre * (against - image_sum))
            direction = pre + (gamma_new / gamma) * direction
            gamma = gamma_new

    pack = jnp.concatenate([left_ref[...], own_ref[...]], axis=1)
    z = one_hot(pack[FEAT + 1 : FEAT + 2], coarse)
    q0 = pack[SYS:]
    d1 = jnp.concatenate([d1l_ref[...], d1_ref[...]], axis=1)
    cargo = jnp.concatenate([cargol_ref[...], cargo_ref[...]], axis=1)
    d2 = cargo[:rows]
    span = q0.shape[1]
    step = -(-coarse // FEAT) * FEAT
    deep = -(-3 * step // LANES) * LANES
    parts, planes = [], []
    for i, rest in enumerate((z, d1[count:], d2[count:])):
        parts.append(answer[:, i * pitch : i * pitch + coarse])
        planes.append(rest)
        if step > coarse:
            parts.append(jnp.zeros((count, step - coarse), f32))
            planes.append(jnp.zeros((step - coarse, span), f32))
    if deep > 3 * step:
        parts.append(jnp.zeros((count, deep - 3 * step), f32))
        planes.append(jnp.zeros((deep - 3 * step, span), f32))
    planes = [plane.astype(bf16) for plane in split(jnp.concatenate(planes, axis=0), 3)]
    x = smooth_pieces(jnp.concatenate(parts, axis=1), planes)
    x = x + scalars(answer, 0) * q0 + scalars(answer, 1) * d1[:count]
    x = x + scalars(answer, 2) * d2[:count]
    mine = slice(width, 2 * width)
    sol_ref[...] = x[:, mine]

    probe = own_ref[FEAT + 2 : FEAT + 3, 0:1]
    line = iota((count, 1), 0).astype(f32) + probe * count
    right = jnp.where(line == 0, x, cargo[rows:])
    coef = jnp.where(line == 0, 0.5 / points, -0.5 / (sides - 1) / points)
    r0, r1 = split(right, 2)
    w0, w1 = split(x * coef, 2)
    rest = jnp.zeros((LANES - 6 * count, span), f32)
    near = jnp.concatenate([w0, w1, w0, r0, r1, r0, rest], axis=0).T.astype(bf16)
    none = jnp.zeros((3 * count, width), f32)
    rest = rest[:, mine]
    ahead = jnp.concatenate([r0, r0, r1], axis=0)[:, mine]
    back = jnp.concatenate([w0, w0, w1], axis=0)[:, mine]
    mates = [
        jnp.concatenate([ahead, none, rest], axis=0).astype(bf16),
        jnp.concatenate([none, back, rest], axis=0).astype(bf16),
    ]
    scaled = pack[0:FEAT]
    table = one_hot(pack[FEAT : FEAT + 1], TASKS)
    ones = jnp.ones((8, span), f32)
    terms = jnp.concatenate([scaled, ones, scaled * scaled], axis=0)
    t0, t1 = split(terms, 2)
    pad8 = jnp.zeros((8, span), f32)
    both = jnp.concatenate([t0, pad8, t1, pad8], axis=0).astype(bf16)
    heads = jnp.concatenate([t0, pad8], axis=0).astype(bf16)
    tables = table.astype(bf16)
    high = 32
    length_total = jnp.zeros((FEAT, 1), f32)
    task_total = jnp.zeros((TASKS, TASKS), f32)
    for m in range(blocks):
        at = slice(m * BS, (m + 1) * BS)
        sums = jnp.zeros((high, BS), f32)
        held_sums = [jnp.zeros((TASKS, BS), f32) for _ in mates]
        places = [(1, row, j + REACH) for row, j, _ in own_places(m)]
        places += [(2, row, j) for row, j, _ in halo_places(m) if j < REACH]
        for orders, row, block in places:
            hi_ref, lo_ref, sim_ref = kernel_refs[3 * orders - 3 : 3 * orders]
            j = slice(block * BS, (block + 1) * BS)
            rows_at = slice(row * BS, (row + 1) * BS)
            outers = [dot(near[j], mate[:, at]) for mate in mates[:orders]]
            kernel = hi_ref[m, rows_at, :].astype(f32) + lo_ref[m, rows_at, :].astype(f32)
            similar = sim_ref[m, rows_at, :]
            energy = sum(outers) * kernel
            e0, e1 = (part.astype(bf16) for part in split(energy, 2))
            first = dot(both[:, j], e0)
            sums = sums + first[:high] + first[high:] + dot(heads[:, j], e1)
            for k in range(orders):
                h0, h1 = (part.astype(bf16) for part in split(outers[k] * similar, 2))
                held_sums[k] = held_sums[k] + dot(tables[:, j], h0) + dot(tables[:, j], h1)
        mid = slice(width + m * BS, width + (m + 1) * BS)
        left = scaled[:, mid]
        value = left * left * sums[FEAT : FEAT + 1] + sums[2 * FEAT : 3 * FEAT]
        value = value - 2.0 * left * sums[:FEAT]
        length_total = length_total + jnp.sum(value, axis=1, keepdims=True)
        task_total = task_total + dot(held_sums[0], table[:, mid], NT, highest)
        task_total = task_total + dot(table[:, mid], held_sums[1], NT, highest)
    half = TASKS // 2
    value = jnp.concatenate(
        [
            task_total[:half],
            task_total[half:],
            jnp.where(iota((half, FEAT), 0) == iota((half, FEAT), 1), length_total, 0.0),
            jnp.zeros((half, LANES - 2 * TASKS - FEAT), f32),
        ],
        axis=1,
    )
    for c in range(grad_ref.shape[0]):
        grad_ref[c] = value


def tail_kernel(parts_ref, length_ref, task_ref):
    total = parts_ref[0]
    for c in range(1, parts_ref.shape[0]):
        total = total + parts_ref[c]
    half = TASKS // 2
    task_ref[0:half, :] = total[:, :TASKS]
    task_ref[half:, :] = total[:, TASKS : 2 * TASKS]
    length_ref[...] = jnp.sum(total[:, 2 * TASKS : 2 * TASKS + FEAT], axis=0)


MIB = 1024 * 1024


def call(body, outs, args, name, smem=0, hbm=0, far_outs=0, scratch=(), flops=0, limit=16):
    if hbm:
        args = args[:-hbm] + [pltpu.with_memory_space_constraint(a, pltpu.HBM) for a in args[-hbm:]]
    if far_outs:
        outs = outs[:-far_outs] + [pltpu.HBM(o.shape, o.dtype) for o in outs[-far_outs:]]
    vm = pl.BlockSpec(memory_space=pltpu.VMEM)
    sm = pl.BlockSpec(memory_space=pltpu.SMEM)
    far = pl.BlockSpec(memory_space=pltpu.HBM)
    return pl.pallas_call(
        body,
        out_shape=outs,
        in_specs=[sm] * smem + [vm] * (len(args) - smem - hbm) + [far] * hbm,
        out_specs=[vm] * (len(outs) - far_outs) + [far] * far_outs,
        scratch_shapes=scratch,
        compiler_params=pltpu.CompilerParams(vmem_limit_bytes=limit * MIB),
        cost_estimate=pl.CostEstimate(flops=flops, bytes_accessed=1 << 20, transcendentals=0),
        name=name,
    )(*args)


def both_sides(cells):
    count = lax.axis_size("pts")
    up = [(i, i + 1) for i in range(count - 1)]
    down = [(i + 1, i) for i in range(count - 1)]
    return lax.ppermute(cells, "pts", up), lax.ppermute(cells, "pts", down)


def from_left(cells):
    count = lax.axis_size("pts")
    return lax.ppermute(cells, "pts", [(i, i + 1) for i in range(count - 1)])


def shards(
    systems, features, task_ids, pattern, aggregate, coarse_inverse, task_cov, lengthscales, noise
):
    count, width = systems.shape
    blocks = width // BS
    coarse = coarse_inverse.shape[1]
    rows = count + coarse
    lanes = lanes_of(coarse)
    assert blocks == REACH
    place = lax.axis_index("pts").astype(jnp.int32)[None]
    probe = lax.axis_index("probe").astype(jnp.int32)[None]
    ranks = lax.axis_size("pts")
    sides = lax.axis_size("probe")

    def shape(*dims, kind=f32):
        return jax.ShapeDtypeStruct(dims, kind)

    jac, pack, extra = call(
        invert_kernel,
        [shape(3, blocks, BS, BS, kind=bf16), shape(SYS + count, width), shape(TASKS + FEAT, width)],
        [place, probe, features, task_ids, aggregate, systems, task_cov, coarse_inverse, pattern, lengthscales, noise],
        "invert",
        smem=2,
        hbm=9,
        scratch=[
            pltpu.VMEM((blocks, BS, BS), f32),
            pltpu.VMEM(features.shape, f32),
            pltpu.VMEM(task_ids.shape, jnp.int32),
            pltpu.VMEM(aggregate.shape, jnp.int32),
            pltpu.VMEM(systems.shape, f32),
            pltpu.VMEM(task_cov.shape, f32),
            pltpu.VMEM(coarse_inverse.shape, f32),
            pltpu.SMEM(pattern.shape, jnp.int32),
            pltpu.SMEM(lengthscales.shape, f32),
            pltpu.SMEM(noise.shape, f32),
            pltpu.SemaphoreType.DMA((9,)),
        ],
        flops=10**10,
    )
    pack_l, pack_r = both_sides(pack)

    def cells_of(deep):
        return [
            shape(blocks, deep, BS, kind=bf16),
            shape(blocks, deep, BS, kind=bf16),
            shape(blocks, deep, BS),
        ]

    own_hi, own_lo, own_sim, part = call(
        build_own_kernel,
        cells_of(width) + [shape(rows, width)],
        [pack, extra],
        "build_own",
        flops=10**9,
    )
    halo_hi, halo_lo, halo_sim = call(
        functools.partial(build_kernel, places=halo_places, sides=2),
        cells_of(BAND - width),
        [pack_l, pack_r, pack, extra],
        "build_halo",
        flops=10**9,
    )
    own, halo = [own_hi, own_lo], [halo_hi, halo_lo]
    v0, d1 = call(
        first_kernel,
        [shape(rows, width), shape(rows, width)],
        [part, pack_l, pack_r] + halo + [jac],
        "first",
        flops=10**9,
    )
    d1_l, d1_r = both_sides(d1)
    early, part = call(
        early_moments_kernel,
        [shape(rows, lanes), shape(rows, width)],
        [pack, systems, d1, v0, extra] + own,
        "early",
        flops=10**9,
    )
    v1, cargo = call(
        second_kernel,
        [shape(rows, width), shape(rows + count, width)],
        [part, d1_l, d1_r, systems] + halo + [jac],
        "second",
        flops=10**9,
    )
    cargo_l = from_left(cargo)
    late, part = call(
        functools.partial(late_moments_kernel, count=count),
        [shape(rows, lanes), shape(rows, width)],
        [early, d1, cargo, v1, extra] + own,
        "late",
        flops=10**9,
    )
    (gram,) = call(
        functools.partial(third_kernel, count=count, held=coarse_inverse.shape[0]),
        [shape(ranks, rows, lanes)],
        [extra, late, cargo, cargo_l, part] + halo,
        "third",
        flops=10**9,
    )
    gram = lax.all_to_all(gram, "pts", 0, 0, tiled=True)
    cells = [own_hi, own_lo, own_sim, halo_hi, halo_lo, halo_sim]
    answer, grads = call(
        functools.partial(final_kernel, sides=sides * count, points=ranks * width),
        [shape(count, width), shape(ranks * sides, FEAT, LANES)],
        [gram, pack, pack_l, d1, d1_l, cargo, cargo_l] + cells,
        "final",
        flops=10**9,
    )
    grads = lax.all_to_all(grads, ("pts", "probe"), 0, 0, tiled=True)
    lengths, tasks = call(
        tail_kernel, [shape(FEAT), shape(TASKS, TASKS)], [grads], "tail", flops=10**5
    )
    return answer, lengths, tasks


def solution(mesh):
    return jax.shard_map(
        shards,
        mesh=mesh,
        in_specs=(
            P("probe", ("groups", "pts")),
            P(None, ("groups", "pts")),
            P(("groups", "pts")),
            P(("groups", "pts"), None),
            P(("groups", "pts")),
            P(("groups", "pts"), None),
            P("groups", None),
            P("groups"),
            P("groups"),
        ),
        out_specs=(P("probe", ("groups", "pts")), P("groups"), P("groups", None)),
        check_vma=False,
    )
```

```python
import functools

import jax
import jax.numpy as jnp
from jax import lax
from jax.experimental import pallas as pl
from jax.experimental.pallas import tpu as pltpu
from jax.sharding import PartitionSpec as P

BS = 256
REACH = 3
FEAT = 8
TASKS = 16
ITERS = 3
SLOTS = 2 * REACH + 1
BAND = SLOTS * BS
BASE = 32
GROUP = 4
LANES = 128
SYS = 2 * FEAT

highest = lax.Precision.HIGHEST
f32 = jnp.float32
bf16 = jnp.bfloat16
NN = (((1,), (0,)), ((), ()))
NT = (((1,), (1,)), ((), ()))
TN = (((0,), (0,)), ((), ()))


def dot(a, b, dims=NN, precision=None):
    return lax.dot_general(a, b, dims, precision=precision, preferred_element_type=f32)


def iota(shape, dim):
    return lax.broadcasted_iota(jnp.int32, shape, dim)


def split(x, parts):
    out = []
    for _ in range(parts - 1):
        head = x.astype(bf16).astype(f32)
        out.append(head)
        x = x - head
    out.append(x.astype(bf16).astype(f32))
    return out


def column(ref, size):
    rows = iota((size, 1), 0)
    out = jnp.zeros((size, 1), f32)
    for i in range(size):
        out = jnp.where(rows == i, ref[i], out)
    return out


def one_hot(ids, size):
    return (iota((size, ids.shape[1]), 0).astype(f32) == ids).astype(f32)


def noise_row(noise_ref, ids):
    out = jnp.zeros(ids.shape, f32)
    for t in range(TASKS):
        out = jnp.where(ids == float(t), noise_ref[t], out)
    return out


def weight(pat_ref, block, offset):
    if offset != REACH:
        return pat_ref[block, offset].astype(f32)
    total = pat_ref[block, 0]
    for o in range(1, SLOTS):
        total = total + pat_ref[block, o]
    return total.astype(f32)


def near_stack(scaled, table):
    s0, s1, s2 = split(scaled, 3)
    n0, n1, n2 = split(-0.5 * jnp.sum(scaled * scaled, axis=0, keepdims=True), 3)
    rows = iota(scaled.shape, 0)
    norms = jnp.where(rows == 0, n0, jnp.where(rows == 1, n1, jnp.where(rows == 2, n2, 0.0)))
    pad = jnp.zeros((LANES - 7 * FEAT - 3 * TASKS, scaled.shape[1]), f32)
    stack = jnp.concatenate([s0, s0, s1, s1, s0, s2, norms, table, table, table, pad], axis=0)
    return stack.T.astype(bf16)


def own_stack(scaled, picked):
    s0, s1, s2 = split(scaled, 3)
    rows = iota(scaled.shape, 0)
    ones = jnp.where(rows < 3, 1.0, 0.0)
    count = scaled.shape[1]
    tail = LANES - 7 * FEAT - 3 * TASKS
    left = jnp.concatenate(
        [s0, s1, s0, s1, s2, s0, ones, jnp.zeros((3 * TASKS + tail, count), f32)], axis=0
    ).astype(bf16)
    right = jnp.concatenate(
        [jnp.zeros((7 * FEAT, count), f32)] + split(picked, 3) + [jnp.zeros((tail, count), f32)],
        axis=0,
    ).astype(bf16)
    sides = [
        jnp.concatenate([left[:, i : i + BS], right[:, i : i + BS]], axis=1)
        for i in range(0, count, BS)
    ]
    return sides, -0.5 * jnp.sum(scaled * scaled, axis=0, keepdims=True)


def small_inverse(p):
    n = len(p)
    if n == 1:
        return [[pltpu.reciprocal(p[0][0], approx=True)]]
    if n == 2:
        a, b, d = p[0][0], p[0][1], p[1][1]
        r = pltpu.reciprocal(a * d - b * b, approx=True)
        off = -b * r
        return [[d * r, off], [off, a * r]]
    h = n // 2
    ainv = small_inverse([row[:h] for row in p[:h]])
    b = [row[h:] for row in p[:h]]
    t = [[sum(ainv[i][k] * b[k][j] for k in range(h)) for j in range(h)] for i in range(h)]
    s = [[None] * h for _ in range(h)]
    for i in range(h):
        for j in range(i, h):
            s[i][j] = s[j][i] = p[h + i][h + j] - sum(b[k][i] * t[k][j] for k in range(h))
    sinv = small_inverse(s)
    u = [[sum(t[i][k] * sinv[k][j] for k in range(h)) for j in range(h)] for i in range(h)]
    out = [[None] * n for _ in range(n)]
    for i in range(h):
        for j in range(h):
            out[h + i][h + j] = sinv[i][j]
            out[i][h + j] = out[h + j][i] = -u[i][j]
    for i in range(h):
        for j in range(i, h):
            out[i][j] = out[j][i] = ainv[i][j] + sum(u[i][k] * t[j][k] for k in range(h))
    return out


def sweep_base(cells, beside):
    tall = range(BASE // 8)
    tiles = [cells[8 * i : 8 * i + 8] for i in tall]
    lane = iota((8, LANES), 1)
    start = lane - lane % BASE
    inner = lane % BASE
    sub = iota((8, LANES), 0)

    def columns(first):
        return [
            [
                jnp.take_along_axis(tile, start + (first + t), axis=1, mode="promise_in_bounds")
                for tile in tiles
            ]
            for t in range(GROUP)
        ]

    def row(parts, r):
        return jnp.broadcast_to(parts[r // 8][r % 8 : r % 8 + 1, :], (8, LANES))

    def with_rows(parts, first, rows):
        part = parts[first // 8]
        for t, value in enumerate(rows):
            part = jnp.where(sub == first % 8 + t, value, part)
        return [part if i == first // 8 else parts[i] for i in tall]

    def less(parts, factor):
        out = []
        for i in tall:
            part = parts[i]
            for t in range(GROUP):
                part = part - cols[t][i] * factor[t]
            out.append(part)
        return out

    cols = columns(0)
    for first in range(0, BASE, GROUP):
        ahead = columns(first + GROUP) if first + GROUP < BASE else []
        pivots = [[None] * GROUP for _ in range(GROUP)]
        for t in range(GROUP):
            for u in range(t, GROUP):
                pivots[t][u] = pivots[u][t] = row(cols[u], first + t)
        inv = small_inverse(pivots)
        coming = []
        for col in ahead:
            head = [row(col, first + t) for t in range(GROUP)]
            factor = [sum(inv[t][u] * head[u] for u in range(GROUP)) for t in range(GROUP)]
            coming.append(with_rows(less(col, factor), first, factor))
        group = (inner >= first) & (inner < first + GROUP)
        rows = []
        for t in range(GROUP):
            value = jnp.where(group, 0.0, row(tiles, first + t))
            rows.append(jnp.where(inner == first + t, -1.0, value))
        new = [sum(inv[t][u] * rows[u] for u in range(GROUP)) for t in range(GROUP)]
        tiles = [jnp.where(group, 0.0, tile) for tile in tiles]
        tiles = with_rows(less(tiles, new), first, new)
        cols = coming
        if beside:
            beside.pop(0)()
    while beside:
        beside.pop(0)()
    return jnp.concatenate(tiles, axis=0)


def fetch(pairs, sems):
    copies = [pltpu.make_async_copy(a, b, sems.at[i]) for i, (a, b) in enumerate(pairs)]
    for copy in copies:
        copy.start()
    return copies


def invert_kernel(
    place_ref, probe_ref, feat_hbm, ids_hbm, agg_hbm, sys_hbm, cov_hbm, coarse_hbm, pat_hbm, len_hbm, noise_hbm,
    jac_ref, pack_ref, extra_ref,
    work, feat_ref, ids_ref, agg_ref, sys_ref, cov_ref, coarse_ref, pat_ref, len_ref, noise_ref, sems,
):
    blocks = work.shape[0]
    width = blocks * BS
    pairs = [
        (feat_hbm, feat_ref), (ids_hbm, ids_ref), (agg_hbm, agg_ref), (cov_hbm, cov_ref),
        (pat_hbm, pat_ref), (len_hbm, len_ref), (noise_hbm, noise_ref), (coarse_hbm, coarse_ref),
        (sys_hbm, sys_ref),
    ]
    for copy in fetch(pairs, sems):
        copy.wait()
    scaled = feat_ref[...] / column(len_ref, FEAT)
    ids = ids_ref[...].astype(f32).reshape(1, width)
    which = agg_ref[...].astype(f32).reshape(1, width)
    table = one_hot(ids, TASKS)
    noise = noise_row(noise_ref, ids)
    c0, c1, c2 = split(cov_ref[...], 3)
    tab = table.astype(bf16)
    picked = (dot(c2.astype(bf16), tab) + dot(c1.astype(bf16), tab)) + dot(c0.astype(bf16), tab)
    rows = iota((FEAT, width), 0)
    weights = jnp.zeros((1, width), f32)
    places = iota((1, width), 1)
    for m in range(blocks):
        for o in range(SLOTS):
            weights = jnp.where(places == m * SLOTS + o, weight(pat_ref, m, o), weights)
    pack_ref[0:FEAT, :] = scaled
    pack_ref[FEAT : 2 * FEAT, :] = jnp.where(
        rows == 0,
        ids,
        jnp.where(rows == 1, which, jnp.where(rows == 2, probe_ref[0].astype(f32), 0.0)),
    )
    extra_ref[0:TASKS, :] = picked
    tail = jnp.where(rows == 0, noise, jnp.where(rows == 1, weights, 0.0))
    held = coarse_ref.shape[0]
    inverse = jnp.concatenate(
        [coarse_ref[...], jnp.zeros((held, width - coarse_ref.shape[1]), f32)], axis=1
    )
    tail = jnp.where(rows == 2, place_ref[0].astype(f32), tail)
    for r in range(held):
        tail = jnp.where(rows == 3 + r, inverse[r : r + 1], tail)
    extra_ref[TASKS : TASKS + FEAT, :] = tail
    near = near_stack(scaled, table)
    mates, norm = own_stack(scaled, picked)
    eye = iota((BS, BS), 0) == iota((BS, BS), 1)
    for m in range(blocks):
        at = slice(m * BS, (m + 1) * BS)
        both = dot(near[at], mates[m])
        block = weight(pat_ref, m, REACH) * jnp.exp(both[:, :BS] + norm[:, at]) * both[:, BS:]
        work[m] = block + jnp.where(eye, noise[:, at], 0.0)
    seg = iota((BASE, LANES), 1) // BASE
    wide = iota((BASE, BS), 1)
    deep = iota((BASE, BS), 0)

    def packed(strips, first):
        tile, inside = first // LANES, first % LANES
        cells = jnp.zeros((BASE, LANES), f32)
        for m in range(blocks):
            piece = strips[m][:, tile * LANES : (tile + 1) * LANES]
            shift = (BASE * m - inside) % LANES
            if shift:
                piece = pltpu.roll(piece, shift, axis=1)
            cells = jnp.where(seg == m, piece, cells)
        return cells

    def diagonal(cells):
        parts = [jnp.where(seg == m, cells, 0.0) for m in range(LANES // BASE)]
        return jnp.concatenate(parts, axis=0)

    eye = jnp.where(iota((BASE, LANES), 1) % BASE == iota((BASE, LANES), 0), 1.0, 0.0)

    def updates(first, inv, strips):
        state = {}

        def product():
            held = (wide >= first) & (wide < first + BASE)
            minus = jnp.where(wide - first == deep, -1.0, 0.0)
            stack = jnp.concatenate(
                [jnp.where(held, minus, s) for s in strips]
                + [jnp.zeros((LANES - blocks * BASE, BS), f32)],
                axis=0,
            )
            spread = diagonal(inv)[: blocks * BASE]
            new = dot(spread, stack, precision=highest)
            for m in range(blocks):
                state[m] = new[m * BASE : (m + 1) * BASE, :]

        def rows_of(m, low, high):
            def piece():
                if (m, 0) not in state:
                    r0, r1, r2 = (part.astype(bf16) for part in split(strips[m], 3))
                    p0, p1, p2 = (part.astype(bf16) for part in split(state[m], 3))
                    state[m, 0] = jnp.concatenate([r0, r0, r1, r1, r0, r2], axis=0)
                    state[m, 1] = jnp.concatenate([p0, p1, p0, p1, p2, p0], axis=0)
                a, b = state[m, 0][:, low:high], state[m, 1]
                gone = (iota((1, BS), 1) >= first) & (iota((1, BS), 1) < first + BASE)
                work[m, low:high, :] = jnp.where(gone, 0.0, work[m, low:high, :]) - dot(a, b, TN)
                if low <= first < high:
                    work[m, first : first + BASE, :] = state[m]

            return piece

        half = BS // 2
        return [product] + [
            rows_of(m, low, low + half) for m in range(blocks) for low in range(0, BS, half)
        ]

    def strips_at(first):
        return [work[m, first : first + BASE, :] for m in range(blocks)]

    cells = jnp.where(seg < blocks, packed(strips_at(0), 0), eye)
    pending = []
    for first in range(0, BS, BASE):
        inv = -sweep_base(cells, pending)
        strips = strips_at(first)
        if first + BASE < BS:
            after = strips_at(first + BASE)
            half = dot(inv, diagonal(packed(strips, first + BASE)), precision=highest)
            drop = dot(packed(after, first), diagonal(half), precision=highest)
            cells = jnp.where(seg < blocks, packed(after, first + BASE) - drop, eye)
        pending = updates(first, inv, strips)
    for piece in pending:
        piece()
    for m in range(blocks):
        inv = -work[m]
        for i, part in enumerate(split(inv, 3)):
            jac_ref[i, m] = part.astype(bf16)
    pack_ref[SYS:, :] = smooth(sys_ref[...], jac_ref)


def own_places(m):
    return [(j, j, REACH + j - m) for j in range(REACH)]


def halo_places(m):
    lefts = [(j - m, j, j - m) for j in range(m, REACH)]
    return lefts + [(REACH - m + j, REACH + j, 2 * REACH - m + j) for j in range(m + 1)]


def build_kernel(*refs, places, sides):
    cells, (own_ref, extra_ref) = refs[:sides], refs[sides : sides + 2]
    hi_ref, lo_ref, sim_ref = refs[sides + 2 :]
    blocks = hi_ref.shape[0]
    near = []
    for ref in cells:
        near.append(near_stack(ref[0:FEAT, :], one_hot(ref[FEAT : FEAT + 1, :], TASKS)))
    mates, norm = own_stack(own_ref[0:FEAT, :], extra_ref[0:TASKS, :])
    weights = extra_ref[TASKS + 1 : TASKS + 2, :]
    for m in range(blocks):
        for row, j, o in places(m):
            part = near[j // REACH][(j % REACH) * BS : (j % REACH + 1) * BS]
            both = dot(part, mates[m])
            place = m * SLOTS + o
            exponent = both[:, :BS] + norm[:, m * BS : (m + 1) * BS]
            similar = weights[:, place : place + 1] * jnp.exp(exponent)
            kernel = similar * both[:, BS:]
            head = kernel.astype(bf16)
            rows = slice(row * BS, (row + 1) * BS)
            if o <= REACH or sides == 1:
                sim_ref[m, rows, :] = similar
            hi_ref[m, rows, :] = head
            lo_ref[m, rows, :] = (kernel - head.astype(f32)).astype(bf16)


def pieces(vectors):
    return jnp.concatenate(split(vectors, 2), axis=0).astype(bf16)


def apply(cells, hi, lo):
    rows = cells.shape[0] // 2
    first = dot(cells, hi)
    return first[:rows] + first[rows:] + dot(cells[:rows], lo)


def operate_own(own, noise, own_hi, own_lo):
    mine = pieces(own)
    out = [apply(mine, own_hi[m], own_lo[m]) for m in range(REACH)]
    return jnp.concatenate(out, axis=1) + noise * own


def operate_left(left, halo_hi, halo_lo):
    cells = pieces(left)
    out = []
    for m in range(REACH):
        part = slice(0, (REACH - m) * BS)
        out.append(apply(cells[:, m * BS :], halo_hi[m, part, :], halo_lo[m, part, :]))
    return jnp.concatenate(out, axis=1)


def operate_halo(left, right, halo_hi, halo_lo):
    lefts, rights = pieces(left), pieces(right)
    out = []
    for m in range(REACH):
        beyond = jnp.concatenate([lefts[:, m * BS :], rights[:, : (m + 1) * BS]], axis=1)
        out.append(apply(beyond, halo_hi[m], halo_lo[m]))
    return jnp.concatenate(out, axis=1)


def smooth_pieces(vectors, parts):
    rows = vectors.shape[0]
    cells = jnp.concatenate(split(vectors, 3), axis=0).astype(bf16)
    a = dot(cells, parts[0])
    b = dot(cells[: 2 * rows], parts[1])
    c = dot(cells[:rows], parts[2])
    return a[:rows] + (a[rows : 2 * rows] + b[:rows] + (a[2 * rows :] + b[rows:] + c))


def smooth(image, jac_ref):
    return jnp.concatenate(
        [
            smooth_pieces(image[:, m * BS : (m + 1) * BS], [jac_ref[i, m] for i in range(3)])
            for m in range(REACH)
        ],
        axis=1,
    )


def basis(pack_ref, coarse):
    z = one_hot(pack_ref[FEAT + 1 : FEAT + 2, :], coarse)
    return jnp.concatenate([pack_ref[SYS:, :], z], axis=0)


def build_own_kernel(own_ref, extra_ref, hi_ref, lo_ref, sim_ref, part_ref):
    build_kernel(
        own_ref, own_ref, extra_ref, hi_ref, lo_ref, sim_ref, places=own_places, sides=1
    )
    coarse = part_ref.shape[0] - (own_ref.shape[0] - SYS)
    noise = extra_ref[TASKS : TASKS + 1, :]
    part_ref[...] = operate_own(basis(own_ref, coarse), noise, hi_ref, lo_ref)


def first_kernel(part_ref, left_ref, right_ref, hi_ref, lo_ref, jac_ref, image_ref, next_ref):
    coarse = part_ref.shape[0] - (left_ref.shape[0] - SYS)
    ends = [basis(ref, coarse) for ref in (left_ref, right_ref)]
    image = part_ref[...] + operate_halo(*ends, hi_ref, lo_ref)
    image_ref[...] = image
    next_ref[...] = smooth(image, jac_ref)


def second_kernel(part_ref, left_ref, right_ref, hi_ref, lo_ref, jac_ref, image_ref, next_ref):
    image = part_ref[...] + operate_halo(left_ref[...], right_ref[...], hi_ref, lo_ref)
    image_ref[...] = image
    next_ref[...] = smooth(image, jac_ref)


def pitch_of(coarse):
    return coarse + 1


def lanes_of(coarse):
    return -(-5 * pitch_of(coarse) // LANES) * LANES


def moment(vectors, images, pairs):
    count = pairs.shape[0]
    table = dot(images, vectors, NT, lax.Precision.HIGH)
    own = jnp.sum(pairs, axis=1, keepdims=True)
    if images.shape[0] > count:
        own = jnp.concatenate([own, jnp.zeros((images.shape[0] - count, 1), f32)], axis=0)
    return jnp.concatenate([table, own], axis=1)


def spread_out(parts, lanes):
    rows, pitch = next(iter(parts.values())).shape
    cells = [parts.get(k, jnp.zeros((rows, pitch), f32)) for k in range(5)]
    if lanes > 5 * pitch:
        cells.append(jnp.zeros((rows, lanes - 5 * pitch), f32))
    return jnp.concatenate(cells, axis=1)


def folded(low, high):
    order = low.shape[0]
    row, col = iota((order, order), 0), iota((order, order), 1)
    diagonal = jnp.sum(jnp.where(row == col, high, 0.0), axis=1, keepdims=True)
    return jnp.concatenate([jnp.where(row >= col, low, high), diagonal], axis=1)


def unfolded(cells):
    order = cells.shape[0]
    row, col = iota((order, order), 0), iota((order, order), 1)
    square = cells[:, :order]
    turned = dot(square, jnp.where(row == col, 1.0, 0.0), TN, highest)
    low = jnp.where(row >= col, square, turned)
    high = jnp.where(row < col, square, jnp.where(row > col, turned, cells[:, order:]))
    return low, high


def early_moments_kernel(
    own_ref, sys_ref, d1_ref, v0_ref, extra_ref, hi_ref, lo_ref, out_ref, part_ref
):
    part_ref[...] = operate_own(d1_ref[...], extra_ref[TASKS : TASKS + 1, :], hi_ref, lo_ref)
    count = own_ref.shape[0] - SYS
    coarse = d1_ref.shape[0] - count
    lanes = out_ref.shape[1]
    pitch = pitch_of(coarse)
    systems = sys_ref[...]
    pre = own_ref[SYS:, :]
    z = one_hot(own_ref[FEAT + 1 : FEAT + 2, :], coarse)
    d1, v0 = d1_ref[...], v0_ref[...]
    m0 = moment(z, v0, pre * v0[:count])
    m1 = moment(d1[count:], v0, d1[:count] * v0[:count])
    out_ref[0:count, :] = spread_out({0: m0[:count], 1: m1[:count]}, lanes)
    start = moment(z, systems, systems * pre)
    if coarse > count:
        start = jnp.concatenate([start, jnp.zeros((coarse - count, pitch), f32)], axis=0)
    fold = folded(m0[count:, :coarse], m1[count:, :coarse])
    out_ref[count:, :] = spread_out({0: fold, 3: start}, lanes)


def late_moments_kernel(
    before_ref, d1_ref, d2_ref, v1_ref, sys_ref, extra_ref, hi_ref, lo_ref, out_ref, part_ref,
    cargo_ref,
):
    cargo_ref[...] = sys_ref[...]
    count = sys_ref.shape[0]
    lanes = out_ref.shape[1]
    d1, d2, v1 = d1_ref[...], d2_ref[...], v1_ref[...]
    part_ref[...] = operate_own(d2, extra_ref[TASKS : TASKS + 1, :], hi_ref, lo_ref)
    coarse = d1.shape[0] - count
    m2 = moment(d1[count:], v1, d1[:count] * v1[:count])
    m3 = moment(d2[count:], v1, d2[:count] * v1[:count])
    out_ref[0:count, :] = before_ref[0:count, :] + spread_out({2: m2[:count], 3: m3[:count]}, lanes)
    fold = folded(m2[count:, :coarse], m3[count:, :coarse])
    out_ref[count:, :] = before_ref[count:, :] + spread_out({1: fold}, lanes)


def third_kernel(
    extra_ref, before_ref, vec_ref, left_ref, part_ref, hi_ref, lo_ref, out_ref, *, count, held
):
    coarse = vec_ref.shape[0] - count
    lanes = out_ref.shape[2]
    pitch = pitch_of(coarse)
    d2 = vec_ref[...]
    rows = d2.shape[0]
    inner = part_ref[...]
    cross = operate_left(left_ref[...], hi_ref, lo_ref)
    m4 = moment(d2[count:], inner + cross, d2[:count] * (inner + 2.0 * cross)[:count])
    mirror = dot(d2, cross[count:], NT, lax.Precision.HIGH)
    m4 = m4 + jnp.concatenate([mirror, jnp.zeros((rows, 1), f32)], axis=1)
    row = iota((coarse, 1), 0).astype(f32)
    start = extra_ref[TASKS + 2 : TASKS + 3, 0:1] * held
    inverse = jnp.zeros((coarse, pitch), f32)
    for r in range(held):
        line = extra_ref[TASKS + 3 + r : TASKS + 4 + r, 0:pitch]
        inverse = jnp.where(row == start + r, line, inverse)
    top = before_ref[0:count, :] + spread_out({4: m4[:count]}, lanes)
    bottom = before_ref[count:, :] + spread_out({2: m4[count:], 4: inverse}, lanes)
    for c in range(out_ref.shape[0]):
        out_ref[c, 0:count, :] = top
        out_ref[c, count:, :] = bottom


def final_kernel(
    gram_ref, own_ref, left_ref, d1_ref, d1l_ref, d2_ref, d2l_ref, sys_ref, sysl_ref, *refs,
    sides, points,
):
    kernel_refs, (sol_ref, grad_ref) = refs[:6], refs[6:]
    width = own_ref.shape[1]
    count = own_ref.shape[0] - SYS
    rows = d1_ref.shape[0]
    coarse = rows - count
    pitch = pitch_of(coarse)
    wide = -(-3 * pitch // LANES) * LANES
    blocks = width // BS
    gram = gram_ref[0]
    for c in range(1, gram_ref.shape[0]):
        gram = gram + gram_ref[c]
    bottom = gram[count:]
    gram = jnp.concatenate([gram[:count], jnp.zeros((count, wide), f32)], axis=1)
    squares = list(unfolded(bottom[:, :pitch])) + list(unfolded(bottom[:, pitch : 2 * pitch]))
    squares.append(bottom[:, 2 * pitch : 2 * pitch + coarse])
    lane = iota((1, wide), 1)
    slot, inside = lane // pitch, lane % pitch
    live = lane < 3 * pitch
    is_vec = live & (inside < coarse)
    is_one = live & (inside == coarse)

    def shifted(j):
        return jnp.where(live, gram[:, j * pitch : j * pitch + wide], 0.0)

    own = [shifted(j) for j in range(3)]
    gap = jnp.zeros((coarse, 1), f32)
    rest = jnp.zeros((coarse, wide - 3 * pitch), f32)
    hankel = []
    for i in range(3):
        line = [squares[i], gap, squares[i + 1], gap, squares[i + 2], gap]
        hankel.append(jnp.concatenate(line + ([rest] if wide > 3 * pitch else []), axis=1))
        hankel.append(jnp.zeros((1, wide), f32))
    if wide > 3 * pitch:
        hankel.append(jnp.zeros((wide - 3 * pitch, wide), f32))
    hankel = jnp.concatenate(hankel, axis=0)
    block0 = lane < pitch
    inverse = bottom[:, 4 * pitch : 4 * pitch + coarse]
    inverse = jnp.concatenate([inverse, jnp.zeros((coarse, wide - coarse), f32)], axis=1)
    inverse = jnp.concatenate([inverse, jnp.zeros((wide - coarse, wide), f32)], axis=0)
    start = bottom[:count, 3 * pitch : 4 * pitch]
    start = jnp.concatenate([start, jnp.zeros((count, wide - pitch), f32)], axis=1)
    against = jnp.where(
        block0, start, jnp.where(live, pltpu.roll(jnp.where(live, own[0], 0.0), pitch, axis=1), 0.0)
    )

    def total(x):
        return jnp.sum(x, axis=1, keepdims=True)

    def scalars(u, i):
        return total(jnp.where(lane == i * pitch + coarse, u, 0.0))

    def metric(u):
        out = dot(jnp.where(is_vec, u, 0.0), hankel, precision=highest)
        for j in range(3):
            out = out + scalars(u, j) * own[j]
        out = jnp.where(is_vec, out, 0.0)
        for i in range(3):
            out = jnp.where(lane == i * pitch + coarse, total(u * own[i]), out)
        return out

    def corrected(w):
        return dot(jnp.where(lane < coarse, w, 0.0), inverse, precision=highest)

    pre = corrected(against) + jnp.where(lane == coarse, 1.0, 0.0)
    direction = pre
    gamma = total(pre * against)
    answer = jnp.zeros_like(pre)
    image_sum = jnp.zeros_like(pre)
    for step in range(ITERS):
        image = metric(direction)
        alpha = gamma / total(direction * image)
        answer = answer + alpha * direction
        if step + 1 < ITERS:
            image_sum = image_sum + alpha * image
            moved_on = jnp.where(live & (slot > 0), pltpu.roll(direction, pitch, axis=1), 0.0)
            pre = pre - alpha * (moved_on + corrected(image))
            gamma_new = total(pre * (against - image_sum))
            direction = pre + (gamma_new / gamma) * direction
            gamma = gamma_new

    pack = jnp.concatenate([left_ref[...], own_ref[...]], axis=1)
    z = one_hot(pack[FEAT + 1 : FEAT + 2], coarse)
    q0 = pack[SYS:]
    d1 = jnp.concatenate([d1l_ref[...], d1_ref[...]], axis=1)
    d2 = jnp.concatenate([d2l_ref[...], d2_ref[...]], axis=1)
    span = q0.shape[1]
    step = -(-coarse // FEAT) * FEAT
    deep = -(-3 * step // LANES) * LANES
    parts, planes = [], []
    for i, rest in enumerate((z, d1[count:], d2[count:])):
        parts.append(answer[:, i * pitch : i * pitch + coarse])
        planes.append(rest)
        if step > coarse:
            parts.append(jnp.zeros((count, step - coarse), f32))
            planes.append(jnp.zeros((step - coarse, span), f32))
    if deep > 3 * step:
        parts.append(jnp.zeros((count, deep - 3 * step), f32))
        planes.append(jnp.zeros((deep - 3 * step, span), f32))
    planes = [plane.astype(bf16) for plane in split(jnp.concatenate(planes, axis=0), 3)]
    x = smooth_pieces(jnp.concatenate(parts, axis=1), planes)
    x = x + scalars(answer, 0) * q0 + scalars(answer, 1) * d1[:count]
    x = x + scalars(answer, 2) * d2[:count]
    mine = slice(width, 2 * width)
    sol_ref[...] = x[:, mine]

    probe = own_ref[FEAT + 2 : FEAT + 3, 0:1]
    line = iota((count, 1), 0).astype(f32) + probe * count
    systems = jnp.concatenate([sysl_ref[...], sys_ref[...]], axis=1)
    right = jnp.where(line == 0, x, systems)
    coef = jnp.where(line == 0, 0.5 / points, -0.5 / (sides - 1) / points)
    r0, r1 = split(right, 2)
    w0, w1 = split(x * coef, 2)
    rest = jnp.zeros((LANES - 6 * count, span), f32)
    near = jnp.concatenate([w0, w1, w0, r0, r1, r0, rest], axis=0).T.astype(bf16)
    none = jnp.zeros((3 * count, width), f32)
    rest = rest[:, mine]
    ahead = jnp.concatenate([r0, r0, r1], axis=0)[:, mine]
    back = jnp.concatenate([w0, w0, w1], axis=0)[:, mine]
    mates = [
        jnp.concatenate([ahead, none, rest], axis=0).astype(bf16),
        jnp.concatenate([none, back, rest], axis=0).astype(bf16),
    ]
    scaled = pack[0:FEAT]
    table = one_hot(pack[FEAT : FEAT + 1], TASKS)
    ones = jnp.ones((8, span), f32)
    terms = jnp.concatenate([scaled, ones, scaled * scaled], axis=0)
    t0, t1 = split(terms, 2)
    pad8 = jnp.zeros((8, span), f32)
    both = jnp.concatenate([t0, pad8, t1, pad8], axis=0).astype(bf16)
    heads = jnp.concatenate([t0, pad8], axis=0).astype(bf16)
    tables = table.astype(bf16)
    high = 32
    length_total = jnp.zeros((FEAT, 1), f32)
    task_total = jnp.zeros((TASKS, TASKS), f32)
    for m in range(blocks):
        at = slice(m * BS, (m + 1) * BS)
        sums = jnp.zeros((high, BS), f32)
        held_sums = [jnp.zeros((TASKS, BS), f32) for _ in mates]
        places = [(1, row, j + REACH) for row, j, _ in own_places(m)]
        places += [(2, row, j) for row, j, _ in halo_places(m) if j < REACH]
        for orders, row, block in places:
            hi_ref, lo_ref, sim_ref = kernel_refs[3 * orders - 3 : 3 * orders]
            j = slice(block * BS, (block + 1) * BS)
            rows_at = slice(row * BS, (row + 1) * BS)
            outers = [dot(near[j], mate[:, at]) for mate in mates[:orders]]
            kernel = hi_ref[m, rows_at, :].astype(f32) + lo_ref[m, rows_at, :].astype(f32)
            similar = sim_ref[m, rows_at, :]
            energy = sum(outers) * kernel
            e0, e1 = (part.astype(bf16) for part in split(energy, 2))
            first = dot(both[:, j], e0)
            sums = sums + first[:high] + first[high:] + dot(heads[:, j], e1)
            for k in range(orders):
                h0, h1 = (part.astype(bf16) for part in split(outers[k] * similar, 2))
                held_sums[k] = held_sums[k] + dot(tables[:, j], h0) + dot(tables[:, j], h1)
        mid = slice(width + m * BS, width + (m + 1) * BS)
        left = scaled[:, mid]
        value = left * left * sums[FEAT : FEAT + 1] + sums[2 * FEAT : 3 * FEAT]
        value = value - 2.0 * left * sums[:FEAT]
        length_total = length_total + jnp.sum(value, axis=1, keepdims=True)
        task_total = task_total + dot(held_sums[0], table[:, mid], NT, highest)
        task_total = task_total + dot(table[:, mid], held_sums[1], NT, highest)
    half = TASKS // 2
    value = jnp.concatenate(
        [
            task_total[:half],
            task_total[half:],
            jnp.where(iota((half, FEAT), 0) == iota((half, FEAT), 1), length_total, 0.0),
            jnp.zeros((half, LANES - 2 * TASKS - FEAT), f32),
        ],
        axis=1,
    )
    for c in range(grad_ref.shape[0]):
        grad_ref[c] = value


def tail_kernel(parts_ref, length_ref, task_ref):
    total = parts_ref[0]
    for c in range(1, parts_ref.shape[0]):
        total = total + parts_ref[c]
    half = TASKS // 2
    task_ref[0:half, :] = total[:, :TASKS]
    task_ref[half:, :] = total[:, TASKS : 2 * TASKS]
    length_ref[...] = jnp.sum(total[:, 2 * TASKS : 2 * TASKS + FEAT], axis=0)


MIB = 1024 * 1024


def call(body, outs, args, name, smem=0, hbm=0, far_outs=0, scratch=(), flops=0, limit=16):
    if hbm:
        args = args[:-hbm] + [pltpu.with_memory_space_constraint(a, pltpu.HBM) for a in args[-hbm:]]
    if far_outs:
        outs = outs[:-far_outs] + [pltpu.HBM(o.shape, o.dtype) for o in outs[-far_outs:]]
    vm = pl.BlockSpec(memory_space=pltpu.VMEM)
    sm = pl.BlockSpec(memory_space=pltpu.SMEM)
    far = pl.BlockSpec(memory_space=pltpu.HBM)
    return pl.pallas_call(
        body,
        out_shape=outs,
        in_specs=[sm] * smem + [vm] * (len(args) - smem - hbm) + [far] * hbm,
        out_specs=[vm] * (len(outs) - far_outs) + [far] * far_outs,
        scratch_shapes=scratch,
        compiler_params=pltpu.CompilerParams(vmem_limit_bytes=limit * MIB),
        cost_estimate=pl.CostEstimate(flops=flops, bytes_accessed=1 << 20, transcendentals=0),
        name=name,
    )(*args)


def both_sides(cells):
    count = lax.axis_size("pts")
    up = [(i, i + 1) for i in range(count - 1)]
    down = [(i + 1, i) for i in range(count - 1)]
    return lax.ppermute(cells, "pts", up), lax.ppermute(cells, "pts", down)


def from_left(cells):
    count = lax.axis_size("pts")
    return lax.ppermute(cells, "pts", [(i, i + 1) for i in range(count - 1)])


def shards(
    systems, features, task_ids, pattern, aggregate, coarse_inverse, task_cov, lengthscales, noise
):
    count, width = systems.shape
    blocks = width // BS
    coarse = coarse_inverse.shape[1]
    rows = count + coarse
    lanes = lanes_of(coarse)
    assert blocks == REACH
    place = lax.axis_index("pts").astype(jnp.int32)[None]
    probe = lax.axis_index("probe").astype(jnp.int32)[None]
    ranks = lax.axis_size("pts")
    sides = lax.axis_size("probe")

    def shape(*dims, kind=f32):
        return jax.ShapeDtypeStruct(dims, kind)

    jac, pack, extra = call(
        invert_kernel,
        [shape(3, blocks, BS, BS, kind=bf16), shape(SYS + count, width), shape(TASKS + FEAT, width)],
        [place, probe, features, task_ids, aggregate, systems, task_cov, coarse_inverse, pattern, lengthscales, noise],
        "invert",
        smem=2,
        hbm=9,
        scratch=[
            pltpu.VMEM((blocks, BS, BS), f32),
            pltpu.VMEM(features.shape, f32),
            pltpu.VMEM(task_ids.shape, jnp.int32),
            pltpu.VMEM(aggregate.shape, jnp.int32),
            pltpu.VMEM(systems.shape, f32),
            pltpu.VMEM(task_cov.shape, f32),
            pltpu.VMEM(coarse_inverse.shape, f32),
            pltpu.SMEM(pattern.shape, jnp.int32),
            pltpu.SMEM(lengthscales.shape, f32),
            pltpu.SMEM(noise.shape, f32),
            pltpu.SemaphoreType.DMA((9,)),
        ],
        flops=10**10,
    )
    pack_l, pack_r = both_sides(pack)

    def cells_of(deep):
        return [
            shape(blocks, deep, BS, kind=bf16),
            shape(blocks, deep, BS, kind=bf16),
            shape(blocks, deep, BS),
        ]

    own_hi, own_lo, own_sim, part = call(
        build_own_kernel,
        cells_of(width) + [shape(rows, width)],
        [pack, extra],
        "build_own",
        flops=10**9,
    )
    halo_hi, halo_lo, halo_sim = call(
        functools.partial(build_kernel, places=halo_places, sides=2),
        cells_of(BAND - width),
        [pack_l, pack_r, pack, extra],
        "build_halo",
        flops=10**9,
    )
    own, halo = [own_hi, own_lo], [halo_hi, halo_lo]
    v0, d1 = call(
        first_kernel,
        [shape(rows, width), shape(rows, width)],
        [part, pack_l, pack_r] + halo + [jac],
        "first",
        flops=10**9,
    )
    d1_l, d1_r = both_sides(d1)
    early, part = call(
        early_moments_kernel,
        [shape(rows, lanes), shape(rows, width)],
        [pack, systems, d1, v0, extra] + own,
        "early",
        flops=10**9,
    )
    v1, d2 = call(
        second_kernel,
        [shape(rows, width), shape(rows, width)],
        [part, d1_l, d1_r] + halo + [jac],
        "second",
        flops=10**9,
    )
    d2_l = from_left(d2)
    late, part, cargo = call(
        late_moments_kernel,
        [shape(rows, lanes), shape(rows, width), shape(count, width)],
        [early, d1, d2, v1, systems, extra] + own,
        "late",
        flops=10**9,
    )
    cargo_l = from_left(cargo)
    (gram,) = call(
        functools.partial(third_kernel, count=count, held=coarse_inverse.shape[0]),
        [shape(ranks, rows, lanes)],
        [extra, late, d2, d2_l, part] + halo,
        "third",
        flops=10**9,
    )
    gram = lax.all_to_all(gram, "pts", 0, 0, tiled=True)
    cells = [own_hi, own_lo, own_sim, halo_hi, halo_lo, halo_sim]
    answer, grads = call(
        functools.partial(final_kernel, sides=sides * count, points=ranks * width),
        [shape(count, width), shape(ranks * sides, FEAT, LANES)],
        [gram, pack, pack_l, d1, d1_l, d2, d2_l, cargo, cargo_l] + cells,
        "final",
        flops=10**9,
    )
    grads = lax.all_to_all(grads, ("pts", "probe"), 0, 0, tiled=True)
    lengths, tasks = call(
        tail_kernel, [shape(FEAT), shape(TASKS, TASKS)], [grads], "tail", flops=10**5
    )
    return answer, lengths, tasks


def solution(mesh):
    return jax.shard_map(
        shards,
        mesh=mesh,
        in_specs=(
            P("probe", ("groups", "pts")),
            P(None, ("groups", "pts")),
            P(("groups", "pts")),
            P(("groups", "pts"), None),
            P(("groups", "pts")),
            P(("groups", "pts"), None),
            P("groups", None),
            P("groups"),
            P("groups"),
        ),
        out_specs=(P("probe", ("groups", "pts")), P("groups"), P("groups", None)),
        check_vma=False,
    )
```

```python
import functools

import jax
import jax.numpy as jnp
from jax import lax
from jax.experimental import pallas as pl
from jax.experimental.pallas import tpu as pltpu
from jax.sharding import PartitionSpec as P

BS = 256
REACH = 3
FEAT = 8
TASKS = 16
ITERS = 3
SLOTS = 2 * REACH + 1
BAND = SLOTS * BS
BASE = 32
GROUP = 4
LANES = 128
SYS = 2 * FEAT

highest = lax.Precision.HIGHEST
f32 = jnp.float32
bf16 = jnp.bfloat16
NN = (((1,), (0,)), ((), ()))
NT = (((1,), (1,)), ((), ()))
TN = (((0,), (0,)), ((), ()))


def dot(a, b, dims=NN, precision=None):
    return lax.dot_general(a, b, dims, precision=precision, preferred_element_type=f32)


def iota(shape, dim):
    return lax.broadcasted_iota(jnp.int32, shape, dim)


def split(x, parts):
    out = []
    for _ in range(parts - 1):
        head = x.astype(bf16).astype(f32)
        out.append(head)
        x = x - head
    out.append(x.astype(bf16).astype(f32))
    return out


def column(ref, size):
    rows = iota((size, 1), 0)
    out = jnp.zeros((size, 1), f32)
    for i in range(size):
        out = jnp.where(rows == i, ref[i], out)
    return out


def one_hot(ids, size):
    return (iota((size, ids.shape[1]), 0).astype(f32) == ids).astype(f32)


def noise_row(noise_ref, ids):
    out = jnp.zeros(ids.shape, f32)
    for t in range(TASKS):
        out = jnp.where(ids == float(t), noise_ref[t], out)
    return out


def weight(pat_ref, block, offset):
    if offset != REACH:
        return pat_ref[block, offset].astype(f32)
    total = pat_ref[block, 0]
    for o in range(1, SLOTS):
        total = total + pat_ref[block, o]
    return total.astype(f32)


def near_stack(scaled, table):
    s0, s1, s2 = split(scaled, 3)
    n0, n1, n2 = split(-0.5 * jnp.sum(scaled * scaled, axis=0, keepdims=True), 3)
    rows = iota(scaled.shape, 0)
    norms = jnp.where(rows == 0, n0, jnp.where(rows == 1, n1, jnp.where(rows == 2, n2, 0.0)))
    pad = jnp.zeros((LANES - 7 * FEAT - 3 * TASKS, scaled.shape[1]), f32)
    stack = jnp.concatenate([s0, s0, s1, s1, s0, s2, norms, table, table, table, pad], axis=0)
    return stack.T.astype(bf16)


def own_stack(scaled, picked):
    s0, s1, s2 = split(scaled, 3)
    rows = iota(scaled.shape, 0)
    ones = jnp.where(rows < 3, 1.0, 0.0)
    count = scaled.shape[1]
    tail = LANES - 7 * FEAT - 3 * TASKS
    left = jnp.concatenate(
        [s0, s1, s0, s1, s2, s0, ones, jnp.zeros((3 * TASKS + tail, count), f32)], axis=0
    ).astype(bf16)
    right = jnp.concatenate(
        [jnp.zeros((7 * FEAT, count), f32)] + split(picked, 3) + [jnp.zeros((tail, count), f32)],
        axis=0,
    ).astype(bf16)
    sides = [
        jnp.concatenate([left[:, i : i + BS], right[:, i : i + BS]], axis=1)
        for i in range(0, count, BS)
    ]
    return sides, -0.5 * jnp.sum(scaled * scaled, axis=0, keepdims=True)


def small_inverse(p):
    n = len(p)
    if n == 1:
        return [[pltpu.reciprocal(p[0][0], approx=True)]]
    if n == 2:
        a, b, d = p[0][0], p[0][1], p[1][1]
        r = pltpu.reciprocal(a * d - b * b, approx=True)
        off = -b * r
        return [[d * r, off], [off, a * r]]
    h = n // 2
    ainv = small_inverse([row[:h] for row in p[:h]])
    b = [row[h:] for row in p[:h]]
    t = [[sum(ainv[i][k] * b[k][j] for k in range(h)) for j in range(h)] for i in range(h)]
    s = [[None] * h for _ in range(h)]
    for i in range(h):
        for j in range(i, h):
            s[i][j] = s[j][i] = p[h + i][h + j] - sum(b[k][i] * t[k][j] for k in range(h))
    sinv = small_inverse(s)
    u = [[sum(t[i][k] * sinv[k][j] for k in range(h)) for j in range(h)] for i in range(h)]
    out = [[None] * n for _ in range(n)]
    for i in range(h):
        for j in range(h):
            out[h + i][h + j] = sinv[i][j]
            out[i][h + j] = out[h + j][i] = -u[i][j]
    for i in range(h):
        for j in range(i, h):
            out[i][j] = out[j][i] = ainv[i][j] + sum(u[i][k] * t[j][k] for k in range(h))
    return out


def sweep_base(cells, beside):
    tall = range(BASE // 8)
    tiles = [cells[8 * i : 8 * i + 8] for i in tall]
    lane = iota((8, LANES), 1)
    start = lane - lane % BASE
    inner = lane % BASE
    sub = iota((8, LANES), 0)

    def columns(first):
        return [
            [
                jnp.take_along_axis(tile, start + (first + t), axis=1, mode="promise_in_bounds")
                for tile in tiles
            ]
            for t in range(GROUP)
        ]

    def row(parts, r):
        return jnp.broadcast_to(parts[r // 8][r % 8 : r % 8 + 1, :], (8, LANES))

    def with_rows(parts, first, rows):
        part = parts[first // 8]
        for t, value in enumerate(rows):
            part = jnp.where(sub == first % 8 + t, value, part)
        return [part if i == first // 8 else parts[i] for i in tall]

    def less(parts, factor):
        out = []
        for i in tall:
            part = parts[i]
            for t in range(GROUP):
                part = part - cols[t][i] * factor[t]
            out.append(part)
        return out

    def symmetric(entry):
        out = [[None] * GROUP for _ in range(GROUP)]
        for t in range(GROUP):
            for u in range(t, GROUP):
                out[t][u] = out[u][t] = entry(t, u)
        return out

    cols = columns(0)
    pivots = symmetric(lambda t, u: row(cols[u], t))
    for first in range(0, BASE, GROUP):
        then = first + GROUP
        ahead = columns(then) if then < BASE else []
        heads = [[row(col, first + t) for t in range(GROUP)] for col in ahead]
        inv = small_inverse(pivots)
        factors = [
            [sum(inv[t][u] * head[u] for u in range(GROUP)) for t in range(GROUP)]
            for head in heads
        ]
        if ahead:
            pivots = symmetric(
                lambda t, u: row(ahead[u], then + t)
                - sum(heads[t][i] * factors[u][i] for i in range(GROUP))
            )
        coming = [
            with_rows(less(col, factor), first, factor) for col, factor in zip(ahead, factors)
        ]
        group = (inner >= first) & (inner < first + GROUP)
        rows = []
        for t in range(GROUP):
            value = jnp.where(group, 0.0, row(tiles, first + t))
            rows.append(jnp.where(inner == first + t, -1.0, value))
        new = [sum(inv[t][u] * rows[u] for u in range(GROUP)) for t in range(GROUP)]
        tiles = [jnp.where(group, 0.0, tile) for tile in tiles]
        tiles = with_rows(less(tiles, new), first, new)
        cols = coming
        if beside:
            beside.pop(0)()
    while beside:
        beside.pop(0)()
    return jnp.concatenate(tiles, axis=0)


def fetch(pairs, sems):
    copies = [pltpu.make_async_copy(a, b, sems.at[i]) for i, (a, b) in enumerate(pairs)]
    for copy in copies:
        copy.start()
    return copies


def invert_kernel(
    place_ref, probe_ref, feat_hbm, ids_hbm, agg_hbm, sys_hbm, cov_hbm, coarse_hbm, pat_hbm, len_hbm, noise_hbm,
    jac_ref, pack_ref, extra_ref,
    work, feat_ref, ids_ref, agg_ref, sys_ref, cov_ref, coarse_ref, pat_ref, len_ref, noise_ref, sems,
):
    blocks = work.shape[0]
    width = blocks * BS
    pairs = [
        (feat_hbm, feat_ref), (ids_hbm, ids_ref), (agg_hbm, agg_ref), (cov_hbm, cov_ref),
        (pat_hbm, pat_ref), (len_hbm, len_ref), (noise_hbm, noise_ref), (coarse_hbm, coarse_ref),
        (sys_hbm, sys_ref),
    ]
    for copy in fetch(pairs, sems):
        copy.wait()
    scaled = feat_ref[...] / column(len_ref, FEAT)
    ids = ids_ref[...].astype(f32).reshape(1, width)
    which = agg_ref[...].astype(f32).reshape(1, width)
    table = one_hot(ids, TASKS)
    noise = noise_row(noise_ref, ids)
    c0, c1, c2 = split(cov_ref[...], 3)
    tab = table.astype(bf16)
    picked = (dot(c2.astype(bf16), tab) + dot(c1.astype(bf16), tab)) + dot(c0.astype(bf16), tab)
    rows = iota((FEAT, width), 0)
    weights = jnp.zeros((1, width), f32)
    places = iota((1, width), 1)
    for m in range(blocks):
        for o in range(SLOTS):
            weights = jnp.where(places == m * SLOTS + o, weight(pat_ref, m, o), weights)
    pack_ref[0:FEAT, :] = scaled
    pack_ref[FEAT : 2 * FEAT, :] = jnp.where(
        rows == 0,
        ids,
        jnp.where(rows == 1, which, jnp.where(rows == 2, probe_ref[0].astype(f32), 0.0)),
    )
    extra_ref[0:TASKS, :] = picked
    tail = jnp.where(rows == 0, noise, jnp.where(rows == 1, weights, 0.0))
    held = coarse_ref.shape[0]
    inverse = jnp.concatenate(
        [coarse_ref[...], jnp.zeros((held, width - coarse_ref.shape[1]), f32)], axis=1
    )
    tail = jnp.where(rows == 2, place_ref[0].astype(f32), tail)
    for r in range(held):
        tail = jnp.where(rows == 3 + r, inverse[r : r + 1], tail)
    extra_ref[TASKS : TASKS + FEAT, :] = tail
    near = near_stack(scaled, table)
    mates, norm = own_stack(scaled, picked)
    eye = iota((BS, BS), 0) == iota((BS, BS), 1)
    for m in range(blocks):
        at = slice(m * BS, (m + 1) * BS)
        both = dot(near[at], mates[m])
        block = weight(pat_ref, m, REACH) * jnp.exp(both[:, :BS] + norm[:, at]) * both[:, BS:]
        work[m] = block + jnp.where(eye, noise[:, at], 0.0)
    seg = iota((BASE, LANES), 1) // BASE
    wide = iota((BASE, BS), 1)
    deep = iota((BASE, BS), 0)

    def packed(strips, first):
        tile, inside = first // LANES, first % LANES
        cells = jnp.zeros((BASE, LANES), f32)
        for m in range(blocks):
            piece = strips[m][:, tile * LANES : (tile + 1) * LANES]
            shift = (BASE * m - inside) % LANES
            if shift:
                piece = pltpu.roll(piece, shift, axis=1)
            cells = jnp.where(seg == m, piece, cells)
        return cells

    def diagonal(cells):
        parts = [jnp.where(seg == m, cells, 0.0) for m in range(LANES // BASE)]
        return jnp.concatenate(parts, axis=0)

    eye = jnp.where(iota((BASE, LANES), 1) % BASE == iota((BASE, LANES), 0), 1.0, 0.0)

    def updates(first, inv, strips):
        state = {}

        def product():
            held = (wide >= first) & (wide < first + BASE)
            minus = jnp.where(wide - first == deep, -1.0, 0.0)
            stack = jnp.concatenate(
                [jnp.where(held, minus, s) for s in strips]
                + [jnp.zeros((LANES - blocks * BASE, BS), f32)],
                axis=0,
            )
            spread = diagonal(inv)[: blocks * BASE]
            new = dot(spread, stack, precision=highest)
            for m in range(blocks):
                state[m] = new[m * BASE : (m + 1) * BASE, :]

        def rows_of(m, low, high):
            def piece():
                r0, r1, r2 = split(strips[m][:, low:high], 3)
                p0, p1, p2 = split(state[m], 3)
                a = jnp.concatenate([r0, r0, r1, r1, r0, r2], axis=0).astype(bf16)
                b = jnp.concatenate([p0, p1, p0, p1, p2, p0], axis=0).astype(bf16)
                gone = (iota((1, BS), 1) >= first) & (iota((1, BS), 1) < first + BASE)
                work[m, low:high, :] = jnp.where(gone, 0.0, work[m, low:high, :]) - dot(a, b, TN)
                if low <= first < high:
                    work[m, first : first + BASE, :] = state[m]

            return piece

        half = BS // 2
        return [product] + [
            rows_of(m, low, low + half) for m in range(blocks) for low in range(0, BS, half)
        ]

    def strips_at(first):
        return [work[m, first : first + BASE, :] for m in range(blocks)]

    cells = jnp.where(seg < blocks, packed(strips_at(0), 0), eye)
    pending = []
    for first in range(0, BS, BASE):
        inv = -sweep_base(cells, pending)
        strips = strips_at(first)
        if first + BASE < BS:
            after = strips_at(first + BASE)
            half = dot(inv, diagonal(packed(strips, first + BASE)), precision=highest)
            drop = dot(packed(after, first), diagonal(half), precision=highest)
            cells = jnp.where(seg < blocks, packed(after, first + BASE) - drop, eye)
        pending = updates(first, inv, strips)
    for piece in pending:
        piece()
    for m in range(blocks):
        inv = -work[m]
        for i, part in enumerate(split(inv, 3)):
            jac_ref[i, m] = part.astype(bf16)
    pack_ref[SYS:, :] = smooth(sys_ref[...], jac_ref)


def own_places(m):
    return [(j, j, REACH + j - m) for j in range(REACH)]


def halo_places(m):
    lefts = [(j - m, j, j - m) for j in range(m, REACH)]
    return lefts + [(REACH - m + j, REACH + j, 2 * REACH - m + j) for j in range(m + 1)]


def build_kernel(*refs, places, sides):
    cells, (own_ref, extra_ref) = refs[:sides], refs[sides : sides + 2]
    hi_ref, lo_ref, sim_ref = refs[sides + 2 :]
    blocks = hi_ref.shape[0]
    near = []
    for ref in cells:
        near.append(near_stack(ref[0:FEAT, :], one_hot(ref[FEAT : FEAT + 1, :], TASKS)))
    mates, norm = own_stack(own_ref[0:FEAT, :], extra_ref[0:TASKS, :])
    weights = extra_ref[TASKS + 1 : TASKS + 2, :]
    for m in range(blocks):
        for row, j, o in places(m):
            part = near[j // REACH][(j % REACH) * BS : (j % REACH + 1) * BS]
            both = dot(part, mates[m])
            place = m * SLOTS + o
            exponent = both[:, :BS] + norm[:, m * BS : (m + 1) * BS]
            similar = weights[:, place : place + 1] * jnp.exp(exponent)
            kernel = similar * both[:, BS:]
            head = kernel.astype(bf16)
            rows = slice(row * BS, (row + 1) * BS)
            if o <= REACH or sides == 1:
                sim_ref[m, rows, :] = similar
            hi_ref[m, rows, :] = head
            lo_ref[m, rows, :] = (kernel - head.astype(f32)).astype(bf16)


def pieces(vectors):
    return jnp.concatenate(split(vectors, 2), axis=0).astype(bf16)


def apply(cells, hi, lo):
    rows = cells.shape[0] // 2
    first = dot(cells, hi)
    return first[:rows] + first[rows:] + dot(cells[:rows], lo)


def operate_own(own, noise, own_hi, own_lo):
    mine = pieces(own)
    out = [apply(mine, own_hi[m], own_lo[m]) for m in range(REACH)]
    return jnp.concatenate(out, axis=1) + noise * own


def operate_left(left, halo_hi, halo_lo):
    cells = pieces(left)
    out = []
    for m in range(REACH):
        part = slice(0, (REACH - m) * BS)
        out.append(apply(cells[:, m * BS :], halo_hi[m, part, :], halo_lo[m, part, :]))
    return jnp.concatenate(out, axis=1)


def operate_halo(left, right, halo_hi, halo_lo):
    lefts, rights = pieces(left), pieces(right)
    out = []
    for m in range(REACH):
        beyond = jnp.concatenate([lefts[:, m * BS :], rights[:, : (m + 1) * BS]], axis=1)
        out.append(apply(beyond, halo_hi[m], halo_lo[m]))
    return jnp.concatenate(out, axis=1)


def smooth_pieces(vectors, parts):
    rows = vectors.shape[0]
    cells = jnp.concatenate(split(vectors, 3), axis=0).astype(bf16)
    a = dot(cells, parts[0])
    b = dot(cells[: 2 * rows], parts[1])
    c = dot(cells[:rows], parts[2])
    return a[:rows] + (a[rows : 2 * rows] + b[:rows] + (a[2 * rows :] + b[rows:] + c))


def smooth(image, jac_ref):
    return jnp.concatenate(
        [
            smooth_pieces(image[:, m * BS : (m + 1) * BS], [jac_ref[i, m] for i in range(3)])
            for m in range(REACH)
        ],
        axis=1,
    )


def basis(pack_ref, coarse):
    z = one_hot(pack_ref[FEAT + 1 : FEAT + 2, :], coarse)
    return jnp.concatenate([pack_ref[SYS:, :], z], axis=0)


def build_own_kernel(own_ref, extra_ref, hi_ref, lo_ref, sim_ref, part_ref):
    build_kernel(
        own_ref, own_ref, extra_ref, hi_ref, lo_ref, sim_ref, places=own_places, sides=1
    )
    coarse = part_ref.shape[0] - (own_ref.shape[0] - SYS)
    noise = extra_ref[TASKS : TASKS + 1, :]
    part_ref[...] = operate_own(basis(own_ref, coarse), noise, hi_ref, lo_ref)


def first_kernel(part_ref, left_ref, right_ref, hi_ref, lo_ref, jac_ref, image_ref, next_ref):
    coarse = part_ref.shape[0] - (left_ref.shape[0] - SYS)
    ends = [basis(ref, coarse) for ref in (left_ref, right_ref)]
    image = part_ref[...] + operate_halo(*ends, hi_ref, lo_ref)
    image_ref[...] = image
    next_ref[...] = smooth(image, jac_ref)


def second_kernel(
    part_ref, left_ref, right_ref, sys_ref, hi_ref, lo_ref, jac_ref, image_ref, cargo_ref
):
    rows = part_ref.shape[0]
    image = part_ref[...] + operate_halo(left_ref[...], right_ref[...], hi_ref, lo_ref)
    image_ref[...] = image
    cargo_ref[0:rows, :] = smooth(image, jac_ref)
    cargo_ref[rows:, :] = sys_ref[...]


def pitch_of(coarse):
    return coarse + 1


def lanes_of(coarse):
    return -(-5 * pitch_of(coarse) // LANES) * LANES


def moment(vectors, images, pairs):
    count = pairs.shape[0]
    table = dot(images, vectors, NT, lax.Precision.HIGH)
    own = jnp.sum(pairs, axis=1, keepdims=True)
    if images.shape[0] > count:
        own = jnp.concatenate([own, jnp.zeros((images.shape[0] - count, 1), f32)], axis=0)
    return jnp.concatenate([table, own], axis=1)


def spread_out(parts, lanes):
    rows, pitch = next(iter(parts.values())).shape
    cells = [parts.get(k, jnp.zeros((rows, pitch), f32)) for k in range(5)]
    if lanes > 5 * pitch:
        cells.append(jnp.zeros((rows, lanes - 5 * pitch), f32))
    return jnp.concatenate(cells, axis=1)


def folded(low, high):
    order = low.shape[0]
    row, col = iota((order, order), 0), iota((order, order), 1)
    diagonal = jnp.sum(jnp.where(row == col, high, 0.0), axis=1, keepdims=True)
    return jnp.concatenate([jnp.where(row >= col, low, high), diagonal], axis=1)


def unfolded(cells):
    order = cells.shape[0]
    row, col = iota((order, order), 0), iota((order, order), 1)
    square = cells[:, :order]
    turned = dot(square, jnp.where(row == col, 1.0, 0.0), TN, highest)
    low = jnp.where(row >= col, square, turned)
    high = jnp.where(row < col, square, jnp.where(row > col, turned, cells[:, order:]))
    return low, high


def early_moments_kernel(
    own_ref, sys_ref, d1_ref, v0_ref, extra_ref, hi_ref, lo_ref, out_ref, part_ref
):
    part_ref[...] = operate_own(d1_ref[...], extra_ref[TASKS : TASKS + 1, :], hi_ref, lo_ref)
    count = own_ref.shape[0] - SYS
    coarse = d1_ref.shape[0] - count
    lanes = out_ref.shape[1]
    pitch = pitch_of(coarse)
    systems = sys_ref[...]
    pre = own_ref[SYS:, :]
    z = one_hot(own_ref[FEAT + 1 : FEAT + 2, :], coarse)
    d1, v0 = d1_ref[...], v0_ref[...]
    m0 = moment(z, v0, pre * v0[:count])
    m1 = moment(d1[count:], v0, d1[:count] * v0[:count])
    out_ref[0:count, :] = spread_out({0: m0[:count], 1: m1[:count]}, lanes)
    start = moment(z, systems, systems * pre)
    if coarse > count:
        start = jnp.concatenate([start, jnp.zeros((coarse - count, pitch), f32)], axis=0)
    fold = folded(m0[count:, :coarse], m1[count:, :coarse])
    out_ref[count:, :] = spread_out({0: fold, 3: start}, lanes)


def late_moments_kernel(
    before_ref, d1_ref, cargo_ref, v1_ref, extra_ref, hi_ref, lo_ref, out_ref, part_ref, *, count
):
    lanes = out_ref.shape[1]
    d1, d2, v1 = d1_ref[...], cargo_ref[0 : d1_ref.shape[0], :], v1_ref[...]
    part_ref[...] = operate_own(d2, extra_ref[TASKS : TASKS + 1, :], hi_ref, lo_ref)
    coarse = d1.shape[0] - count
    m2 = moment(d1[count:], v1, d1[:count] * v1[:count])
    m3 = moment(d2[count:], v1, d2[:count] * v1[:count])
    out_ref[0:count, :] = before_ref[0:count, :] + spread_out({2: m2[:count], 3: m3[:count]}, lanes)
    fold = folded(m2[count:, :coarse], m3[count:, :coarse])
    out_ref[count:, :] = before_ref[count:, :] + spread_out({1: fold}, lanes)


def third_kernel(
    extra_ref, before_ref, cargo_ref, left_ref, part_ref, hi_ref, lo_ref, out_ref, *, count, held
):
    rows = cargo_ref.shape[0] - count
    coarse = rows - count
    lanes = out_ref.shape[2]
    pitch = pitch_of(coarse)
    d2 = cargo_ref[0:rows, :]
    inner = part_ref[...]
    cross = operate_left(left_ref[0:rows, :], hi_ref, lo_ref)
    m4 = moment(d2[count:], inner + cross, d2[:count] * (inner + 2.0 * cross)[:count])
    mirror = dot(d2, cross[count:], NT, lax.Precision.HIGH)
    m4 = m4 + jnp.concatenate([mirror, jnp.zeros((rows, 1), f32)], axis=1)
    row = iota((coarse, 1), 0).astype(f32)
    start = extra_ref[TASKS + 2 : TASKS + 3, 0:1] * held
    inverse = jnp.zeros((coarse, pitch), f32)
    for r in range(held):
        line = extra_ref[TASKS + 3 + r : TASKS + 4 + r, 0:pitch]
        inverse = jnp.where(row == start + r, line, inverse)
    top = before_ref[0:count, :] + spread_out({4: m4[:count]}, lanes)
    bottom = before_ref[count:, :] + spread_out({2: m4[count:], 4: inverse}, lanes)
    for c in range(out_ref.shape[0]):
        out_ref[c, 0:count, :] = top
        out_ref[c, count:, :] = bottom


def final_kernel(
    gram_ref, own_ref, left_ref, d1_ref, d1l_ref, cargo_ref, cargol_ref, *refs, sides, points,
):
    kernel_refs, (sol_ref, grad_ref) = refs[:6], refs[6:]
    width = own_ref.shape[1]
    count = own_ref.shape[0] - SYS
    rows = d1_ref.shape[0]
    coarse = rows - count
    pitch = pitch_of(coarse)
    wide = -(-3 * pitch // LANES) * LANES
    blocks = width // BS
    gram = gram_ref[0]
    for c in range(1, gram_ref.shape[0]):
        gram = gram + gram_ref[c]
    bottom = gram[count:]
    gram = jnp.concatenate([gram[:count], jnp.zeros((count, wide), f32)], axis=1)
    squares = list(unfolded(bottom[:, :pitch])) + list(unfolded(bottom[:, pitch : 2 * pitch]))
    squares.append(bottom[:, 2 * pitch : 2 * pitch + coarse])
    lane = iota((1, wide), 1)
    slot, inside = lane // pitch, lane % pitch
    live = lane < 3 * pitch
    is_vec = live & (inside < coarse)
    is_one = live & (inside == coarse)

    def shifted(j):
        return jnp.where(live, gram[:, j * pitch : j * pitch + wide], 0.0)

    own = [shifted(j) for j in range(3)]
    gap = jnp.zeros((coarse, 1), f32)
    rest = jnp.zeros((coarse, wide - 3 * pitch), f32)
    hankel = []
    for i in range(3):
        line = [squares[i], gap, squares[i + 1], gap, squares[i + 2], gap]
        hankel.append(jnp.concatenate(line + ([rest] if wide > 3 * pitch else []), axis=1))
        hankel.append(jnp.zeros((1, wide), f32))
    if wide > 3 * pitch:
        hankel.append(jnp.zeros((wide - 3 * pitch, wide), f32))
    hankel = jnp.concatenate(hankel, axis=0)
    block0 = lane < pitch
    inverse = bottom[:, 4 * pitch : 4 * pitch + coarse]
    inverse = jnp.concatenate([inverse, jnp.zeros((coarse, wide - coarse), f32)], axis=1)
    inverse = jnp.concatenate([inverse, jnp.zeros((wide - coarse, wide), f32)], axis=0)
    start = bottom[:count, 3 * pitch : 4 * pitch]
    start = jnp.concatenate([start, jnp.zeros((count, wide - pitch), f32)], axis=1)
    against = jnp.where(
        block0, start, jnp.where(live, pltpu.roll(jnp.where(live, own[0], 0.0), pitch, axis=1), 0.0)
    )

    def total(x):
        return jnp.sum(x, axis=1, keepdims=True)

    def scalars(u, i):
        return total(jnp.where(lane == i * pitch + coarse, u, 0.0))

    def metric(u):
        out = dot(jnp.where(is_vec, u, 0.0), hankel, precision=highest)
        for j in range(3):
            out = out + scalars(u, j) * own[j]
        out = jnp.where(is_vec, out, 0.0)
        for i in range(3):
            out = jnp.where(lane == i * pitch + coarse, total(u * own[i]), out)
        return out

    def corrected(w):
        return dot(jnp.where(lane < coarse, w, 0.0), inverse, precision=highest)

    pre = corrected(against) + jnp.where(lane == coarse, 1.0, 0.0)
    direction = pre
    gamma = total(pre * against)
    answer = jnp.zeros_like(pre)
    image_sum = jnp.zeros_like(pre)
    for step in range(ITERS):
        image = metric(direction)
        alpha = gamma / total(direction * image)
        answer = answer + alpha * direction
        if step + 1 < ITERS:
            image_sum = image_sum + alpha * image
            moved_on = jnp.where(live & (slot > 0), pltpu.roll(direction, pitch, axis=1), 0.0)
            pre = pre - alpha * (moved_on + corrected(image))
            gamma_new = total(pre * (against - image_sum))
            direction = pre + (gamma_new / gamma) * direction
            gamma = gamma_new

    pack = jnp.concatenate([left_ref[...], own_ref[...]], axis=1)
    z = one_hot(pack[FEAT + 1 : FEAT + 2], coarse)
    q0 = pack[SYS:]
    d1 = jnp.concatenate([d1l_ref[...], d1_ref[...]], axis=1)
    cargo = jnp.concatenate([cargol_ref[...], cargo_ref[...]], axis=1)
    d2 = cargo[:rows]
    span = q0.shape[1]
    step = -(-coarse // FEAT) * FEAT
    deep = -(-3 * step // LANES) * LANES
    parts, planes = [], []
    for i, rest in enumerate((z, d1[count:], d2[count:])):
        parts.append(answer[:, i * pitch : i * pitch + coarse])
        planes.append(rest)
        if step > coarse:
            parts.append(jnp.zeros((count, step - coarse), f32))
            planes.append(jnp.zeros((step - coarse, span), f32))
    if deep > 3 * step:
        parts.append(jnp.zeros((count, deep - 3 * step), f32))
        planes.append(jnp.zeros((deep - 3 * step, span), f32))
    planes = [plane.astype(bf16) for plane in split(jnp.concatenate(planes, axis=0), 3)]
    x = smooth_pieces(jnp.concatenate(parts, axis=1), planes)
    x = x + scalars(answer, 0) * q0 + scalars(answer, 1) * d1[:count]
    x = x + scalars(answer, 2) * d2[:count]
    mine = slice(width, 2 * width)
    sol_ref[...] = x[:, mine]

    probe = own_ref[FEAT + 2 : FEAT + 3, 0:1]
    line = iota((count, 1), 0).astype(f32) + probe * count
    right = jnp.where(line == 0, x, cargo[rows:])
    coef = jnp.where(line == 0, 0.5 / points, -0.5 / (sides - 1) / points)
    r0, r1 = split(right, 2)
    w0, w1 = split(x * coef, 2)
    rest = jnp.zeros((LANES - 6 * count, span), f32)
    near = jnp.concatenate([w0, w1, w0, r0, r1, r0, rest], axis=0).T.astype(bf16)
    none = jnp.zeros((3 * count, width), f32)
    rest = rest[:, mine]
    ahead = jnp.concatenate([r0, r0, r1], axis=0)[:, mine]
    back = jnp.concatenate([w0, w0, w1], axis=0)[:, mine]
    mates = [
        jnp.concatenate([ahead, none, rest], axis=0).astype(bf16),
        jnp.concatenate([none, back, rest], axis=0).astype(bf16),
    ]
    scaled = pack[0:FEAT]
    table = one_hot(pack[FEAT : FEAT + 1], TASKS)
    ones = jnp.ones((8, span), f32)
    terms = jnp.concatenate([scaled, ones, scaled * scaled], axis=0)
    t0, t1 = split(terms, 2)
    pad8 = jnp.zeros((8, span), f32)
    both = jnp.concatenate([t0, pad8, t1, pad8], axis=0).astype(bf16)
    heads = jnp.concatenate([t0, pad8], axis=0).astype(bf16)
    tables = table.astype(bf16)
    high = 32
    length_total = jnp.zeros((FEAT, 1), f32)
    task_total = jnp.zeros((TASKS, TASKS), f32)
    for m in range(blocks):
        at = slice(m * BS, (m + 1) * BS)
        sums = jnp.zeros((high, BS), f32)
        held_sums = [jnp.zeros((TASKS, BS), f32) for _ in mates]
        places = [(1, row, j + REACH) for row, j, _ in own_places(m)]
        places += [(2, row, j) for row, j, _ in halo_places(m) if j < REACH]
        for orders, row, block in places:
            hi_ref, lo_ref, sim_ref = kernel_refs[3 * orders - 3 : 3 * orders]
            j = slice(block * BS, (block + 1) * BS)
            rows_at = slice(row * BS, (row + 1) * BS)
            outers = [dot(near[j], mate[:, at]) for mate in mates[:orders]]
            kernel = hi_ref[m, rows_at, :].astype(f32) + lo_ref[m, rows_at, :].astype(f32)
            similar = sim_ref[m, rows_at, :]
            energy = sum(outers) * kernel
            e0, e1 = (part.astype(bf16) for part in split(energy, 2))
            first = dot(both[:, j], e0)
            sums = sums + first[:high] + first[high:] + dot(heads[:, j], e1)
            for k in range(orders):
                h0, h1 = (part.astype(bf16) for part in split(outers[k] * similar, 2))
                held_sums[k] = held_sums[k] + dot(tables[:, j], h0) + dot(tables[:, j], h1)
        mid = slice(width + m * BS, width + (m + 1) * BS)
        left = scaled[:, mid]
        value = left * left * sums[FEAT : FEAT + 1] + sums[2 * FEAT : 3 * FEAT]
        value = value - 2.0 * left * sums[:FEAT]
        length_total = length_total + jnp.sum(value, axis=1, keepdims=True)
        task_total = task_total + dot(held_sums[0], table[:, mid], NT, highest)
        task_total = task_total + dot(table[:, mid], held_sums[1], NT, highest)
    half = TASKS // 2
    value = jnp.concatenate(
        [
            task_total[:half],
            task_total[half:],
            jnp.where(iota((half, FEAT), 0) == iota((half, FEAT), 1), length_total, 0.0),
            jnp.zeros((half, LANES - 2 * TASKS - FEAT), f32),
        ],
        axis=1,
    )
    for c in range(grad_ref.shape[0]):
        grad_ref[c] = value


def tail_kernel(parts_ref, length_ref, task_ref):
    total = parts_ref[0]
    for c in range(1, parts_ref.shape[0]):
        total = total + parts_ref[c]
    half = TASKS // 2
    task_ref[0:half, :] = total[:, :TASKS]
    task_ref[half:, :] = total[:, TASKS : 2 * TASKS]
    length_ref[...] = jnp.sum(total[:, 2 * TASKS : 2 * TASKS + FEAT], axis=0)


MIB = 1024 * 1024


def call(body, outs, args, name, smem=0, hbm=0, far_outs=0, scratch=(), flops=0, limit=16):
    if hbm:
        args = args[:-hbm] + [pltpu.with_memory_space_constraint(a, pltpu.HBM) for a in args[-hbm:]]
    if far_outs:
        outs = outs[:-far_outs] + [pltpu.HBM(o.shape, o.dtype) for o in outs[-far_outs:]]
    vm = pl.BlockSpec(memory_space=pltpu.VMEM)
    sm = pl.BlockSpec(memory_space=pltpu.SMEM)
    far = pl.BlockSpec(memory_space=pltpu.HBM)
    return pl.pallas_call(
        body,
        out_shape=outs,
        in_specs=[sm] * smem + [vm] * (len(args) - smem - hbm) + [far] * hbm,
        out_specs=[vm] * (len(outs) - far_outs) + [far] * far_outs,
        scratch_shapes=scratch,
        compiler_params=pltpu.CompilerParams(vmem_limit_bytes=limit * MIB),
        cost_estimate=pl.CostEstimate(flops=flops, bytes_accessed=1 << 20, transcendentals=0),
        name=name,
    )(*args)


def both_sides(cells):
    count = lax.axis_size("pts")
    up = [(i, i + 1) for i in range(count - 1)]
    down = [(i + 1, i) for i in range(count - 1)]
    return lax.ppermute(cells, "pts", up), lax.ppermute(cells, "pts", down)


def from_left(cells):
    count = lax.axis_size("pts")
    return lax.ppermute(cells, "pts", [(i, i + 1) for i in range(count - 1)])


def shards(
    systems, features, task_ids, pattern, aggregate, coarse_inverse, task_cov, lengthscales, noise
):
    count, width = systems.shape
    blocks = width // BS
    coarse = coarse_inverse.shape[1]
    rows = count + coarse
    lanes = lanes_of(coarse)
    assert blocks == REACH
    place = lax.axis_index("pts").astype(jnp.int32)[None]
    probe = lax.axis_index("probe").astype(jnp.int32)[None]
    ranks = lax.axis_size("pts")
    sides = lax.axis_size("probe")

    def shape(*dims, kind=f32):
        return jax.ShapeDtypeStruct(dims, kind)

    jac, pack, extra = call(
        invert_kernel,
        [shape(3, blocks, BS, BS, kind=bf16), shape(SYS + count, width), shape(TASKS + FEAT, width)],
        [place, probe, features, task_ids, aggregate, systems, task_cov, coarse_inverse, pattern, lengthscales, noise],
        "invert",
        smem=2,
        hbm=9,
        scratch=[
            pltpu.VMEM((blocks, BS, BS), f32),
            pltpu.VMEM(features.shape, f32),
            pltpu.VMEM(task_ids.shape, jnp.int32),
            pltpu.VMEM(aggregate.shape, jnp.int32),
            pltpu.VMEM(systems.shape, f32),
            pltpu.VMEM(task_cov.shape, f32),
            pltpu.VMEM(coarse_inverse.shape, f32),
            pltpu.SMEM(pattern.shape, jnp.int32),
            pltpu.SMEM(lengthscales.shape, f32),
            pltpu.SMEM(noise.shape, f32),
            pltpu.SemaphoreType.DMA((9,)),
        ],
        flops=10**10,
    )
    pack_l, pack_r = both_sides(pack)

    def cells_of(deep):
        return [
            shape(blocks, deep, BS, kind=bf16),
            shape(blocks, deep, BS, kind=bf16),
            shape(blocks, deep, BS),
        ]

    own_hi, own_lo, own_sim, part = call(
        build_own_kernel,
        cells_of(width) + [shape(rows, width)],
        [pack, extra],
        "build_own",
        flops=10**9,
    )
    halo_hi, halo_lo, halo_sim = call(
        functools.partial(build_kernel, places=halo_places, sides=2),
        cells_of(BAND - width),
        [pack_l, pack_r, pack, extra],
        "build_halo",
        flops=10**9,
    )
    own, halo = [own_hi, own_lo], [halo_hi, halo_lo]
    v0, d1 = call(
        first_kernel,
        [shape(rows, width), shape(rows, width)],
        [part, pack_l, pack_r] + halo + [jac],
        "first",
        flops=10**9,
    )
    d1_l, d1_r = both_sides(d1)
    early, part = call(
        early_moments_kernel,
        [shape(rows, lanes), shape(rows, width)],
        [pack, systems, d1, v0, extra] + own,
        "early",
        flops=10**9,
    )
    v1, cargo = call(
        second_kernel,
        [shape(rows, width), shape(rows + count, width)],
        [part, d1_l, d1_r, systems] + halo + [jac],
        "second",
        flops=10**9,
    )
    cargo_l = from_left(cargo)
    late, part = call(
        functools.partial(late_moments_kernel, count=count),
        [shape(rows, lanes), shape(rows, width)],
        [early, d1, cargo, v1, extra] + own,
        "late",
        flops=10**9,
    )
    (gram,) = call(
        functools.partial(third_kernel, count=count, held=coarse_inverse.shape[0]),
        [shape(ranks, rows, lanes)],
        [extra, late, cargo, cargo_l, part] + halo,
        "third",
        flops=10**9,
    )
    gram = lax.all_to_all(gram, "pts", 0, 0, tiled=True)
    cells = [own_hi, own_lo, own_sim, halo_hi, halo_lo, halo_sim]
    answer, grads = call(
        functools.partial(final_kernel, sides=sides * count, points=ranks * width),
        [shape(count, width), shape(ranks * sides, FEAT, LANES)],
        [gram, pack, pack_l, d1, d1_l, cargo, cargo_l] + cells,
        "final",
        flops=10**9,
    )
    grads = lax.all_to_all(grads, ("pts", "probe"), 0, 0, tiled=True)
    lengths, tasks = call(
        tail_kernel, [shape(FEAT), shape(TASKS, TASKS)], [grads], "tail", flops=10**5
    )
    return answer, lengths, tasks


def solution(mesh):
    return jax.shard_map(
        shards,
        mesh=mesh,
        in_specs=(
            P("probe", ("groups", "pts")),
            P(None, ("groups", "pts")),
            P(("groups", "pts")),
            P(("groups", "pts"), None),
            P(("groups", "pts")),
            P(("groups", "pts"), None),
            P("groups", None),
            P("groups"),
            P("groups"),
        ),
        out_specs=(P("probe", ("groups", "pts")), P("groups"), P("groups", None)),
        check_vma=False,
    )
```

```python
import functools

import jax
import jax.numpy as jnp
from jax import lax
from jax.experimental import pallas as pl
from jax.experimental.pallas import tpu as pltpu
from jax.sharding import PartitionSpec as P

BS = 256
REACH = 3
FEAT = 8
TASKS = 16
ITERS = 3
SLOTS = 2 * REACH + 1
BAND = SLOTS * BS
BASE = 32
GROUP = 4
LANES = 128
SYS = 2 * FEAT

highest = lax.Precision.HIGHEST
f32 = jnp.float32
bf16 = jnp.bfloat16
NN = (((1,), (0,)), ((), ()))
NT = (((1,), (1,)), ((), ()))
TN = (((0,), (0,)), ((), ()))


def dot(a, b, dims=NN, precision=None):
    return lax.dot_general(a, b, dims, precision=precision, preferred_element_type=f32)


def iota(shape, dim):
    return lax.broadcasted_iota(jnp.int32, shape, dim)


def split(x, parts):
    out = []
    for _ in range(parts - 1):
        head = x.astype(bf16).astype(f32)
        out.append(head)
        x = x - head
    out.append(x.astype(bf16).astype(f32))
    return out


def column(ref, size):
    rows = iota((size, 1), 0)
    out = jnp.zeros((size, 1), f32)
    for i in range(size):
        out = jnp.where(rows == i, ref[i], out)
    return out


def one_hot(ids, size):
    return (iota((size, ids.shape[1]), 0).astype(f32) == ids).astype(f32)


def noise_row(noise_ref, ids):
    out = jnp.zeros(ids.shape, f32)
    for t in range(TASKS):
        out = jnp.where(ids == float(t), noise_ref[t], out)
    return out


def weight(pat_ref, block, offset):
    if offset != REACH:
        return pat_ref[block, offset].astype(f32)
    total = pat_ref[block, 0]
    for o in range(1, SLOTS):
        total = total + pat_ref[block, o]
    return total.astype(f32)


def near_stack(scaled, table):
    s0, s1, s2 = split(scaled, 3)
    n0, n1, n2 = split(-0.5 * jnp.sum(scaled * scaled, axis=0, keepdims=True), 3)
    rows = iota(scaled.shape, 0)
    norms = jnp.where(rows == 0, n0, jnp.where(rows == 1, n1, jnp.where(rows == 2, n2, 0.0)))
    pad = jnp.zeros((LANES - 7 * FEAT - 3 * TASKS, scaled.shape[1]), f32)
    stack = jnp.concatenate([s0, s0, s1, s1, s0, s2, norms, table, table, table, pad], axis=0)
    return stack.T.astype(bf16)


def own_stack(scaled, picked):
    s0, s1, s2 = split(scaled, 3)
    rows = iota(scaled.shape, 0)
    ones = jnp.where(rows < 3, 1.0, 0.0)
    count = scaled.shape[1]
    tail = LANES - 7 * FEAT - 3 * TASKS
    left = jnp.concatenate(
        [s0, s1, s0, s1, s2, s0, ones, jnp.zeros((3 * TASKS + tail, count), f32)], axis=0
    ).astype(bf16)
    right = jnp.concatenate(
        [jnp.zeros((7 * FEAT, count), f32)] + split(picked, 3) + [jnp.zeros((tail, count), f32)],
        axis=0,
    ).astype(bf16)
    sides = [
        jnp.concatenate([left[:, i : i + BS], right[:, i : i + BS]], axis=1)
        for i in range(0, count, BS)
    ]
    return sides, -0.5 * jnp.sum(scaled * scaled, axis=0, keepdims=True)


def small_inverse(p):
    n = len(p)
    if n == 1:
        return [[pltpu.reciprocal(p[0][0], approx=True)]]
    if n == 2:
        a, b, d = p[0][0], p[0][1], p[1][1]
        r = pltpu.reciprocal(a * d - b * b, approx=True)
        off = -b * r
        return [[d * r, off], [off, a * r]]
    h = n // 2
    ainv = small_inverse([row[:h] for row in p[:h]])
    b = [row[h:] for row in p[:h]]
    t = [[sum(ainv[i][k] * b[k][j] for k in range(h)) for j in range(h)] for i in range(h)]
    s = [[None] * h for _ in range(h)]
    for i in range(h):
        for j in range(i, h):
            s[i][j] = s[j][i] = p[h + i][h + j] - sum(b[k][i] * t[k][j] for k in range(h))
    sinv = small_inverse(s)
    u = [[sum(t[i][k] * sinv[k][j] for k in range(h)) for j in range(h)] for i in range(h)]
    out = [[None] * n for _ in range(n)]
    for i in range(h):
        for j in range(h):
            out[h + i][h + j] = sinv[i][j]
            out[i][h + j] = out[h + j][i] = -u[i][j]
    for i in range(h):
        for j in range(i, h):
            out[i][j] = out[j][i] = ainv[i][j] + sum(u[i][k] * t[j][k] for k in range(h))
    return out


def sweep_base(cells, beside):
    tall = range(BASE // 8)
    tiles = [cells[8 * i : 8 * i + 8] for i in tall]
    lane = iota((8, LANES), 1)
    start = lane - lane % BASE
    inner = lane % BASE
    sub = iota((8, LANES), 0)

    def columns(first):
        return [
            [
                jnp.take_along_axis(tile, start + (first + t), axis=1, mode="promise_in_bounds")
                for tile in tiles
            ]
            for t in range(GROUP)
        ]

    def row(parts, r):
        return jnp.broadcast_to(parts[r // 8][r % 8 : r % 8 + 1, :], (8, LANES))

    def with_rows(parts, first, rows):
        part = parts[first // 8]
        for t, value in enumerate(rows):
            part = jnp.where(sub == first % 8 + t, value, part)
        return [part if i == first // 8 else parts[i] for i in tall]

    def less(parts, factor):
        out = []
        for i in tall:
            part = parts[i]
            for t in range(GROUP):
                part = part - cols[t][i] * factor[t]
            out.append(part)
        return out

    cols = columns(0)
    for first in range(0, BASE, GROUP):
        ahead = columns(first + GROUP) if first + GROUP < BASE else []
        pivots = [[None] * GROUP for _ in range(GROUP)]
        for t in range(GROUP):
            for u in range(t, GROUP):
                pivots[t][u] = pivots[u][t] = row(cols[u], first + t)
        inv = small_inverse(pivots)
        coming = []
        for col in ahead:
            head = [row(col, first + t) for t in range(GROUP)]
            factor = [sum(inv[t][u] * head[u] for u in range(GROUP)) for t in range(GROUP)]
            coming.append(with_rows(less(col, factor), first, factor))
        group = (inner >= first) & (inner < first + GROUP)
        rows = []
        for t in range(GROUP):
            value = jnp.where(group, 0.0, row(tiles, first + t))
            rows.append(jnp.where(inner == first + t, -1.0, value))
        new = [sum(inv[t][u] * rows[u] for u in range(GROUP)) for t in range(GROUP)]
        tiles = [jnp.where(group, 0.0, tile) for tile in tiles]
        tiles = with_rows(less(tiles, new), first, new)
        cols = coming
        if beside:
            beside.pop(0)()
    while beside:
        beside.pop(0)()
    return jnp.concatenate(tiles, axis=0)


def fetch(pairs, sems):
    copies = [pltpu.make_async_copy(a, b, sems.at[i]) for i, (a, b) in enumerate(pairs)]
    for copy in copies:
        copy.start()
    return copies


def invert_kernel(
    place_ref, probe_ref, feat_hbm, ids_hbm, agg_hbm, sys_hbm, cov_hbm, coarse_hbm, pat_hbm, len_hbm, noise_hbm,
    jac_ref, pack_ref, extra_ref,
    work, feat_ref, ids_ref, agg_ref, sys_ref, cov_ref, coarse_ref, pat_ref, len_ref, noise_ref, sems,
):
    blocks = work.shape[0]
    width = blocks * BS
    pairs = [
        (feat_hbm, feat_ref), (ids_hbm, ids_ref), (agg_hbm, agg_ref), (cov_hbm, cov_ref),
        (pat_hbm, pat_ref), (len_hbm, len_ref), (noise_hbm, noise_ref), (coarse_hbm, coarse_ref),
        (sys_hbm, sys_ref),
    ]
    copies = fetch(pairs, sems)
    for copy in copies[:-1]:
        copy.wait()
    scaled = feat_ref[...] / column(len_ref, FEAT)
    ids = ids_ref[...].astype(f32).reshape(1, width)
    which = agg_ref[...].astype(f32).reshape(1, width)
    table = one_hot(ids, TASKS)
    noise = noise_row(noise_ref, ids)
    c0, c1, c2 = split(cov_ref[...], 3)
    tab = table.astype(bf16)
    picked = (dot(c2.astype(bf16), tab) + dot(c1.astype(bf16), tab)) + dot(c0.astype(bf16), tab)
    rows = iota((FEAT, width), 0)
    weights = jnp.zeros((1, width), f32)
    places = iota((1, width), 1)
    for m in range(blocks):
        for o in range(SLOTS):
            weights = jnp.where(places == m * SLOTS + o, weight(pat_ref, m, o), weights)
    pack_ref[0:FEAT, :] = scaled
    pack_ref[FEAT : 2 * FEAT, :] = jnp.where(
        rows == 0,
        ids,
        jnp.where(rows == 1, which, jnp.where(rows == 2, probe_ref[0].astype(f32), 0.0)),
    )
    extra_ref[0:TASKS, :] = picked
    tail = jnp.where(rows == 0, noise, jnp.where(rows == 1, weights, 0.0))
    held = coarse_ref.shape[0]
    inverse = jnp.concatenate(
        [coarse_ref[...], jnp.zeros((held, width - coarse_ref.shape[1]), f32)], axis=1
    )
    tail = jnp.where(rows == 2, place_ref[0].astype(f32), tail)
    for r in range(held):
        tail = jnp.where(rows == 3 + r, inverse[r : r + 1], tail)
    extra_ref[TASKS : TASKS + FEAT, :] = tail
    near = near_stack(scaled, table)
    mates, norm = own_stack(scaled, picked)
    eye = iota((BS, BS), 0) == iota((BS, BS), 1)
    for m in range(blocks):
        at = slice(m * BS, (m + 1) * BS)
        both = dot(near[at], mates[m])
        block = weight(pat_ref, m, REACH) * jnp.exp(both[:, :BS] + norm[:, at]) * both[:, BS:]
        work[m] = block + jnp.where(eye, noise[:, at], 0.0)
    seg = iota((BASE, LANES), 1) // BASE
    wide = iota((BASE, BS), 1)
    deep = iota((BASE, BS), 0)

    def packed(strips, first):
        tile, inside = first // LANES, first % LANES
        cells = jnp.zeros((BASE, LANES), f32)
        for m in range(blocks):
            piece = strips[m][:, tile * LANES : (tile + 1) * LANES]
            shift = (BASE * m - inside) % LANES
            if shift:
                piece = pltpu.roll(piece, shift, axis=1)
            cells = jnp.where(seg == m, piece, cells)
        return cells

    def diagonal(cells):
        parts = [jnp.where(seg == m, cells, 0.0) for m in range(LANES // BASE)]
        return jnp.concatenate(parts, axis=0)

    eye = jnp.where(iota((BASE, LANES), 1) % BASE == iota((BASE, LANES), 0), 1.0, 0.0)

    def updates(first, inv, strips):
        state = {}

        def product():
            held = (wide >= first) & (wide < first + BASE)
            minus = jnp.where(wide - first == deep, -1.0, 0.0)
            stack = jnp.concatenate(
                [jnp.where(held, minus, s) for s in strips]
                + [jnp.zeros((LANES - blocks * BASE, BS), f32)],
                axis=0,
            )
            spread = diagonal(inv)[: blocks * BASE]
            new = dot(spread, stack, precision=highest)
            for m in range(blocks):
                state[m] = new[m * BASE : (m + 1) * BASE, :]

        def rows_of(m, low, high):
            def piece():
                r0, r1, r2 = split(strips[m][:, low:high], 3)
                p0, p1, p2 = split(state[m], 3)
                a = jnp.concatenate([r0, r0, r1, r1, r0, r2], axis=0).astype(bf16)
                b = jnp.concatenate([p0, p1, p0, p1, p2, p0], axis=0).astype(bf16)
                gone = (iota((1, BS), 1) >= first) & (iota((1, BS), 1) < first + BASE)
                work[m, low:high, :] = jnp.where(gone, 0.0, work[m, low:high, :]) - dot(a, b, TN)
                if low <= first < high:
                    work[m, first : first + BASE, :] = state[m]

            return piece

        half = BS // 2
        return [product] + [
            rows_of(m, low, low + half) for m in range(blocks) for low in range(0, BS, half)
        ]

    def strips_at(first):
        return [work[m, first : first + BASE, :] for m in range(blocks)]

    cells = jnp.where(seg < blocks, packed(strips_at(0), 0), eye)
    pending = []
    for first in range(0, BS, BASE):
        inv = -sweep_base(cells, pending)
        strips = strips_at(first)
        if first + BASE < BS:
            after = strips_at(first + BASE)
            half = dot(inv, diagonal(packed(strips, first + BASE)), precision=highest)
            drop = dot(packed(after, first), diagonal(half), precision=highest)
            cells = jnp.where(seg < blocks, packed(after, first + BASE) - drop, eye)
        pending = updates(first, inv, strips)
    for piece in pending:
        piece()
    for m in range(blocks):
        inv = -work[m]
        for i, part in enumerate(split(inv, 3)):
            jac_ref[i, m] = part.astype(bf16)
    copies[-1].wait()
    pack_ref[SYS:, :] = smooth(sys_ref[...], jac_ref)


def own_places(m):
    return [(j, j, REACH + j - m) for j in range(REACH)]


def halo_places(m):
    lefts = [(j - m, j, j - m) for j in range(m, REACH)]
    return lefts + [(REACH - m + j, REACH + j, 2 * REACH - m + j) for j in range(m + 1)]


def build_kernel(*refs, places, sides):
    cells, (own_ref, extra_ref) = refs[:sides], refs[sides : sides + 2]
    hi_ref, lo_ref, sim_ref = refs[sides + 2 :]
    blocks = hi_ref.shape[0]
    near = []
    for ref in cells:
        near.append(near_stack(ref[0:FEAT, :], one_hot(ref[FEAT : FEAT + 1, :], TASKS)))
    mates, norm = own_stack(own_ref[0:FEAT, :], extra_ref[0:TASKS, :])
    weights = extra_ref[TASKS + 1 : TASKS + 2, :]
    for m in range(blocks):
        for row, j, o in places(m):
            part = near[j // REACH][(j % REACH) * BS : (j % REACH + 1) * BS]
            both = dot(part, mates[m])
            place = m * SLOTS + o
            exponent = both[:, :BS] + norm[:, m * BS : (m + 1) * BS]
            similar = weights[:, place : place + 1] * jnp.exp(exponent)
            kernel = similar * both[:, BS:]
            head = kernel.astype(bf16)
            rows = slice(row * BS, (row + 1) * BS)
            if o <= REACH or sides == 1:
                sim_ref[m, rows, :] = similar
            hi_ref[m, rows, :] = head
            lo_ref[m, rows, :] = (kernel - head.astype(f32)).astype(bf16)


def pieces(vectors):
    return jnp.concatenate(split(vectors, 2), axis=0).astype(bf16)


def apply(cells, hi, lo):
    rows = cells.shape[0] // 2
    first = dot(cells, hi)
    return first[:rows] + first[rows:] + dot(cells[:rows], lo)


def operate_own(own, noise, own_hi, own_lo):
    mine = pieces(own)
    out = [apply(mine, own_hi[m], own_lo[m]) for m in range(REACH)]
    return jnp.concatenate(out, axis=1) + noise * own


def operate_left(left, halo_hi, halo_lo):
    cells = pieces(left)
    out = []
    for m in range(REACH):
        part = slice(0, (REACH - m) * BS)
        out.append(apply(cells[:, m * BS :], halo_hi[m, part, :], halo_lo[m, part, :]))
    return jnp.concatenate(out, axis=1)


def operate_halo(left, right, halo_hi, halo_lo):
    lefts, rights = pieces(left), pieces(right)
    out = []
    for m in range(REACH):
        beyond = jnp.concatenate([lefts[:, m * BS :], rights[:, : (m + 1) * BS]], axis=1)
        out.append(apply(beyond, halo_hi[m], halo_lo[m]))
    return jnp.concatenate(out, axis=1)


def smooth_pieces(vectors, parts):
    rows = vectors.shape[0]
    cells = jnp.concatenate(split(vectors, 3), axis=0).astype(bf16)
    a = dot(cells, parts[0])
    b = dot(cells[: 2 * rows], parts[1])
    c = dot(cells[:rows], parts[2])
    return a[:rows] + (a[rows : 2 * rows] + b[:rows] + (a[2 * rows :] + b[rows:] + c))


def smooth(image, jac_ref):
    return jnp.concatenate(
        [
            smooth_pieces(image[:, m * BS : (m + 1) * BS], [jac_ref[i, m] for i in range(3)])
            for m in range(REACH)
        ],
        axis=1,
    )


def basis(pack_ref, coarse):
    z = one_hot(pack_ref[FEAT + 1 : FEAT + 2, :], coarse)
    return jnp.concatenate([pack_ref[SYS:, :], z], axis=0)


def build_own_kernel(own_ref, extra_ref, hi_ref, lo_ref, sim_ref, part_ref):
    build_kernel(
        own_ref, own_ref, extra_ref, hi_ref, lo_ref, sim_ref, places=own_places, sides=1
    )
    coarse = part_ref.shape[0] - (own_ref.shape[0] - SYS)
    noise = extra_ref[TASKS : TASKS + 1, :]
    part_ref[...] = operate_own(basis(own_ref, coarse), noise, hi_ref, lo_ref)


def first_kernel(part_ref, left_ref, right_ref, hi_ref, lo_ref, jac_ref, image_ref, next_ref):
    coarse = part_ref.shape[0] - (left_ref.shape[0] - SYS)
    ends = [basis(ref, coarse) for ref in (left_ref, right_ref)]
    image = part_ref[...] + operate_halo(*ends, hi_ref, lo_ref)
    image_ref[...] = image
    next_ref[...] = smooth(image, jac_ref)


def second_kernel(
    part_ref, left_ref, right_ref, sys_ref, hi_ref, lo_ref, jac_ref, image_ref, cargo_ref
):
    rows = part_ref.shape[0]
    image = part_ref[...] + operate_halo(left_ref[...], right_ref[...], hi_ref, lo_ref)
    image_ref[...] = image
    cargo_ref[0:rows, :] = smooth(image, jac_ref)
    cargo_ref[rows:, :] = sys_ref[...]


def pitch_of(coarse):
    return coarse + 1


def lanes_of(coarse):
    return -(-5 * pitch_of(coarse) // LANES) * LANES


def moment(vectors, images, pairs):
    count = pairs.shape[0]
    table = dot(images, vectors, NT, lax.Precision.HIGH)
    own = jnp.sum(pairs, axis=1, keepdims=True)
    if images.shape[0] > count:
        own = jnp.concatenate([own, jnp.zeros((images.shape[0] - count, 1), f32)], axis=0)
    return jnp.concatenate([table, own], axis=1)


def spread_out(parts, lanes):
    rows, pitch = next(iter(parts.values())).shape
    cells = [parts.get(k, jnp.zeros((rows, pitch), f32)) for k in range(5)]
    if lanes > 5 * pitch:
        cells.append(jnp.zeros((rows, lanes - 5 * pitch), f32))
    return jnp.concatenate(cells, axis=1)


def folded(low, high):
    order = low.shape[0]
    row, col = iota((order, order), 0), iota((order, order), 1)
    diagonal = jnp.sum(jnp.where(row == col, high, 0.0), axis=1, keepdims=True)
    return jnp.concatenate([jnp.where(row >= col, low, high), diagonal], axis=1)


def unfolded(cells):
    order = cells.shape[0]
    row, col = iota((order, order), 0), iota((order, order), 1)
    square = cells[:, :order]
    turned = dot(square, jnp.where(row == col, 1.0, 0.0), TN, highest)
    low = jnp.where(row >= col, square, turned)
    high = jnp.where(row < col, square, jnp.where(row > col, turned, cells[:, order:]))
    return low, high


def early_moments_kernel(
    own_ref, sys_ref, d1_ref, v0_ref, extra_ref, hi_ref, lo_ref, out_ref, part_ref
):
    part_ref[...] = operate_own(d1_ref[...], extra_ref[TASKS : TASKS + 1, :], hi_ref, lo_ref)
    count = own_ref.shape[0] - SYS
    coarse = d1_ref.shape[0] - count
    lanes = out_ref.shape[1]
    pitch = pitch_of(coarse)
    systems = sys_ref[...]
    pre = own_ref[SYS:, :]
    z = one_hot(own_ref[FEAT + 1 : FEAT + 2, :], coarse)
    d1, v0 = d1_ref[...], v0_ref[...]
    m0 = moment(z, v0, pre * v0[:count])
    m1 = moment(d1[count:], v0, d1[:count] * v0[:count])
    out_ref[0:count, :] = spread_out({0: m0[:count], 1: m1[:count]}, lanes)
    start = moment(z, systems, systems * pre)
    if coarse > count:
        start = jnp.concatenate([start, jnp.zeros((coarse - count, pitch), f32)], axis=0)
    fold = folded(m0[count:, :coarse], m1[count:, :coarse])
    out_ref[count:, :] = spread_out({0: fold, 3: start}, lanes)


def late_moments_kernel(
    before_ref, d1_ref, cargo_ref, v1_ref, extra_ref, hi_ref, lo_ref, out_ref, part_ref, *, count
):
    lanes = out_ref.shape[1]
    d1, d2, v1 = d1_ref[...], cargo_ref[0 : d1_ref.shape[0], :], v1_ref[...]
    part_ref[...] = operate_own(d2, extra_ref[TASKS : TASKS + 1, :], hi_ref, lo_ref)
    coarse = d1.shape[0] - count
    m2 = moment(d1[count:], v1, d1[:count] * v1[:count])
    m3 = moment(d2[count:], v1, d2[:count] * v1[:count])
    out_ref[0:count, :] = before_ref[0:count, :] + spread_out({2: m2[:count], 3: m3[:count]}, lanes)
    fold = folded(m2[count:, :coarse], m3[count:, :coarse])
    out_ref[count:, :] = before_ref[count:, :] + spread_out({1: fold}, lanes)


def third_kernel(
    extra_ref, before_ref, cargo_ref, left_ref, part_ref, hi_ref, lo_ref, out_ref, *, count, held
):
    rows = cargo_ref.shape[0] - count
    coarse = rows - count
    lanes = out_ref.shape[2]
    pitch = pitch_of(coarse)
    d2 = cargo_ref[0:rows, :]
    inner = part_ref[...]
    cross = operate_left(left_ref[0:rows, :], hi_ref, lo_ref)
    m4 = moment(d2[count:], inner + cross, d2[:count] * (inner + 2.0 * cross)[:count])
    mirror = dot(d2, cross[count:], NT, lax.Precision.HIGH)
    m4 = m4 + jnp.concatenate([mirror, jnp.zeros((rows, 1), f32)], axis=1)
    row = iota((coarse, 1), 0).astype(f32)
    start = extra_ref[TASKS + 2 : TASKS + 3, 0:1] * held
    inverse = jnp.zeros((coarse, pitch), f32)
    for r in range(held):
        line = extra_ref[TASKS + 3 + r : TASKS + 4 + r, 0:pitch]
        inverse = jnp.where(row == start + r, line, inverse)
    top = before_ref[0:count, :] + spread_out({4: m4[:count]}, lanes)
    bottom = before_ref[count:, :] + spread_out({2: m4[count:], 4: inverse}, lanes)
    for c in range(out_ref.shape[0]):
        out_ref[c, 0:count, :] = top
        out_ref[c, count:, :] = bottom


def final_kernel(
    gram_ref, own_ref, left_ref, d1_ref, d1l_ref, cargo_ref, cargol_ref, *refs, sides, points,
):
    kernel_refs, (grad_ref, sol_hbm, sol_ref, sem) = refs[:6], refs[6:]
    width = own_ref.shape[1]
    count = own_ref.shape[0] - SYS
    rows = d1_ref.shape[0]
    coarse = rows - count
    pitch = pitch_of(coarse)
    wide = -(-3 * pitch // LANES) * LANES
    blocks = width // BS
    gram = gram_ref[0]
    for c in range(1, gram_ref.shape[0]):
        gram = gram + gram_ref[c]
    bottom = gram[count:]
    gram = jnp.concatenate([gram[:count], jnp.zeros((count, wide), f32)], axis=1)
    squares = list(unfolded(bottom[:, :pitch])) + list(unfolded(bottom[:, pitch : 2 * pitch]))
    squares.append(bottom[:, 2 * pitch : 2 * pitch + coarse])
    lane = iota((1, wide), 1)
    slot, inside = lane // pitch, lane % pitch
    live = lane < 3 * pitch
    is_vec = live & (inside < coarse)
    is_one = live & (inside == coarse)

    def shifted(j):
        return jnp.where(live, gram[:, j * pitch : j * pitch + wide], 0.0)

    own = [shifted(j) for j in range(3)]
    gap = jnp.zeros((coarse, 1), f32)
    rest = jnp.zeros((coarse, wide - 3 * pitch), f32)
    hankel = []
    for i in range(3):
        line = [squares[i], gap, squares[i + 1], gap, squares[i + 2], gap]
        hankel.append(jnp.concatenate(line + ([rest] if wide > 3 * pitch else []), axis=1))
        hankel.append(jnp.zeros((1, wide), f32))
    if wide > 3 * pitch:
        hankel.append(jnp.zeros((wide - 3 * pitch, wide), f32))
    hankel = jnp.concatenate(hankel, axis=0)
    block0 = lane < pitch
    inverse = bottom[:, 4 * pitch : 4 * pitch + coarse]
    inverse = jnp.concatenate([inverse, jnp.zeros((coarse, wide - coarse), f32)], axis=1)
    inverse = jnp.concatenate([inverse, jnp.zeros((wide - coarse, wide), f32)], axis=0)
    start = bottom[:count, 3 * pitch : 4 * pitch]
    start = jnp.concatenate([start, jnp.zeros((count, wide - pitch), f32)], axis=1)
    against = jnp.where(
        block0, start, jnp.where(live, pltpu.roll(jnp.where(live, own[0], 0.0), pitch, axis=1), 0.0)
    )

    def total(x):
        return jnp.sum(x, axis=1, keepdims=True)

    def metric(u, chain):
        vec = dot(jnp.where(is_vec, u, 0.0), hankel, precision=highest)
        for j in range(3):
            vec = vec + chain[j] * own[j]
        vec = jnp.where(is_vec, vec, 0.0)
        picked = [total(u * own[i]) for i in range(3)]
        out = vec
        for i in range(3):
            out = jnp.where(lane == i * pitch + coarse, picked[i], out)
        curve = total(u * vec)
        for i in range(3):
            curve = curve + chain[i] * picked[i]
        return out, curve

    def corrected(w):
        return dot(jnp.where(lane < coarse, w, 0.0), inverse, precision=highest)

    one, zero = jnp.ones((count, 1), f32), jnp.zeros((count, 1), f32)
    pre = corrected(against) + jnp.where(lane == coarse, 1.0, 0.0)
    pre_chain = [one, zero, zero]
    direction, chain = pre, pre_chain
    gamma = total(pre * against)
    answer = jnp.zeros_like(pre)
    answer_chain = [zero] * 3
    image_sum = jnp.zeros_like(pre)
    for step in range(ITERS):
        image, curve = metric(direction, chain)
        alpha = gamma / curve
        answer = answer + alpha * direction
        answer_chain = [a + alpha * c for a, c in zip(answer_chain, chain)]
        if step + 1 < ITERS:
            image_sum = image_sum + alpha * image
            moved_on = jnp.where(live & (slot > 0), pltpu.roll(direction, pitch, axis=1), 0.0)
            pre = pre - alpha * (moved_on + corrected(image))
            pre_chain = [p - alpha * c for p, c in zip(pre_chain, [zero] + chain[:2])]
            gamma_new = total(pre * (against - image_sum))
            beta = gamma_new / gamma
            direction = pre + beta * direction
            chain = [p + beta * c for p, c in zip(pre_chain, chain)]
            gamma = gamma_new

    pack = jnp.concatenate([left_ref[...], own_ref[...]], axis=1)
    z = one_hot(pack[FEAT + 1 : FEAT + 2], coarse)
    q0 = pack[SYS:]
    d1 = jnp.concatenate([d1l_ref[...], d1_ref[...]], axis=1)
    cargo = jnp.concatenate([cargol_ref[...], cargo_ref[...]], axis=1)
    d2 = cargo[:rows]
    span = q0.shape[1]
    step = -(-coarse // FEAT) * FEAT
    deep = -(-3 * step // LANES) * LANES
    parts, planes = [], []
    for i, rest in enumerate((z, d1[count:], d2[count:])):
        parts.append(answer[:, i * pitch : i * pitch + coarse])
        planes.append(rest)
        if step > coarse:
            parts.append(jnp.zeros((count, step - coarse), f32))
            planes.append(jnp.zeros((step - coarse, span), f32))
    if deep > 3 * step:
        parts.append(jnp.zeros((count, deep - 3 * step), f32))
        planes.append(jnp.zeros((deep - 3 * step, span), f32))
    planes = [plane.astype(bf16) for plane in split(jnp.concatenate(planes, axis=0), 3)]
    x = smooth_pieces(jnp.concatenate(parts, axis=1), planes)
    x = x + answer_chain[0] * q0 + answer_chain[1] * d1[:count] + answer_chain[2] * d2[:count]
    mine = slice(width, 2 * width)
    sol_ref[...] = x[:, mine]
    leave = pltpu.make_async_copy(sol_ref, sol_hbm, sem)
    leave.start()

    probe = own_ref[FEAT + 2 : FEAT + 3, 0:1]
    line = iota((count, 1), 0).astype(f32) + probe * count
    right = jnp.where(line == 0, x, cargo[rows:])
    coef = jnp.where(line == 0, 0.5 / points, -0.5 / (sides - 1) / points)
    r0, r1 = split(right, 2)
    w0, w1 = split(x * coef, 2)
    rest = jnp.zeros((LANES - 6 * count, span), f32)
    near = jnp.concatenate([w0, w1, w0, r0, r1, r0, rest], axis=0).T.astype(bf16)
    none = jnp.zeros((3 * count, width), f32)
    rest = rest[:, mine]
    ahead = jnp.concatenate([r0, r0, r1], axis=0)[:, mine]
    back = jnp.concatenate([w0, w0, w1], axis=0)[:, mine]
    mates = [
        jnp.concatenate([ahead, none, rest], axis=0).astype(bf16),
        jnp.concatenate([none, back, rest], axis=0).astype(bf16),
    ]
    scaled = pack[0:FEAT]
    table = one_hot(pack[FEAT : FEAT + 1], TASKS)
    ones = jnp.ones((8, span), f32)
    terms = jnp.concatenate([scaled, ones, scaled * scaled], axis=0)
    t0, t1 = split(terms, 2)
    pad8 = jnp.zeros((8, span), f32)
    both = jnp.concatenate([t0, pad8, t1, pad8], axis=0).astype(bf16)
    heads = jnp.concatenate([t0, pad8], axis=0).astype(bf16)
    tables = table.astype(bf16)
    high = 32
    length_total = jnp.zeros((FEAT, 1), f32)
    task_total = jnp.zeros((TASKS, TASKS), f32)
    for m in range(blocks):
        at = slice(m * BS, (m + 1) * BS)
        sums = jnp.zeros((high, BS), f32)
        held_sums = [jnp.zeros((TASKS, BS), f32) for _ in mates]
        places = [(1, row, j + REACH) for row, j, _ in own_places(m)]
        places += [(2, row, j) for row, j, _ in halo_places(m) if j < REACH]
        for orders, row, block in places:
            hi_ref, lo_ref, sim_ref = kernel_refs[3 * orders - 3 : 3 * orders]
            j = slice(block * BS, (block + 1) * BS)
            rows_at = slice(row * BS, (row + 1) * BS)
            outers = [dot(near[j], mate[:, at]) for mate in mates[:orders]]
            kernel = hi_ref[m, rows_at, :].astype(f32) + lo_ref[m, rows_at, :].astype(f32)
            similar = sim_ref[m, rows_at, :]
            energy = sum(outers) * kernel
            e0, e1 = (part.astype(bf16) for part in split(energy, 2))
            first = dot(both[:, j], e0)
            sums = sums + first[:high] + first[high:] + dot(heads[:, j], e1)
            for k in range(orders):
                h0, h1 = (part.astype(bf16) for part in split(outers[k] * similar, 2))
                held_sums[k] = held_sums[k] + dot(tables[:, j], h0) + dot(tables[:, j], h1)
        mid = slice(width + m * BS, width + (m + 1) * BS)
        left = scaled[:, mid]
        value = left * left * sums[FEAT : FEAT + 1] + sums[2 * FEAT : 3 * FEAT]
        value = value - 2.0 * left * sums[:FEAT]
        length_total = length_total + jnp.sum(value, axis=1, keepdims=True)
        task_total = task_total + dot(held_sums[0], table[:, mid], NT, highest)
        task_total = task_total + dot(table[:, mid], held_sums[1], NT, highest)
    half = TASKS // 2
    value = jnp.concatenate(
        [
            task_total[:half],
            task_total[half:],
            jnp.where(iota((half, FEAT), 0) == iota((half, FEAT), 1), length_total, 0.0),
            jnp.zeros((half, LANES - 2 * TASKS - FEAT), f32),
        ],
        axis=1,
    )
    for c in range(grad_ref.shape[0]):
        grad_ref[c] = value
    leave.wait()


def tail_kernel(parts_ref, length_ref, task_ref):
    total = parts_ref[0]
    for c in range(1, parts_ref.shape[0]):
        total = total + parts_ref[c]
    half = TASKS // 2
    task_ref[0:half, :] = total[:, :TASKS]
    task_ref[half:, :] = total[:, TASKS : 2 * TASKS]
    length_ref[...] = jnp.sum(total[:, 2 * TASKS : 2 * TASKS + FEAT], axis=0)


MIB = 1024 * 1024


def call(body, outs, args, name, smem=0, hbm=0, far_outs=0, scratch=(), flops=0, limit=16):
    if hbm:
        args = args[:-hbm] + [pltpu.with_memory_space_constraint(a, pltpu.HBM) for a in args[-hbm:]]
    if far_outs:
        outs = outs[:-far_outs] + [pltpu.HBM(o.shape, o.dtype) for o in outs[-far_outs:]]
    vm = pl.BlockSpec(memory_space=pltpu.VMEM)
    sm = pl.BlockSpec(memory_space=pltpu.SMEM)
    far = pl.BlockSpec(memory_space=pltpu.HBM)
    return pl.pallas_call(
        body,
        out_shape=outs,
        in_specs=[sm] * smem + [vm] * (len(args) - smem - hbm) + [far] * hbm,
        out_specs=[vm] * (len(outs) - far_outs) + [far] * far_outs,
        scratch_shapes=scratch,
        compiler_params=pltpu.CompilerParams(vmem_limit_bytes=limit * MIB),
        cost_estimate=pl.CostEstimate(flops=flops, bytes_accessed=1 << 20, transcendentals=0),
        name=name,
    )(*args)


def both_sides(cells):
    count = lax.axis_size("pts")
    up = [(i, i + 1) for i in range(count - 1)]
    down = [(i + 1, i) for i in range(count - 1)]
    return lax.ppermute(cells, "pts", up), lax.ppermute(cells, "pts", down)


def from_left(cells):
    count = lax.axis_size("pts")
    return lax.ppermute(cells, "pts", [(i, i + 1) for i in range(count - 1)])


def shards(
    systems, features, task_ids, pattern, aggregate, coarse_inverse, task_cov, lengthscales, noise
):
    count, width = systems.shape
    blocks = width // BS
    coarse = coarse_inverse.shape[1]
    rows = count + coarse
    lanes = lanes_of(coarse)
    assert blocks == REACH
    place = lax.axis_index("pts").astype(jnp.int32)[None]
    probe = lax.axis_index("probe").astype(jnp.int32)[None]
    ranks = lax.axis_size("pts")
    sides = lax.axis_size("probe")

    def shape(*dims, kind=f32):
        return jax.ShapeDtypeStruct(dims, kind)

    jac, pack, extra = call(
        invert_kernel,
        [shape(3, blocks, BS, BS, kind=bf16), shape(SYS + count, width), shape(TASKS + FEAT, width)],
        [place, probe, features, task_ids, aggregate, systems, task_cov, coarse_inverse, pattern, lengthscales, noise],
        "invert",
        smem=2,
        hbm=9,
        scratch=[
            pltpu.VMEM((blocks, BS, BS), f32),
            pltpu.VMEM(features.shape, f32),
            pltpu.VMEM(task_ids.shape, jnp.int32),
            pltpu.VMEM(aggregate.shape, jnp.int32),
            pltpu.VMEM(systems.shape, f32),
            pltpu.VMEM(task_cov.shape, f32),
            pltpu.VMEM(coarse_inverse.shape, f32),
            pltpu.SMEM(pattern.shape, jnp.int32),
            pltpu.SMEM(lengthscales.shape, f32),
            pltpu.SMEM(noise.shape, f32),
            pltpu.SemaphoreType.DMA((9,)),
        ],
        flops=10**10,
    )
    pack_l, pack_r = both_sides(pack)

    def cells_of(deep):
        return [
            shape(blocks, deep, BS, kind=bf16),
            shape(blocks, deep, BS, kind=bf16),
            shape(blocks, deep, BS),
        ]

    own_hi, own_lo, own_sim, part = call(
        build_own_kernel,
        cells_of(width) + [shape(rows, width)],
        [pack, extra],
        "build_own",
        flops=10**9,
    )
    halo_hi, halo_lo, halo_sim = call(
        functools.partial(build_kernel, places=halo_places, sides=2),
        cells_of(BAND - width),
        [pack_l, pack_r, pack, extra],
        "build_halo",
        flops=10**9,
    )
    own, halo = [own_hi, own_lo], [halo_hi, halo_lo]
    v0, d1 = call(
        first_kernel,
        [shape(rows, width), shape(rows, width)],
        [part, pack_l, pack_r] + halo + [jac],
        "first",
        flops=10**9,
    )
    d1_l, d1_r = both_sides(d1)
    early, part = call(
        early_moments_kernel,
        [shape(rows, lanes), shape(rows, width)],
        [pack, systems, d1, v0, extra] + own,
        "early",
        flops=10**9,
    )
    v1, cargo = call(
        second_kernel,
        [shape(rows, width), shape(rows + count, width)],
        [part, d1_l, d1_r, systems] + halo + [jac],
        "second",
        flops=10**9,
    )
    cargo_l = from_left(cargo)
    late, part = call(
        functools.partial(late_moments_kernel, count=count),
        [shape(rows, lanes), shape(rows, width)],
        [early, d1, cargo, v1, extra] + own,
        "late",
        flops=10**9,
    )
    (gram,) = call(
        functools.partial(third_kernel, count=count, held=coarse_inverse.shape[0]),
        [shape(ranks, rows, lanes)],
        [extra, late, cargo, cargo_l, part] + halo,
        "third",
        flops=10**9,
    )
    gram = lax.all_to_all(gram, "pts", 0, 0, tiled=True)
    cells = [own_hi, own_lo, own_sim, halo_hi, halo_lo, halo_sim]
    grads, answer = call(
        functools.partial(final_kernel, sides=sides * count, points=ranks * width),
        [shape(ranks * sides, FEAT, LANES), shape(count, width)],
        [gram, pack, pack_l, d1, d1_l, cargo, cargo_l] + cells,
        "final",
        far_outs=1,
        scratch=[pltpu.VMEM((count, width), f32), pltpu.SemaphoreType.DMA],
        flops=10**9,
    )
    grads = lax.all_to_all(grads, ("pts", "probe"), 0, 0, tiled=True)
    lengths, tasks = call(
        tail_kernel, [shape(FEAT), shape(TASKS, TASKS)], [grads], "tail", flops=10**5
    )
    return answer, lengths, tasks


def solution(mesh):
    return jax.shard_map(
        shards,
        mesh=mesh,
        in_specs=(
            P("probe", ("groups", "pts")),
            P(None, ("groups", "pts")),
            P(("groups", "pts")),
            P(("groups", "pts"), None),
            P(("groups", "pts")),
            P(("groups", "pts"), None),
            P("groups", None),
            P("groups"),
            P("groups"),
        ),
        out_specs=(P("probe", ("groups", "pts")), P("groups"), P("groups", None)),
        check_vma=False,
    )
```

```python
import functools

import jax
import jax.numpy as jnp
from jax import lax
from jax.experimental import pallas as pl
from jax.experimental.pallas import tpu as pltpu
from jax.sharding import PartitionSpec as P

BS = 256
REACH = 3
FEAT = 8
TASKS = 16
ITERS = 3
SLOTS = 2 * REACH + 1
BAND = SLOTS * BS
BASE = 32
GROUP = 4
LANES = 128
SYS = 2 * FEAT

highest = lax.Precision.HIGHEST
f32 = jnp.float32
bf16 = jnp.bfloat16
NN = (((1,), (0,)), ((), ()))
NT = (((1,), (1,)), ((), ()))
TN = (((0,), (0,)), ((), ()))


def dot(a, b, dims=NN, precision=None):
    return lax.dot_general(a, b, dims, precision=precision, preferred_element_type=f32)


def iota(shape, dim):
    return lax.broadcasted_iota(jnp.int32, shape, dim)


def split(x, parts):
    out = []
    for _ in range(parts - 1):
        head = x.astype(bf16).astype(f32)
        out.append(head)
        x = x - head
    out.append(x.astype(bf16).astype(f32))
    return out


def halves(x, parts):
    out = []
    for _ in range(parts - 1):
        out.append(x.astype(bf16))
        x = x - out[-1].astype(f32)
    return out + [x.astype(bf16)]


def column(ref, size):
    rows = iota((size, 1), 0)
    out = jnp.zeros((size, 1), f32)
    for i in range(size):
        out = jnp.where(rows == i, ref[i], out)
    return out


def one_hot(ids, size):
    return (iota((size, ids.shape[1]), 0).astype(f32) == ids).astype(f32)


def noise_row(noise_ref, ids):
    out = jnp.zeros(ids.shape, f32)
    for t in range(TASKS):
        out = jnp.where(ids == float(t), noise_ref[t], out)
    return out


def weight(pat_ref, block, offset):
    if offset != REACH:
        return pat_ref[block, offset].astype(f32)
    total = pat_ref[block, 0]
    for o in range(1, SLOTS):
        total = total + pat_ref[block, o]
    return total.astype(f32)


def near_stack(scaled, table):
    s0, s1, s2 = split(scaled, 3)
    n0, n1, n2 = split(-0.5 * jnp.sum(scaled * scaled, axis=0, keepdims=True), 3)
    rows = iota(scaled.shape, 0)
    norms = jnp.where(rows == 0, n0, jnp.where(rows == 1, n1, jnp.where(rows == 2, n2, 0.0)))
    pad = jnp.zeros((LANES - 7 * FEAT - 3 * TASKS, scaled.shape[1]), f32)
    stack = jnp.concatenate([s0, s0, s1, s1, s0, s2, norms, table, table, table, pad], axis=0)
    return stack.T.astype(bf16)


def own_stack(scaled, picked):
    s0, s1, s2 = split(scaled, 3)
    rows = iota(scaled.shape, 0)
    ones = jnp.where(rows < 3, 1.0, 0.0)
    count = scaled.shape[1]
    tail = LANES - 7 * FEAT - 3 * TASKS
    left = jnp.concatenate(
        [s0, s1, s0, s1, s2, s0, ones, jnp.zeros((3 * TASKS + tail, count), f32)], axis=0
    ).astype(bf16)
    right = jnp.concatenate(
        [jnp.zeros((7 * FEAT, count), f32)] + split(picked, 3) + [jnp.zeros((tail, count), f32)],
        axis=0,
    ).astype(bf16)
    sides = [
        jnp.concatenate([left[:, i : i + BS], right[:, i : i + BS]], axis=1)
        for i in range(0, count, BS)
    ]
    return sides, -0.5 * jnp.sum(scaled * scaled, axis=0, keepdims=True)


def small_inverse(p):
    n = len(p)
    if n == 1:
        return [[pltpu.reciprocal(p[0][0], approx=True)]]
    if n == 2:
        a, b, d = p[0][0], p[0][1], p[1][1]
        r = pltpu.reciprocal(a * d - b * b, approx=True)
        off = -b * r
        return [[d * r, off], [off, a * r]]
    h = n // 2
    ainv = small_inverse([row[:h] for row in p[:h]])
    b = [row[h:] for row in p[:h]]
    t = [[sum(ainv[i][k] * b[k][j] for k in range(h)) for j in range(h)] for i in range(h)]
    s = [[None] * h for _ in range(h)]
    for i in range(h):
        for j in range(i, h):
            s[i][j] = s[j][i] = p[h + i][h + j] - sum(b[k][i] * t[k][j] for k in range(h))
    sinv = small_inverse(s)
    u = [[sum(t[i][k] * sinv[k][j] for k in range(h)) for j in range(h)] for i in range(h)]
    out = [[None] * n for _ in range(n)]
    for i in range(h):
        for j in range(h):
            out[h + i][h + j] = sinv[i][j]
            out[i][h + j] = out[h + j][i] = -u[i][j]
    for i in range(h):
        for j in range(i, h):
            out[i][j] = out[j][i] = ainv[i][j] + sum(u[i][k] * t[j][k] for k in range(h))
    return out


def sweep_base(cells, beside):
    tall = range(BASE // 8)
    tiles = [cells[8 * i : 8 * i + 8] for i in tall]
    lane = iota((8, LANES), 1)
    start = lane - lane % BASE
    inner = lane % BASE
    sub = iota((8, LANES), 0)

    def columns(first):
        return [
            [
                jnp.take_along_axis(tile, start + (first + t), axis=1, mode="promise_in_bounds")
                for tile in tiles
            ]
            for t in range(GROUP)
        ]

    def row(parts, r):
        return jnp.broadcast_to(parts[r // 8][r % 8 : r % 8 + 1, :], (8, LANES))

    def with_rows(parts, first, rows):
        part = parts[first // 8]
        for t, value in enumerate(rows):
            part = jnp.where(sub == first % 8 + t, value, part)
        return [part if i == first // 8 else parts[i] for i in tall]

    def less(parts, factor):
        out = []
        for i in tall:
            part = parts[i]
            for t in range(GROUP):
                part = part - cols[t][i] * factor[t]
            out.append(part)
        return out

    cols = columns(0)
    for first in range(0, BASE, GROUP):
        ahead = columns(first + GROUP) if first + GROUP < BASE else []
        pivots = [[None] * GROUP for _ in range(GROUP)]
        for t in range(GROUP):
            for u in range(t, GROUP):
                pivots[t][u] = pivots[u][t] = row(cols[u], first + t)
        inv = small_inverse(pivots)
        coming = []
        for col in ahead:
            head = [row(col, first + t) for t in range(GROUP)]
            factor = [sum(inv[t][u] * head[u] for u in range(GROUP)) for t in range(GROUP)]
            coming.append(with_rows(less(col, factor), first, factor))
        group = (inner >= first) & (inner < first + GROUP)
        rows = []
        for t in range(GROUP):
            value = jnp.where(group, 0.0, row(tiles, first + t))
            rows.append(jnp.where(inner == first + t, -1.0, value))
        new = [sum(inv[t][u] * rows[u] for u in range(GROUP)) for t in range(GROUP)]
        tiles = [jnp.where(group, 0.0, tile) for tile in tiles]
        tiles = with_rows(less(tiles, new), first, new)
        cols = coming
        if beside:
            beside.pop(0)()
    while beside:
        beside.pop(0)()
    return jnp.concatenate(tiles, axis=0)


def fetch(pairs, sems):
    copies = [pltpu.make_async_copy(a, b, sems.at[i]) for i, (a, b) in enumerate(pairs)]
    for copy in copies:
        copy.start()
    return copies


def invert_kernel(
    place_ref, probe_ref, feat_hbm, ids_hbm, agg_hbm, sys_hbm, cov_hbm, coarse_hbm, pat_hbm, len_hbm, noise_hbm,
    jac_ref, pack_ref, extra_ref,
    work, feat_ref, ids_ref, agg_ref, sys_ref, cov_ref, coarse_ref, pat_ref, len_ref, noise_ref, sems,
):
    blocks = work.shape[0]
    width = blocks * BS
    pairs = [
        (feat_hbm, feat_ref), (ids_hbm, ids_ref), (agg_hbm, agg_ref), (cov_hbm, cov_ref),
        (pat_hbm, pat_ref), (len_hbm, len_ref), (noise_hbm, noise_ref), (coarse_hbm, coarse_ref),
        (sys_hbm, sys_ref),
    ]
    for copy in fetch(pairs, sems):
        copy.wait()
    scaled = feat_ref[...] / column(len_ref, FEAT)
    ids = ids_ref[...].astype(f32).reshape(1, width)
    which = agg_ref[...].astype(f32).reshape(1, width)
    table = one_hot(ids, TASKS)
    noise = noise_row(noise_ref, ids)
    c0, c1, c2 = split(cov_ref[...], 3)
    tab = table.astype(bf16)
    picked = (dot(c2.astype(bf16), tab) + dot(c1.astype(bf16), tab)) + dot(c0.astype(bf16), tab)
    rows = iota((FEAT, width), 0)
    weights = jnp.zeros((1, width), f32)
    places = iota((1, width), 1)
    for m in range(blocks):
        for o in range(SLOTS):
            weights = jnp.where(places == m * SLOTS + o, weight(pat_ref, m, o), weights)
    pack_ref[0:FEAT, :] = scaled
    pack_ref[FEAT : 2 * FEAT, :] = jnp.where(
        rows == 0,
        ids,
        jnp.where(rows == 1, which, jnp.where(rows == 2, probe_ref[0].astype(f32), 0.0)),
    )
    extra_ref[0:TASKS, :] = picked
    tail = jnp.where(rows == 0, noise, jnp.where(rows == 1, weights, 0.0))
    held = coarse_ref.shape[0]
    inverse = jnp.concatenate(
        [coarse_ref[...], jnp.zeros((held, width - coarse_ref.shape[1]), f32)], axis=1
    )
    tail = jnp.where(rows == 2, place_ref[0].astype(f32), tail)
    for r in range(held):
        tail = jnp.where(rows == 3 + r, inverse[r : r + 1], tail)
    extra_ref[TASKS : TASKS + FEAT, :] = tail
    near = near_stack(scaled, table)
    mates, norm = own_stack(scaled, picked)
    eye = iota((BS, BS), 0) == iota((BS, BS), 1)
    for m in range(blocks):
        at = slice(m * BS, (m + 1) * BS)
        both = dot(near[at], mates[m])
        block = weight(pat_ref, m, REACH) * jnp.exp(both[:, :BS] + norm[:, at]) * both[:, BS:]
        work[m] = block + jnp.where(eye, noise[:, at], 0.0)
    seg = iota((BASE, LANES), 1) // BASE
    wide = iota((BASE, BS), 1)
    deep = iota((BASE, BS), 0)

    def packed(strips, first):
        tile, inside = first // LANES, first % LANES
        cells = jnp.zeros((BASE, LANES), f32)
        for m in range(blocks):
            piece = strips[m][:, tile * LANES : (tile + 1) * LANES]
            shift = (BASE * m - inside) % LANES
            if shift:
                piece = pltpu.roll(piece, shift, axis=1)
            cells = jnp.where(seg == m, piece, cells)
        return cells

    def diagonal(cells):
        parts = [jnp.where(seg == m, cells, 0.0) for m in range(LANES // BASE)]
        return jnp.concatenate(parts, axis=0)

    eye = jnp.where(iota((BASE, LANES), 1) % BASE == iota((BASE, LANES), 0), 1.0, 0.0)

    def updates(first, inv, strips):
        state = {}

        def product():
            held = (wide >= first) & (wide < first + BASE)
            minus = jnp.where(wide - first == deep, -1.0, 0.0)
            stack = jnp.concatenate(
                [jnp.where(held, minus, s) for s in strips]
                + [jnp.zeros((LANES - blocks * BASE, BS), f32)],
                axis=0,
            )
            spread = diagonal(inv)[: blocks * BASE]
            new = dot(spread, stack, precision=highest)
            for m in range(blocks):
                state[m] = new[m * BASE : (m + 1) * BASE, :]

        def rows_of(m, low, high):
            def piece():
                if (m, 0) not in state:
                    r0, r1, r2 = halves(strips[m], 3)
                    p0, p1, p2 = halves(state[m], 3)
                    state[m, 0] = jnp.concatenate([r0, r0, r1, r1, r0, r2], axis=0)
                    state[m, 1] = jnp.concatenate([p0, p1, p0, p1, p2, p0], axis=0)
                a, b = state[m, 0][:, low:high], state[m, 1]
                gone = (iota((1, BS), 1) >= first) & (iota((1, BS), 1) < first + BASE)
                work[m, low:high, :] = jnp.where(gone, 0.0, work[m, low:high, :]) - dot(a, b, TN)
                if low <= first < high:
                    work[m, first : first + BASE, :] = state[m]

            return piece

        half = BS // 2
        return [product] + [
            rows_of(m, low, low + half) for m in range(blocks) for low in range(0, BS, half)
        ]

    def strips_at(first):
        return [work[m, first : first + BASE, :] for m in range(blocks)]

    cells = jnp.where(seg < blocks, packed(strips_at(0), 0), eye)
    pending = []
    for first in range(0, BS, BASE):
        inv = -sweep_base(cells, pending)
        strips = strips_at(first)
        if first + BASE < BS:
            after = strips_at(first + BASE)
            half = dot(inv, diagonal(packed(strips, first + BASE)), precision=highest)
            drop = dot(packed(after, first), diagonal(half), precision=highest)
            cells = jnp.where(seg < blocks, packed(after, first + BASE) - drop, eye)
        pending = updates(first, inv, strips)
    for piece in pending:
        piece()
    for m in range(blocks):
        inv = -work[m]
        for i, part in enumerate(halves(inv, 3)):
            jac_ref[i, m] = part
    pack_ref[SYS:, :] = smooth(sys_ref[...], jac_ref)


def own_places(m):
    return [(j, j, REACH + j - m) for j in range(REACH)]


def halo_places(m):
    lefts = [(j - m, j, j - m) for j in range(m, REACH)]
    return lefts + [(REACH - m + j, REACH + j, 2 * REACH - m + j) for j in range(m + 1)]


def build_kernel(*refs, places, sides):
    cells, (own_ref, extra_ref) = refs[:sides], refs[sides : sides + 2]
    hi_ref, lo_ref, sim_ref, full_ref = refs[sides + 2 :]
    blocks = hi_ref.shape[0]
    near = []
    for ref in cells:
        near.append(near_stack(ref[0:FEAT, :], one_hot(ref[FEAT : FEAT + 1, :], TASKS)))
    mates, norm = own_stack(own_ref[0:FEAT, :], extra_ref[0:TASKS, :])
    weights = extra_ref[TASKS + 1 : TASKS + 2, :]
    for m in range(blocks):
        for row, j, o in places(m):
            part = near[j // REACH][(j % REACH) * BS : (j % REACH + 1) * BS]
            both = dot(part, mates[m])
            place = m * SLOTS + o
            exponent = both[:, :BS] + norm[:, m * BS : (m + 1) * BS]
            similar = weights[:, place : place + 1] * jnp.exp(exponent)
            kernel = similar * both[:, BS:]
            head = kernel.astype(bf16)
            rows = slice(row * BS, (row + 1) * BS)
            if o <= REACH or sides == 1:
                sim_ref[m, rows, :] = similar
                full_ref[m, rows, :] = kernel
            hi_ref[m, rows, :] = head
            lo_ref[m, rows, :] = (kernel - head.astype(f32)).astype(bf16)


def pieces(vectors):
    return jnp.concatenate(split(vectors, 2), axis=0).astype(bf16)


def apply(cells, hi, lo):
    rows = cells.shape[0] // 2
    first = dot(cells, hi)
    return first[:rows] + first[rows:] + dot(cells[:rows], lo)


def operate_own(own, noise, own_hi, own_lo):
    mine = pieces(own)
    out = [apply(mine, own_hi[m], own_lo[m]) for m in range(REACH)]
    return jnp.concatenate(out, axis=1) + noise * own


def operate_left(left, halo_hi, halo_lo):
    cells = pieces(left)
    out = []
    for m in range(REACH):
        part = slice(0, (REACH - m) * BS)
        out.append(apply(cells[:, m * BS :], halo_hi[m, part, :], halo_lo[m, part, :]))
    return jnp.concatenate(out, axis=1)


def operate_halo(left, right, halo_hi, halo_lo):
    lefts, rights = pieces(left), pieces(right)
    out = []
    for m in range(REACH):
        beyond = jnp.concatenate([lefts[:, m * BS :], rights[:, : (m + 1) * BS]], axis=1)
        out.append(apply(beyond, halo_hi[m], halo_lo[m]))
    return jnp.concatenate(out, axis=1)


def smooth_pieces(vectors, parts):
    rows = vectors.shape[0]
    cells = jnp.concatenate(split(vectors, 3), axis=0).astype(bf16)
    a = dot(cells, parts[0])
    b = dot(cells[: 2 * rows], parts[1])
    c = dot(cells[:rows], parts[2])
    return a[:rows] + (a[rows : 2 * rows] + b[:rows] + (a[2 * rows :] + b[rows:] + c))


def smooth(image, jac_ref):
    return jnp.concatenate(
        [
            smooth_pieces(image[:, m * BS : (m + 1) * BS], [jac_ref[i, m] for i in range(3)])
            for m in range(REACH)
        ],
        axis=1,
    )


def basis(pack_ref, coarse):
    z = one_hot(pack_ref[FEAT + 1 : FEAT + 2, :], coarse)
    return jnp.concatenate([pack_ref[SYS:, :], z], axis=0)


def build_own_kernel(own_ref, extra_ref, hi_ref, lo_ref, sim_ref, full_ref, part_ref):
    build_kernel(
        own_ref, own_ref, extra_ref, hi_ref, lo_ref, sim_ref, full_ref, places=own_places, sides=1
    )
    coarse = part_ref.shape[0] - (own_ref.shape[0] - SYS)
    noise = extra_ref[TASKS : TASKS + 1, :]
    part_ref[...] = operate_own(basis(own_ref, coarse), noise, hi_ref, lo_ref)


def first_kernel(part_ref, left_ref, right_ref, hi_ref, lo_ref, jac_ref, image_ref, next_ref):
    coarse = part_ref.shape[0] - (left_ref.shape[0] - SYS)
    ends = [basis(ref, coarse) for ref in (left_ref, right_ref)]
    image = part_ref[...] + operate_halo(*ends, hi_ref, lo_ref)
    image_ref[...] = image
    next_ref[...] = smooth(image, jac_ref)


def second_kernel(
    part_ref, left_ref, right_ref, sys_ref, hi_ref, lo_ref, jac_ref, image_ref, cargo_ref
):
    rows = part_ref.shape[0]
    image = part_ref[...] + operate_halo(left_ref[...], right_ref[...], hi_ref, lo_ref)
    image_ref[...] = image
    cargo_ref[0:rows, :] = smooth(image, jac_ref)
    cargo_ref[rows:, :] = sys_ref[...]


def pitch_of(coarse):
    return coarse + 1


def lanes_of(coarse):
    return -(-5 * pitch_of(coarse) // LANES) * LANES


def moment(vectors, images, pairs):
    count = pairs.shape[0]
    table = dot(images, vectors, NT, lax.Precision.HIGH)
    own = jnp.sum(pairs, axis=1, keepdims=True)
    if images.shape[0] > count:
        own = jnp.concatenate([own, jnp.zeros((images.shape[0] - count, 1), f32)], axis=0)
    return jnp.concatenate([table, own], axis=1)


def spread_out(parts, lanes):
    rows, pitch = next(iter(parts.values())).shape
    cells = [parts.get(k, jnp.zeros((rows, pitch), f32)) for k in range(5)]
    if lanes > 5 * pitch:
        cells.append(jnp.zeros((rows, lanes - 5 * pitch), f32))
    return jnp.concatenate(cells, axis=1)


def folded(low, high):
    order = low.shape[0]
    row, col = iota((order, order), 0), iota((order, order), 1)
    diagonal = jnp.sum(jnp.where(row == col, high, 0.0), axis=1, keepdims=True)
    return jnp.concatenate([jnp.where(row >= col, low, high), diagonal], axis=1)


def unfolded(cells):
    order = cells.shape[0]
    row, col = iota((order, order), 0), iota((order, order), 1)
    square = cells[:, :order]
    turned = dot(square, jnp.where(row == col, 1.0, 0.0), TN, highest)
    low = jnp.where(row >= col, square, turned)
    high = jnp.where(row < col, square, jnp.where(row > col, turned, cells[:, order:]))
    return low, high


def early_moments_kernel(
    own_ref, sys_ref, d1_ref, v0_ref, extra_ref, hi_ref, lo_ref, out_ref, part_ref
):
    part_ref[...] = operate_own(d1_ref[...], extra_ref[TASKS : TASKS + 1, :], hi_ref, lo_ref)
    count = own_ref.shape[0] - SYS
    coarse = d1_ref.shape[0] - count
    lanes = out_ref.shape[1]
    pitch = pitch_of(coarse)
    systems = sys_ref[...]
    pre = own_ref[SYS:, :]
    z = one_hot(own_ref[FEAT + 1 : FEAT + 2, :], coarse)
    d1, v0 = d1_ref[...], v0_ref[...]
    m0 = moment(z, v0, pre * v0[:count])
    m1 = moment(d1[count:], v0, d1[:count] * v0[:count])
    out_ref[0:count, :] = spread_out({0: m0[:count], 1: m1[:count]}, lanes)
    start = moment(z, systems, systems * pre)
    if coarse > count:
        start = jnp.concatenate([start, jnp.zeros((coarse - count, pitch), f32)], axis=0)
    fold = folded(m0[count:, :coarse], m1[count:, :coarse])
    out_ref[count:, :] = spread_out({0: fold, 3: start}, lanes)


def late_moments_kernel(
    before_ref, d1_ref, cargo_ref, v1_ref, extra_ref, hi_ref, lo_ref, out_ref, part_ref, *, count
):
    lanes = out_ref.shape[1]
    d1, d2, v1 = d1_ref[...], cargo_ref[0 : d1_ref.shape[0], :], v1_ref[...]
    part_ref[...] = operate_own(d2, extra_ref[TASKS : TASKS + 1, :], hi_ref, lo_ref)
    coarse = d1.shape[0] - count
    m2 = moment(d1[count:], v1, d1[:count] * v1[:count])
    m3 = moment(d2[count:], v1, d2[:count] * v1[:count])
    out_ref[0:count, :] = before_ref[0:count, :] + spread_out({2: m2[:count], 3: m3[:count]}, lanes)
    fold = folded(m2[count:, :coarse], m3[count:, :coarse])
    out_ref[count:, :] = before_ref[count:, :] + spread_out({1: fold}, lanes)


def third_kernel(
    extra_ref, before_ref, cargo_ref, left_ref, part_ref, hi_ref, lo_ref, out_ref, *, count, held
):
    rows = cargo_ref.shape[0] - count
    coarse = rows - count
    lanes = out_ref.shape[2]
    pitch = pitch_of(coarse)
    d2 = cargo_ref[0:rows, :]
    inner = part_ref[...]
    cross = operate_left(left_ref[0:rows, :], hi_ref, lo_ref)
    m4 = moment(d2[count:], inner + cross, d2[:count] * (inner + 2.0 * cross)[:count])
    mirror = dot(d2, cross[count:], NT, lax.Precision.HIGH)
    m4 = m4 + jnp.concatenate([mirror, jnp.zeros((rows, 1), f32)], axis=1)
    row = iota((coarse, 1), 0).astype(f32)
    start = extra_ref[TASKS + 2 : TASKS + 3, 0:1] * held
    inverse = jnp.zeros((coarse, pitch), f32)
    for r in range(held):
        line = extra_ref[TASKS + 3 + r : TASKS + 4 + r, 0:pitch]
        inverse = jnp.where(row == start + r, line, inverse)
    top = before_ref[0:count, :] + spread_out({4: m4[:count]}, lanes)
    bottom = before_ref[count:, :] + spread_out({2: m4[count:], 4: inverse}, lanes)
    for c in range(out_ref.shape[0]):
        out_ref[c, 0:count, :] = top
        out_ref[c, count:, :] = bottom


def final_kernel(
    gram_ref, own_ref, left_ref, d1_ref, d1l_ref, cargo_ref, cargol_ref, *refs, sides, points,
):
    kernel_refs, (sol_ref, grad_ref) = refs[:4], refs[4:]
    width = own_ref.shape[1]
    count = own_ref.shape[0] - SYS
    rows = d1_ref.shape[0]
    coarse = rows - count
    pitch = pitch_of(coarse)
    wide = -(-3 * pitch // LANES) * LANES
    blocks = width // BS
    gram = gram_ref[0]
    for c in range(1, gram_ref.shape[0]):
        gram = gram + gram_ref[c]
    bottom = gram[count:]
    gram = jnp.concatenate([gram[:count], jnp.zeros((count, wide), f32)], axis=1)
    squares = list(unfolded(bottom[:, :pitch])) + list(unfolded(bottom[:, pitch : 2 * pitch]))
    squares.append(bottom[:, 2 * pitch : 2 * pitch + coarse])
    lane = iota((1, wide), 1)
    slot, inside = lane // pitch, lane % pitch
    live = lane < 3 * pitch
    is_vec = live & (inside < coarse)
    is_one = live & (inside == coarse)

    def shifted(j):
        return jnp.where(live, gram[:, j * pitch : j * pitch + wide], 0.0)

    own = [shifted(j) for j in range(3)]
    gap = jnp.zeros((coarse, 1), f32)
    rest = jnp.zeros((coarse, wide - 3 * pitch), f32)
    hankel = []
    for i in range(3):
        line = [squares[i], gap, squares[i + 1], gap, squares[i + 2], gap]
        hankel.append(jnp.concatenate(line + ([rest] if wide > 3 * pitch else []), axis=1))
        hankel.append(jnp.zeros((1, wide), f32))
    if wide > 3 * pitch:
        hankel.append(jnp.zeros((wide - 3 * pitch, wide), f32))
    hankel = jnp.concatenate(hankel, axis=0)
    block0 = lane < pitch
    inverse = bottom[:, 4 * pitch : 4 * pitch + coarse]
    inverse = jnp.concatenate([inverse, jnp.zeros((coarse, wide - coarse), f32)], axis=1)
    inverse = jnp.concatenate([inverse, jnp.zeros((wide - coarse, wide), f32)], axis=0)
    start = bottom[:count, 3 * pitch : 4 * pitch]
    start = jnp.concatenate([start, jnp.zeros((count, wide - pitch), f32)], axis=1)
    against = jnp.where(
        block0, start, jnp.where(live, pltpu.roll(jnp.where(live, own[0], 0.0), pitch, axis=1), 0.0)
    )

    def total(x):
        return jnp.sum(x, axis=1, keepdims=True)

    def scalars(u, i):
        return total(jnp.where(lane == i * pitch + coarse, u, 0.0))

    def metric(u):
        out = dot(jnp.where(is_vec, u, 0.0), hankel, precision=highest)
        for j in range(3):
            out = out + scalars(u, j) * own[j]
        out = jnp.where(is_vec, out, 0.0)
        for i in range(3):
            out = jnp.where(lane == i * pitch + coarse, total(u * own[i]), out)
        return out

    def corrected(w):
        return dot(jnp.where(lane < coarse, w, 0.0), inverse, precision=highest)

    pre = corrected(against) + jnp.where(lane == coarse, 1.0, 0.0)
    direction = pre
    gamma = total(pre * against)
    answer = jnp.zeros_like(pre)
    image_sum = jnp.zeros_like(pre)
    for step in range(ITERS):
        image = metric(direction)
        alpha = gamma / total(direction * image)
        answer = answer + alpha * direction
        if step + 1 < ITERS:
            image_sum = image_sum + alpha * image
            moved_on = jnp.where(live & (slot > 0), pltpu.roll(direction, pitch, axis=1), 0.0)
            pre = pre - alpha * (moved_on + corrected(image))
            gamma_new = total(pre * (against - image_sum))
            direction = pre + (gamma_new / gamma) * direction
            gamma = gamma_new

    pack = jnp.concatenate([left_ref[...], own_ref[...]], axis=1)
    z = one_hot(pack[FEAT + 1 : FEAT + 2], coarse)
    q0 = pack[SYS:]
    d1 = jnp.concatenate([d1l_ref[...], d1_ref[...]], axis=1)
    cargo = jnp.concatenate([cargol_ref[...], cargo_ref[...]], axis=1)
    d2 = cargo[:rows]
    span = q0.shape[1]
    step = -(-coarse // FEAT) * FEAT
    deep = -(-3 * step // LANES) * LANES
    parts, planes = [], []
    for i, rest in enumerate((z, d1[count:], d2[count:])):
        parts.append(answer[:, i * pitch : i * pitch + coarse])
        planes.append(rest)
        if step > coarse:
            parts.append(jnp.zeros((count, step - coarse), f32))
            planes.append(jnp.zeros((step - coarse, span), f32))
    if deep > 3 * step:
        parts.append(jnp.zeros((count, deep - 3 * step), f32))
        planes.append(jnp.zeros((deep - 3 * step, span), f32))
    planes = halves(jnp.concatenate(planes, axis=0), 3)
    x = smooth_pieces(jnp.concatenate(parts, axis=1), planes)
    x = x + scalars(answer, 0) * q0 + scalars(answer, 1) * d1[:count]
    x = x + scalars(answer, 2) * d2[:count]
    mine = slice(width, 2 * width)
    sol_ref[...] = x[:, mine]

    probe = own_ref[FEAT + 2 : FEAT + 3, 0:1]
    line = iota((count, 1), 0).astype(f32) + probe * count
    right = jnp.where(line == 0, x, cargo[rows:])
    coef = jnp.where(line == 0, 0.5 / points, -0.5 / (sides - 1) / points)
    r0, r1 = split(right, 2)
    w0, w1 = split(x * coef, 2)
    rest = jnp.zeros((LANES - 6 * count, span), f32)
    near = jnp.concatenate([w0, w1, w0, r0, r1, r0, rest], axis=0).T.astype(bf16)
    none = jnp.zeros((3 * count, width), f32)
    rest = rest[:, mine]
    ahead = jnp.concatenate([r0, r0, r1], axis=0)[:, mine]
    back = jnp.concatenate([w0, w0, w1], axis=0)[:, mine]
    mates = [
        jnp.concatenate([ahead, none, rest], axis=0).astype(bf16),
        jnp.concatenate([none, back, rest], axis=0).astype(bf16),
    ]
    scaled = pack[0:FEAT]
    table = one_hot(pack[FEAT : FEAT + 1], TASKS)
    ones = jnp.ones((8, span), f32)
    terms = jnp.concatenate([scaled, ones, scaled * scaled], axis=0)
    t0, t1 = split(terms, 2)
    pad8 = jnp.zeros((8, span), f32)
    both = jnp.concatenate([t0, pad8, t1, pad8], axis=0).astype(bf16)
    heads = jnp.concatenate([t0, pad8], axis=0).astype(bf16)
    tables = table.astype(bf16)
    high = 32
    length_total = jnp.zeros((FEAT, 1), f32)
    task_total = jnp.zeros((TASKS, TASKS), f32)
    for m in range(blocks):
        at = slice(m * BS, (m + 1) * BS)
        sums = jnp.zeros((high, BS), f32)
        held_sums = [jnp.zeros((TASKS, BS), f32) for _ in mates]
        places = [(1, row, j + REACH) for row, j, _ in own_places(m)]
        places += [(2, row, j) for row, j, _ in halo_places(m) if j < REACH]
        for orders, row, block in places:
            full_ref, sim_ref = kernel_refs[2 * orders - 2 : 2 * orders]
            j = slice(block * BS, (block + 1) * BS)
            rows_at = slice(row * BS, (row + 1) * BS)
            outers = [dot(near[j], mate[:, at]) for mate in mates[:orders]]
            similar = sim_ref[m, rows_at, :]
            energy = sum(outers[1:], outers[0]) * full_ref[m, rows_at, :]
            e0, e1 = halves(energy, 2)
            first = dot(both[:, j], e0)
            sums = sums + first[:high] + first[high:] + dot(heads[:, j], e1)
            for k in range(orders):
                h0, h1 = halves(outers[k] * similar, 2)
                held_sums[k] = held_sums[k] + dot(tables[:, j], h0) + dot(tables[:, j], h1)
        mid = slice(width + m * BS, width + (m + 1) * BS)
        left = scaled[:, mid]
        value = left * left * sums[FEAT : FEAT + 1] + sums[2 * FEAT : 3 * FEAT]
        value = value - 2.0 * left * sums[:FEAT]
        length_total = length_total + jnp.sum(value, axis=1, keepdims=True)
        task_total = task_total + dot(held_sums[0], table[:, mid], NT, highest)
        task_total = task_total + dot(table[:, mid], held_sums[1], NT, highest)
    half = TASKS // 2
    value = jnp.concatenate(
        [
            task_total[:half],
            task_total[half:],
            jnp.where(iota((half, FEAT), 0) == iota((half, FEAT), 1), length_total, 0.0),
            jnp.zeros((half, LANES - 2 * TASKS - FEAT), f32),
        ],
        axis=1,
    )
    for c in range(grad_ref.shape[0]):
        grad_ref[c] = value


def tail_kernel(parts_ref, length_ref, task_ref):
    total = parts_ref[0]
    for c in range(1, parts_ref.shape[0]):
        total = total + parts_ref[c]
    half = TASKS // 2
    task_ref[0:half, :] = total[:, :TASKS]
    task_ref[half:, :] = total[:, TASKS : 2 * TASKS]
    length_ref[...] = jnp.sum(total[:, 2 * TASKS : 2 * TASKS + FEAT], axis=0)


MIB = 1024 * 1024


def call(body, outs, args, name, smem=0, hbm=0, far_outs=0, scratch=(), flops=0, limit=16):
    if hbm:
        args = args[:-hbm] + [pltpu.with_memory_space_constraint(a, pltpu.HBM) for a in args[-hbm:]]
    if far_outs:
        outs = outs[:-far_outs] + [pltpu.HBM(o.shape, o.dtype) for o in outs[-far_outs:]]
    vm = pl.BlockSpec(memory_space=pltpu.VMEM)
    sm = pl.BlockSpec(memory_space=pltpu.SMEM)
    far = pl.BlockSpec(memory_space=pltpu.HBM)
    return pl.pallas_call(
        body,
        out_shape=outs,
        in_specs=[sm] * smem + [vm] * (len(args) - smem - hbm) + [far] * hbm,
        out_specs=[vm] * (len(outs) - far_outs) + [far] * far_outs,
        scratch_shapes=scratch,
        compiler_params=pltpu.CompilerParams(vmem_limit_bytes=limit * MIB),
        cost_estimate=pl.CostEstimate(flops=flops, bytes_accessed=1 << 20, transcendentals=0),
        name=name,
    )(*args)


def both_sides(cells):
    count = lax.axis_size("pts")
    up = [(i, i + 1) for i in range(count - 1)]
    down = [(i + 1, i) for i in range(count - 1)]
    return lax.ppermute(cells, "pts", up), lax.ppermute(cells, "pts", down)


def from_left(cells):
    count = lax.axis_size("pts")
    return lax.ppermute(cells, "pts", [(i, i + 1) for i in range(count - 1)])


def shards(
    systems, features, task_ids, pattern, aggregate, coarse_inverse, task_cov, lengthscales, noise
):
    count, width = systems.shape
    blocks = width // BS
    coarse = coarse_inverse.shape[1]
    rows = count + coarse
    lanes = lanes_of(coarse)
    assert blocks == REACH
    place = lax.axis_index("pts").astype(jnp.int32)[None]
    probe = lax.axis_index("probe").astype(jnp.int32)[None]
    ranks = lax.axis_size("pts")
    sides = lax.axis_size("probe")

    def shape(*dims, kind=f32):
        return jax.ShapeDtypeStruct(dims, kind)

    jac, pack, extra = call(
        invert_kernel,
        [shape(3, blocks, BS, BS, kind=bf16), shape(SYS + count, width), shape(TASKS + FEAT, width)],
        [place, probe, features, task_ids, aggregate, systems, task_cov, coarse_inverse, pattern, lengthscales, noise],
        "invert",
        smem=2,
        hbm=9,
        scratch=[
            pltpu.VMEM((blocks, BS, BS), f32),
            pltpu.VMEM(features.shape, f32),
            pltpu.VMEM(task_ids.shape, jnp.int32),
            pltpu.VMEM(aggregate.shape, jnp.int32),
            pltpu.VMEM(systems.shape, f32),
            pltpu.VMEM(task_cov.shape, f32),
            pltpu.VMEM(coarse_inverse.shape, f32),
            pltpu.SMEM(pattern.shape, jnp.int32),
            pltpu.SMEM(lengthscales.shape, f32),
            pltpu.SMEM(noise.shape, f32),
            pltpu.SemaphoreType.DMA((9,)),
        ],
        flops=10**10,
    )
    pack_l, pack_r = both_sides(pack)

    def cells_of(deep):
        return [
            shape(blocks, deep, BS, kind=bf16),
            shape(blocks, deep, BS, kind=bf16),
            shape(blocks, deep, BS),
            shape(blocks, deep, BS),
        ]

    own_hi, own_lo, own_sim, own_full, part = call(
        build_own_kernel,
        cells_of(width) + [shape(rows, width)],
        [pack, extra],
        "build_own",
        flops=10**9,
    )
    halo_hi, halo_lo, halo_sim, halo_full = call(
        functools.partial(build_kernel, places=halo_places, sides=2),
        cells_of(BAND - width),
        [pack_l, pack_r, pack, extra],
        "build_halo",
        flops=10**9,
    )
    own, halo = [own_hi, own_lo], [halo_hi, halo_lo]
    v0, d1 = call(
        first_kernel,
        [shape(rows, width), shape(rows, width)],
        [part, pack_l, pack_r] + halo + [jac],
        "first",
        flops=10**9,
    )
    d1_l, d1_r = both_sides(d1)
    early, part = call(
        early_moments_kernel,
        [shape(rows, lanes), shape(rows, width)],
        [pack, systems, d1, v0, extra] + own,
        "early",
        flops=10**9,
    )
    v1, cargo = call(
        second_kernel,
        [shape(rows, width), shape(rows + count, width)],
        [part, d1_l, d1_r, systems] + halo + [jac],
        "second",
        flops=10**9,
    )
    cargo_l = from_left(cargo)
    late, part = call(
        functools.partial(late_moments_kernel, count=count),
        [shape(rows, lanes), shape(rows, width)],
        [early, d1, cargo, v1, extra] + own,
        "late",
        flops=10**9,
    )
    (gram,) = call(
        functools.partial(third_kernel, count=count, held=coarse_inverse.shape[0]),
        [shape(ranks, rows, lanes)],
        [extra, late, cargo, cargo_l, part] + halo,
        "third",
        flops=10**9,
    )
    gram = lax.all_to_all(gram, "pts", 0, 0, tiled=True)
    cells = [own_full, own_sim, halo_full, halo_sim]
    answer, grads = call(
        functools.partial(final_kernel, sides=sides * count, points=ranks * width),
        [shape(count, width), shape(ranks * sides, FEAT, LANES)],
        [gram, pack, pack_l, d1, d1_l, cargo, cargo_l] + cells,
        "final",
        flops=10**9,
    )
    grads = lax.all_to_all(grads, ("pts", "probe"), 0, 0, tiled=True)
    lengths, tasks = call(
        tail_kernel, [shape(FEAT), shape(TASKS, TASKS)], [grads], "tail", flops=10**5
    )
    return answer, lengths, tasks


def solution(mesh):
    return jax.shard_map(
        shards,
        mesh=mesh,
        in_specs=(
            P("probe", ("groups", "pts")),
            P(None, ("groups", "pts")),
            P(("groups", "pts")),
            P(("groups", "pts"), None),
            P(("groups", "pts")),
            P(("groups", "pts"), None),
            P("groups", None),
            P("groups"),
            P("groups"),
        ),
        out_specs=(P("probe", ("groups", "pts")), P("groups"), P("groups", None)),
        check_vma=False,
    )
```

```python
import functools

import jax
import jax.numpy as jnp
from jax import lax
from jax.experimental import pallas as pl
from jax.experimental.pallas import tpu as pltpu
from jax.sharding import PartitionSpec as P

BS = 256
REACH = 3
FEAT = 8
TASKS = 16
ITERS = 3
SLOTS = 2 * REACH + 1
BAND = SLOTS * BS
BASE = 32
GROUP = 4
LANES = 128
SYS = 2 * FEAT

highest = lax.Precision.HIGHEST
f32 = jnp.float32
bf16 = jnp.bfloat16
NN = (((1,), (0,)), ((), ()))
NT = (((1,), (1,)), ((), ()))
TN = (((0,), (0,)), ((), ()))


def dot(a, b, dims=NN, precision=None):
    return lax.dot_general(a, b, dims, precision=precision, preferred_element_type=f32)


def iota(shape, dim):
    return lax.broadcasted_iota(jnp.int32, shape, dim)


def split(x, parts):
    out = []
    for _ in range(parts - 1):
        head = x.astype(bf16).astype(f32)
        out.append(head)
        x = x - head
    out.append(x.astype(bf16).astype(f32))
    return out


def halves(x, parts):
    out = []
    for _ in range(parts - 1):
        out.append(x.astype(bf16))
        x = x - out[-1].astype(f32)
    return out + [x.astype(bf16)]


def column(ref, size):
    rows = iota((size, 1), 0)
    out = jnp.zeros((size, 1), f32)
    for i in range(size):
        out = jnp.where(rows == i, ref[i], out)
    return out


def one_hot(ids, size):
    return (iota((size, ids.shape[1]), 0).astype(f32) == ids).astype(f32)


def noise_row(noise_ref, ids):
    out = jnp.zeros(ids.shape, f32)
    for t in range(TASKS):
        out = jnp.where(ids == float(t), noise_ref[t], out)
    return out


def weight(pat_ref, block, offset):
    if offset != REACH:
        return pat_ref[block, offset].astype(f32)
    total = pat_ref[block, 0]
    for o in range(1, SLOTS):
        total = total + pat_ref[block, o]
    return total.astype(f32)


def near_stack(scaled, table):
    s0, s1, s2 = split(scaled, 3)
    n0, n1, n2 = split(-0.5 * jnp.sum(scaled * scaled, axis=0, keepdims=True), 3)
    rows = iota(scaled.shape, 0)
    norms = jnp.where(rows == 0, n0, jnp.where(rows == 1, n1, jnp.where(rows == 2, n2, 0.0)))
    pad = jnp.zeros((LANES - 7 * FEAT - 3 * TASKS, scaled.shape[1]), f32)
    stack = jnp.concatenate([s0, s0, s1, s1, s0, s2, norms, table, table, table, pad], axis=0)
    return stack.T.astype(bf16)


def own_stack(scaled, picked):
    s0, s1, s2 = split(scaled, 3)
    rows = iota(scaled.shape, 0)
    ones = jnp.where(rows < 3, 1.0, 0.0)
    count = scaled.shape[1]
    tail = LANES - 7 * FEAT - 3 * TASKS
    left = jnp.concatenate(
        [s0, s1, s0, s1, s2, s0, ones, jnp.zeros((3 * TASKS + tail, count), f32)], axis=0
    ).astype(bf16)
    right = jnp.concatenate(
        [jnp.zeros((7 * FEAT, count), f32)] + split(picked, 3) + [jnp.zeros((tail, count), f32)],
        axis=0,
    ).astype(bf16)
    sides = [
        jnp.concatenate([left[:, i : i + BS], right[:, i : i + BS]], axis=1)
        for i in range(0, count, BS)
    ]
    return sides, -0.5 * jnp.sum(scaled * scaled, axis=0, keepdims=True)


def small_inverse(p):
    n = len(p)
    if n == 1:
        return [[pltpu.reciprocal(p[0][0], approx=True)]]
    if n == 2:
        a, b, d = p[0][0], p[0][1], p[1][1]
        r = pltpu.reciprocal(a * d - b * b, approx=True)
        off = -b * r
        return [[d * r, off], [off, a * r]]
    h = n // 2
    ainv = small_inverse([row[:h] for row in p[:h]])
    b = [row[h:] for row in p[:h]]
    t = [[sum(ainv[i][k] * b[k][j] for k in range(h)) for j in range(h)] for i in range(h)]
    s = [[None] * h for _ in range(h)]
    for i in range(h):
        for j in range(i, h):
            s[i][j] = s[j][i] = p[h + i][h + j] - sum(b[k][i] * t[k][j] for k in range(h))
    sinv = small_inverse(s)
    u = [[sum(t[i][k] * sinv[k][j] for k in range(h)) for j in range(h)] for i in range(h)]
    out = [[None] * n for _ in range(n)]
    for i in range(h):
        for j in range(h):
            out[h + i][h + j] = sinv[i][j]
            out[i][h + j] = out[h + j][i] = -u[i][j]
    for i in range(h):
        for j in range(i, h):
            out[i][j] = out[j][i] = ainv[i][j] + sum(u[i][k] * t[j][k] for k in range(h))
    return out


def sweep_base(cells, beside):
    tall = range(BASE // 8)
    tiles = [cells[8 * i : 8 * i + 8] for i in tall]
    lane = iota((8, LANES), 1)
    start = lane - lane % BASE
    inner = lane % BASE
    sub = iota((8, LANES), 0)

    def columns(first):
        return [
            [
                jnp.take_along_axis(tile, start + (first + t), axis=1, mode="promise_in_bounds")
                for tile in tiles
            ]
            for t in range(GROUP)
        ]

    def row(parts, r):
        return jnp.broadcast_to(parts[r // 8][r % 8 : r % 8 + 1, :], (8, LANES))

    def with_rows(parts, first, rows):
        part = parts[first // 8]
        for t, value in enumerate(rows):
            part = jnp.where(sub == first % 8 + t, value, part)
        return [part if i == first // 8 else parts[i] for i in tall]

    def less(parts, factor):
        out = []
        for i in tall:
            part = parts[i]
            for t in range(GROUP):
                part = part - cols[t][i] * factor[t]
            out.append(part)
        return out

    cols = columns(0)
    for first in range(0, BASE, GROUP):
        ahead = columns(first + GROUP) if first + GROUP < BASE else []
        pivots = [[None] * GROUP for _ in range(GROUP)]
        for t in range(GROUP):
            for u in range(t, GROUP):
                pivots[t][u] = pivots[u][t] = row(cols[u], first + t)
        inv = small_inverse(pivots)
        coming = []
        for col in ahead:
            head = [row(col, first + t) for t in range(GROUP)]
            factor = [sum(inv[t][u] * head[u] for u in range(GROUP)) for t in range(GROUP)]
            coming.append(with_rows(less(col, factor), first, factor))
        group = (inner >= first) & (inner < first + GROUP)
        rows = []
        for t in range(GROUP):
            value = jnp.where(group, 0.0, row(tiles, first + t))
            rows.append(jnp.where(inner == first + t, -1.0, value))
        new = [sum(inv[t][u] * rows[u] for u in range(GROUP)) for t in range(GROUP)]
        tiles = [jnp.where(group, 0.0, tile) for tile in tiles]
        tiles = with_rows(less(tiles, new), first, new)
        cols = coming
        if beside:
            beside.pop(0)()
    while beside:
        beside.pop(0)()
    return jnp.concatenate(tiles, axis=0)


def fetch(pairs, sems):
    copies = [pltpu.make_async_copy(a, b, sems.at[i]) for i, (a, b) in enumerate(pairs)]
    for copy in copies:
        copy.start()
    return copies


def invert_kernel(
    place_ref, probe_ref, feat_hbm, ids_hbm, agg_hbm, sys_hbm, cov_hbm, coarse_hbm, pat_hbm, len_hbm, noise_hbm,
    jac_ref, pack_ref, extra_ref,
    work, feat_ref, ids_ref, agg_ref, sys_ref, cov_ref, coarse_ref, pat_ref, len_ref, noise_ref, sems,
):
    blocks = work.shape[0]
    width = blocks * BS
    pairs = [
        (feat_hbm, feat_ref), (ids_hbm, ids_ref), (agg_hbm, agg_ref), (cov_hbm, cov_ref),
        (pat_hbm, pat_ref), (len_hbm, len_ref), (noise_hbm, noise_ref), (coarse_hbm, coarse_ref),
        (sys_hbm, sys_ref),
    ]
    for copy in fetch(pairs, sems):
        copy.wait()
    scaled = feat_ref[...] / column(len_ref, FEAT)
    ids = ids_ref[...].astype(f32).reshape(1, width)
    which = agg_ref[...].astype(f32).reshape(1, width)
    table = one_hot(ids, TASKS)
    noise = noise_row(noise_ref, ids)
    c0, c1, c2 = split(cov_ref[...], 3)
    tab = table.astype(bf16)
    picked = (dot(c2.astype(bf16), tab) + dot(c1.astype(bf16), tab)) + dot(c0.astype(bf16), tab)
    rows = iota((FEAT, width), 0)
    weights = jnp.zeros((1, width), f32)
    places = iota((1, width), 1)
    for m in range(blocks):
        for o in range(SLOTS):
            weights = jnp.where(places == m * SLOTS + o, weight(pat_ref, m, o), weights)
    pack_ref[0:FEAT, :] = scaled
    pack_ref[FEAT : 2 * FEAT, :] = jnp.where(
        rows == 0,
        ids,
        jnp.where(rows == 1, which, jnp.where(rows == 2, probe_ref[0].astype(f32), 0.0)),
    )
    extra_ref[0:TASKS, :] = picked
    tail = jnp.where(rows == 0, noise, jnp.where(rows == 1, weights, 0.0))
    held = coarse_ref.shape[0]
    inverse = jnp.concatenate(
        [coarse_ref[...], jnp.zeros((held, width - coarse_ref.shape[1]), f32)], axis=1
    )
    tail = jnp.where(rows == 2, place_ref[0].astype(f32), tail)
    for r in range(held):
        tail = jnp.where(rows == 3 + r, inverse[r : r + 1], tail)
    extra_ref[TASKS : TASKS + FEAT, :] = tail
    near = near_stack(scaled, table)
    mates, norm = own_stack(scaled, picked)
    eye = iota((BS, BS), 0) == iota((BS, BS), 1)
    for m in range(blocks):
        at = slice(m * BS, (m + 1) * BS)
        both = dot(near[at], mates[m])
        block = weight(pat_ref, m, REACH) * jnp.exp(both[:, :BS] + norm[:, at]) * both[:, BS:]
        work[m] = block + jnp.where(eye, noise[:, at], 0.0)
    seg = iota((BASE, LANES), 1) // BASE
    wide = iota((BASE, BS), 1)
    deep = iota((BASE, BS), 0)

    def packed(strips, first):
        tile, inside = first // LANES, first % LANES
        cells = jnp.zeros((BASE, LANES), f32)
        for m in range(blocks):
            piece = strips[m][:, tile * LANES : (tile + 1) * LANES]
            shift = (BASE * m - inside) % LANES
            if shift:
                piece = pltpu.roll(piece, shift, axis=1)
            cells = jnp.where(seg == m, piece, cells)
        return cells

    def diagonal(cells):
        parts = [jnp.where(seg == m, cells, 0.0) for m in range(LANES // BASE)]
        return jnp.concatenate(parts, axis=0)

    eye = jnp.where(iota((BASE, LANES), 1) % BASE == iota((BASE, LANES), 0), 1.0, 0.0)

    def updates(first, inv, strips):
        state = {}

        def product():
            held = (wide >= first) & (wide < first + BASE)
            minus = jnp.where(wide - first == deep, -1.0, 0.0)
            stack = jnp.concatenate(
                [jnp.where(held, minus, s) for s in strips]
                + [jnp.zeros((LANES - blocks * BASE, BS), f32)],
                axis=0,
            )
            spread = diagonal(inv)[: blocks * BASE]
            new = dot(spread, stack, precision=highest)
            for m in range(blocks):
                state[m] = new[m * BASE : (m + 1) * BASE, :]

        def rows_of(m, low, high):
            def piece():
                if (m, 0) not in state:
                    r0, r1, r2 = halves(strips[m], 3)
                    p0, p1, p2 = halves(state[m], 3)
                    state[m, 0] = jnp.concatenate([r0, r0, r1, r1, r0, r2], axis=0)
                    state[m, 1] = jnp.concatenate([p0, p1, p0, p1, p2, p0], axis=0)
                a, b = state[m, 0][:, low:high], state[m, 1]
                gone = (iota((1, BS), 1) >= first) & (iota((1, BS), 1) < first + BASE)
                work[m, low:high, :] = jnp.where(gone, 0.0, work[m, low:high, :]) - dot(a, b, TN)
                if low <= first < high:
                    work[m, first : first + BASE, :] = state[m]

            return piece

        half = BS // 2
        return [product] + [
            rows_of(m, low, low + half) for m in range(blocks) for low in range(0, BS, half)
        ]

    def strips_at(first):
        return [work[m, first : first + BASE, :] for m in range(blocks)]

    cells = jnp.where(seg < blocks, packed(strips_at(0), 0), eye)
    pending = []
    for first in range(0, BS, BASE):
        inv = -sweep_base(cells, pending)
        strips = strips_at(first)
        if first + BASE < BS:
            after = strips_at(first + BASE)
            half = dot(inv, diagonal(packed(strips, first + BASE)), precision=highest)
            drop = dot(packed(after, first), diagonal(half), precision=highest)
            cells = jnp.where(seg < blocks, packed(after, first + BASE) - drop, eye)
        pending = updates(first, inv, strips)
    for piece in pending:
        piece()
    for m in range(blocks):
        inv = -work[m]
        for i, part in enumerate(halves(inv, 3)):
            jac_ref[i, m] = part
    pack_ref[SYS:, :] = smooth(sys_ref[...], jac_ref)


def own_places(m):
    return [(j, j, REACH + j - m) for j in range(REACH)]


def halo_places(m):
    lefts = [(j - m, j, j - m) for j in range(m, REACH)]
    return lefts + [(REACH - m + j, REACH + j, 2 * REACH - m + j) for j in range(m + 1)]


def build_kernel(*refs, places, sides):
    cells, (own_ref, extra_ref) = refs[:sides], refs[sides : sides + 2]
    hi_ref, lo_ref, sim_ref, full_ref = refs[sides + 2 :]
    blocks = hi_ref.shape[0]
    near = []
    for ref in cells:
        near.append(near_stack(ref[0:FEAT, :], one_hot(ref[FEAT : FEAT + 1, :], TASKS)))
    mates, norm = own_stack(own_ref[0:FEAT, :], extra_ref[0:TASKS, :])
    weights = extra_ref[TASKS + 1 : TASKS + 2, :]
    for m in range(blocks):
        for row, j, o in places(m):
            part = near[j // REACH][(j % REACH) * BS : (j % REACH + 1) * BS]
            both = dot(part, mates[m])
            place = m * SLOTS + o
            exponent = both[:, :BS] + norm[:, m * BS : (m + 1) * BS]
            similar = weights[:, place : place + 1] * jnp.exp(exponent)
            kernel = similar * both[:, BS:]
            head = kernel.astype(bf16)
            rows = slice(row * BS, (row + 1) * BS)
            if o <= REACH or sides == 1:
                sim_ref[m, rows, :] = similar
                full_ref[m, rows, :] = kernel
            hi_ref[m, rows, :] = head
            lo_ref[m, rows, :] = (kernel - head.astype(f32)).astype(bf16)


def pieces(vectors):
    return jnp.concatenate(split(vectors, 2), axis=0).astype(bf16)


def apply(cells, hi, lo):
    rows = cells.shape[0] // 2
    first = dot(cells, hi)
    return first[:rows] + first[rows:] + dot(cells[:rows], lo)


def operate_own(own, noise, own_hi, own_lo):
    mine = pieces(own)
    out = [apply(mine, own_hi[m], own_lo[m]) for m in range(REACH)]
    return jnp.concatenate(out, axis=1) + noise * own


def operate_left(left, halo_hi, halo_lo):
    cells = pieces(left)
    out = []
    for m in range(REACH):
        part = slice(0, (REACH - m) * BS)
        out.append(apply(cells[:, m * BS :], halo_hi[m, part, :], halo_lo[m, part, :]))
    return jnp.concatenate(out, axis=1)


def operate_halo(left, right, halo_hi, halo_lo):
    lefts, rights = pieces(left), pieces(right)
    out = []
    for m in range(REACH):
        beyond = jnp.concatenate([lefts[:, m * BS :], rights[:, : (m + 1) * BS]], axis=1)
        out.append(apply(beyond, halo_hi[m], halo_lo[m]))
    return jnp.concatenate(out, axis=1)


def smooth_pieces(vectors, parts):
    rows = vectors.shape[0]
    cells = jnp.concatenate(split(vectors, 3), axis=0).astype(bf16)
    a = dot(cells, parts[0])
    b = dot(cells[: 2 * rows], parts[1])
    c = dot(cells[:rows], parts[2])
    return a[:rows] + (a[rows : 2 * rows] + b[:rows] + (a[2 * rows :] + b[rows:] + c))


def smooth(image, jac_ref):
    return jnp.concatenate(
        [
            smooth_pieces(image[:, m * BS : (m + 1) * BS], [jac_ref[i, m] for i in range(3)])
            for m in range(REACH)
        ],
        axis=1,
    )


def basis(pack_ref, coarse):
    z = one_hot(pack_ref[FEAT + 1 : FEAT + 2, :], coarse)
    return jnp.concatenate([pack_ref[SYS:, :], z], axis=0)


def build_own_kernel(own_ref, extra_ref, hi_ref, lo_ref, sim_ref, full_ref, part_ref):
    build_kernel(
        own_ref, own_ref, extra_ref, hi_ref, lo_ref, sim_ref, full_ref, places=own_places, sides=1
    )
    coarse = part_ref.shape[0] - (own_ref.shape[0] - SYS)
    noise = extra_ref[TASKS : TASKS + 1, :]
    part_ref[...] = operate_own(basis(own_ref, coarse), noise, hi_ref, lo_ref)


def first_kernel(part_ref, left_ref, right_ref, hi_ref, lo_ref, jac_ref, image_ref, next_ref):
    coarse = part_ref.shape[0] - (left_ref.shape[0] - SYS)
    ends = [basis(ref, coarse) for ref in (left_ref, right_ref)]
    image = part_ref[...] + operate_halo(*ends, hi_ref, lo_ref)
    image_ref[...] = image
    next_ref[...] = smooth(image, jac_ref)


def second_kernel(
    part_ref, left_ref, right_ref, sys_ref, hi_ref, lo_ref, jac_ref, image_ref, cargo_ref
):
    rows = part_ref.shape[0]
    image = part_ref[...] + operate_halo(left_ref[...], right_ref[...], hi_ref, lo_ref)
    image_ref[...] = image
    cargo_ref[0:rows, :] = smooth(image, jac_ref)
    cargo_ref[rows:, :] = sys_ref[...]


def pitch_of(coarse):
    return coarse + 1


def lanes_of(coarse):
    return -(-5 * pitch_of(coarse) // LANES) * LANES


def moment(vectors, images, pairs):
    count = pairs.shape[0]
    table = dot(images, vectors, NT, lax.Precision.HIGH)
    own = jnp.sum(pairs, axis=1, keepdims=True)
    if images.shape[0] > count:
        own = jnp.concatenate([own, jnp.zeros((images.shape[0] - count, 1), f32)], axis=0)
    return jnp.concatenate([table, own], axis=1)


def spread_out(parts, lanes):
    rows, pitch = next(iter(parts.values())).shape
    cells = [parts.get(k, jnp.zeros((rows, pitch), f32)) for k in range(5)]
    if lanes > 5 * pitch:
        cells.append(jnp.zeros((rows, lanes - 5 * pitch), f32))
    return jnp.concatenate(cells, axis=1)


def folded(low, high):
    order = low.shape[0]
    row, col = iota((order, order), 0), iota((order, order), 1)
    diagonal = jnp.sum(jnp.where(row == col, high, 0.0), axis=1, keepdims=True)
    return jnp.concatenate([jnp.where(row >= col, low, high), diagonal], axis=1)


def unfolded(cells):
    order = cells.shape[0]
    row, col = iota((order, order), 0), iota((order, order), 1)
    square = cells[:, :order]
    turned = dot(square, jnp.where(row == col, 1.0, 0.0), TN, highest)
    low = jnp.where(row >= col, square, turned)
    high = jnp.where(row < col, square, jnp.where(row > col, turned, cells[:, order:]))
    return low, high


def early_moments_kernel(
    own_ref, sys_ref, d1_ref, v0_ref, extra_ref, hi_ref, lo_ref, out_ref, part_ref
):
    part_ref[...] = operate_own(d1_ref[...], extra_ref[TASKS : TASKS + 1, :], hi_ref, lo_ref)
    count = own_ref.shape[0] - SYS
    coarse = d1_ref.shape[0] - count
    lanes = out_ref.shape[1]
    pitch = pitch_of(coarse)
    systems = sys_ref[...]
    pre = own_ref[SYS:, :]
    z = one_hot(own_ref[FEAT + 1 : FEAT + 2, :], coarse)
    d1, v0 = d1_ref[...], v0_ref[...]
    m0 = moment(z, v0, pre * v0[:count])
    m1 = moment(d1[count:], v0, d1[:count] * v0[:count])
    out_ref[0:count, :] = spread_out({0: m0[:count], 1: m1[:count]}, lanes)
    start = moment(z, systems, systems * pre)
    if coarse > count:
        start = jnp.concatenate([start, jnp.zeros((coarse - count, pitch), f32)], axis=0)
    fold = folded(m0[count:, :coarse], m1[count:, :coarse])
    out_ref[count:, :] = spread_out({0: fold, 3: start}, lanes)


def late_moments_kernel(
    before_ref, d1_ref, cargo_ref, v1_ref, extra_ref, hi_ref, lo_ref, out_ref, part_ref, *, count
):
    lanes = out_ref.shape[1]
    d1, d2, v1 = d1_ref[...], cargo_ref[0 : d1_ref.shape[0], :], v1_ref[...]
    part_ref[...] = operate_own(d2, extra_ref[TASKS : TASKS + 1, :], hi_ref, lo_ref)
    coarse = d1.shape[0] - count
    m2 = moment(d1[count:], v1, d1[:count] * v1[:count])
    m3 = moment(d2[count:], v1, d2[:count] * v1[:count])
    out_ref[0:count, :] = before_ref[0:count, :] + spread_out({2: m2[:count], 3: m3[:count]}, lanes)
    fold = folded(m2[count:, :coarse], m3[count:, :coarse])
    out_ref[count:, :] = before_ref[count:, :] + spread_out({1: fold}, lanes)


def third_kernel(
    extra_ref, before_ref, cargo_ref, left_ref, part_ref, hi_ref, lo_ref, out_ref, *, count, held
):
    rows = cargo_ref.shape[0] - count
    coarse = rows - count
    lanes = out_ref.shape[2]
    pitch = pitch_of(coarse)
    d2 = cargo_ref[0:rows, :]
    inner = part_ref[...]
    cross = operate_left(left_ref[0:rows, :], hi_ref, lo_ref)
    m4 = moment(d2[count:], inner + cross, d2[:count] * (inner + 2.0 * cross)[:count])
    mirror = dot(d2, cross[count:], NT, lax.Precision.HIGH)
    m4 = m4 + jnp.concatenate([mirror, jnp.zeros((rows, 1), f32)], axis=1)
    row = iota((coarse, 1), 0).astype(f32)
    start = extra_ref[TASKS + 2 : TASKS + 3, 0:1] * held
    inverse = jnp.zeros((coarse, pitch), f32)
    for r in range(held):
        line = extra_ref[TASKS + 3 + r : TASKS + 4 + r, 0:pitch]
        inverse = jnp.where(row == start + r, line, inverse)
    top = before_ref[0:count, :] + spread_out({4: m4[:count]}, lanes)
    bottom = before_ref[count:, :] + spread_out({2: m4[count:], 4: inverse}, lanes)
    for c in range(out_ref.shape[0]):
        out_ref[c, 0:count, :] = top
        out_ref[c, count:, :] = bottom


def final_kernel(
    gram_ref, own_ref, left_ref, d1_ref, d1l_ref, cargo_ref, cargol_ref, *refs, sides, points,
):
    kernel_refs, (grad_ref, sol_hbm, sol_ref, sem) = refs[:4], refs[4:]
    width = own_ref.shape[1]
    count = own_ref.shape[0] - SYS
    rows = d1_ref.shape[0]
    coarse = rows - count
    pitch = pitch_of(coarse)
    wide = -(-3 * pitch // LANES) * LANES
    blocks = width // BS
    gram = gram_ref[0]
    for c in range(1, gram_ref.shape[0]):
        gram = gram + gram_ref[c]
    bottom = gram[count:]
    gram = jnp.concatenate([gram[:count], jnp.zeros((count, wide), f32)], axis=1)
    squares = list(unfolded(bottom[:, :pitch])) + list(unfolded(bottom[:, pitch : 2 * pitch]))
    squares.append(bottom[:, 2 * pitch : 2 * pitch + coarse])
    lane = iota((1, wide), 1)
    slot, inside = lane // pitch, lane % pitch
    live = lane < 3 * pitch
    is_vec = live & (inside < coarse)
    is_one = live & (inside == coarse)

    def shifted(j):
        return jnp.where(live, gram[:, j * pitch : j * pitch + wide], 0.0)

    own = [shifted(j) for j in range(3)]
    gap = jnp.zeros((coarse, 1), f32)
    rest = jnp.zeros((coarse, wide - 3 * pitch), f32)
    hankel = []
    for i in range(3):
        line = [squares[i], gap, squares[i + 1], gap, squares[i + 2], gap]
        hankel.append(jnp.concatenate(line + ([rest] if wide > 3 * pitch else []), axis=1))
        hankel.append(jnp.zeros((1, wide), f32))
    if wide > 3 * pitch:
        hankel.append(jnp.zeros((wide - 3 * pitch, wide), f32))
    hankel = jnp.concatenate(hankel, axis=0)
    block0 = lane < pitch
    inverse = bottom[:, 4 * pitch : 4 * pitch + coarse]
    inverse = jnp.concatenate([inverse, jnp.zeros((coarse, wide - coarse), f32)], axis=1)
    inverse = jnp.concatenate([inverse, jnp.zeros((wide - coarse, wide), f32)], axis=0)
    start = bottom[:count, 3 * pitch : 4 * pitch]
    start = jnp.concatenate([start, jnp.zeros((count, wide - pitch), f32)], axis=1)
    against = jnp.where(
        block0, start, jnp.where(live, pltpu.roll(jnp.where(live, own[0], 0.0), pitch, axis=1), 0.0)
    )

    def total(x):
        return jnp.sum(x, axis=1, keepdims=True)

    hankel, inverse = halves(hankel, 3), halves(inverse, 3)

    def metric(u, chain):
        vec = smooth_pieces(jnp.where(is_vec, u, 0.0), hankel)
        for j in range(3):
            vec = vec + chain[j] * own[j]
        vec = jnp.where(is_vec, vec, 0.0)
        picked = [total(u * own[i]) for i in range(3)]
        out = vec
        for i in range(3):
            out = jnp.where(lane == i * pitch + coarse, picked[i], out)
        curve = total(u * vec)
        for i in range(3):
            curve = curve + chain[i] * picked[i]
        return out, curve

    def corrected(w):
        return smooth_pieces(jnp.where(lane < coarse, w, 0.0), inverse)

    one, zero = jnp.ones((count, 1), f32), jnp.zeros((count, 1), f32)
    pre = corrected(against) + jnp.where(lane == coarse, 1.0, 0.0)
    pre_chain = [one, zero, zero]
    direction, chain = pre, pre_chain
    gamma = total(pre * against)
    answer = jnp.zeros_like(pre)
    answer_chain = [zero] * 3
    image_sum = jnp.zeros_like(pre)
    for step in range(ITERS):
        image, curve = metric(direction, chain)
        alpha = gamma / curve
        answer = answer + alpha * direction
        answer_chain = [a + alpha * c for a, c in zip(answer_chain, chain)]
        if step + 1 < ITERS:
            image_sum = image_sum + alpha * image
            moved_on = jnp.where(live & (slot > 0), pltpu.roll(direction, pitch, axis=1), 0.0)
            pre = pre - alpha * (moved_on + corrected(image))
            pre_chain = [p - alpha * c for p, c in zip(pre_chain, [zero] + chain[:2])]
            gamma_new = total(pre * (against - image_sum))
            beta = gamma_new / gamma
            direction = pre + beta * direction
            chain = [p + beta * c for p, c in zip(pre_chain, chain)]
            gamma = gamma_new

    pack = jnp.concatenate([left_ref[...], own_ref[...]], axis=1)
    z = one_hot(pack[FEAT + 1 : FEAT + 2], coarse)
    q0 = pack[SYS:]
    d1 = jnp.concatenate([d1l_ref[...], d1_ref[...]], axis=1)
    cargo = jnp.concatenate([cargol_ref[...], cargo_ref[...]], axis=1)
    d2 = cargo[:rows]
    span = q0.shape[1]
    step = -(-coarse // FEAT) * FEAT
    deep = -(-3 * step // LANES) * LANES
    parts, planes = [], []
    for i, rest in enumerate((z, d1[count:], d2[count:])):
        parts.append(answer[:, i * pitch : i * pitch + coarse])
        planes.append(rest)
        if step > coarse:
            parts.append(jnp.zeros((count, step - coarse), f32))
            planes.append(jnp.zeros((step - coarse, span), f32))
    if deep > 3 * step:
        parts.append(jnp.zeros((count, deep - 3 * step), f32))
        planes.append(jnp.zeros((deep - 3 * step, span), f32))
    planes = halves(jnp.concatenate(planes, axis=0), 3)
    x = smooth_pieces(jnp.concatenate(parts, axis=1), planes)
    x = x + answer_chain[0] * q0 + answer_chain[1] * d1[:count] + answer_chain[2] * d2[:count]
    mine = slice(width, 2 * width)
    sol_ref[...] = x[:, mine]
    leave = pltpu.make_async_copy(sol_ref, sol_hbm, sem)
    leave.start()

    probe = own_ref[FEAT + 2 : FEAT + 3, 0:1]
    line = iota((count, 1), 0).astype(f32) + probe * count
    right = jnp.where(line == 0, x, cargo[rows:])
    coef = jnp.where(line == 0, 0.5 / points, -0.5 / (sides - 1) / points)
    r0, r1 = split(right, 2)
    w0, w1 = split(x * coef, 2)
    rest = jnp.zeros((LANES - 6 * count, span), f32)
    near = jnp.concatenate([w0, w1, w0, r0, r1, r0, rest], axis=0).T.astype(bf16)
    none = jnp.zeros((3 * count, width), f32)
    rest = rest[:, mine]
    ahead = jnp.concatenate([r0, r0, r1], axis=0)[:, mine]
    back = jnp.concatenate([w0, w0, w1], axis=0)[:, mine]
    mates = [
        jnp.concatenate([ahead, none, rest], axis=0).astype(bf16),
        jnp.concatenate([none, back, rest], axis=0).astype(bf16),
    ]
    scaled = pack[0:FEAT]
    table = one_hot(pack[FEAT : FEAT + 1], TASKS)
    ones = jnp.ones((8, span), f32)
    terms = jnp.concatenate([scaled, ones, scaled * scaled], axis=0)
    t0, t1 = split(terms, 2)
    pad8 = jnp.zeros((8, span), f32)
    both = jnp.concatenate([t0, pad8, t1, pad8], axis=0).astype(bf16)
    heads = jnp.concatenate([t0, pad8], axis=0).astype(bf16)
    tables = table.astype(bf16)
    high = 32
    length_total = jnp.zeros((FEAT, 1), f32)
    task_total = jnp.zeros((TASKS, TASKS), f32)
    for m in range(blocks):
        at = slice(m * BS, (m + 1) * BS)
        sums = jnp.zeros((high, BS), f32)
        held_sums = [jnp.zeros((TASKS, BS), f32) for _ in mates]
        places = [(1, row, j + REACH) for row, j, _ in own_places(m)]
        places += [(2, row, j) for row, j, _ in halo_places(m) if j < REACH]
        for orders, row, block in places:
            full_ref, sim_ref = kernel_refs[2 * orders - 2 : 2 * orders]
            j = slice(block * BS, (block + 1) * BS)
            rows_at = slice(row * BS, (row + 1) * BS)
            outers = [dot(near[j], mate[:, at]) for mate in mates[:orders]]
            similar = sim_ref[m, rows_at, :]
            energy = sum(outers[1:], outers[0]) * full_ref[m, rows_at, :]
            e0, e1 = halves(energy, 2)
            first = dot(both[:, j], e0)
            sums = sums + first[:high] + first[high:] + dot(heads[:, j], e1)
            for k in range(orders):
                h0, h1 = halves(outers[k] * similar, 2)
                held_sums[k] = held_sums[k] + dot(tables[:, j], h0) + dot(tables[:, j], h1)
        mid = slice(width + m * BS, width + (m + 1) * BS)
        left = scaled[:, mid]
        value = left * left * sums[FEAT : FEAT + 1] + sums[2 * FEAT : 3 * FEAT]
        value = value - 2.0 * left * sums[:FEAT]
        length_total = length_total + jnp.sum(value, axis=1, keepdims=True)
        task_total = task_total + dot(held_sums[0], table[:, mid], NT, highest)
        task_total = task_total + dot(table[:, mid], held_sums[1], NT, highest)
    half = TASKS // 2
    value = jnp.concatenate(
        [
            task_total[:half],
            task_total[half:],
            jnp.where(iota((half, FEAT), 0) == iota((half, FEAT), 1), length_total, 0.0),
            jnp.zeros((half, LANES - 2 * TASKS - FEAT), f32),
        ],
        axis=1,
    )
    for c in range(grad_ref.shape[0]):
        grad_ref[c] = value
    leave.wait()


def tail_kernel(parts_ref, length_ref, task_ref):
    total = parts_ref[0]
    for c in range(1, parts_ref.shape[0]):
        total = total + parts_ref[c]
    half = TASKS // 2
    task_ref[0:half, :] = total[:, :TASKS]
    task_ref[half:, :] = total[:, TASKS : 2 * TASKS]
    length_ref[...] = jnp.sum(total[:, 2 * TASKS : 2 * TASKS + FEAT], axis=0)


MIB = 1024 * 1024


def call(body, outs, args, name, smem=0, hbm=0, far_outs=0, scratch=(), flops=0, limit=16):
    if hbm:
        args = args[:-hbm] + [pltpu.with_memory_space_constraint(a, pltpu.HBM) for a in args[-hbm:]]
    if far_outs:
        outs = outs[:-far_outs] + [pltpu.HBM(o.shape, o.dtype) for o in outs[-far_outs:]]
    vm = pl.BlockSpec(memory_space=pltpu.VMEM)
    sm = pl.BlockSpec(memory_space=pltpu.SMEM)
    far = pl.BlockSpec(memory_space=pltpu.HBM)
    return pl.pallas_call(
        body,
        out_shape=outs,
        in_specs=[sm] * smem + [vm] * (len(args) - smem - hbm) + [far] * hbm,
        out_specs=[vm] * (len(outs) - far_outs) + [far] * far_outs,
        scratch_shapes=scratch,
        compiler_params=pltpu.CompilerParams(vmem_limit_bytes=limit * MIB),
        cost_estimate=pl.CostEstimate(flops=flops, bytes_accessed=1 << 20, transcendentals=0),
        name=name,
    )(*args)


def both_sides(cells):
    count = lax.axis_size("pts")
    up = [(i, i + 1) for i in range(count - 1)]
    down = [(i + 1, i) for i in range(count - 1)]
    return lax.ppermute(cells, "pts", up), lax.ppermute(cells, "pts", down)


def from_left(cells):
    count = lax.axis_size("pts")
    return lax.ppermute(cells, "pts", [(i, i + 1) for i in range(count - 1)])


def shards(
    systems, features, task_ids, pattern, aggregate, coarse_inverse, task_cov, lengthscales, noise
):
    count, width = systems.shape
    blocks = width // BS
    coarse = coarse_inverse.shape[1]
    rows = count + coarse
    lanes = lanes_of(coarse)
    assert blocks == REACH
    place = lax.axis_index("pts").astype(jnp.int32)[None]
    probe = lax.axis_index("probe").astype(jnp.int32)[None]
    ranks = lax.axis_size("pts")
    sides = lax.axis_size("probe")

    def shape(*dims, kind=f32):
        return jax.ShapeDtypeStruct(dims, kind)

    jac, pack, extra = call(
        invert_kernel,
        [shape(3, blocks, BS, BS, kind=bf16), shape(SYS + count, width), shape(TASKS + FEAT, width)],
        [place, probe, features, task_ids, aggregate, systems, task_cov, coarse_inverse, pattern, lengthscales, noise],
        "invert",
        smem=2,
        hbm=9,
        scratch=[
            pltpu.VMEM((blocks, BS, BS), f32),
            pltpu.VMEM(features.shape, f32),
            pltpu.VMEM(task_ids.shape, jnp.int32),
            pltpu.VMEM(aggregate.shape, jnp.int32),
            pltpu.VMEM(systems.shape, f32),
            pltpu.VMEM(task_cov.shape, f32),
            pltpu.VMEM(coarse_inverse.shape, f32),
            pltpu.SMEM(pattern.shape, jnp.int32),
            pltpu.SMEM(lengthscales.shape, f32),
            pltpu.SMEM(noise.shape, f32),
            pltpu.SemaphoreType.DMA((9,)),
        ],
        flops=10**10,
    )
    pack_l, pack_r = both_sides(pack)

    def cells_of(deep):
        return [
            shape(blocks, deep, BS, kind=bf16),
            shape(blocks, deep, BS, kind=bf16),
            shape(blocks, deep, BS),
            shape(blocks, deep, BS),
        ]

    own_hi, own_lo, own_sim, own_full, part = call(
        build_own_kernel,
        cells_of(width) + [shape(rows, width)],
        [pack, extra],
        "build_own",
        flops=10**9,
    )
    halo_hi, halo_lo, halo_sim, halo_full = call(
        functools.partial(build_kernel, places=halo_places, sides=2),
        cells_of(BAND - width),
        [pack_l, pack_r, pack, extra],
        "build_halo",
        flops=10**9,
    )
    own, halo = [own_hi, own_lo], [halo_hi, halo_lo]
    v0, d1 = call(
        first_kernel,
        [shape(rows, width), shape(rows, width)],
        [part, pack_l, pack_r] + halo + [jac],
        "first",
        flops=10**9,
    )
    d1_l, d1_r = both_sides(d1)
    early, part = call(
        early_moments_kernel,
        [shape(rows, lanes), shape(rows, width)],
        [pack, systems, d1, v0, extra] + own,
        "early",
        flops=10**9,
    )
    v1, cargo = call(
        second_kernel,
        [shape(rows, width), shape(rows + count, width)],
        [part, d1_l, d1_r, systems] + halo + [jac],
        "second",
        flops=10**9,
    )
    cargo_l = from_left(cargo)
    late, part = call(
        functools.partial(late_moments_kernel, count=count),
        [shape(rows, lanes), shape(rows, width)],
        [early, d1, cargo, v1, extra] + own,
        "late",
        flops=10**9,
    )
    (gram,) = call(
        functools.partial(third_kernel, count=count, held=coarse_inverse.shape[0]),
        [shape(ranks, rows, lanes)],
        [extra, late, cargo, cargo_l, part] + halo,
        "third",
        flops=10**9,
    )
    gram = lax.all_to_all(gram, "pts", 0, 0, tiled=True)
    cells = [own_full, own_sim, halo_full, halo_sim]
    grads, answer = call(
        functools.partial(final_kernel, sides=sides * count, points=ranks * width),
        [shape(ranks * sides, FEAT, LANES), shape(count, width)],
        [gram, pack, pack_l, d1, d1_l, cargo, cargo_l] + cells,
        "final",
        far_outs=1,
        scratch=[pltpu.VMEM((count, width), f32), pltpu.SemaphoreType.DMA],
        flops=10**9,
    )
    grads = lax.all_to_all(grads, ("pts", "probe"), 0, 0, tiled=True)
    lengths, tasks = call(
        tail_kernel, [shape(FEAT), shape(TASKS, TASKS)], [grads], "tail", flops=10**5
    )
    return answer, lengths, tasks


def solution(mesh):
    return jax.shard_map(
        shards,
        mesh=mesh,
        in_specs=(
            P("probe", ("groups", "pts")),
            P(None, ("groups", "pts")),
            P(("groups", "pts")),
            P(("groups", "pts"), None),
            P(("groups", "pts")),
            P(("groups", "pts"), None),
            P("groups", None),
            P("groups"),
            P("groups"),
        ),
        out_specs=(P("probe", ("groups", "pts")), P("groups"), P("groups", None)),
        check_vma=False,
    )
```
